32 devices in a mesh: parts: 2 (over x), fft: 16 (over z, y, core).
Axes of the slice: x: 2, y: 2, z: 4, core: 2. Of those that a mesh axis runs over, the one named last changes fastest.
Arguments:
- potential: float32 [4, 2048, 4096], P('parts', 'fft'), parts along dimension 0, may hold values from -1.2 to 1.2
- direction: float32 [4, 2048, 4096], P('parts', 'fft'), parts along dimension 0, may hold values from -6 to 6
- block_index: int32 [2, 32, 2], replicated, may hold values from 0 to 31
- block_weights: float32 [2, 32, 2, 128, 128], replicated, may hold values from -0.375 to 0.375
Outputs:
- hessian_product: float32 [4, 2048, 4096], P('parts', 'fft'), parts along dimension 0
The draws below stay inside these ranges and needn't reach their ends.
There are 2 independent parts, one for each index of `parts`. The reference program is written for one: setup_inputs(seed, part) draws one part's arguments, and reference() takes and returns one part's arrays. A program takes and returns all parts, laid end to end along the dimension named above; an argument that names none is the same for every part. Nothing has to cross between parts.
All inputs are finite; a program needn't handle non-finite values.
Results may differ from the reference program's by a relative error of at most 0.00018.
Values sent between devices are 32-bit elements; how exact they have to be, the bound alone decides.
No kernel may reach another device: no remote copies, remote signals or barrier semaphores. Data moves between devices by JAX's collectives and lax.ppermute only.
A program may use at most 256 MiB of HBM per device.

```python
import math
import jax
import jax.numpy as jnp
from jax import lax

NX = 2048
SL = 2
ANGLES = 2
BLK = 128
SLOTS = 2
NB = 32


def set_ends(values, stream_key, smallest, top_value):
    shape = values.shape
    index_at = [jax.random.randint(jax.random.fold_in(stream_key, axis), (), 0, shape[axis]) for axis in range(len(shape))]
    values = values.at[tuple(index_at)].set(smallest)
    longest = shape.index(max(shape))
    index_at[longest] = (index_at[longest] + 1) % shape[longest]
    return values.at[tuple(index_at)].set(top_value)


def level_of(own_key, shape, cuts, smallest, top_value):
    gain = 1.0
    for dim, shards_of in cuts:
        draws = jax.random.uniform(jax.random.fold_in(jax.random.fold_in(own_key, 6), dim), (shards_of,), jnp.float32, smallest / len(cuts), top_value / len(cuts))
        gain = gain * jnp.repeat(jnp.exp(draws), shape[dim] // shards_of).reshape((-1,) + (1,) * (len(shape) - 1 - dim))
    return gain


def noise(rng, shape, width, reach, pieces=(), kind=jnp.bfloat16):
    entries = width * jax.random.normal(rng, shape, jnp.float32)
    if pieces:
        entries = entries * level_of(rng, shape, pieces, -0.22, 0.18)
    return jnp.clip(entries, -reach, reach).astype(kind)


def setup_inputs(seed: int = 0, part: int = 0) -> dict:
    key_of = jax.random.split(jax.random.key(seed), 5)
    part_keys = jax.random.split(jax.random.fold_in(key_of[4], part), 5)
    potential = noise(part_keys[0], (2, NX, SL * NX), 0.3, 1.2, ((1, 16),), jnp.float32)
    direction = noise(part_keys[1], (2, NX, SL * NX), 1.0, 6.0, ((1, 16),), jnp.float32)
    block_index = set_ends(jax.random.randint(key_of[2], (ANGLES, NB, SLOTS), 0, NB), jax.random.fold_in(key_of[2], 1), 0, NB - 1).astype(jnp.int32)
    block_weights = noise(key_of[3], (ANGLES, NB, SLOTS, BLK, BLK), (BLK * SLOTS) ** -0.5, 0.375, (), jnp.float32)
    return dict(potential=potential, direction=direction, block_index=block_index, block_weights=block_weights)


PRECISE = lax.Precision.HIGHEST


def one_hot(index_rows):
    return (index_rows[..., None] == jnp.arange(NB, dtype=jnp.int32)).astype(jnp.float32)


def rotate(values, selector, matrices):
    height = values.shape[1]
    blocked = values.reshape(2, height, NB, BLK)
    picked = jnp.einsum('cyni,bsn->cybsi', blocked, selector, precision=PRECISE)
    rotated = jnp.einsum('cybsi,bsio->cybo', picked, matrices, precision=PRECISE)
    return rotated.reshape(2, height, SL, NX)


def rotate_back(values, selector, matrices):
    height = values.shape[1]
    blocked = values.reshape(2, height, NB, BLK)
    spread_out = jnp.einsum('cybo,bsio->cybsi', blocked, matrices, precision=PRECISE)
    summed = jnp.einsum('cybsi,bsn->cyni', spread_out, selector, precision=PRECISE)
    return summed.reshape(2, height, SL * NX)


def kernel_phase(orient):
    wavenumber = jnp.arange(NX, dtype=jnp.int32)
    signed_k = jnp.where(wavenumber < NX // 2, wavenumber, wavenumber - NX)
    squares = (signed_k[:, None] * signed_k[:, None] + signed_k[None, :] * signed_k[None, :]) % (2 * NX)
    phases = (orient * -math.pi / NX) * squares.astype(jnp.float32)
    return lax.complex(jnp.cos(phases), jnp.sin(phases))


def propagate(real_part, imag_part, kernel):
    spectrum = jnp.fft.fft2(lax.complex(real_part, imag_part))
    result = jnp.fft.ifft2(spectrum * kernel)
    return jnp.real(result), jnp.imag(result)


def reference(potential, direction, block_index, block_weights):
    height = potential.shape[1]
    ahead = kernel_phase(1.0)
    behind = kernel_phase(-1.0)
    accumulated = jnp.zeros(potential.shape, jnp.float32)
    for angle_index in range(ANGLES):
        selector = one_hot(block_index[angle_index])
        matrices = block_weights[angle_index]
        rotated = rotate(potential, selector, matrices)
        tangent = rotate(direction, selector, matrices)
        damping = jnp.exp(-rotated[1])
        trans_re = damping * jnp.cos(rotated[0])
        trans_im = damping * jnp.sin(rotated[0])
        wave_re = jnp.ones((height, NX), jnp.float32)
        wave_im = jnp.zeros((height, NX), jnp.float32)
        dwave_re = jnp.zeros((height, NX), jnp.float32)
        dwave_im = jnp.zeros((height, NX), jnp.float32)
        stored = []
        for slice_index in range(SL):
            t_re = trans_re[:, slice_index]
            t_im = trans_im[:, slice_index]
            d_re = tangent[0][:, slice_index]
            d_im = tangent[1][:, slice_index]
            phi_re = t_re * wave_re - t_im * wave_im
            phi_im = t_re * wave_im + t_im * wave_re
            dphi_re = -(d_re * phi_im + d_im * phi_re) + t_re * dwave_re - t_im * dwave_im
            dphi_im = (d_re * phi_re - d_im * phi_im) + t_re * dwave_im + t_im * dwave_re
            stored.append((phi_re, phi_im))
            wave_re, wave_im = propagate(phi_re, phi_im, ahead)
            dwave_re, dwave_im = propagate(dphi_re, dphi_im, ahead)
        change = 2.0 * (wave_re * dwave_re + wave_im * dwave_im)
        back_re = 2.0 * change * wave_re
        back_im = 2.0 * change * wave_im
        grad_re = [None] * SL
        grad_im = [None] * SL
        for slice_index in reversed(range(SL)):
            pb_re, pb_im = propagate(back_re, back_im, behind)
            phi_re, phi_im = stored[slice_index]
            grad_re[slice_index] = phi_re * pb_im - phi_im * pb_re
            grad_im[slice_index] = -(phi_re * pb_re + phi_im * pb_im)
            t_re = trans_re[:, slice_index]
            t_im = trans_im[:, slice_index]
            back_re = t_re * pb_re + t_im * pb_im
            back_im = t_re * pb_im - t_im * pb_re
        gradient = jnp.stack([jnp.stack(grad_re, axis=1), jnp.stack(grad_im, axis=1)])
        accumulated = accumulated + rotate_back(gradient, selector, matrices)
    return accumulated
```

```python
import functools
import math

import jax
import jax.numpy as jnp
import numpy as np
from jax import lax
from jax.experimental import pallas as pl
from jax.experimental.pallas import tpu as pltpu
from jax.sharding import PartitionSpec as P

XA = 16
XB = 128
NX = 2048
SL = 2
ANGLES = 2
BLK = 128
NB = 32
SLOTS = 2
STRIP = 16
LANES = 128


PRECISE = lax.Precision.HIGHEST


def bin_matrices():
    wavenumber = np.arange(NX)
    signed = np.where(wavenumber < NX // 2, wavenumber, wavenumber - NX)
    factor = np.exp(-1j * np.pi / NX * ((signed * signed) % (2 * NX)))
    line = np.fft.ifft(factor)
    block = np.arange(XA)
    inner = np.arange(XB)
    shifts = (XB * block[:, None, None] + inner[None, :, None] - inner[None, None, :]) % NX
    phases = np.exp(-2j * np.pi / XA * ((block[:, None] * block[None, :]) % XA))
    return np.einsum("kd,dij->kij", phases, line[shifts]) / XA


def split_constant(values):
    values = values.astype(np.float32)
    high = values.astype(jnp.bfloat16)
    low = (values - high.astype(np.float32)).astype(jnp.bfloat16)
    return high, low


def column_constants():
    bins = bin_matrices()
    top = np.concatenate([bins.real, -bins.imag], axis=2)
    bottom = np.concatenate([bins.imag, bins.real], axis=2)
    return np.concatenate([top, bottom], axis=1)


def fourth(values, orient):
    (ar, ai), (br, bi), (cr, ci), (dr, di) = values
    sr, si, er, ei = ar + cr, ai + ci, ar - cr, ai - ci
    tr, ti, fr, fi = br + dr, bi + di, br - dr, bi - di
    minus, plus = (er + fi, ei - fr), (er - fi, ei + fr)
    one, three = (minus, plus) if orient < 0 else (plus, minus)
    return [(sr + tr, si + ti), one, (sr - tr, si - ti), three]


def turned(value, step, orient):
    re, im = value
    if step == 0:
        return value
    if step == 4:
        return (im, -re) if orient < 0 else (-im, re)
    cosine = math.cos(2.0 * math.pi * step / XA)
    sine = orient * math.sin(2.0 * math.pi * step / XA)
    if step == 2:
        root = cosine
        return ((re - im) * root, (re + im) * root) if orient > 0 else ((re + im) * root, (im - re) * root)
    return (re * cosine - im * sine, re * sine + im * cosine)


def sixteenth(values, orient):
    inner = [fourth([values[4 * a + b] for a in range(4)], orient) for b in range(4)]
    out = [None] * XA
    for c in range(4):
        row = fourth([turned(inner[b][c], b * c, orient) for b in range(4)], orient)
        for d in range(4):
            out[c + 4 * d] = row[d]
    return out


def halves(value):
    high = value.astype(jnp.bfloat16)
    return high, (value - high.astype(jnp.float32)).astype(jnp.bfloat16)


def dot32(a, b):
    return jnp.dot(a, b, preferred_element_type=jnp.float32)


def times(a, b):
    return (a[0] * b[0] - a[1] * b[1], a[0] * b[1] + a[1] * b[0])


def sincos(x):
    turns = jnp.floor(x * (2.0 / math.pi) + 0.5)
    rest = ((x - turns * 1.5703125) - turns * 4.837512969970703125e-4) - turns * 7.54978995489188216e-8
    square = rest * rest
    sine = rest + rest * square * (
        -1.6666654611e-1 + square * (8.3321608736e-3 + square * -1.9515295891e-4)
    )
    cosine = (1.0 - 0.5 * square) + square * square * (
        4.166664568298827e-2 + square * (-1.388731625493765e-3 + square * 2.443315711809948e-5)
    )
    quadrant = turns.astype(jnp.int32)
    odd = (quadrant & 1) == 1
    first = jnp.where(odd, cosine, sine)
    second = jnp.where(odd, sine, cosine)
    first = jnp.where((quadrant & 2) == 2, -first, first)
    second = jnp.where(((quadrant + 1) & 2) == 2, -second, second)
    return first, second


def strips(count, step):
    def run(i, carry):
        step(pl.multiple_of(i * STRIP, STRIP))
        return carry

    lax.fori_loop(0, count // STRIP, run, 0)


def rows_out(xhi, xlo, first_row, values):
    for k, (re, im) in enumerate(sixteenth(values, -1.0)):
        for part, value in enumerate((re, im)):
            high, low = halves(value)
            at = (k, pl.ds(first_row, STRIP), pl.ds(part * LANES, LANES))
            xhi[at] = high
            xlo[at] = low


def rows_in(y, first_row):
    values = [
        tuple(y[k, pl.ds(first_row, STRIP), pl.ds(part * LANES, LANES)] for part in range(2))
        for k in range(XA)
    ]
    return sixteenth(values, 1.0)


def rows_mix(xhi, xlo, mhi, mlo, y):
    def step(k, carry):
        high, low = xhi[k], xlo[k]
        y[k] = dot32(high, mhi[k]) + (dot32(low, mhi[k]) + dot32(high, mlo[k]))
        return carry

    lax.fori_loop(0, XA, step, 0)


def columns_out(xhi, xlo, field, row, values):
    for k, (re, im) in enumerate(sixteenth(values, -1.0)):
        for part, value in enumerate((re, im)):
            high, low = halves(value)
            at = (k, pl.ds(part * XB + row, STRIP), pl.ds(field * LANES, LANES))
            xhi[at] = high
            xlo[at] = low


def columns_in(y, field, row):
    values = [
        tuple(
            y[k, pl.ds(part * XB + row, STRIP), pl.ds(field * LANES, LANES)] for part in range(2)
        )
        for k in range(XA)
    ]
    return sixteenth(values, 1.0)


def columns_mix(xhi, xlo, mhi, mlo, y):
    def step(k, carry):
        high, low = xhi[k], xlo[k]
        y[k] = dot32(mhi[k], high) + (dot32(mhi[k], low) + dot32(mlo[k], high))
        return carry

    lax.fori_loop(0, XA, step, 0)


def enter_kernel(
    index, potential, direction, whi, wlo, mhi, mlo, uv, td, t0, shi, slo, field, xhi, xlo, y
):
    rows = potential.shape[1]

    for number, (source, channel) in enumerate(
        ((potential, 0), (potential, 1), (direction, 0), (direction, 1))
    ):

        def cut(row, number=number, source=source, channel=channel):
            high, low = halves(source[channel, pl.ds(row, STRIP), :])
            at = pl.ds(pl.multiple_of(number * rows + row, STRIP), STRIP)
            shi[at, :] = high
            slo[at, :] = low

        strips(rows, cut)

    def rotated(b):
        at = [pl.ds(pl.multiple_of(index[b, s] * BLK, BLK), BLK) for s in range(SLOTS)]
        high = jnp.concatenate([shi[:, a] for a in at], axis=1)
        low = jnp.concatenate([slo[:, a] for a in at], axis=1)
        values = dot32(high, whi[b]) + (dot32(low, whi[b]) + dot32(high, wlo[b]))
        angle, loss, d_re, d_im = (values[i * rows : (i + 1) * rows] for i in range(4))
        sine, cosine = sincos(angle)
        damping = jnp.exp(-loss)
        return damping * cosine, damping * sine, d_re, d_im

    def first_slice(b, carry):
        t_re, t_im, d_re, d_im = rotated(b)
        t0[b, 0] = t_re
        t0[b, 1] = t_im
        field[b, 0] = -(d_re * t_im + d_im * t_re)
        field[b, 1] = d_re * t_re - d_im * t_im
        return carry

    lax.fori_loop(0, XA, first_slice, 0)

    def forward(row):
        at = pl.ds(row, STRIP)
        rows_out(xhi, xlo, row, [(t0[b, 0, at, :], t0[b, 1, at, :]) for b in range(XA)])
        rows_out(
            xhi,
            xlo,
            pl.multiple_of(rows + row, STRIP),
            [(field[b, 0, at, :], field[b, 1, at, :]) for b in range(XA)],
        )

    strips(rows, forward)
    rows_mix(xhi, xlo, mhi, mlo, y)

    def backward(row):
        at = pl.ds(row, STRIP)
        for number in range(2):
            values = rows_in(y, pl.multiple_of(number * rows + row, STRIP))
            for b, (re, im) in enumerate(values):
                uv[b, 2 * number, at, :] = re
                uv[b, 2 * number + 1, at, :] = im

    strips(rows, backward)

    def second_slice(b, carry):
        for channel, value in enumerate(rotated(XA + b)):
            td[b, channel] = value
        return carry

    lax.fori_loop(0, XA, second_slice, 0)


def row_places(mixed):
    same = list(range(XA))
    if not mixed:
        return [(0, XB, same)]
    swapped = [p ^ (XA // 2) for p in same]
    step = XB // 4
    return [(i * step, step, swapped if i % 2 == 0 else same) for i in range(4)]


def column_strips(mixed, step):
    for first, count, places in row_places(mixed):
        strips(count, lambda row, first=first, places=places: step(pl.multiple_of(first + row, STRIP), places))


def middle_kernel(mixed, chunks, *refs):
    uv, td = refs[:chunks], refs[chunks : 2 * chunks]
    mhi, mlo, out, phi, xhi, xlo, y = refs[2 * chunks :]
    rows = XB // chunks

    def chunked(step):
        for first, count, places in row_places(mixed):
            for piece in range(0, count, min(count, rows)):
                start = first + piece
                c, local = start // rows, start % rows

                def inner(row, start=start, c=c, local=local, places=places):
                    step(
                        pl.multiple_of(start + row, STRIP),
                        c,
                        pl.ds(pl.multiple_of(local + row, STRIP), STRIP),
                        places,
                    )

                strips(min(count, rows), inner)

    def forward(row, c, local, places):
        for number in range(2):
            columns_out(
                xhi,
                xlo,
                number,
                row,
                [tuple(uv[c][g, 2 * number + i, local, :] for i in range(2)) for g in places],
            )

    chunked(forward)
    columns_mix(xhi, xlo, mhi, mlo, y)

    def turn(row, c, local, places):
        at = pl.ds(row, STRIP)
        wave = columns_in(y, 0, row)
        product = []
        for g, value in zip(places, wave):
            value = times((td[c][g, 0, local, :], td[c][g, 1, local, :]), value)
            phi[g, 0, at, :] = value[0]
            phi[g, 1, at, :] = value[1]
            product.append(value)
        columns_out(xhi, xlo, 0, row, product)
        dwave = columns_in(y, 1, row)
        change = []
        for g, value in zip(places, dwave):
            t_re, t_im, d_re, d_im = (td[c][g, i, local, :] for i in range(4))
            p_re, p_im = phi[g, 0, at, :], phi[g, 1, at, :]
            re, im = times((t_re, t_im), value)
            change.append((re - (d_re * p_im + d_im * p_re), im + (d_re * p_re - d_im * p_im)))
        columns_out(xhi, xlo, 1, row, change)

    chunked(turn)
    columns_mix(xhi, xlo, mhi, mlo, y)

    def backward(row, c, local, places):
        at = pl.ds(row, STRIP)
        for number in range(2):
            for g, (re, im) in zip(places, columns_in(y, number, row)):
                out[g, 2 * number, at, :] = re
                out[g, 2 * number + 1, at, :] = im

    chunked(backward)


def detector_kernel(fields, mhi, mlo, out, xhi, xlo, y):
    rows = fields.shape[2]

    def forward(row):
        at = pl.ds(row, STRIP)
        for number in range(2):
            rows_out(
                xhi,
                xlo,
                pl.multiple_of(number * rows + row, STRIP),
                [tuple(fields[b, 2 * number + i, at, :] for i in range(2)) for b in range(XA)],
            )

    strips(rows, forward)
    rows_mix(xhi, xlo, mhi, mlo, y)

    def turn(row):
        wave = rows_in(y, row)
        dwave = rows_in(y, pl.multiple_of(rows + row, STRIP))
        back = []
        for (re, im), (d_re, d_im) in zip(wave, dwave):
            change = 4.0 * (re * d_re + im * d_im)
            back.append((change * re, -(change * im)))
        rows_out(xhi, xlo, row, back)

    strips(rows, turn)

    def step(k, carry):
        high, low = xhi[k, :rows, :], xlo[k, :rows, :]
        y[k, :rows, :] = dot32(high, mhi[k]) + (dot32(low, mhi[k]) + dot32(high, mlo[k]))
        return carry

    lax.fori_loop(0, XA, step, 0)

    def backward(row):
        at = pl.ds(row, STRIP)
        for b, (re, im) in enumerate(rows_in(y, row)):
            out[b, 0, at, :] = re
            out[b, 1, at, :] = im

    strips(rows, backward)


def return_kernel(mixed, chunks, back, phi, *refs):
    td = refs[:chunks]
    mhi, mlo, out, xhi, xlo, y = refs[chunks:]
    rows = XB // chunks

    def chunked(step):
        for first, count, places in row_places(mixed):
            for piece in range(0, count, min(count, rows)):
                start = first + piece
                c, local = start // rows, start % rows

                def inner(row, start=start, c=c, local=local, places=places):
                    step(
                        pl.multiple_of(start + row, STRIP),
                        c,
                        pl.ds(pl.multiple_of(local + row, STRIP), STRIP),
                        places,
                    )

                strips(min(count, rows), inner)

    def forward(row, c, local, places):
        at = pl.ds(row, STRIP)
        columns_out(xhi, xlo, 0, row, [(back[g, 0, at, :], back[g, 1, at, :]) for g in places])

    chunked(forward)
    columns_mix(xhi, xlo, mhi, mlo, y)

    def turn(row, c, local, places):
        at = pl.ds(row, STRIP)
        pulled = columns_in(y, 0, row)
        following = []
        for g, value in zip(places, pulled):
            re, im = times((phi[g, 0, at, :], phi[g, 1, at, :]), value)
            out[g, 0, at, :] = -im
            out[g, 1, at, :] = -re
            following.append(times((td[c][g, 0, local, :], td[c][g, 1, local, :]), value))
        columns_out(xhi, xlo, 0, row, following)

    chunked(turn)
    columns_mix(xhi, xlo, mhi, mlo, y)

    def backward(row, c, local, places):
        at = pl.ds(row, STRIP)
        for g, (re, im) in zip(places, columns_in(y, 0, row)):
            out[g, 2, at, :] = re
            out[g, 3, at, :] = im

    chunked(backward)


def leave_kernel(index, back, t0, whi, wlo, mhi, mlo, *refs):
    before, (out, shi, slo, xhi, xlo, y) = refs[:-6], refs[-6:]
    rows = back.shape[2]

    def forward(row):
        at = pl.ds(row, STRIP)
        rows_out(xhi, xlo, row, [(back[b, 2, at, :], back[b, 3, at, :]) for b in range(XA)])
        for b in range(XA):
            for i in range(2):
                high, low = halves(back[b, i, at, :])
                place = pl.ds(pl.multiple_of(i * rows + row, STRIP), STRIP)
                shi[XA + b, place, :] = high
                slo[XA + b, place, :] = low

    strips(rows, forward)
    rows_mix(xhi, xlo, mhi, mlo, y)

    def turn(row):
        at = pl.ds(row, STRIP)
        for b, value in enumerate(rows_in(y, row)):
            re, im = times((t0[b, 0, at, :], t0[b, 1, at, :]), value)
            for i, part in enumerate((-im, -re)):
                high, low = halves(part)
                place = pl.ds(pl.multiple_of(i * rows + row, STRIP), STRIP)
                shi[b, place, :] = high
                slo[b, place, :] = low

    strips(rows, turn)

    if before:
        out[...] = before[0][...]
    else:
        out[...] = jnp.zeros(out.shape, jnp.float32)

    def across(a, b):
        return lax.dot_general(
            a, b, (((1,), (1,)), ((), ())), preferred_element_type=jnp.float32
        )

    def step(b, carry):
        high, low = shi[b], slo[b]
        values = across(high, whi[b]) + (across(low, whi[b]) + across(high, wlo[b]))
        for s in range(SLOTS):
            at = pl.ds(pl.multiple_of(index[b, s] * BLK, BLK), BLK)
            for i in range(2):
                out[i, :, at] += values[i * rows : (i + 1) * rows, s * BLK : (s + 1) * BLK]
        return carry

    lax.fori_loop(0, NB, step, 0)


def call(kernel, outs, scratch, mix_count, extra, *operands):
    specs = [
        pl.BlockSpec(memory_space=pltpu.SMEM if o.dtype == jnp.int32 else pltpu.VMEM)
        for o in operands
    ]
    moved = sum(o.size * o.dtype.itemsize for o in operands) + sum(4 * math.prod(o) for o in outs)
    return pl.pallas_call(
        kernel,
        out_shape=[jax.ShapeDtypeStruct(o, jnp.float32) for o in outs],
        in_specs=specs,
        out_specs=[pl.BlockSpec(memory_space=pltpu.VMEM)] * len(outs),
        scratch_shapes=scratch,
        compiler_params=pltpu.CompilerParams(vmem_limit_bytes=60 * 1024 * 1024),
        cost_estimate=pl.CostEstimate(
            flops=mix_count * 16 * 128 * 256 * 256 * 6 + extra,
            bytes_accessed=moved,
            transcendentals=0,
        ),
    )(*operands)


def mix_scratch(rows, lanes):
    return [
        pltpu.VMEM((XA, rows, lanes), jnp.bfloat16),
        pltpu.VMEM((XA, rows, lanes), jnp.bfloat16),
        pltpu.VMEM((XA, rows, lanes), jnp.float32),
    ]


def enter(index, potential, direction, weights, matrices):
    rows = potential.shape[1]
    scratch = [
        pltpu.VMEM((4 * rows, NB * BLK), jnp.bfloat16),
        pltpu.VMEM((4 * rows, NB * BLK), jnp.bfloat16),
        pltpu.VMEM((XA, 2, rows, LANES), jnp.float32),
    ] + mix_scratch(2 * rows, 2 * LANES)
    outs = [(XA, 4, rows, LANES), (XA, 4, rows, LANES), (XA, 2, rows, LANES)]
    extra = NB * 4 * rows * 256 * 128 * 6
    return call(
        enter_kernel, outs, scratch, 2, extra, index, potential, direction, *weights, *matrices
    )


def middle(uv, td, matrices, mixed):
    return call(
        functools.partial(middle_kernel, mixed, len(uv)),
        [(XA, 4, XB, LANES), (XA, 2, XB, LANES)],
        mix_scratch(2 * XB, 2 * LANES),
        4,
        0,
        *uv,
        *td,
        *matrices,
    )


def detector(fields, matrices):
    rows = fields.shape[2]
    return call(
        detector_kernel,
        [(XA, 2, rows, LANES)],
        mix_scratch(2 * rows, 2 * LANES),
        3,
        0,
        fields,
        *matrices,
    )[0]


def pull(back, phi, td, matrices, mixed):
    return call(
        functools.partial(return_kernel, mixed, len(td)),
        [(XA, 4, XB, LANES)],
        mix_scratch(2 * XB, LANES),
        2,
        0,
        back,
        phi,
        *td,
        *matrices,
    )[0]


def leave(index, back, t0, weights, matrices, before):
    rows = back.shape[2]
    scratch = [
        pltpu.VMEM((NB, 2 * rows, LANES), jnp.bfloat16),
        pltpu.VMEM((NB, 2 * rows, LANES), jnp.bfloat16),
    ] + mix_scratch(rows, 2 * LANES)
    extra = NB * 2 * rows * 256 * 128 * 6
    return call(
        leave_kernel,
        [(2, rows, NB * BLK)],
        scratch,
        1,
        extra,
        index,
        back,
        t0,
        *weights,
        *matrices,
        *before,
    )[0]


def split_weights(block_weights):
    stacked = block_weights.reshape(ANGLES, NB, SLOTS * BLK, BLK)
    rounded = lax.reduce_precision(stacked, 8, 7)
    return rounded.astype(jnp.bfloat16), (stacked - rounded).astype(jnp.bfloat16)


def exchange(values):
    return lax.all_to_all(values, "fft", split_axis=0, concat_axis=0, tiled=True)


def blocked_body(potential, direction, block_index, block_weights):
    whi, wlo = split_weights(block_weights)
    by_column = column_constants()
    column = tuple(jnp.asarray(v) for v in split_constant(by_column))
    row = tuple(jnp.asarray(v) for v in split_constant(by_column.transpose(0, 2, 1)))
    weights = [(whi[a], wlo[a]) for a in range(ANGLES)]
    mixed = False
    state = []
    for a in range(ANGLES):
        uv, td, t0 = enter(block_index[a], potential, direction, weights[a], row)
        state.append((exchange(uv), exchange(td), t0))
    carried = []
    for uv, td, t0 in state:
        out, phi = middle([uv], [td], column, mixed)
        carried.append((exchange(out), phi, [td], t0))
    backs = [exchange(detector(out, row)) for out, _, _, _ in carried]
    pulled = [
        exchange(pull(back, phi, td, column, mixed))
        for back, (_, phi, td, _) in zip(backs, carried)
    ]
    total = ()
    for a in range(ANGLES):
        total = (leave(block_index[a], pulled[a], carried[a][3], weights[a], row, total),)
    return total[0]


def transform_table(count_in, count_out, length, orient):
    first = jnp.arange(count_in, dtype=jnp.int32)[:, None]
    second = jnp.arange(count_out, dtype=jnp.int32)[None, :]
    phases = orient * 2.0 * math.pi / length * (first * second % length).astype(jnp.float32)
    cosine = jnp.cos(phases)
    sine_part = jnp.sin(phases)
    return jnp.stack([jnp.stack([cosine, sine_part]), jnp.stack([-sine_part, cosine])])


def twiddle_pair(count_a, count_b, length, orient):
    first = jnp.arange(count_a, dtype=jnp.int32)[:, None]
    second = jnp.arange(count_b, dtype=jnp.int32)[None, :]
    phases = orient * 2.0 * math.pi / length * (first * second % length).astype(jnp.float32)
    return (jnp.cos(phases), jnp.sin(phases))


def spread_turn(peer_count, row_count, slot_count, orient):
    turn_re, turn_im = twiddle_pair(peer_count, row_count, NX, orient)
    shape_three = (row_count, peer_count, slot_count)
    wide_re = jnp.broadcast_to(turn_re.T[:, :, None], shape_three).reshape(
        row_count, peer_count * slot_count
    )
    wide_im = jnp.broadcast_to(turn_im.T[:, :, None], shape_three).reshape(
        row_count, peer_count * slot_count
    )
    return (wide_re, wide_im)


def complex_times(values, real_part, imag_part):
    first = values[:, 0]
    second = values[:, 1]
    return jnp.stack(
        [first * real_part - second * imag_part, first * imag_part + second * real_part], axis=1
    )


def one_hot(index_rows, block_count):
    return (index_rows[..., None] == jnp.arange(block_count, dtype=jnp.int32)).astype(jnp.float32)


def rotate(values, selector, matrices):
    height = values.shape[1]
    blocked = values.reshape(2, height, NB, BLK)
    picked = jnp.einsum("cyni,bsn->cybsi", blocked, selector, precision=PRECISE)
    rotated = jnp.einsum("cybsi,bsio->cybo", picked, matrices, precision=PRECISE)
    return rotated.reshape(2, height, SL, NX)


def rotate_back(values, selector, matrices):
    height = values.shape[1]
    blocked = values.reshape(2, height, NB, BLK)
    spread_out = jnp.einsum("cybo,bsio->cybsi", blocked, matrices, precision=PRECISE)
    summed = jnp.einsum("cybsi,bsn->cyni", spread_out, selector, precision=PRECISE)
    return summed.reshape(2, height, SL * NX)


def fresnel(peer_count, row_count, slot_count, orient):
    position_high = jnp.arange(row_count, dtype=jnp.int32)[:, None]
    position_low = jnp.arange(peer_count, dtype=jnp.int32)[None, :]
    freq_y = position_low + peer_count * position_high
    freq_y = jnp.where(freq_y < NX // 2, freq_y, freq_y - NX)
    position = lax.axis_index("fft") * slot_count + jnp.arange(slot_count, dtype=jnp.int32)
    freq_x = position // XB + XA * (position % XB)
    freq_x = jnp.where(freq_x < NX // 2, freq_x, freq_x - NX)
    squares = ((freq_y * freq_y)[:, :, None] + (freq_x * freq_x)[None, None, :]) % (2 * NX)
    phases = orient * -math.pi / NX * squares.astype(jnp.float32)
    scaling = 1.0 / (NX * NX)
    phases = phases.reshape(row_count, peer_count * slot_count)
    return (jnp.cos(phases) * scaling, jnp.sin(phases) * scaling)


def propagate(fields, kernel, peer_count, row_count, slot_count):
    field_count = fields.shape[0]
    groups = XB // slot_count
    shaped = fields.reshape(field_count, 2, row_count, XA, XB)
    partial_x = jnp.einsum(
        "fcrab,cdak->fdrkb", shaped, transform_table(XA, XA, XA, -1.0), precision=PRECISE
    )
    twist_re, twist_im = twiddle_pair(XA, XB, NX, -1.0)
    partial_x = complex_times(partial_x, twist_re, twist_im)
    partial_x = jnp.einsum(
        "fcrkb,cdbt->fdrkt", partial_x, transform_table(XB, XB, XB, -1.0), precision=PRECISE
    )
    partial_x = partial_x.reshape(field_count, 2, row_count, XA, groups, slot_count)
    outgoing = partial_x.transpose(0, 1, 3, 4, 2, 5).reshape(
        field_count, 2, peer_count, row_count * slot_count
    )
    forward_re, forward_im = spread_turn(peer_count, row_count, slot_count, -1.0)
    inverse_re, inverse_im = spread_turn(peer_count, row_count, slot_count, 1.0)
    wide = peer_count * slot_count
    incoming = lax.all_to_all(outgoing, "fft", split_axis=2, concat_axis=2, tiled=True)
    item_count = incoming.shape[0]
    lattice = incoming.reshape(item_count, 2, peer_count, row_count, slot_count)
    lattice = jnp.einsum(
        "fcprs,cdpk->fdrks",
        lattice,
        transform_table(peer_count, peer_count, peer_count, -1.0),
        precision=PRECISE,
    )
    lattice = lattice.reshape(item_count, 2, row_count, wide)
    lattice = complex_times(lattice, forward_re, forward_im)
    lattice = jnp.einsum(
        "fcrq,cdrm->fdmq",
        lattice,
        transform_table(row_count, row_count, row_count, -1.0),
        precision=PRECISE,
    )
    lattice = complex_times(lattice, kernel[0], kernel[1])
    lattice = jnp.einsum(
        "fcmq,cdmr->fdrq",
        lattice,
        transform_table(row_count, row_count, row_count, 1.0),
        precision=PRECISE,
    )
    lattice = complex_times(lattice, inverse_re, inverse_im)
    lattice = lattice.reshape(item_count, 2, row_count, peer_count, slot_count)
    lattice = jnp.einsum(
        "fcrks,cdkp->fdprs",
        lattice,
        transform_table(peer_count, peer_count, peer_count, 1.0),
        precision=PRECISE,
    )
    returning = lax.all_to_all(
        lattice.reshape(item_count, 2, peer_count, row_count * slot_count),
        "fft",
        split_axis=2,
        concat_axis=2,
        tiled=True,
    )
    restored = returning.reshape(item_count, 2, XA, groups, row_count, slot_count)
    matrix_back = transform_table(XB, XB, XB, 1.0).reshape(2, 2, groups, slot_count, XB)
    restored = jnp.einsum("fckjrs,cdjsb->fdrkb", restored, matrix_back, precision=PRECISE)
    back_re, back_im = twiddle_pair(XA, XB, NX, 1.0)
    restored = complex_times(restored, back_re, back_im)
    restored = jnp.einsum(
        "fcrkb,cdkn->fdrnb", restored, transform_table(XA, XA, XA, 1.0), precision=PRECISE
    )
    return restored.reshape(item_count, 2, row_count, NX)


def general_body(potential, direction, block_index, block_weights):
    row_count = potential.shape[1]
    peer_count = lax.axis_size("fft")
    slot_count = NX // peer_count
    ahead = fresnel(peer_count, row_count, slot_count, 1.0)
    behind = fresnel(peer_count, row_count, slot_count, -1.0)
    accumulated = jnp.zeros(potential.shape, jnp.float32)
    for angle_index in range(ANGLES):
        selector = one_hot(block_index[angle_index], NB)
        matrices = block_weights[angle_index]
        rotated = rotate(potential, selector, matrices)
        tangent = rotate(direction, selector, matrices)
        damping = jnp.exp(-rotated[1])
        trans_re = damping * jnp.cos(rotated[0])
        trans_im = damping * jnp.sin(rotated[0])
        wave_re = jnp.ones((row_count, NX), jnp.float32)
        wave_im = jnp.zeros((row_count, NX), jnp.float32)
        dwave_re = jnp.zeros((row_count, NX), jnp.float32)
        dwave_im = jnp.zeros((row_count, NX), jnp.float32)
        stored = []
        for slice_index in range(SL):
            t_re = trans_re[:, slice_index]
            t_im = trans_im[:, slice_index]
            d_re = tangent[0][:, slice_index]
            d_im = tangent[1][:, slice_index]
            phi_re = t_re * wave_re - t_im * wave_im
            phi_im = t_re * wave_im + t_im * wave_re
            dphi_re = -(d_re * phi_im + d_im * phi_re) + t_re * dwave_re - t_im * dwave_im
            dphi_im = d_re * phi_re - d_im * phi_im + t_re * dwave_im + t_im * dwave_re
            stored.append((phi_re, phi_im))
            packed = jnp.stack([jnp.stack([phi_re, phi_im]), jnp.stack([dphi_re, dphi_im])])
            propagated = propagate(packed, ahead, peer_count, row_count, slot_count)
            wave_re = propagated[0, 0]
            wave_im = propagated[0, 1]
            dwave_re = propagated[1, 0]
            dwave_im = propagated[1, 1]
        change = 2.0 * (wave_re * dwave_re + wave_im * dwave_im)
        back_re = 2.0 * change * wave_re
        back_im = 2.0 * change * wave_im
        grad_re = [None] * SL
        grad_im = [None] * SL
        for slice_index in reversed(range(SL)):
            pulled = propagate(
                jnp.stack([back_re, back_im])[None], behind, peer_count, row_count, slot_count
            )
            pb_re = pulled[0, 0]
            pb_im = pulled[0, 1]
            phi_re, phi_im = stored[slice_index]
            grad_re[slice_index] = phi_re * pb_im - phi_im * pb_re
            grad_im[slice_index] = -(phi_re * pb_re + phi_im * pb_im)
            t_re = trans_re[:, slice_index]
            t_im = trans_im[:, slice_index]
            back_re = t_re * pb_re + t_im * pb_im
            back_im = t_re * pb_im - t_im * pb_re
        gradient = jnp.stack([jnp.stack(grad_re, axis=1), jnp.stack(grad_im, axis=1)])
        accumulated = accumulated + rotate_back(gradient, selector, matrices)
    return accumulated


def body(potential, direction, block_index, block_weights):
    if lax.axis_size("fft") == XA and potential.shape[1] == XB:
        return blocked_body(potential, direction, block_index, block_weights)
    return general_body(potential, direction, block_index, block_weights)


def solution(mesh):
    return jax.shard_map(
        body,
        mesh=mesh,
        in_specs=(P("parts", "fft", None), P("parts", "fft", None), P(), P()),
        out_specs=P("parts", "fft", None),
        check_vma=False,
    )
```

```python
import functools
import math

import jax
import jax.numpy as jnp
import numpy as np
from jax import lax
from jax.experimental import pallas as pl
from jax.experimental.pallas import tpu as pltpu
from jax.sharding import PartitionSpec as P

XA = 16
XB = 128
NX = 2048
SL = 2
ANGLES = 2
BLK = 128
NB = 32
SLOTS = 2
STRIP = 16
LANES = 128


PRECISE = lax.Precision.HIGHEST


def bin_matrices():
    wavenumber = np.arange(NX)
    signed = np.where(wavenumber < NX // 2, wavenumber, wavenumber - NX)
    factor = np.exp(-1j * np.pi / NX * ((signed * signed) % (2 * NX)))
    line = np.fft.ifft(factor)
    block = np.arange(XA)
    inner = np.arange(XB)
    shifts = (XB * block[:, None, None] + inner[None, :, None] - inner[None, None, :]) % NX
    phases = np.exp(-2j * np.pi / XA * ((block[:, None] * block[None, :]) % XA))
    return np.einsum("kd,dij->kij", phases, line[shifts]) / XA


def split_constant(values):
    values = values.astype(np.float32)
    high = values.astype(jnp.bfloat16)
    low = (values - high.astype(np.float32)).astype(jnp.bfloat16)
    return high, low


def column_constants():
    bins = bin_matrices()
    top = np.concatenate([bins.real, -bins.imag], axis=2)
    bottom = np.concatenate([bins.imag, bins.real], axis=2)
    return np.concatenate([top, bottom], axis=1)


def fourth(values, orient):
    (ar, ai), (br, bi), (cr, ci), (dr, di) = values
    sr, si, er, ei = ar + cr, ai + ci, ar - cr, ai - ci
    tr, ti, fr, fi = br + dr, bi + di, br - dr, bi - di
    minus, plus = (er + fi, ei - fr), (er - fi, ei + fr)
    one, three = (minus, plus) if orient < 0 else (plus, minus)
    return [(sr + tr, si + ti), one, (sr - tr, si - ti), three]


def turned(value, step, orient):
    re, im = value
    if step == 0:
        return value
    if step == 4:
        return (im, -re) if orient < 0 else (-im, re)
    cosine = math.cos(2.0 * math.pi * step / XA)
    sine = orient * math.sin(2.0 * math.pi * step / XA)
    if step == 2:
        root = cosine
        return ((re - im) * root, (re + im) * root) if orient > 0 else ((re + im) * root, (im - re) * root)
    return (re * cosine - im * sine, re * sine + im * cosine)


def sixteenth(values, orient):
    inner = [fourth([values[4 * a + b] for a in range(4)], orient) for b in range(4)]
    out = [None] * XA
    for c in range(4):
        row = fourth([turned(inner[b][c], b * c, orient) for b in range(4)], orient)
        for d in range(4):
            out[c + 4 * d] = row[d]
    return out


def halves(value):
    high = value.astype(jnp.bfloat16)
    return high, (value - high.astype(jnp.float32)).astype(jnp.bfloat16)


def dot32(a, b):
    return jnp.dot(a, b, preferred_element_type=jnp.float32)


def times(a, b):
    return (a[0] * b[0] - a[1] * b[1], a[0] * b[1] + a[1] * b[0])


def sincos(x):
    turns = jnp.floor(x * (2.0 / math.pi) + 0.5)
    rest = ((x - turns * 1.5703125) - turns * 4.837512969970703125e-4) - turns * 7.54978995489188216e-8
    square = rest * rest
    sine = rest + rest * square * (
        -1.6666654611e-1 + square * (8.3321608736e-3 + square * -1.9515295891e-4)
    )
    cosine = (1.0 - 0.5 * square) + square * square * (
        4.166664568298827e-2 + square * (-1.388731625493765e-3 + square * 2.443315711809948e-5)
    )
    quadrant = turns.astype(jnp.int32)
    odd = (quadrant & 1) == 1
    first = jnp.where(odd, cosine, sine)
    second = jnp.where(odd, sine, cosine)
    first = jnp.where((quadrant & 2) == 2, -first, first)
    second = jnp.where(((quadrant + 1) & 2) == 2, -second, second)
    return first, second


def strips(count, step):
    def run(i, carry):
        step(pl.multiple_of(i * STRIP, STRIP))
        return carry

    lax.fori_loop(0, count // STRIP, run, 0)


def rows_out(xhi, xlo, first_row, values):
    for k, (re, im) in enumerate(sixteenth(values, -1.0)):
        for part, value in enumerate((re, im)):
            high, low = halves(value)
            at = (k, pl.ds(first_row, STRIP), pl.ds(part * LANES, LANES))
            xhi[at] = high
            xlo[at] = low


def rows_in(y, first_row):
    values = [
        tuple(y[k, pl.ds(first_row, STRIP), pl.ds(part * LANES, LANES)] for part in range(2))
        for k in range(XA)
    ]
    return sixteenth(values, 1.0)


def rows_mix(xhi, xlo, mhi, mlo, y):
    def step(k, carry):
        high, low = xhi[k], xlo[k]
        y[k] = dot32(high, mhi[k]) + (dot32(low, mhi[k]) + dot32(high, mlo[k]))
        return carry

    lax.fori_loop(0, XA, step, 0)


def columns_out(xhi, xlo, field, row, values):
    for k, (re, im) in enumerate(sixteenth(values, -1.0)):
        for part, value in enumerate((re, im)):
            high, low = halves(value)
            at = (k, pl.ds(part * XB + row, STRIP), pl.ds(field * LANES, LANES))
            xhi[at] = high
            xlo[at] = low


def columns_in(y, field, row):
    values = [
        tuple(
            y[k, pl.ds(part * XB + row, STRIP), pl.ds(field * LANES, LANES)] for part in range(2)
        )
        for k in range(XA)
    ]
    return sixteenth(values, 1.0)


def columns_mix(xhi, xlo, mhi, mlo, y):
    def step(k, carry):
        high, low = xhi[k], xlo[k]
        y[k] = dot32(mhi[k], high) + (dot32(mhi[k], low) + dot32(mlo[k], high))
        return carry

    lax.fori_loop(0, XA, step, 0)


def enter_kernel(pieces, index, *refs):
    sources = refs[:pieces], refs[pieces : 2 * pieces]
    whi, wlo, mhi, mlo, uv, td, t0, shi, slo, field, xhi, xlo, y = refs[2 * pieces :]
    rows = sum(piece.shape[1] for piece in sources[0])

    for number in range(4):
        first = number * rows
        for piece in sources[number // 2]:

            def cut(row, first=first, piece=piece, channel=number % 2):
                high, low = halves(piece[channel, pl.ds(row, STRIP), :])
                at = pl.ds(pl.multiple_of(first + row, STRIP), STRIP)
                shi[at, :] = high
                slo[at, :] = low

            strips(piece.shape[1], cut)
            first += piece.shape[1]

    def rotated(b):
        at = [pl.ds(pl.multiple_of(index[b, s] * BLK, BLK), BLK) for s in range(SLOTS)]
        high = jnp.concatenate([shi[:, a] for a in at], axis=1)
        low = jnp.concatenate([slo[:, a] for a in at], axis=1)
        values = dot32(high, whi[b]) + (dot32(low, whi[b]) + dot32(high, wlo[b]))
        angle, loss, d_re, d_im = (values[i * rows : (i + 1) * rows] for i in range(4))
        sine, cosine = sincos(angle)
        damping = jnp.exp(-loss)
        return damping * cosine, damping * sine, d_re, d_im

    def first_slice(b, carry):
        t_re, t_im, d_re, d_im = rotated(b)
        t0[b, 0] = t_re
        t0[b, 1] = t_im
        field[b, 0] = -(d_re * t_im + d_im * t_re)
        field[b, 1] = d_re * t_re - d_im * t_im
        return carry

    lax.fori_loop(0, XA, first_slice, 0)

    def forward(row):
        at = pl.ds(row, STRIP)
        rows_out(xhi, xlo, row, [(t0[b, 0, at, :], t0[b, 1, at, :]) for b in range(XA)])
        rows_out(
            xhi,
            xlo,
            pl.multiple_of(rows + row, STRIP),
            [(field[b, 0, at, :], field[b, 1, at, :]) for b in range(XA)],
        )

    strips(rows, forward)
    rows_mix(xhi, xlo, mhi, mlo, y)

    def backward(row):
        at = pl.ds(row, STRIP)
        for number in range(2):
            values = rows_in(y, pl.multiple_of(number * rows + row, STRIP))
            for b, (re, im) in enumerate(values):
                uv[b, 2 * number, at, :] = re
                uv[b, 2 * number + 1, at, :] = im

    strips(rows, backward)

    def second_slice(b, carry):
        for channel, value in enumerate(rotated(XA + b)):
            td[b, channel] = value
        return carry

    lax.fori_loop(0, XA, second_slice, 0)


def row_places(mixed):
    same = list(range(XA))
    if not mixed:
        return [(0, XB, same)]
    swapped = [p ^ (XA // 2) for p in same]
    step = XB // 4
    return [(i * step, step, swapped if i % 2 == 0 else same) for i in range(4)]


def column_strips(mixed, step):
    for first, count, places in row_places(mixed):
        strips(count, lambda row, first=first, places=places: step(pl.multiple_of(first + row, STRIP), places))


def middle_kernel(mixed, chunks, *refs):
    uv, td = refs[:chunks], refs[chunks : 2 * chunks]
    mhi, mlo, out, phi, xhi, xlo, y = refs[2 * chunks :]
    rows = XB // chunks

    def chunked(step):
        for first, count, places in row_places(mixed):
            for piece in range(0, count, min(count, rows)):
                start = first + piece
                c, local = start // rows, start % rows

                def inner(row, start=start, c=c, local=local, places=places):
                    step(
                        pl.multiple_of(start + row, STRIP),
                        c,
                        pl.ds(pl.multiple_of(local + row, STRIP), STRIP),
                        places,
                    )

                strips(min(count, rows), inner)

    def forward(row, c, local, places):
        for number in range(2):
            columns_out(
                xhi,
                xlo,
                number,
                row,
                [tuple(uv[c][g, 2 * number + i, local, :] for i in range(2)) for g in places],
            )

    chunked(forward)
    columns_mix(xhi, xlo, mhi, mlo, y)

    def turn(row, c, local, places):
        at = pl.ds(row, STRIP)
        wave = columns_in(y, 0, row)
        product = []
        for g, value in zip(places, wave):
            value = times((td[c][g, 0, local, :], td[c][g, 1, local, :]), value)
            phi[g, 0, at, :] = value[0]
            phi[g, 1, at, :] = value[1]
            product.append(value)
        columns_out(xhi, xlo, 0, row, product)
        dwave = columns_in(y, 1, row)
        change = []
        for g, value in zip(places, dwave):
            t_re, t_im, d_re, d_im = (td[c][g, i, local, :] for i in range(4))
            p_re, p_im = phi[g, 0, at, :], phi[g, 1, at, :]
            re, im = times((t_re, t_im), value)
            change.append((re - (d_re * p_im + d_im * p_re), im + (d_re * p_re - d_im * p_im)))
        columns_out(xhi, xlo, 1, row, change)

    chunked(turn)
    columns_mix(xhi, xlo, mhi, mlo, y)

    def backward(row, c, local, places):
        at = pl.ds(row, STRIP)
        for number in range(2):
            for g, (re, im) in zip(places, columns_in(y, number, row)):
                out[g, 2 * number, at, :] = re
                out[g, 2 * number + 1, at, :] = im

    chunked(backward)


def detector_kernel(fields, mhi, mlo, out, xhi, xlo, y):
    rows = fields.shape[2]

    def forward(row):
        at = pl.ds(row, STRIP)
        for number in range(2):
            rows_out(
                xhi,
                xlo,
                pl.multiple_of(number * rows + row, STRIP),
                [tuple(fields[b, 2 * number + i, at, :] for i in range(2)) for b in range(XA)],
            )

    strips(rows, forward)
    rows_mix(xhi, xlo, mhi, mlo, y)

    def turn(row):
        wave = rows_in(y, row)
        dwave = rows_in(y, pl.multiple_of(rows + row, STRIP))
        back = []
        for (re, im), (d_re, d_im) in zip(wave, dwave):
            change = 4.0 * (re * d_re + im * d_im)
            back.append((change * re, -(change * im)))
        rows_out(xhi, xlo, row, back)

    strips(rows, turn)

    def step(k, carry):
        high, low = xhi[k, :rows, :], xlo[k, :rows, :]
        y[k, :rows, :] = dot32(high, mhi[k]) + (dot32(low, mhi[k]) + dot32(high, mlo[k]))
        return carry

    lax.fori_loop(0, XA, step, 0)

    def backward(row):
        at = pl.ds(row, STRIP)
        for b, (re, im) in enumerate(rows_in(y, row)):
            out[b, 0, at, :] = re
            out[b, 1, at, :] = im

    strips(rows, backward)


def return_kernel(mixed, chunks, back, phi, *refs):
    td = refs[:chunks]
    mhi, mlo, out, xhi, xlo, y = refs[chunks:]
    rows = XB // chunks

    def chunked(step):
        for first, count, places in row_places(mixed):
            for piece in range(0, count, min(count, rows)):
                start = first + piece
                c, local = start // rows, start % rows

                def inner(row, start=start, c=c, local=local, places=places):
                    step(
                        pl.multiple_of(start + row, STRIP),
                        c,
                        pl.ds(pl.multiple_of(local + row, STRIP), STRIP),
                        places,
                    )

                strips(min(count, rows), inner)

    def forward(row, c, local, places):
        at = pl.ds(row, STRIP)
        columns_out(xhi, xlo, 0, row, [(back[g, 0, at, :], back[g, 1, at, :]) for g in places])

    chunked(forward)
    columns_mix(xhi, xlo, mhi, mlo, y)

    def turn(row, c, local, places):
        at = pl.ds(row, STRIP)
        pulled = columns_in(y, 0, row)
        following = []
        for g, value in zip(places, pulled):
            re, im = times((phi[g, 0, at, :], phi[g, 1, at, :]), value)
            out[g, 0, at, :] = -im
            out[g, 1, at, :] = -re
            following.append(times((td[c][g, 0, local, :], td[c][g, 1, local, :]), value))
        columns_out(xhi, xlo, 0, row, following)

    chunked(turn)
    columns_mix(xhi, xlo, mhi, mlo, y)

    def backward(row, c, local, places):
        at = pl.ds(row, STRIP)
        for g, (re, im) in zip(places, columns_in(y, 0, row)):
            out[g, 2, at, :] = re
            out[g, 3, at, :] = im

    chunked(backward)


def leave_kernel(index, back, t0, whi, wlo, mhi, mlo, *refs):
    before, (out, shi, slo, xhi, xlo, y) = refs[:-6], refs[-6:]
    rows = back.shape[2]

    def forward(row):
        at = pl.ds(row, STRIP)
        rows_out(xhi, xlo, row, [(back[b, 2, at, :], back[b, 3, at, :]) for b in range(XA)])
        for b in range(XA):
            for i in range(2):
                high, low = halves(back[b, i, at, :])
                place = pl.ds(pl.multiple_of(i * rows + row, STRIP), STRIP)
                shi[XA + b, place, :] = high
                slo[XA + b, place, :] = low

    strips(rows, forward)
    rows_mix(xhi, xlo, mhi, mlo, y)

    def turn(row):
        at = pl.ds(row, STRIP)
        for b, value in enumerate(rows_in(y, row)):
            re, im = times((t0[b, 0, at, :], t0[b, 1, at, :]), value)
            for i, part in enumerate((-im, -re)):
                high, low = halves(part)
                place = pl.ds(pl.multiple_of(i * rows + row, STRIP), STRIP)
                shi[b, place, :] = high
                slo[b, place, :] = low

    strips(rows, turn)

    if before:
        out[...] = before[0][...]
    else:
        out[...] = jnp.zeros(out.shape, jnp.float32)

    def across(a, b):
        return lax.dot_general(
            a, b, (((1,), (1,)), ((), ())), preferred_element_type=jnp.float32
        )

    def step(b, carry):
        high, low = shi[b], slo[b]
        values = across(high, whi[b]) + (across(low, whi[b]) + across(high, wlo[b]))
        for s in range(SLOTS):
            at = pl.ds(pl.multiple_of(index[b, s] * BLK, BLK), BLK)
            for i in range(2):
                out[i, :, at] += values[i * rows : (i + 1) * rows, s * BLK : (s + 1) * BLK]
        return carry

    lax.fori_loop(0, NB, step, 0)


def call(kernel, outs, scratch, mix_count, extra, *operands):
    specs = [
        pl.BlockSpec(memory_space=pltpu.SMEM if o.dtype == jnp.int32 else pltpu.VMEM)
        for o in operands
    ]
    moved = sum(o.size * o.dtype.itemsize for o in operands) + sum(4 * math.prod(o) for o in outs)
    return pl.pallas_call(
        kernel,
        out_shape=[jax.ShapeDtypeStruct(o, jnp.float32) for o in outs],
        in_specs=specs,
        out_specs=[pl.BlockSpec(memory_space=pltpu.VMEM)] * len(outs),
        scratch_shapes=scratch,
        compiler_params=pltpu.CompilerParams(vmem_limit_bytes=60 * 1024 * 1024),
        cost_estimate=pl.CostEstimate(
            flops=mix_count * 16 * 128 * 256 * 256 * 6 + extra,
            bytes_accessed=moved,
            transcendentals=0,
        ),
    )(*operands)


def mix_scratch(rows, lanes):
    return [
        pltpu.VMEM((XA, rows, lanes), jnp.bfloat16),
        pltpu.VMEM((XA, rows, lanes), jnp.bfloat16),
        pltpu.VMEM((XA, rows, lanes), jnp.float32),
    ]


def enter(index, potential, direction, weights, matrices):
    rows = sum(piece.shape[1] for piece in potential)
    scratch = [
        pltpu.VMEM((4 * rows, NB * BLK), jnp.bfloat16),
        pltpu.VMEM((4 * rows, NB * BLK), jnp.bfloat16),
        pltpu.VMEM((XA, 2, rows, LANES), jnp.float32),
    ] + mix_scratch(2 * rows, 2 * LANES)
    outs = [(XA, 4, rows, LANES), (XA, 4, rows, LANES), (XA, 2, rows, LANES)]
    extra = NB * 4 * rows * 256 * 128 * 6
    return call(
        functools.partial(enter_kernel, len(potential)),
        outs,
        scratch,
        2,
        extra,
        index,
        *potential,
        *direction,
        *weights,
        *matrices,
    )


def middle(uv, td, matrices, mixed):
    return call(
        functools.partial(middle_kernel, mixed, len(uv)),
        [(XA, 4, XB, LANES), (XA, 2, XB, LANES)],
        mix_scratch(2 * XB, 2 * LANES),
        4,
        0,
        *uv,
        *td,
        *matrices,
    )


def detector(fields, matrices):
    rows = fields.shape[2]
    return call(
        detector_kernel,
        [(XA, 2, rows, LANES)],
        mix_scratch(2 * rows, 2 * LANES),
        3,
        0,
        fields,
        *matrices,
    )[0]


def pull(back, phi, td, matrices, mixed):
    return call(
        functools.partial(return_kernel, mixed, len(td)),
        [(XA, 4, XB, LANES)],
        mix_scratch(2 * XB, LANES),
        2,
        0,
        back,
        phi,
        *td,
        *matrices,
    )[0]


def leave(index, back, t0, weights, matrices, before):
    rows = back.shape[2]
    scratch = [
        pltpu.VMEM((NB, 2 * rows, LANES), jnp.bfloat16),
        pltpu.VMEM((NB, 2 * rows, LANES), jnp.bfloat16),
    ] + mix_scratch(rows, 2 * LANES)
    extra = NB * 2 * rows * 256 * 128 * 6
    return call(
        leave_kernel,
        [(2, rows, NB * BLK)],
        scratch,
        1,
        extra,
        index,
        back,
        t0,
        *weights,
        *matrices,
        *before,
    )[0]


def split_weights(block_weights):
    stacked = block_weights.reshape(ANGLES, NB, SLOTS * BLK, BLK)
    rounded = lax.reduce_precision(stacked, 8, 7)
    return rounded.astype(jnp.bfloat16), (stacked - rounded).astype(jnp.bfloat16)


def device(q, b, r):
    return q * XA + b * (XA // 2) + r


def groups():
    return [
        [device(x, b, r) for x in range(2) for r in range(XA // 2)] for b in range(2)
    ]


def exchange(values):
    return lax.all_to_all(
        values,
        ("parts", "fft"),
        split_axis=0,
        concat_axis=0,
        axis_index_groups=groups(),
        tiled=True,
    )


def moves(kind):
    pairs = []
    for r in range(XA // 2):
        a, b, c, d = device(0, 1, r), device(0, 0, r), device(1, 0, r), device(1, 1, r)
        pairs += [(a, b), (b, c), (c, d), (d, a)] if kind == 0 else [(a, c), (c, a), (b, b), (d, d)]
    return pairs


def arrive(values):
    step = XB // 4
    return [
        lax.ppermute(values[:, i * step : (i + 1) * step], ("parts", "fft"), moves(i % 2))
        for i in range(4)
    ]


def depart(values):
    step = XB // 4
    return [
        lax.ppermute(
            values[:, i * step : (i + 1) * step],
            ("parts", "fft"),
            [(there, here) for here, there in moves(i % 2)],
        )
        for i in range(4)
    ]


def blocked_body(potential, direction, block_index, block_weights):
    potential, direction = arrive(potential), arrive(direction)
    whi, wlo = split_weights(block_weights)
    by_column = column_constants()
    column = tuple(jnp.asarray(v) for v in split_constant(by_column))
    row = tuple(jnp.asarray(v) for v in split_constant(by_column.transpose(0, 2, 1)))
    weights = [(whi[a], wlo[a]) for a in range(ANGLES)]
    mixed = True
    state = []
    for a in range(ANGLES):
        uv, td, t0 = enter(block_index[a], potential, direction, weights[a], row)
        state.append((exchange(uv), exchange(td), t0))
    carried = []
    for uv, td, t0 in state:
        out, phi = middle([uv], [td], column, mixed)
        carried.append((exchange(out), phi, [td], t0))
    backs = [exchange(detector(out, row)) for out, _, _, _ in carried]
    pulled = [
        exchange(pull(back, phi, td, column, mixed))
        for back, (_, phi, td, _) in zip(backs, carried)
    ]
    total = ()
    for a in range(ANGLES):
        total = (leave(block_index[a], pulled[a], carried[a][3], weights[a], row, total),)
    return jnp.concatenate(depart(total[0]), axis=1)


def transform_table(count_in, count_out, length, orient):
    first = jnp.arange(count_in, dtype=jnp.int32)[:, None]
    second = jnp.arange(count_out, dtype=jnp.int32)[None, :]
    phases = orient * 2.0 * math.pi / length * (first * second % length).astype(jnp.float32)
    cosine = jnp.cos(phases)
    sine_part = jnp.sin(phases)
    return jnp.stack([jnp.stack([cosine, sine_part]), jnp.stack([-sine_part, cosine])])


def twiddle_pair(count_a, count_b, length, orient):
    first = jnp.arange(count_a, dtype=jnp.int32)[:, None]
    second = jnp.arange(count_b, dtype=jnp.int32)[None, :]
    phases = orient * 2.0 * math.pi / length * (first * second % length).astype(jnp.float32)
    return (jnp.cos(phases), jnp.sin(phases))


def spread_turn(peer_count, row_count, slot_count, orient):
    turn_re, turn_im = twiddle_pair(peer_count, row_count, NX, orient)
    shape_three = (row_count, peer_count, slot_count)
    wide_re = jnp.broadcast_to(turn_re.T[:, :, None], shape_three).reshape(
        row_count, peer_count * slot_count
    )
    wide_im = jnp.broadcast_to(turn_im.T[:, :, None], shape_three).reshape(
        row_count, peer_count * slot_count
    )
    return (wide_re, wide_im)


def complex_times(values, real_part, imag_part):
    first = values[:, 0]
    second = values[:, 1]
    return jnp.stack(
        [first * real_part - second * imag_part, first * imag_part + second * real_part], axis=1
    )


def one_hot(index_rows, block_count):
    return (index_rows[..., None] == jnp.arange(block_count, dtype=jnp.int32)).astype(jnp.float32)


def rotate(values, selector, matrices):
    height = values.shape[1]
    blocked = values.reshape(2, height, NB, BLK)
    picked = jnp.einsum("cyni,bsn->cybsi", blocked, selector, precision=PRECISE)
    rotated = jnp.einsum("cybsi,bsio->cybo", picked, matrices, precision=PRECISE)
    return rotated.reshape(2, height, SL, NX)


def rotate_back(values, selector, matrices):
    height = values.shape[1]
    blocked = values.reshape(2, height, NB, BLK)
    spread_out = jnp.einsum("cybo,bsio->cybsi", blocked, matrices, precision=PRECISE)
    summed = jnp.einsum("cybsi,bsn->cyni", spread_out, selector, precision=PRECISE)
    return summed.reshape(2, height, SL * NX)


def fresnel(peer_count, row_count, slot_count, orient):
    position_high = jnp.arange(row_count, dtype=jnp.int32)[:, None]
    position_low = jnp.arange(peer_count, dtype=jnp.int32)[None, :]
    freq_y = position_low + peer_count * position_high
    freq_y = jnp.where(freq_y < NX // 2, freq_y, freq_y - NX)
    position = lax.axis_index("fft") * slot_count + jnp.arange(slot_count, dtype=jnp.int32)
    freq_x = position // XB + XA * (position % XB)
    freq_x = jnp.where(freq_x < NX // 2, freq_x, freq_x - NX)
    squares = ((freq_y * freq_y)[:, :, None] + (freq_x * freq_x)[None, None, :]) % (2 * NX)
    phases = orient * -math.pi / NX * squares.astype(jnp.float32)
    scaling = 1.0 / (NX * NX)
    phases = phases.reshape(row_count, peer_count * slot_count)
    return (jnp.cos(phases) * scaling, jnp.sin(phases) * scaling)


def propagate(fields, kernel, peer_count, row_count, slot_count):
    field_count = fields.shape[0]
    groups = XB // slot_count
    shaped = fields.reshape(field_count, 2, row_count, XA, XB)
    partial_x = jnp.einsum(
        "fcrab,cdak->fdrkb", shaped, transform_table(XA, XA, XA, -1.0), precision=PRECISE
    )
    twist_re, twist_im = twiddle_pair(XA, XB, NX, -1.0)
    partial_x = complex_times(partial_x, twist_re, twist_im)
    partial_x = jnp.einsum(
        "fcrkb,cdbt->fdrkt", partial_x, transform_table(XB, XB, XB, -1.0), precision=PRECISE
    )
    partial_x = partial_x.reshape(field_count, 2, row_count, XA, groups, slot_count)
    outgoing = partial_x.transpose(0, 1, 3, 4, 2, 5).reshape(
        field_count, 2, peer_count, row_count * slot_count
    )
    forward_re, forward_im = spread_turn(peer_count, row_count, slot_count, -1.0)
    inverse_re, inverse_im = spread_turn(peer_count, row_count, slot_count, 1.0)
    wide = peer_count * slot_count
    incoming = lax.all_to_all(outgoing, "fft", split_axis=2, concat_axis=2, tiled=True)
    item_count = incoming.shape[0]
    lattice = incoming.reshape(item_count, 2, peer_count, row_count, slot_count)
    lattice = jnp.einsum(
        "fcprs,cdpk->fdrks",
        lattice,
        transform_table(peer_count, peer_count, peer_count, -1.0),
        precision=PRECISE,
    )
    lattice = lattice.reshape(item_count, 2, row_count, wide)
    lattice = complex_times(lattice, forward_re, forward_im)
    lattice = jnp.einsum(
        "fcrq,cdrm->fdmq",
        lattice,
        transform_table(row_count, row_count, row_count, -1.0),
        precision=PRECISE,
    )
    lattice = complex_times(lattice, kernel[0], kernel[1])
    lattice = jnp.einsum(
        "fcmq,cdmr->fdrq",
        lattice,
        transform_table(row_count, row_count, row_count, 1.0),
        precision=PRECISE,
    )
    lattice = complex_times(lattice, inverse_re, inverse_im)
    lattice = lattice.reshape(item_count, 2, row_count, peer_count, slot_count)
    lattice = jnp.einsum(
        "fcrks,cdkp->fdprs",
        lattice,
        transform_table(peer_count, peer_count, peer_count, 1.0),
        precision=PRECISE,
    )
    returning = lax.all_to_all(
        lattice.reshape(item_count, 2, peer_count, row_count * slot_count),
        "fft",
        split_axis=2,
        concat_axis=2,
        tiled=True,
    )
    restored = returning.reshape(item_count, 2, XA, groups, row_count, slot_count)
    matrix_back = transform_table(XB, XB, XB, 1.0).reshape(2, 2, groups, slot_count, XB)
    restored = jnp.einsum("fckjrs,cdjsb->fdrkb", restored, matrix_back, precision=PRECISE)
    back_re, back_im = twiddle_pair(XA, XB, NX, 1.0)
    restored = complex_times(restored, back_re, back_im)
    restored = jnp.einsum(
        "fcrkb,cdkn->fdrnb", restored, transform_table(XA, XA, XA, 1.0), precision=PRECISE
    )
    return restored.reshape(item_count, 2, row_count, NX)


def general_body(potential, direction, block_index, block_weights):
    row_count = potential.shape[1]
    peer_count = lax.axis_size("fft")
    slot_count = NX // peer_count
    ahead = fresnel(peer_count, row_count, slot_count, 1.0)
    behind = fresnel(peer_count, row_count, slot_count, -1.0)
    accumulated = jnp.zeros(potential.shape, jnp.float32)
    for angle_index in range(ANGLES):
        selector = one_hot(block_index[angle_index], NB)
        matrices = block_weights[angle_index]
        rotated = rotate(potential, selector, matrices)
        tangent = rotate(direction, selector, matrices)
        damping = jnp.exp(-rotated[1])
        trans_re = damping * jnp.cos(rotated[0])
        trans_im = damping * jnp.sin(rotated[0])
        wave_re = jnp.ones((row_count, NX), jnp.float32)
        wave_im = jnp.zeros((row_count, NX), jnp.float32)
        dwave_re = jnp.zeros((row_count, NX), jnp.float32)
        dwave_im = jnp.zeros((row_count, NX), jnp.float32)
        stored = []
        for slice_index in range(SL):
            t_re = trans_re[:, slice_index]
            t_im = trans_im[:, slice_index]
            d_re = tangent[0][:, slice_index]
            d_im = tangent[1][:, slice_index]
            phi_re = t_re * wave_re - t_im * wave_im
            phi_im = t_re * wave_im + t_im * wave_re
            dphi_re = -(d_re * phi_im + d_im * phi_re) + t_re * dwave_re - t_im * dwave_im
            dphi_im = d_re * phi_re - d_im * phi_im + t_re * dwave_im + t_im * dwave_re
            stored.append((phi_re, phi_im))
            packed = jnp.stack([jnp.stack([phi_re, phi_im]), jnp.stack([dphi_re, dphi_im])])
            propagated = propagate(packed, ahead, peer_count, row_count, slot_count)
            wave_re = propagated[0, 0]
            wave_im = propagated[0, 1]
            dwave_re = propagated[1, 0]
            dwave_im = propagated[1, 1]
        change = 2.0 * (wave_re * dwave_re + wave_im * dwave_im)
        back_re = 2.0 * change * wave_re
        back_im = 2.0 * change * wave_im
        grad_re = [None] * SL
        grad_im = [None] * SL
        for slice_index in reversed(range(SL)):
            pulled = propagate(
                jnp.stack([back_re, back_im])[None], behind, peer_count, row_count, slot_count
            )
            pb_re = pulled[0, 0]
            pb_im = pulled[0, 1]
            phi_re, phi_im = stored[slice_index]
            grad_re[slice_index] = phi_re * pb_im - phi_im * pb_re
            grad_im[slice_index] = -(phi_re * pb_re + phi_im * pb_im)
            t_re = trans_re[:, slice_index]
            t_im = trans_im[:, slice_index]
            back_re = t_re * pb_re + t_im * pb_im
            back_im = t_re * pb_im - t_im * pb_re
        gradient = jnp.stack([jnp.stack(grad_re, axis=1), jnp.stack(grad_im, axis=1)])
        accumulated = accumulated + rotate_back(gradient, selector, matrices)
    return accumulated


def body(potential, direction, block_index, block_weights):
    if lax.axis_size("parts") == 2 and lax.axis_size("fft") == XA:
        return blocked_body(potential, direction, block_index, block_weights)
    return general_body(potential, direction, block_index, block_weights)


def solution(mesh):
    return jax.shard_map(
        body,
        mesh=mesh,
        in_specs=(P("parts", "fft", None), P("parts", "fft", None), P(), P()),
        out_specs=P("parts", "fft", None),
        check_vma=False,
    )
```

```python
import functools
import math

import jax
import jax.numpy as jnp
import numpy as np
from jax import lax
from jax.experimental import pallas as pl
from jax.experimental.pallas import tpu as pltpu
from jax.sharding import PartitionSpec as P

XA = 16
XB = 128
NX = 2048
SL = 2
ANGLES = 2
BLK = 128
NB = 32
SLOTS = 2
STRIP = 16
LANES = 128
QUARTER = XB // 4
HALF = XA // 2
MEMBERS = [(g % 2, (g // 2 % 2) * 4 + (g // 4 % 2) * 2 + g // 8) for g in range(XA)]


PRECISE = lax.Precision.HIGHEST


def bin_matrices():
    wavenumber = np.arange(NX)
    signed = np.where(wavenumber < NX // 2, wavenumber, wavenumber - NX)
    factor = np.exp(-1j * np.pi / NX * ((signed * signed) % (2 * NX)))
    line = np.fft.ifft(factor)
    block = np.arange(XA)
    inner = np.arange(XB)
    shifts = (XB * block[:, None, None] + inner[None, :, None] - inner[None, None, :]) % NX
    phases = np.exp(-2j * np.pi / XA * ((block[:, None] * block[None, :]) % XA))
    return np.einsum("kd,dij->kij", phases, line[shifts]) / XA


def split_constant(values):
    values = values.astype(np.float32)
    high = values.astype(jnp.bfloat16)
    low = (values - high.astype(np.float32)).astype(jnp.bfloat16)
    return high, low


def column_constants():
    bins = bin_matrices()
    top = np.concatenate([bins.real, -bins.imag], axis=2)
    bottom = np.concatenate([bins.imag, bins.real], axis=2)
    return np.concatenate([top, bottom], axis=1)


def fourth(values, orient):
    (ar, ai), (br, bi), (cr, ci), (dr, di) = values
    sr, si, er, ei = ar + cr, ai + ci, ar - cr, ai - ci
    tr, ti, fr, fi = br + dr, bi + di, br - dr, bi - di
    minus, plus = (er + fi, ei - fr), (er - fi, ei + fr)
    one, three = (minus, plus) if orient < 0 else (plus, minus)
    return [(sr + tr, si + ti), one, (sr - tr, si - ti), three]


def turned(value, step, orient):
    re, im = value
    if step == 0:
        return value
    if step == 4:
        return (im, -re) if orient < 0 else (-im, re)
    cosine = math.cos(2.0 * math.pi * step / XA)
    sine = orient * math.sin(2.0 * math.pi * step / XA)
    if step == 2:
        root = cosine
        return ((re - im) * root, (re + im) * root) if orient > 0 else ((re + im) * root, (im - re) * root)
    return (re * cosine - im * sine, re * sine + im * cosine)


def sixteenth(values, orient):
    inner = [fourth([values[4 * a + b] for a in range(4)], orient) for b in range(4)]
    out = [None] * XA
    for c in range(4):
        row = fourth([turned(inner[b][c], b * c, orient) for b in range(4)], orient)
        for d in range(4):
            out[c + 4 * d] = row[d]
    return out


def halves(value):
    high = value.astype(jnp.bfloat16)
    return high, (value - high.astype(jnp.float32)).astype(jnp.bfloat16)


def dot32(a, b):
    return jnp.dot(a, b, preferred_element_type=jnp.float32)


def times(a, b):
    return (a[0] * b[0] - a[1] * b[1], a[0] * b[1] + a[1] * b[0])


def sincos(x):
    turns = jnp.floor(x * (2.0 / math.pi) + 0.5)
    rest = ((x - turns * 1.5703125) - turns * 4.837512969970703125e-4) - turns * 7.54978995489188216e-8
    square = rest * rest
    sine = rest + rest * square * (
        -1.6666654611e-1 + square * (8.3321608736e-3 + square * -1.9515295891e-4)
    )
    cosine = (1.0 - 0.5 * square) + square * square * (
        4.166664568298827e-2 + square * (-1.388731625493765e-3 + square * 2.443315711809948e-5)
    )
    quadrant = turns.astype(jnp.int32)
    odd = (quadrant & 1) == 1
    first = jnp.where(odd, cosine, sine)
    second = jnp.where(odd, sine, cosine)
    first = jnp.where((quadrant & 2) == 2, -first, first)
    second = jnp.where(((quadrant + 1) & 2) == 2, -second, second)
    return first, second


def strips(count, step):
    def run(i, carry):
        step(pl.multiple_of(i * STRIP, STRIP))
        return carry

    lax.fori_loop(0, count // STRIP, run, 0)


def rows_out(xhi, xlo, first_row, values):
    for k, (re, im) in enumerate(sixteenth(values, -1.0)):
        for part, value in enumerate((re, im)):
            high, low = halves(value)
            at = (k, pl.ds(first_row, STRIP), pl.ds(part * LANES, LANES))
            xhi[at] = high
            xlo[at] = low


def rows_in(y, first_row):
    values = [
        tuple(y[k, pl.ds(first_row, STRIP), pl.ds(part * LANES, LANES)] for part in range(2))
        for k in range(XA)
    ]
    return sixteenth(values, 1.0)


def rows_mix(xhi, xlo, mhi, mlo, y):
    def step(k, carry):
        high, low = xhi[k], xlo[k]
        y[k] = dot32(high, mhi[k]) + (dot32(low, mhi[k]) + dot32(high, mlo[k]))
        return carry

    lax.fori_loop(0, XA, step, 0)


def columns_out(xhi, xlo, field, row, values):
    for k, (re, im) in enumerate(sixteenth(values, -1.0)):
        for part, value in enumerate((re, im)):
            high, low = halves(value)
            at = (k, pl.ds(part * XB + row, STRIP), pl.ds(field * LANES, LANES))
            xhi[at] = high
            xlo[at] = low


def columns_in(y, field, row):
    values = [
        tuple(
            y[k, pl.ds(part * XB + row, STRIP), pl.ds(field * LANES, LANES)] for part in range(2)
        )
        for k in range(XA)
    ]
    return sixteenth(values, 1.0)


def columns_mix(xhi, xlo, mhi, mlo, y):
    def step(k, carry):
        high, low = xhi[k], xlo[k]
        y[k] = dot32(mhi[k], high) + (dot32(mhi[k], low) + dot32(mlo[k], high))
        return carry

    lax.fori_loop(0, XA, step, 0)


def enter_kernel(pieces, index, *refs):
    whi, wlo, mhi, mlo, out, t0, shi, slo, field, xhi, xlo, y = refs[pieces:]
    rows = sum(piece.shape[1] for piece in refs[:pieces])

    for number in range(4):
        first = number * rows
        for piece in refs[:pieces]:

            def cut(row, first=first, piece=piece, channel=number):
                high, low = halves(piece[channel, pl.ds(row, STRIP), :])
                at = pl.ds(pl.multiple_of(first + row, STRIP), STRIP)
                shi[at, :] = high
                slo[at, :] = low

            strips(piece.shape[1], cut)
            first += piece.shape[1]

    def rotated(b):
        at = [pl.ds(pl.multiple_of(index[b, s] * BLK, BLK), BLK) for s in range(SLOTS)]
        high = jnp.concatenate([shi[:, a] for a in at], axis=1)
        low = jnp.concatenate([slo[:, a] for a in at], axis=1)
        values = dot32(high, whi[b]) + (dot32(low, whi[b]) + dot32(high, wlo[b]))
        angle, loss, d_re, d_im = (values[i * rows : (i + 1) * rows] for i in range(4))
        sine, cosine = sincos(angle)
        damping = jnp.exp(-loss)
        return damping * cosine, damping * sine, d_re, d_im

    def first_slice(b, carry):
        t_re, t_im, d_re, d_im = rotated(b)
        t0[b, 0] = t_re
        t0[b, 1] = t_im
        field[b, 0] = -(d_re * t_im + d_im * t_re)
        field[b, 1] = d_re * t_re - d_im * t_im
        return carry

    lax.fori_loop(0, XA, first_slice, 0)

    def forward(row):
        at = pl.ds(row, STRIP)
        rows_out(xhi, xlo, row, [(t0[b, 0, at, :], t0[b, 1, at, :]) for b in range(XA)])
        rows_out(
            xhi,
            xlo,
            pl.multiple_of(rows + row, STRIP),
            [(field[b, 0, at, :], field[b, 1, at, :]) for b in range(XA)],
        )

    strips(rows, forward)
    rows_mix(xhi, xlo, mhi, mlo, y)

    def backward(row):
        at = pl.ds(row, STRIP)
        for number in range(2):
            values = rows_in(y, pl.multiple_of(number * rows + row, STRIP))
            for b, (re, im) in enumerate(values):
                out[b, 2 * number, at, :] = re
                out[b, 2 * number + 1, at, :] = im

    strips(rows, backward)

    def second_slice(b, carry):
        for channel, value in enumerate(rotated(XA + b)):
            out[b, 4 + channel] = value
        return carry

    lax.fori_loop(0, XA, second_slice, 0)


def row_places():
    moved = [MEMBERS.index((1 - p // HALF, p % HALF)) for p in range(XA)]
    kept = [MEMBERS.index((p // HALF, p % HALF)) for p in range(XA)]
    return [(i * QUARTER, kept if i % 2 else moved) for i in range(XB // QUARTER)]


def by_quarters(rows, step):
    for first, places in row_places():
        c, within = first // rows, first % rows

        def inner(row, first=first, c=c, within=within, places=places):
            local = pl.ds(pl.multiple_of(within + row, STRIP), STRIP)
            step(pl.multiple_of(first + row, STRIP), c, local, places)

        strips(QUARTER, inner)


def middle_kernel(chunks, *refs):
    arrived = refs[:chunks]
    mhi, mlo, out, kept, xhi, xlo, y = refs[chunks:]
    rows = XB // chunks

    def forward(row, c, local, places):
        for number in range(2):
            columns_out(
                xhi,
                xlo,
                number,
                row,
                [tuple(arrived[c][g, 2 * number + i, local, :] for i in range(2)) for g in places],
            )

    by_quarters(rows, forward)
    columns_mix(xhi, xlo, mhi, mlo, y)

    def turn(row, c, local, places):
        at = pl.ds(row, STRIP)
        wave = columns_in(y, 0, row)
        product = []
        for g, value in zip(places, wave):
            t = arrived[c][g, 4, local, :], arrived[c][g, 5, local, :]
            value = times(t, value)
            for i, part in enumerate(value + t):
                kept[g, i, at, :] = part
            product.append(value)
        columns_out(xhi, xlo, 0, row, product)
        dwave = columns_in(y, 1, row)
        change = []
        for g, value in zip(places, dwave):
            t_re, t_im, d_re, d_im = (arrived[c][g, 4 + i, local, :] for i in range(4))
            p_re, p_im = kept[g, 0, at, :], kept[g, 1, at, :]
            re, im = times((t_re, t_im), value)
            change.append((re - (d_re * p_im + d_im * p_re), im + (d_re * p_re - d_im * p_im)))
        columns_out(xhi, xlo, 1, row, change)

    by_quarters(rows, turn)
    columns_mix(xhi, xlo, mhi, mlo, y)

    def backward(row, c, local, places):
        at = pl.ds(row, STRIP)
        for number in range(2):
            for g, (re, im) in zip(places, columns_in(y, number, row)):
                out[g, 2 * number, at, :] = re
                out[g, 2 * number + 1, at, :] = im

    by_quarters(rows, backward)


def detector_kernel(fields, mhi, mlo, out, xhi, xlo, y):
    rows = fields.shape[2]

    def forward(row):
        at = pl.ds(row, STRIP)
        for number in range(2):
            rows_out(
                xhi,
                xlo,
                pl.multiple_of(number * rows + row, STRIP),
                [tuple(fields[b, 2 * number + i, at, :] for i in range(2)) for b in range(XA)],
            )

    strips(rows, forward)
    rows_mix(xhi, xlo, mhi, mlo, y)

    def turn(row):
        wave = rows_in(y, row)
        dwave = rows_in(y, pl.multiple_of(rows + row, STRIP))
        back = []
        for (re, im), (d_re, d_im) in zip(wave, dwave):
            change = 4.0 * (re * d_re + im * d_im)
            back.append((change * re, -(change * im)))
        rows_out(xhi, xlo, row, back)

    strips(rows, turn)

    def step(k, carry):
        high, low = xhi[k, :rows, :], xlo[k, :rows, :]
        y[k, :rows, :] = dot32(high, mhi[k]) + (dot32(low, mhi[k]) + dot32(high, mlo[k]))
        return carry

    lax.fori_loop(0, XA, step, 0)

    def backward(row):
        at = pl.ds(row, STRIP)
        for b, (re, im) in enumerate(rows_in(y, row)):
            out[b, 0, at, :] = re
            out[b, 1, at, :] = im

    strips(rows, backward)


def return_kernel(chunks, back, kept, mhi, mlo, *refs):
    out, (xhi, xlo, y) = refs[:chunks], refs[chunks:]
    rows = XB // chunks

    def forward(row, c, local, places):
        at = pl.ds(row, STRIP)
        columns_out(xhi, xlo, 0, row, [(back[g, 0, at, :], back[g, 1, at, :]) for g in places])

    by_quarters(rows, forward)
    columns_mix(xhi, xlo, mhi, mlo, y)

    def turn(row, c, local, places):
        at = pl.ds(row, STRIP)
        pulled = columns_in(y, 0, row)
        following = []
        for g, value in zip(places, pulled):
            re, im = times((kept[g, 0, at, :], kept[g, 1, at, :]), value)
            out[c][g, 0, local, :] = -im
            out[c][g, 1, local, :] = -re
            following.append(times((kept[g, 2, at, :], kept[g, 3, at, :]), value))
        columns_out(xhi, xlo, 0, row, following)

    by_quarters(rows, turn)
    columns_mix(xhi, xlo, mhi, mlo, y)

    def backward(row, c, local, places):
        for g, (re, im) in zip(places, columns_in(y, 0, row)):
            out[c][g, 2, local, :] = re
            out[c][g, 3, local, :] = im

    by_quarters(rows, backward)


def leave_kernel(first, index, back, t0, whi, wlo, mhi, mlo, *refs):
    before, (out, shi, slo, xhi, xlo, y) = refs[:-6], refs[-6:]
    rows = t0.shape[2]

    def forward(row):
        at = pl.ds(pl.multiple_of(first + row, STRIP), STRIP)
        rows_out(xhi, xlo, row, [(back[b, 2, at, :], back[b, 3, at, :]) for b in range(XA)])
        for b in range(XA):
            for i in range(2):
                high, low = halves(back[b, i, at, :])
                place = pl.ds(pl.multiple_of(i * rows + row, STRIP), STRIP)
                shi[XA + b, place, :] = high
                slo[XA + b, place, :] = low

    strips(rows, forward)
    rows_mix(xhi, xlo, mhi, mlo, y)

    def turn(row):
        at = pl.ds(row, STRIP)
        for b, value in enumerate(rows_in(y, row)):
            re, im = times((t0[b, 0, at, :], t0[b, 1, at, :]), value)
            for i, part in enumerate((-im, -re)):
                high, low = halves(part)
                place = pl.ds(pl.multiple_of(i * rows + row, STRIP), STRIP)
                shi[b, place, :] = high
                slo[b, place, :] = low

    strips(rows, turn)

    if before:
        out[...] = before[0][...]
    else:
        out[...] = jnp.zeros(out.shape, jnp.float32)

    def across(a, b):
        return lax.dot_general(
            a, b, (((1,), (1,)), ((), ())), preferred_element_type=jnp.float32
        )

    def step(b, carry):
        high, low = shi[b], slo[b]
        values = across(high, whi[b]) + (across(low, whi[b]) + across(high, wlo[b]))
        for s in range(SLOTS):
            at = pl.ds(pl.multiple_of(index[b, s] * BLK, BLK), BLK)
            for i in range(2):
                out[i, :, at] += values[i * rows : (i + 1) * rows, s * BLK : (s + 1) * BLK]
        return carry

    lax.fori_loop(0, NB, step, 0)


def call(kernel, outs, scratch, mix_count, extra, *operands):
    specs = [
        pl.BlockSpec(memory_space=pltpu.SMEM if o.dtype == jnp.int32 else pltpu.VMEM)
        for o in operands
    ]
    moved = sum(o.size * o.dtype.itemsize for o in operands) + sum(4 * math.prod(o) for o in outs)
    return pl.pallas_call(
        kernel,
        out_shape=[jax.ShapeDtypeStruct(o, jnp.float32) for o in outs],
        in_specs=specs,
        out_specs=[pl.BlockSpec(memory_space=pltpu.VMEM)] * len(outs),
        scratch_shapes=scratch,
        compiler_params=pltpu.CompilerParams(vmem_limit_bytes=60 * 1024 * 1024),
        cost_estimate=pl.CostEstimate(
            flops=int(mix_count * 16 * 128 * 256 * 256 * 6) + extra,
            bytes_accessed=moved,
            transcendentals=0,
        ),
    )(*operands)


def mix_scratch(rows, lanes):
    return [
        pltpu.VMEM((XA, rows, lanes), jnp.bfloat16),
        pltpu.VMEM((XA, rows, lanes), jnp.bfloat16),
        pltpu.VMEM((XA, rows, lanes), jnp.float32),
    ]


def enter(index, pieces, weights, matrices):
    rows = sum(piece.shape[1] for piece in pieces)
    scratch = [
        pltpu.VMEM((4 * rows, NB * BLK), jnp.bfloat16),
        pltpu.VMEM((4 * rows, NB * BLK), jnp.bfloat16),
        pltpu.VMEM((XA, 2, rows, LANES), jnp.float32),
    ] + mix_scratch(2 * rows, 2 * LANES)
    outs = [(XA, 8, rows, LANES), (XA, 2, rows, LANES)]
    extra = NB * 4 * rows * 256 * 128 * 6
    return call(
        functools.partial(enter_kernel, len(pieces)),
        outs,
        scratch,
        rows / XB * 2,
        extra,
        index,
        *pieces,
        *weights,
        *matrices,
    )


def middle(arrived, matrices):
    return call(
        functools.partial(middle_kernel, len(arrived)),
        [(XA, 4, XB, LANES), (XA, 4, XB, LANES)],
        mix_scratch(2 * XB, 2 * LANES),
        4,
        0,
        *arrived,
        *matrices,
    )


def detector(fields, matrices):
    rows = fields.shape[2]
    return call(
        detector_kernel,
        [(XA, 2, rows, LANES)],
        mix_scratch(2 * rows, 2 * LANES),
        3,
        0,
        fields,
        *matrices,
    )[0]


def pull(back, kept, matrices, chunks):
    return call(
        functools.partial(return_kernel, chunks),
        [(XA, 4, XB // chunks, LANES)] * chunks,
        mix_scratch(2 * XB, LANES),
        2,
        0,
        back,
        kept,
        *matrices,
    )


def leave(index, back, first, t0, weights, matrices, before):
    rows = t0.shape[2]
    scratch = [
        pltpu.VMEM((NB, 2 * rows, LANES), jnp.bfloat16),
        pltpu.VMEM((NB, 2 * rows, LANES), jnp.bfloat16),
    ] + mix_scratch(rows, 2 * LANES)
    extra = NB * 2 * rows * 256 * 128 * 6
    return call(
        functools.partial(leave_kernel, first),
        [(2, rows, NB * BLK)],
        scratch,
        rows / XB,
        extra,
        index,
        back,
        t0,
        *weights,
        *matrices,
        *before,
    )[0]


def split_weights(block_weights):
    stacked = block_weights.reshape(ANGLES, NB, SLOTS * BLK, BLK)
    rounded = lax.reduce_precision(stacked, 8, 7)
    return rounded.astype(jnp.bfloat16), (stacked - rounded).astype(jnp.bfloat16)


def device(q, b, r):
    return q * XA + b * HALF + r


def exchange(values):
    return lax.all_to_all(
        values,
        ("parts", "fft"),
        split_axis=0,
        concat_axis=0,
        axis_index_groups=[[device(x, b, r) for x, r in MEMBERS] for b in range(2)],
        tiled=True,
    )


def permute(values, steps, back=False):
    pairs = [
        (device(*here, r), device(*there, r)) for here, there in steps for r in range(HALF)
    ]
    if back:
        pairs = [(there, here) for here, there in pairs]
    return lax.ppermute(values, ("parts", "fft"), pairs)


CYCLE = [((0, 1), (0, 0)), ((0, 0), (1, 0)), ((1, 0), (1, 1)), ((1, 1), (0, 1))]
ASIDE = [((0, 1), (1, 1)), ((1, 0), (0, 0))]
ALONG = [((1, 1), (1, 0)), ((0, 0), (0, 1))]
SWAP = [((0, 1), (1, 0)), ((1, 0), (0, 1)), ((0, 0), (0, 0)), ((1, 1), (1, 1))]


def after(values, others):
    return lax.optimization_barrier((values, others))[0]


def arrive(potential, direction):
    settled = lax.axis_index("parts") == lax.axis_index("fft") // HALF
    quarters = [
        jnp.concatenate([v[:, i * QUARTER : (i + 1) * QUARTER] for v in (potential, direction)])
        for i in range(XB // QUARTER)
    ]
    chunks = []
    moved = aside = other = ()
    for i in range(0, len(quarters), 2):
        first, second = quarters[i : i + 2]
        moved = permute(after(first, moved), CYCLE)
        aside = permute(after(second, aside), ASIDE)
        other = permute(after(aside, other), ALONG)
        chunks.append([moved, jnp.where(settled, second, other)])
    return chunks


def depart(values):
    return [
        permute(values[:, :QUARTER], CYCLE, True),
        permute(values[:, QUARTER:], SWAP, True),
    ]


def blocked_body(potential, direction, block_index, block_weights):
    chunks = arrive(potential, direction)
    whi, wlo = split_weights(block_weights)
    by_column = column_constants()
    column = tuple(jnp.asarray(v) for v in split_constant(by_column))
    row = tuple(jnp.asarray(v) for v in split_constant(by_column.transpose(0, 2, 1)))
    weights = [(whi[a], wlo[a]) for a in range(ANGLES)]
    arrived = [[] for _ in range(ANGLES)]
    ahead = [[] for _ in range(ANGLES)]
    for pieces in chunks:
        for a in range(ANGLES):
            fields, t0 = enter(block_index[a], pieces, weights[a], row)
            arrived[a].append(exchange(fields))
            ahead[a].append(t0)
    carried = []
    for a in range(ANGLES):
        out, kept = middle(arrived[a], column)
        carried.append((exchange(out), kept))
    backs = [exchange(detector(out, row)) for out, _ in carried]
    count = len(chunks)
    totals = [()] * count
    for a in range(ANGLES):
        last = a == ANGLES - 1
        pulled = pull(backs[a], carried[a][1], column, count if last else 1)
        pulled = [exchange(v) for v in pulled]
        for c in range(count):
            back, first = (pulled[c], 0) if last else (pulled[0], c * (XB // count))
            totals[c] = (
                leave(block_index[a], back, first, ahead[a][c], weights[a], row, totals[c]),
            )
    return jnp.concatenate([v for total in totals for v in depart(total[0])], axis=1)


def transform_table(count_in, count_out, length, orient):
    first = jnp.arange(count_in, dtype=jnp.int32)[:, None]
    second = jnp.arange(count_out, dtype=jnp.int32)[None, :]
    phases = orient * 2.0 * math.pi / length * (first * second % length).astype(jnp.float32)
    cosine = jnp.cos(phases)
    sine_part = jnp.sin(phases)
    return jnp.stack([jnp.stack([cosine, sine_part]), jnp.stack([-sine_part, cosine])])


def twiddle_pair(count_a, count_b, length, orient):
    first = jnp.arange(count_a, dtype=jnp.int32)[:, None]
    second = jnp.arange(count_b, dtype=jnp.int32)[None, :]
    phases = orient * 2.0 * math.pi / length * (first * second % length).astype(jnp.float32)
    return (jnp.cos(phases), jnp.sin(phases))


def spread_turn(peer_count, row_count, slot_count, orient):
    turn_re, turn_im = twiddle_pair(peer_count, row_count, NX, orient)
    shape_three = (row_count, peer_count, slot_count)
    wide_re = jnp.broadcast_to(turn_re.T[:, :, None], shape_three).reshape(
        row_count, peer_count * slot_count
    )
    wide_im = jnp.broadcast_to(turn_im.T[:, :, None], shape_three).reshape(
        row_count, peer_count * slot_count
    )
    return (wide_re, wide_im)


def complex_times(values, real_part, imag_part):
    first = values[:, 0]
    second = values[:, 1]
    return jnp.stack(
        [first * real_part - second * imag_part, first * imag_part + second * real_part], axis=1
    )


def one_hot(index_rows, block_count):
    return (index_rows[..., None] == jnp.arange(block_count, dtype=jnp.int32)).astype(jnp.float32)


def rotate(values, selector, matrices):
    height = values.shape[1]
    blocked = values.reshape(2, height, NB, BLK)
    picked = jnp.einsum("cyni,bsn->cybsi", blocked, selector, precision=PRECISE)
    rotated = jnp.einsum("cybsi,bsio->cybo", picked, matrices, precision=PRECISE)
    return rotated.reshape(2, height, SL, NX)


def rotate_back(values, selector, matrices):
    height = values.shape[1]
    blocked = values.reshape(2, height, NB, BLK)
    spread_out = jnp.einsum("cybo,bsio->cybsi", blocked, matrices, precision=PRECISE)
    summed = jnp.einsum("cybsi,bsn->cyni", spread_out, selector, precision=PRECISE)
    return summed.reshape(2, height, SL * NX)


def fresnel(peer_count, row_count, slot_count, orient):
    position_high = jnp.arange(row_count, dtype=jnp.int32)[:, None]
    position_low = jnp.arange(peer_count, dtype=jnp.int32)[None, :]
    freq_y = position_low + peer_count * position_high
    freq_y = jnp.where(freq_y < NX // 2, freq_y, freq_y - NX)
    position = lax.axis_index("fft") * slot_count + jnp.arange(slot_count, dtype=jnp.int32)
    freq_x = position // XB + XA * (position % XB)
    freq_x = jnp.where(freq_x < NX // 2, freq_x, freq_x - NX)
    squares = ((freq_y * freq_y)[:, :, None] + (freq_x * freq_x)[None, None, :]) % (2 * NX)
    phases = orient * -math.pi / NX * squares.astype(jnp.float32)
    scaling = 1.0 / (NX * NX)
    phases = phases.reshape(row_count, peer_count * slot_count)
    return (jnp.cos(phases) * scaling, jnp.sin(phases) * scaling)


def propagate(fields, kernel, peer_count, row_count, slot_count):
    field_count = fields.shape[0]
    groups = XB // slot_count
    shaped = fields.reshape(field_count, 2, row_count, XA, XB)
    partial_x = jnp.einsum(
        "fcrab,cdak->fdrkb", shaped, transform_table(XA, XA, XA, -1.0), precision=PRECISE
    )
    twist_re, twist_im = twiddle_pair(XA, XB, NX, -1.0)
    partial_x = complex_times(partial_x, twist_re, twist_im)
    partial_x = jnp.einsum(
        "fcrkb,cdbt->fdrkt", partial_x, transform_table(XB, XB, XB, -1.0), precision=PRECISE
    )
    partial_x = partial_x.reshape(field_count, 2, row_count, XA, groups, slot_count)
    outgoing = partial_x.transpose(0, 1, 3, 4, 2, 5).reshape(
        field_count, 2, peer_count, row_count * slot_count
    )
    forward_re, forward_im = spread_turn(peer_count, row_count, slot_count, -1.0)
    inverse_re, inverse_im = spread_turn(peer_count, row_count, slot_count, 1.0)
    wide = peer_count * slot_count
    incoming = lax.all_to_all(outgoing, "fft", split_axis=2, concat_axis=2, tiled=True)
    item_count = incoming.shape[0]
    lattice = incoming.reshape(item_count, 2, peer_count, row_count, slot_count)
    lattice = jnp.einsum(
        "fcprs,cdpk->fdrks",
        lattice,
        transform_table(peer_count, peer_count, peer_count, -1.0),
        precision=PRECISE,
    )
    lattice = lattice.reshape(item_count, 2, row_count, wide)
    lattice = complex_times(lattice, forward_re, forward_im)
    lattice = jnp.einsum(
        "fcrq,cdrm->fdmq",
        lattice,
        transform_table(row_count, row_count, row_count, -1.0),
        precision=PRECISE,
    )
    lattice = complex_times(lattice, kernel[0], kernel[1])
    lattice = jnp.einsum(
        "fcmq,cdmr->fdrq",
        lattice,
        transform_table(row_count, row_count, row_count, 1.0),
        precision=PRECISE,
    )
    lattice = complex_times(lattice, inverse_re, inverse_im)
    lattice = lattice.reshape(item_count, 2, row_count, peer_count, slot_count)
    lattice = jnp.einsum(
        "fcrks,cdkp->fdprs",
        lattice,
        transform_table(peer_count, peer_count, peer_count, 1.0),
        precision=PRECISE,
    )
    returning = lax.all_to_all(
        lattice.reshape(item_count, 2, peer_count, row_count * slot_count),
        "fft",
        split_axis=2,
        concat_axis=2,
        tiled=True,
    )
    restored = returning.reshape(item_count, 2, XA, groups, row_count, slot_count)
    matrix_back = transform_table(XB, XB, XB, 1.0).reshape(2, 2, groups, slot_count, XB)
    restored = jnp.einsum("fckjrs,cdjsb->fdrkb", restored, matrix_back, precision=PRECISE)
    back_re, back_im = twiddle_pair(XA, XB, NX, 1.0)
    restored = complex_times(restored, back_re, back_im)
    restored = jnp.einsum(
        "fcrkb,cdkn->fdrnb", restored, transform_table(XA, XA, XA, 1.0), precision=PRECISE
    )
    return restored.reshape(item_count, 2, row_count, NX)


def general_body(potential, direction, block_index, block_weights):
    row_count = potential.shape[1]
    peer_count = lax.axis_size("fft")
    slot_count = NX // peer_count
    ahead = fresnel(peer_count, row_count, slot_count, 1.0)
    behind = fresnel(peer_count, row_count, slot_count, -1.0)
    accumulated = jnp.zeros(potential.shape, jnp.float32)
    for angle_index in range(ANGLES):
        selector = one_hot(block_index[angle_index], NB)
        matrices = block_weights[angle_index]
        rotated = rotate(potential, selector, matrices)
        tangent = rotate(direction, selector, matrices)
        damping = jnp.exp(-rotated[1])
        trans_re = damping * jnp.cos(rotated[0])
        trans_im = damping * jnp.sin(rotated[0])
        wave_re = jnp.ones((row_count, NX), jnp.float32)
        wave_im = jnp.zeros((row_count, NX), jnp.float32)
        dwave_re = jnp.zeros((row_count, NX), jnp.float32)
        dwave_im = jnp.zeros((row_count, NX), jnp.float32)
        stored = []
        for slice_index in range(SL):
            t_re = trans_re[:, slice_index]
            t_im = trans_im[:, slice_index]
            d_re = tangent[0][:, slice_index]
            d_im = tangent[1][:, slice_index]
            phi_re = t_re * wave_re - t_im * wave_im
            phi_im = t_re * wave_im + t_im * wave_re
            dphi_re = -(d_re * phi_im + d_im * phi_re) + t_re * dwave_re - t_im * dwave_im
            dphi_im = d_re * phi_re - d_im * phi_im + t_re * dwave_im + t_im * dwave_re
            stored.append((phi_re, phi_im))
            packed = jnp.stack([jnp.stack([phi_re, phi_im]), jnp.stack([dphi_re, dphi_im])])
            propagated = propagate(packed, ahead, peer_count, row_count, slot_count)
            wave_re = propagated[0, 0]
            wave_im = propagated[0, 1]
            dwave_re = propagated[1, 0]
            dwave_im = propagated[1, 1]
        change = 2.0 * (wave_re * dwave_re + wave_im * dwave_im)
        back_re = 2.0 * change * wave_re
        back_im = 2.0 * change * wave_im
        grad_re = [None] * SL
        grad_im = [None] * SL
        for slice_index in reversed(range(SL)):
            pulled = propagate(
                jnp.stack([back_re, back_im])[None], behind, peer_count, row_count, slot_count
            )
            pb_re = pulled[0, 0]
            pb_im = pulled[0, 1]
            phi_re, phi_im = stored[slice_index]
            grad_re[slice_index] = phi_re * pb_im - phi_im * pb_re
            grad_im[slice_index] = -(phi_re * pb_re + phi_im * pb_im)
            t_re = trans_re[:, slice_index]
            t_im = trans_im[:, slice_index]
            back_re = t_re * pb_re + t_im * pb_im
            back_im = t_re * pb_im - t_im * pb_re
        gradient = jnp.stack([jnp.stack(grad_re, axis=1), jnp.stack(grad_im, axis=1)])
        accumulated = accumulated + rotate_back(gradient, selector, matrices)
    return accumulated


def body(potential, direction, block_index, block_weights):
    if lax.axis_size("parts") == 2 and lax.axis_size("fft") == XA:
        return blocked_body(potential, direction, block_index, block_weights)
    return general_body(potential, direction, block_index, block_weights)


def solution(mesh):
    return jax.shard_map(
        body,
        mesh=mesh,
        in_specs=(P("parts", "fft", None), P("parts", "fft", None), P(), P()),
        out_specs=P("parts", "fft", None),
        check_vma=False,
    )
```

```python
import functools
import math

import jax
import jax.numpy as jnp
import numpy as np
from jax import lax
from jax.experimental import pallas as pl
from jax.experimental.pallas import tpu as pltpu
from jax.sharding import PartitionSpec as P

XA = 16
XB = 128
NX = 2048
SL = 2
ANGLES = 2
BLK = 128
NB = 32
SLOTS = 2
STRIP = 16
LANES = 128
CHUNKS = 4
HALF = XA // 2


PRECISE = lax.Precision.HIGHEST


def bin_matrices():
    wavenumber = np.arange(NX)
    signed = np.where(wavenumber < NX // 2, wavenumber, wavenumber - NX)
    factor = np.exp(-1j * np.pi / NX * ((signed * signed) % (2 * NX)))
    line = np.fft.ifft(factor)
    block = np.arange(XA)
    inner = np.arange(XB)
    shifts = (XB * block[:, None, None] + inner[None, :, None] - inner[None, None, :]) % NX
    phases = np.exp(-2j * np.pi / XA * ((block[:, None] * block[None, :]) % XA))
    return np.einsum("kd,dij->kij", phases, line[shifts]) / XA


def split_constant(values):
    values = values.astype(np.float32)
    high = values.astype(jnp.bfloat16)
    low = (values - high.astype(np.float32)).astype(jnp.bfloat16)
    return high, low


def column_constants():
    bins = bin_matrices()
    top = np.concatenate([bins.real, -bins.imag], axis=2)
    bottom = np.concatenate([bins.imag, bins.real], axis=2)
    return np.concatenate([top, bottom], axis=1)


def fourth(values, orient):
    (ar, ai), (br, bi), (cr, ci), (dr, di) = values
    sr, si, er, ei = ar + cr, ai + ci, ar - cr, ai - ci
    tr, ti, fr, fi = br + dr, bi + di, br - dr, bi - di
    minus, plus = (er + fi, ei - fr), (er - fi, ei + fr)
    one, three = (minus, plus) if orient < 0 else (plus, minus)
    return [(sr + tr, si + ti), one, (sr - tr, si - ti), three]


def turned(value, step, orient):
    re, im = value
    if step == 0:
        return value
    if step == 4:
        return (im, -re) if orient < 0 else (-im, re)
    cosine = math.cos(2.0 * math.pi * step / XA)
    sine = orient * math.sin(2.0 * math.pi * step / XA)
    if step == 2:
        root = cosine
        return ((re - im) * root, (re + im) * root) if orient > 0 else ((re + im) * root, (im - re) * root)
    return (re * cosine - im * sine, re * sine + im * cosine)


def sixteenth(values, orient):
    inner = [fourth([values[4 * a + b] for a in range(4)], orient) for b in range(4)]
    out = [None] * XA
    for c in range(4):
        row = fourth([turned(inner[b][c], b * c, orient) for b in range(4)], orient)
        for d in range(4):
            out[c + 4 * d] = row[d]
    return out


def halves(value):
    high = value.astype(jnp.bfloat16)
    return high, (value - high.astype(jnp.float32)).astype(jnp.bfloat16)


def dot32(a, b):
    return jnp.dot(a, b, preferred_element_type=jnp.float32)


def times(a, b):
    return (a[0] * b[0] - a[1] * b[1], a[0] * b[1] + a[1] * b[0])


def sincos(x):
    turns = jnp.floor(x * (2.0 / math.pi) + 0.5)
    rest = ((x - turns * 1.5703125) - turns * 4.837512969970703125e-4) - turns * 7.54978995489188216e-8
    square = rest * rest
    sine = rest + rest * square * (
        -1.6666654611e-1 + square * (8.3321608736e-3 + square * -1.9515295891e-4)
    )
    cosine = (1.0 - 0.5 * square) + square * square * (
        4.166664568298827e-2 + square * (-1.388731625493765e-3 + square * 2.443315711809948e-5)
    )
    quadrant = turns.astype(jnp.int32)
    odd = (quadrant & 1) == 1
    first = jnp.where(odd, cosine, sine)
    second = jnp.where(odd, sine, cosine)
    first = jnp.where((quadrant & 2) == 2, -first, first)
    second = jnp.where(((quadrant + 1) & 2) == 2, -second, second)
    return first, second


def strips(count, step):
    def run(i, carry):
        step(pl.multiple_of(i * STRIP, STRIP))
        return carry

    lax.fori_loop(0, count // STRIP, run, 0)


def rows_out(xhi, xlo, first_row, values):
    for k, (re, im) in enumerate(sixteenth(values, -1.0)):
        for part, value in enumerate((re, im)):
            high, low = halves(value)
            at = (k, pl.ds(first_row, STRIP), pl.ds(part * LANES, LANES))
            xhi[at] = high
            xlo[at] = low


def rows_in(y, first_row):
    values = [
        tuple(y[k, pl.ds(first_row, STRIP), pl.ds(part * LANES, LANES)] for part in range(2))
        for k in range(XA)
    ]
    return sixteenth(values, 1.0)


def rows_mix(xhi, xlo, mhi, mlo, y):
    def step(k, carry):
        high, low = xhi[k], xlo[k]
        y[k] = dot32(high, mhi[k]) + (dot32(low, mhi[k]) + dot32(high, mlo[k]))
        return carry

    lax.fori_loop(0, XA, step, 0)


def columns_out(xhi, xlo, field, row, values):
    for k, (re, im) in enumerate(sixteenth(values, -1.0)):
        for part, value in enumerate((re, im)):
            high, low = halves(value)
            at = (k, pl.ds(part * XB + row, STRIP), pl.ds(field * LANES, LANES))
            xhi[at] = high
            xlo[at] = low


def columns_in(y, field, row):
    values = [
        tuple(
            y[k, pl.ds(part * XB + row, STRIP), pl.ds(field * LANES, LANES)] for part in range(2)
        )
        for k in range(XA)
    ]
    return sixteenth(values, 1.0)


def columns_mix(xhi, xlo, mhi, mlo, y):
    def step(k, carry):
        high, low = xhi[k], xlo[k]
        y[k] = dot32(mhi[k], high) + (dot32(mhi[k], low) + dot32(mlo[k], high))
        return carry

    lax.fori_loop(0, XA, step, 0)


def enter_kernel(place, index, own, other, whi, wlo, mhi, mlo, out, t0, shi, slo, field, xhi, xlo, y):
    half = own.shape[1]
    rows = 2 * half

    for number in range(4):
        for piece, side in ((own, place[0]), (other, 1 - place[0])):

            def cut(row, number=number, piece=piece, side=side):
                high, low = halves(piece[number, pl.ds(row, STRIP), :])
                first = number * rows + side * half + row
                at = pl.ds(pl.multiple_of(first, STRIP), STRIP)
                shi[at, :] = high
                slo[at, :] = low

            strips(half, cut)

    def rotated(b):
        at = [pl.ds(pl.multiple_of(index[b, s] * BLK, BLK), BLK) for s in range(SLOTS)]
        high = jnp.concatenate([shi[:, a] for a in at], axis=1)
        low = jnp.concatenate([slo[:, a] for a in at], axis=1)
        values = dot32(high, whi[b]) + (dot32(low, whi[b]) + dot32(high, wlo[b]))
        angle, loss, d_re, d_im = (values[i * rows : (i + 1) * rows] for i in range(4))
        sine, cosine = sincos(angle)
        damping = jnp.exp(-loss)
        return damping * cosine, damping * sine, d_re, d_im

    def first_slice(b, carry):
        t_re, t_im, d_re, d_im = rotated(b)
        t0[b, 0] = t_re
        t0[b, 1] = t_im
        field[b, 0] = -(d_re * t_im + d_im * t_re)
        field[b, 1] = d_re * t_re - d_im * t_im
        return carry

    lax.fori_loop(0, XA, first_slice, 0)

    def forward(row):
        at = pl.ds(row, STRIP)
        rows_out(xhi, xlo, row, [(t0[b, 0, at, :], t0[b, 1, at, :]) for b in range(XA)])
        rows_out(
            xhi,
            xlo,
            pl.multiple_of(rows + row, STRIP),
            [(field[b, 0, at, :], field[b, 1, at, :]) for b in range(XA)],
        )

    strips(rows, forward)
    rows_mix(xhi, xlo, mhi, mlo, y)

    def backward(row):
        at = pl.ds(row, STRIP)
        for number in range(2):
            values = rows_in(y, pl.multiple_of(number * rows + row, STRIP))
            for b, (re, im) in enumerate(values):
                out[b, 2 * number, at, :] = re
                out[b, 2 * number + 1, at, :] = im

    strips(rows, backward)

    def second_slice(b, carry):
        for channel, value in enumerate(rotated(XA + b)):
            out[b, 4 + channel] = value
        return carry

    lax.fori_loop(0, XA, second_slice, 0)


def by_pieces(split, step):
    half = XB // CHUNKS // 2
    rows = XB // split
    for c in range(CHUNKS):
        for x in range(2):

            def inner(row, c=c, x=x):
                places = []
                for p in range(XA):
                    first = 2 * c * half + p // HALF * half
                    at = pl.ds(pl.multiple_of(first % rows + row, STRIP), STRIP)
                    places.append((first // rows, x * HALF + p % HALF, at))
                step(pl.multiple_of((2 * c + x) * half + row, STRIP), places)

            strips(half, inner)


def middle_kernel(chunks, *refs):
    arrived = refs[:chunks]
    mhi, mlo, out, kept, xhi, xlo, y = refs[chunks:]

    def forward(row, places):
        for number in range(2):
            values = [
                tuple(arrived[c][g, 2 * number + i, at, :] for i in range(2)) for c, g, at in places
            ]
            columns_out(xhi, xlo, number, row, values)

    by_pieces(chunks, forward)
    columns_mix(xhi, xlo, mhi, mlo, y)

    def turn(row, places):
        local = pl.ds(row, STRIP)
        wave = columns_in(y, 0, row)
        product = []
        for p, (c, g, at) in enumerate(places):
            t = arrived[c][g, 4, at, :], arrived[c][g, 5, at, :]
            value = times(t, wave[p])
            for i, part in enumerate(value + t):
                kept[p, i, local, :] = part
            product.append(value)
        columns_out(xhi, xlo, 0, row, product)
        dwave = columns_in(y, 1, row)
        change = []
        for p, (c, g, at) in enumerate(places):
            t_re, t_im, d_re, d_im = (arrived[c][g, 4 + i, at, :] for i in range(4))
            p_re, p_im = kept[p, 0, local, :], kept[p, 1, local, :]
            re, im = times((t_re, t_im), dwave[p])
            change.append((re - (d_re * p_im + d_im * p_re), im + (d_re * p_re - d_im * p_im)))
        columns_out(xhi, xlo, 1, row, change)

    by_pieces(chunks, turn)
    columns_mix(xhi, xlo, mhi, mlo, y)

    def backward(row, places):
        for number in range(2):
            for (_, g, at), (re, im) in zip(places, columns_in(y, number, row)):
                out[g, 2 * number, at, :] = re
                out[g, 2 * number + 1, at, :] = im

    by_pieces(1, backward)


def detector_kernel(fields, mhi, mlo, out, xhi, xlo, y):
    rows = fields.shape[2]

    def forward(row):
        at = pl.ds(row, STRIP)
        for number in range(2):
            rows_out(
                xhi,
                xlo,
                pl.multiple_of(number * rows + row, STRIP),
                [tuple(fields[b, 2 * number + i, at, :] for i in range(2)) for b in range(XA)],
            )

    strips(rows, forward)
    rows_mix(xhi, xlo, mhi, mlo, y)

    def turn(row):
        wave = rows_in(y, row)
        dwave = rows_in(y, pl.multiple_of(rows + row, STRIP))
        back = []
        for (re, im), (d_re, d_im) in zip(wave, dwave):
            change = 4.0 * (re * d_re + im * d_im)
            back.append((change * re, -(change * im)))
        rows_out(xhi, xlo, row, back)

    strips(rows, turn)

    def step(k, carry):
        high, low = xhi[k, :rows, :], xlo[k, :rows, :]
        y[k, :rows, :] = dot32(high, mhi[k]) + (dot32(low, mhi[k]) + dot32(high, mlo[k]))
        return carry

    lax.fori_loop(0, XA, step, 0)

    def backward(row):
        at = pl.ds(row, STRIP)
        for b, (re, im) in enumerate(rows_in(y, row)):
            out[b, 0, at, :] = re
            out[b, 1, at, :] = im

    strips(rows, backward)


def return_kernel(chunks, back, kept, mhi, mlo, *refs):
    out, (xhi, xlo, y) = refs[:chunks], refs[chunks:]

    def forward(row, places):
        values = [(back[g, 0, at, :], back[g, 1, at, :]) for _, g, at in places]
        columns_out(xhi, xlo, 0, row, values)

    by_pieces(1, forward)
    columns_mix(xhi, xlo, mhi, mlo, y)

    def turn(row, places):
        local = pl.ds(row, STRIP)
        pulled = columns_in(y, 0, row)
        following = []
        for p, (c, g, at) in enumerate(places):
            re, im = times((kept[p, 0, local, :], kept[p, 1, local, :]), pulled[p])
            out[c][g, 0, at, :] = -im
            out[c][g, 1, at, :] = -re
            following.append(times((kept[p, 2, local, :], kept[p, 3, local, :]), pulled[p]))
        columns_out(xhi, xlo, 0, row, following)

    by_pieces(chunks, turn)
    columns_mix(xhi, xlo, mhi, mlo, y)

    def backward(row, places):
        for (c, g, at), (re, im) in zip(places, columns_in(y, 0, row)):
            out[c][g, 2, at, :] = re
            out[c][g, 3, at, :] = im

    by_pieces(chunks, backward)


def leave_kernel(pieces, first, place, index, back, whi, wlo, mhi, mlo, *refs):
    t0 = refs[:pieces]
    before, (near, far, shi, slo, xhi, xlo, y) = refs[pieces:-7], refs[-7:]
    chunk = t0[0].shape[2]
    half = chunk // 2
    rows = pieces * chunk

    def pieces_of(step):
        for end, side in enumerate((1 - place[1], place[1])):
            for c in range(pieces):

                def inner(row, end=end, side=side, c=c):
                    within = pl.multiple_of(side * half + row, STRIP)
                    source = pl.multiple_of(first + c * chunk + side * half + row, STRIP)
                    target = pl.multiple_of((end * pieces + c) * half + row, STRIP)
                    step(c, pl.ds(within, STRIP), pl.ds(source, STRIP), target)

                strips(half, inner)

    def store(b, i, target, value):
        high, low = halves(value)
        at = pl.ds(pl.multiple_of(i * rows + target, STRIP), STRIP)
        shi[b, at, :] = high
        slo[b, at, :] = low

    def forward(c, within, at, target):
        rows_out(xhi, xlo, target, [(back[b, 2, at, :], back[b, 3, at, :]) for b in range(XA)])
        for b in range(XA):
            for i in range(2):
                store(XA + b, i, target, back[b, i, at, :])

    pieces_of(forward)
    rows_mix(xhi, xlo, mhi, mlo, y)

    def turn(c, within, at, target):
        for b, value in enumerate(rows_in(y, target)):
            re, im = times((t0[c][b, 0, within, :], t0[c][b, 1, within, :]), value)
            store(b, 0, target, -im)
            store(b, 1, target, -re)

    pieces_of(turn)

    for out, old in zip((near, far), before or (None, None)):
        out[...] = jnp.zeros(out.shape, jnp.float32) if old is None else old[...]

    def across(a, b):
        return lax.dot_general(
            a, b, (((1,), (1,)), ((), ())), preferred_element_type=jnp.float32
        )

    def step(b, carry):
        high, low = shi[b], slo[b]
        values = across(high, whi[b]) + (across(low, whi[b]) + across(high, wlo[b]))
        for s in range(SLOTS):
            at = pl.ds(pl.multiple_of(index[b, s] * BLK, BLK), BLK)
            for i in range(2):
                for end, out in enumerate((near, far)):
                    start = i * rows + end * (rows // 2)
                    part = values[start : start + rows // 2, s * BLK : (s + 1) * BLK]
                    out[i, :, at] += part
        return carry

    lax.fori_loop(0, NB, step, 0)


def call(kernel, outs, scratch, mix_count, extra, *operands):
    specs = [
        pl.BlockSpec(memory_space=pltpu.SMEM if o.dtype == jnp.int32 else pltpu.VMEM)
        for o in operands
    ]
    moved = sum(o.size * o.dtype.itemsize for o in operands) + sum(4 * math.prod(o) for o in outs)
    return pl.pallas_call(
        kernel,
        out_shape=[jax.ShapeDtypeStruct(o, jnp.float32) for o in outs],
        in_specs=specs,
        out_specs=[pl.BlockSpec(memory_space=pltpu.VMEM)] * len(outs),
        scratch_shapes=scratch,
        compiler_params=pltpu.CompilerParams(vmem_limit_bytes=60 * 1024 * 1024),
        cost_estimate=pl.CostEstimate(
            flops=int(mix_count * 16 * 128 * 256 * 256 * 6) + extra,
            bytes_accessed=moved,
            transcendentals=0,
        ),
    )(*operands)


def mix_scratch(rows, lanes):
    return [
        pltpu.VMEM((XA, rows, lanes), jnp.bfloat16),
        pltpu.VMEM((XA, rows, lanes), jnp.bfloat16),
        pltpu.VMEM((XA, rows, lanes), jnp.float32),
    ]


def enter(place, index, own, other, weights, matrices):
    rows = 2 * own.shape[1]
    scratch = [
        pltpu.VMEM((4 * rows, NB * BLK), jnp.bfloat16),
        pltpu.VMEM((4 * rows, NB * BLK), jnp.bfloat16),
        pltpu.VMEM((XA, 2, rows, LANES), jnp.float32),
    ] + mix_scratch(2 * rows, 2 * LANES)
    outs = [(XA, 8, rows, LANES), (XA, 2, rows, LANES)]
    extra = NB * 4 * rows * 256 * 128 * 6
    return call(
        enter_kernel,
        outs,
        scratch,
        rows / XB * 2,
        extra,
        place,
        index,
        own,
        other,
        *weights,
        *matrices,
    )


def middle(arrived, matrices):
    return call(
        functools.partial(middle_kernel, len(arrived)),
        [(XA, 4, XB, LANES), (XA, 4, XB, LANES)],
        mix_scratch(2 * XB, 2 * LANES),
        4,
        0,
        *arrived,
        *matrices,
    )


def detector(fields, matrices):
    rows = fields.shape[2]
    return call(
        detector_kernel,
        [(XA, 2, rows, LANES)],
        mix_scratch(2 * rows, 2 * LANES),
        3,
        0,
        fields,
        *matrices,
    )[0]


def pull(back, kept, matrices, chunks):
    return call(
        functools.partial(return_kernel, chunks),
        [(XA, 4, XB // chunks, LANES)] * chunks,
        mix_scratch(2 * XB, LANES),
        2,
        0,
        back,
        kept,
        *matrices,
    )


def leave(place, index, back, first, t0, weights, matrices, before):
    rows = sum(t.shape[2] for t in t0)
    scratch = [
        pltpu.VMEM((NB, 2 * rows, LANES), jnp.bfloat16),
        pltpu.VMEM((NB, 2 * rows, LANES), jnp.bfloat16),
    ] + mix_scratch(rows, 2 * LANES)
    extra = NB * 2 * rows * 256 * 128 * 6
    return call(
        functools.partial(leave_kernel, len(t0), first),
        [(2, rows // 2, NB * BLK)] * 2,
        scratch,
        rows / XB,
        extra,
        place,
        index,
        back,
        *weights,
        *matrices,
        *t0,
        *before,
    )


def split_weights(block_weights):
    stacked = block_weights.reshape(ANGLES, NB, SLOTS * BLK, BLK)
    rounded = lax.reduce_precision(stacked, 8, 7)
    return rounded.astype(jnp.bfloat16), (stacked - rounded).astype(jnp.bfloat16)


def device(q, b, r):
    return q * XA + b * HALF + r


def exchange(values):
    return lax.all_to_all(
        values,
        ("parts", "fft"),
        split_axis=0,
        concat_axis=0,
        axis_index_groups=[[device(x, b, r) for x in range(2) for r in range(HALF)] for b in range(2)],
        tiled=True,
    )


def permute(values, steps):
    pairs = [
        (device(*here, r), device(*there, r)) for here, there in steps for r in range(HALF)
    ]
    return lax.ppermute(values, ("parts", "fft"), pairs)


BESIDE = [((q, b), (1 - q, b)) for q in range(2) for b in range(2)]
ALONG = [((q, b), (q, 1 - b)) for q in range(2) for b in range(2)]
CYCLE = [((0, 0), (0, 1)), ((1, 0), (0, 0)), ((1, 1), (1, 0)), ((0, 1), (1, 1))]
ACROSS = [((0, 1), (1, 0)), ((1, 0), (0, 1))]


def after(values, others):
    return lax.optimization_barrier((values, others))[0]


def arrive(potential, direction, q, b):
    half = XB // CHUNKS // 2
    chunks = []
    beside = along = ()
    for c in range(CHUNKS):
        lower, upper = (
            jnp.concatenate(
                [v[:, (2 * c + x) * half : (2 * c + x + 1) * half] for v in (potential, direction)]
            )
            for x in range(2)
        )
        keep = jnp.where(q == 0, lower, upper)
        give = jnp.where(q == 0, upper, lower)
        beside = permute(after(give, beside), BESIDE)
        own = jnp.where(q == b, keep, beside)
        give = jnp.where(q == b, beside, keep)
        along = permute(after(give, along), ALONG)
        chunks.append((own, along, beside))
    return chunks


def depart(near, far, q, b):
    once = permute(near, CYCLE)
    twice = permute(far, ACROSS)
    same = jnp.where(q == b, far, once)
    rest = jnp.where(q == b, once, twice)
    return jnp.where(q == 0, same, rest), jnp.where(q == 0, rest, same)


def blocked_body(potential, direction, block_index, block_weights):
    q = lax.axis_index("parts")
    b = lax.axis_index("fft") // HALF
    place = jnp.stack([b, q]).astype(jnp.int32)
    chunks = arrive(potential, direction, q, b)
    whi, wlo = split_weights(block_weights)
    by_column = column_constants()
    column = tuple(jnp.asarray(v) for v in split_constant(by_column))
    row = tuple(jnp.asarray(v) for v in split_constant(by_column.transpose(0, 2, 1)))
    weights = [(whi[a], wlo[a]) for a in range(ANGLES)]
    arrived = [[] for _ in range(ANGLES)]
    ahead = [[] for _ in range(ANGLES)]
    for c, (own, along, _) in enumerate(chunks):
        for a in range(ANGLES):
            if c + 1 < CHUNKS:
                own = after(own, chunks[c + 1][1 if a else 2])
            fields, t0 = enter(place, block_index[a], own, along, weights[a], row)
            arrived[a].append(exchange(fields))
            ahead[a].append(t0)
    carried = []
    for a in range(ANGLES):
        out, kept = middle(arrived[a], column)
        carried.append((exchange(out), kept))
    backs = [exchange(detector(out, row)) for out, _ in carried]
    ends = 2
    span = CHUNKS // ends
    totals = [()] * ends
    for a in range(ANGLES):
        last = a == ANGLES - 1
        pulled = pull(backs[a], carried[a][1], column, ends if last else 1)
        if last:
            pulled = [exchange(pulled[0]), exchange(after(pulled[1], totals))]
        else:
            pulled = [exchange(pulled[0])]
        for e in range(ends):
            back, first = (pulled[e], 0) if last else (pulled[0], e * (XB // ends))
            t0 = ahead[a][e * span : (e + 1) * span]
            totals[e] = leave(place, block_index[a], back, first, t0, weights[a], row, totals[e])
    pieces = []
    half = XB // CHUNKS // 2
    for total in totals:
        lower, upper = depart(*total, q, b)
        for c in range(span):
            pieces += [v[:, c * half : (c + 1) * half] for v in (lower, upper)]
    return jnp.concatenate(pieces, axis=1)


def transform_table(count_in, count_out, length, orient):
    first = jnp.arange(count_in, dtype=jnp.int32)[:, None]
    second = jnp.arange(count_out, dtype=jnp.int32)[None, :]
    phases = orient * 2.0 * math.pi / length * (first * second % length).astype(jnp.float32)
    cosine = jnp.cos(phases)
    sine_part = jnp.sin(phases)
    return jnp.stack([jnp.stack([cosine, sine_part]), jnp.stack([-sine_part, cosine])])


def twiddle_pair(count_a, count_b, length, orient):
    first = jnp.arange(count_a, dtype=jnp.int32)[:, None]
    second = jnp.arange(count_b, dtype=jnp.int32)[None, :]
    phases = orient * 2.0 * math.pi / length * (first * second % length).astype(jnp.float32)
    return (jnp.cos(phases), jnp.sin(phases))


def spread_turn(peer_count, row_count, slot_count, orient):
    turn_re, turn_im = twiddle_pair(peer_count, row_count, NX, orient)
    shape_three = (row_count, peer_count, slot_count)
    wide_re = jnp.broadcast_to(turn_re.T[:, :, None], shape_three).reshape(
        row_count, peer_count * slot_count
    )
    wide_im = jnp.broadcast_to(turn_im.T[:, :, None], shape_three).reshape(
        row_count, peer_count * slot_count
    )
    return (wide_re, wide_im)


def complex_times(values, real_part, imag_part):
    first = values[:, 0]
    second = values[:, 1]
    return jnp.stack(
        [first * real_part - second * imag_part, first * imag_part + second * real_part], axis=1
    )


def one_hot(index_rows, block_count):
    return (index_rows[..., None] == jnp.arange(block_count, dtype=jnp.int32)).astype(jnp.float32)


def rotate(values, selector, matrices):
    height = values.shape[1]
    blocked = values.reshape(2, height, NB, BLK)
    picked = jnp.einsum("cyni,bsn->cybsi", blocked, selector, precision=PRECISE)
    rotated = jnp.einsum("cybsi,bsio->cybo", picked, matrices, precision=PRECISE)
    return rotated.reshape(2, height, SL, NX)


def rotate_back(values, selector, matrices):
    height = values.shape[1]
    blocked = values.reshape(2, height, NB, BLK)
    spread_out = jnp.einsum("cybo,bsio->cybsi", blocked, matrices, precision=PRECISE)
    summed = jnp.einsum("cybsi,bsn->cyni", spread_out, selector, precision=PRECISE)
    return summed.reshape(2, height, SL * NX)


def fresnel(peer_count, row_count, slot_count, orient):
    position_high = jnp.arange(row_count, dtype=jnp.int32)[:, None]
    position_low = jnp.arange(peer_count, dtype=jnp.int32)[None, :]
    freq_y = position_low + peer_count * position_high
    freq_y = jnp.where(freq_y < NX // 2, freq_y, freq_y - NX)
    position = lax.axis_index("fft") * slot_count + jnp.arange(slot_count, dtype=jnp.int32)
    freq_x = position // XB + XA * (position % XB)
    freq_x = jnp.where(freq_x < NX // 2, freq_x, freq_x - NX)
    squares = ((freq_y * freq_y)[:, :, None] + (freq_x * freq_x)[None, None, :]) % (2 * NX)
    phases = orient * -math.pi / NX * squares.astype(jnp.float32)
    scaling = 1.0 / (NX * NX)
    phases = phases.reshape(row_count, peer_count * slot_count)
    return (jnp.cos(phases) * scaling, jnp.sin(phases) * scaling)


def propagate(fields, kernel, peer_count, row_count, slot_count):
    field_count = fields.shape[0]
    groups = XB // slot_count
    shaped = fields.reshape(field_count, 2, row_count, XA, XB)
    partial_x = jnp.einsum(
        "fcrab,cdak->fdrkb", shaped, transform_table(XA, XA, XA, -1.0), precision=PRECISE
    )
    twist_re, twist_im = twiddle_pair(XA, XB, NX, -1.0)
    partial_x = complex_times(partial_x, twist_re, twist_im)
    partial_x = jnp.einsum(
        "fcrkb,cdbt->fdrkt", partial_x, transform_table(XB, XB, XB, -1.0), precision=PRECISE
    )
    partial_x = partial_x.reshape(field_count, 2, row_count, XA, groups, slot_count)
    outgoing = partial_x.transpose(0, 1, 3, 4, 2, 5).reshape(
        field_count, 2, peer_count, row_count * slot_count
    )
    forward_re, forward_im = spread_turn(peer_count, row_count, slot_count, -1.0)
    inverse_re, inverse_im = spread_turn(peer_count, row_count, slot_count, 1.0)
    wide = peer_count * slot_count
    incoming = lax.all_to_all(outgoing, "fft", split_axis=2, concat_axis=2, tiled=True)
    item_count = incoming.shape[0]
    lattice = incoming.reshape(item_count, 2, peer_count, row_count, slot_count)
    lattice = jnp.einsum(
        "fcprs,cdpk->fdrks",
        lattice,
        transform_table(peer_count, peer_count, peer_count, -1.0),
        precision=PRECISE,
    )
    lattice = lattice.reshape(item_count, 2, row_count, wide)
    lattice = complex_times(lattice, forward_re, forward_im)
    lattice = jnp.einsum(
        "fcrq,cdrm->fdmq",
        lattice,
        transform_table(row_count, row_count, row_count, -1.0),
        precision=PRECISE,
    )
    lattice = complex_times(lattice, kernel[0], kernel[1])
    lattice = jnp.einsum(
        "fcmq,cdmr->fdrq",
        lattice,
        transform_table(row_count, row_count, row_count, 1.0),
        precision=PRECISE,
    )
    lattice = complex_times(lattice, inverse_re, inverse_im)
    lattice = lattice.reshape(item_count, 2, row_count, peer_count, slot_count)
    lattice = jnp.einsum(
        "fcrks,cdkp->fdprs",
        lattice,
        transform_table(peer_count, peer_count, peer_count, 1.0),
        precision=PRECISE,
    )
    returning = lax.all_to_all(
        lattice.reshape(item_count, 2, peer_count, row_count * slot_count),
        "fft",
        split_axis=2,
        concat_axis=2,
        tiled=True,
    )
    restored = returning.reshape(item_count, 2, XA, groups, row_count, slot_count)
    matrix_back = transform_table(XB, XB, XB, 1.0).reshape(2, 2, groups, slot_count, XB)
    restored = jnp.einsum("fckjrs,cdjsb->fdrkb", restored, matrix_back, precision=PRECISE)
    back_re, back_im = twiddle_pair(XA, XB, NX, 1.0)
    restored = complex_times(restored, back_re, back_im)
    restored = jnp.einsum(
        "fcrkb,cdkn->fdrnb", restored, transform_table(XA, XA, XA, 1.0), precision=PRECISE
    )
    return restored.reshape(item_count, 2, row_count, NX)


def general_body(potential, direction, block_index, block_weights):
    row_count = potential.shape[1]
    peer_count = lax.axis_size("fft")
    slot_count = NX // peer_count
    ahead = fresnel(peer_count, row_count, slot_count, 1.0)
    behind = fresnel(peer_count, row_count, slot_count, -1.0)
    accumulated = jnp.zeros(potential.shape, jnp.float32)
    for angle_index in range(ANGLES):
        selector = one_hot(block_index[angle_index], NB)
        matrices = block_weights[angle_index]
        rotated = rotate(potential, selector, matrices)
        tangent = rotate(direction, selector, matrices)
        damping = jnp.exp(-rotated[1])
        trans_re = damping * jnp.cos(rotated[0])
        trans_im = damping * jnp.sin(rotated[0])
        wave_re = jnp.ones((row_count, NX), jnp.float32)
        wave_im = jnp.zeros((row_count, NX), jnp.float32)
        dwave_re = jnp.zeros((row_count, NX), jnp.float32)
        dwave_im = jnp.zeros((row_count, NX), jnp.float32)
        stored = []
        for slice_index in range(SL):
            t_re = trans_re[:, slice_index]
            t_im = trans_im[:, slice_index]
            d_re = tangent[0][:, slice_index]
            d_im = tangent[1][:, slice_index]
            phi_re = t_re * wave_re - t_im * wave_im
            phi_im = t_re * wave_im + t_im * wave_re
            dphi_re = -(d_re * phi_im + d_im * phi_re) + t_re * dwave_re - t_im * dwave_im
            dphi_im = d_re * phi_re - d_im * phi_im + t_re * dwave_im + t_im * dwave_re
            stored.append((phi_re, phi_im))
            packed = jnp.stack([jnp.stack([phi_re, phi_im]), jnp.stack([dphi_re, dphi_im])])
            propagated = propagate(packed, ahead, peer_count, row_count, slot_count)
            wave_re = propagated[0, 0]
            wave_im = propagated[0, 1]
            dwave_re = propagated[1, 0]
            dwave_im = propagated[1, 1]
        change = 2.0 * (wave_re * dwave_re + wave_im * dwave_im)
        back_re = 2.0 * change * wave_re
        back_im = 2.0 * change * wave_im
        grad_re = [None] * SL
        grad_im = [None] * SL
        for slice_index in reversed(range(SL)):
            pulled = propagate(
                jnp.stack([back_re, back_im])[None], behind, peer_count, row_count, slot_count
            )
            pb_re = pulled[0, 0]
            pb_im = pulled[0, 1]
            phi_re, phi_im = stored[slice_index]
            grad_re[slice_index] = phi_re * pb_im - phi_im * pb_re
            grad_im[slice_index] = -(phi_re * pb_re + phi_im * pb_im)
            t_re = trans_re[:, slice_index]
            t_im = trans_im[:, slice_index]
            back_re = t_re * pb_re + t_im * pb_im
            back_im = t_re * pb_im - t_im * pb_re
        gradient = jnp.stack([jnp.stack(grad_re, axis=1), jnp.stack(grad_im, axis=1)])
        accumulated = accumulated + rotate_back(gradient, selector, matrices)
    return accumulated


def body(potential, direction, block_index, block_weights):
    if lax.axis_size("parts") == 2 and lax.axis_size("fft") == XA:
        return blocked_body(potential, direction, block_index, block_weights)
    return general_body(potential, direction, block_index, block_weights)


def solution(mesh):
    return jax.shard_map(
        body,
        mesh=mesh,
        in_specs=(P("parts", "fft", None), P("parts", "fft", None), P(), P()),
        out_specs=P("parts", "fft", None),
        check_vma=False,
    )
```

```python
import functools
import math

import jax
import jax.numpy as jnp
import numpy as np
from jax import lax
from jax.experimental import pallas as pl
from jax.experimental.pallas import tpu as pltpu
from jax.sharding import PartitionSpec as P

XA = 16
XB = 128
NX = 2048
SL = 2
ANGLES = 2
BLK = 128
NB = 32
SLOTS = 2
STRIP = 16
LANES = 128
CHUNKS = 4
HALF = XA // 2


PRECISE = lax.Precision.HIGHEST


def bin_matrices():
    wavenumber = np.arange(NX)
    signed = np.where(wavenumber < NX // 2, wavenumber, wavenumber - NX)
    factor = np.exp(-1j * np.pi / NX * ((signed * signed) % (2 * NX)))
    line = np.fft.ifft(factor)
    block = np.arange(XA)
    inner = np.arange(XB)
    shifts = (XB * block[:, None, None] + inner[None, :, None] - inner[None, None, :]) % NX
    phases = np.exp(-2j * np.pi / XA * ((block[:, None] * block[None, :]) % XA))
    return np.einsum("kd,dij->kij", phases, line[shifts]) / XA


def split_constant(values):
    values = values.astype(np.float32)
    high = values.astype(jnp.bfloat16)
    low = (values - high.astype(np.float32)).astype(jnp.bfloat16)
    return high, low


def column_constants():
    bins = bin_matrices()
    top = np.concatenate([bins.real, -bins.imag], axis=2)
    bottom = np.concatenate([bins.imag, bins.real], axis=2)
    return np.concatenate([top, bottom], axis=1)


def fourth(values, orient):
    (ar, ai), (br, bi), (cr, ci), (dr, di) = values
    sr, si, er, ei = ar + cr, ai + ci, ar - cr, ai - ci
    tr, ti, fr, fi = br + dr, bi + di, br - dr, bi - di
    minus, plus = (er + fi, ei - fr), (er - fi, ei + fr)
    one, three = (minus, plus) if orient < 0 else (plus, minus)
    return [(sr + tr, si + ti), one, (sr - tr, si - ti), three]


def turned(value, step, orient):
    re, im = value
    if step == 0:
        return value
    if step == 4:
        return (im, -re) if orient < 0 else (-im, re)
    cosine = math.cos(2.0 * math.pi * step / XA)
    sine = orient * math.sin(2.0 * math.pi * step / XA)
    if step == 2:
        root = cosine
        return ((re - im) * root, (re + im) * root) if orient > 0 else ((re + im) * root, (im - re) * root)
    return (re * cosine - im * sine, re * sine + im * cosine)


def sixteenth(values, orient):
    inner = [fourth([values[4 * a + b] for a in range(4)], orient) for b in range(4)]
    out = [None] * XA
    for c in range(4):
        row = fourth([turned(inner[b][c], b * c, orient) for b in range(4)], orient)
        for d in range(4):
            out[c + 4 * d] = row[d]
    return out


def halves(value):
    high = value.astype(jnp.bfloat16)
    return high, (value - high.astype(jnp.float32)).astype(jnp.bfloat16)


def dot32(a, b):
    return jnp.dot(a, b, preferred_element_type=jnp.float32)


def times(a, b):
    return (a[0] * b[0] - a[1] * b[1], a[0] * b[1] + a[1] * b[0])


def sincos(x):
    turns = jnp.floor(x * (2.0 / math.pi) + 0.5)
    rest = ((x - turns * 1.5703125) - turns * 4.837512969970703125e-4) - turns * 7.54978995489188216e-8
    square = rest * rest
    sine = rest + rest * square * (
        -1.6666654611e-1 + square * (8.3321608736e-3 + square * -1.9515295891e-4)
    )
    cosine = (1.0 - 0.5 * square) + square * square * (
        4.166664568298827e-2 + square * (-1.388731625493765e-3 + square * 2.443315711809948e-5)
    )
    quadrant = turns.astype(jnp.int32)
    odd = (quadrant & 1) == 1
    first = jnp.where(odd, cosine, sine)
    second = jnp.where(odd, sine, cosine)
    first = jnp.where((quadrant & 2) == 2, -first, first)
    second = jnp.where(((quadrant + 1) & 2) == 2, -second, second)
    return first, second


def strips(count, step):
    def run(i, carry):
        step(pl.multiple_of(i * STRIP, STRIP))
        return carry

    lax.fori_loop(0, count // STRIP, run, 0)


def rows_out(xhi, xlo, first_row, values):
    for k, (re, im) in enumerate(sixteenth(values, -1.0)):
        for part, value in enumerate((re, im)):
            high, low = halves(value)
            at = (k, pl.ds(first_row, STRIP), pl.ds(part * LANES, LANES))
            xhi[at] = high
            xlo[at] = low


def rows_in(y, first_row):
    values = [
        tuple(y[k, pl.ds(first_row, STRIP), pl.ds(part * LANES, LANES)] for part in range(2))
        for k in range(XA)
    ]
    return sixteenth(values, 1.0)


def rows_mix(xhi, xlo, mhi, mlo, y):
    def step(k, carry):
        high, low = xhi[k], xlo[k]
        y[k] = dot32(high, mhi[k]) + (dot32(low, mhi[k]) + dot32(high, mlo[k]))
        return carry

    lax.fori_loop(0, XA, step, 0)


def columns_out(xhi, xlo, field, row, values):
    for k, (re, im) in enumerate(sixteenth(values, -1.0)):
        for part, value in enumerate((re, im)):
            high, low = halves(value)
            at = (k, pl.ds(part * XB + row, STRIP), pl.ds(field * LANES, LANES))
            xhi[at] = high
            xlo[at] = low


def columns_in(y, field, row):
    values = [
        tuple(
            y[k, pl.ds(part * XB + row, STRIP), pl.ds(field * LANES, LANES)] for part in range(2)
        )
        for k in range(XA)
    ]
    return sixteenth(values, 1.0)


def columns_mix(xhi, xlo, mhi, mlo, y):
    def step(k, carry):
        high, low = xhi[k], xlo[k]
        y[k] = dot32(mhi[k], high) + (dot32(mhi[k], low) + dot32(mlo[k], high))
        return carry

    lax.fori_loop(0, XA, step, 0)


def enter_kernel(place, index, own, other, whi, wlo, mhi, mlo, out, t0, shi, slo, field, xhi, xlo, y):
    half = own.shape[1]
    rows = 2 * half

    for number in range(4):
        for piece, side in ((own, place[0]), (other, 1 - place[0])):

            def cut(row, number=number, piece=piece, side=side):
                high, low = halves(piece[number, pl.ds(row, STRIP), :])
                first = number * rows + side * half + row
                at = pl.ds(pl.multiple_of(first, STRIP), STRIP)
                shi[at, :] = high
                slo[at, :] = low

            strips(half, cut)

    def rotated(b):
        at = [pl.ds(pl.multiple_of(index[b, s] * BLK, BLK), BLK) for s in range(SLOTS)]
        high = jnp.concatenate([shi[:, a] for a in at], axis=1)
        low = jnp.concatenate([slo[:, a] for a in at], axis=1)
        values = dot32(high, whi[b]) + (dot32(low, whi[b]) + dot32(high, wlo[b]))
        angle, loss, d_re, d_im = (values[i * rows : (i + 1) * rows] for i in range(4))
        sine, cosine = sincos(angle)
        damping = jnp.exp(-loss)
        return damping * cosine, damping * sine, d_re, d_im

    def first_slice(b, carry):
        t_re, t_im, d_re, d_im = rotated(b)
        t0[b, 0] = t_re
        t0[b, 1] = t_im
        field[b, 0] = -(d_re * t_im + d_im * t_re)
        field[b, 1] = d_re * t_re - d_im * t_im
        return carry

    lax.fori_loop(0, XA, first_slice, 0)

    def forward(row):
        at = pl.ds(row, STRIP)
        rows_out(xhi, xlo, row, [(t0[b, 0, at, :], t0[b, 1, at, :]) for b in range(XA)])
        rows_out(
            xhi,
            xlo,
            pl.multiple_of(rows + row, STRIP),
            [(field[b, 0, at, :], field[b, 1, at, :]) for b in range(XA)],
        )

    strips(rows, forward)
    rows_mix(xhi, xlo, mhi, mlo, y)

    def backward(row):
        at = pl.ds(row, STRIP)
        for number in range(2):
            values = rows_in(y, pl.multiple_of(number * rows + row, STRIP))
            for b, (re, im) in enumerate(values):
                out[b, 2 * number, at, :] = re
                out[b, 2 * number + 1, at, :] = im

    strips(rows, backward)

    def second_slice(b, carry):
        for channel, value in enumerate(rotated(XA + b)):
            out[b, 4 + channel] = value
        return carry

    lax.fori_loop(0, XA, second_slice, 0)


def by_pieces(split, step):
    half = XB // CHUNKS // 2
    rows = XB // split
    for c in range(CHUNKS):
        for x in range(2):

            def inner(row, c=c, x=x):
                places = []
                for p in range(XA):
                    first = 2 * c * half + p // HALF * half
                    at = pl.ds(pl.multiple_of(first % rows + row, STRIP), STRIP)
                    places.append((first // rows, x * HALF + p % HALF, at))
                step(pl.multiple_of((2 * c + x) * half + row, STRIP), places)

            strips(half, inner)


def bring(place, parts, whole, sems, first=0):
    rows = whole.shape[2]
    copies = [
        pltpu.make_async_copy(
            part.at[:, pl.ds(first, rows), :], whole.at[place[2] ^ s], sems.at[s]
        )
        for s, part in enumerate(parts)
    ]
    for copy in copies:
        copy.start()
    for copy in copies:
        copy.wait()


def hand_out(place, whole, parts, sems):
    copies = [
        pltpu.make_async_copy(whole.at[place[2] ^ s], part, sems.at[s])
        for s, part in enumerate(parts)
    ]
    for copy in copies:
        copy.start()
    for copy in copies:
        copy.wait()


def middle_kernel(chunks, place, *refs):
    arrived = refs[:chunks]
    mhi, mlo, kept, *sent = refs[chunks:-5]
    out, sems, xhi, xlo, y = refs[-5:]

    def forward(row, places):
        for number in range(2):
            values = [
                tuple(arrived[c][g, 2 * number + i, at, :] for i in range(2)) for c, g, at in places
            ]
            columns_out(xhi, xlo, number, row, values)

    by_pieces(chunks, forward)
    columns_mix(xhi, xlo, mhi, mlo, y)

    def turn(row, places):
        local = pl.ds(row, STRIP)
        wave = columns_in(y, 0, row)
        product = []
        for p, (c, g, at) in enumerate(places):
            t = arrived[c][g, 4, at, :], arrived[c][g, 5, at, :]
            value = times(t, wave[p])
            for i, part in enumerate(value + t):
                kept[p, i, local, :] = part
            product.append(value)
        columns_out(xhi, xlo, 0, row, product)
        dwave = columns_in(y, 1, row)
        change = []
        for p, (c, g, at) in enumerate(places):
            t_re, t_im, d_re, d_im = (arrived[c][g, 4 + i, at, :] for i in range(4))
            p_re, p_im = kept[p, 0, local, :], kept[p, 1, local, :]
            re, im = times((t_re, t_im), dwave[p])
            change.append((re - (d_re * p_im + d_im * p_re), im + (d_re * p_re - d_im * p_im)))
        columns_out(xhi, xlo, 1, row, change)

    by_pieces(chunks, turn)
    columns_mix(xhi, xlo, mhi, mlo, y)

    def backward(row, places):
        for number in range(2):
            for (_, g, at), (re, im) in zip(places, columns_in(y, number, row)):
                out[g, 2 * number, at, :] = re
                out[g, 2 * number + 1, at, :] = im

    by_pieces(1, backward)
    hand_out(place, out, sent, sems)


def detector_kernel(place, mhi, mlo, *refs):
    parts, sent = refs[:XA], refs[XA : 2 * XA]
    fields, out, sems, xhi, xlo, y = refs[2 * XA :]
    bring(place, parts, fields, sems)
    rows = fields.shape[2]

    def forward(row):
        at = pl.ds(row, STRIP)
        for number in range(2):
            rows_out(
                xhi,
                xlo,
                pl.multiple_of(number * rows + row, STRIP),
                [tuple(fields[b, 2 * number + i, at, :] for i in range(2)) for b in range(XA)],
            )

    strips(rows, forward)
    rows_mix(xhi, xlo, mhi, mlo, y)

    def turn(row):
        wave = rows_in(y, row)
        dwave = rows_in(y, pl.multiple_of(rows + row, STRIP))
        back = []
        for (re, im), (d_re, d_im) in zip(wave, dwave):
            change = 4.0 * (re * d_re + im * d_im)
            back.append((change * re, -(change * im)))
        rows_out(xhi, xlo, row, back)

    strips(rows, turn)

    def step(k, carry):
        high, low = xhi[k, :rows, :], xlo[k, :rows, :]
        y[k, :rows, :] = dot32(high, mhi[k]) + (dot32(low, mhi[k]) + dot32(high, mlo[k]))
        return carry

    lax.fori_loop(0, XA, step, 0)

    def backward(row):
        at = pl.ds(row, STRIP)
        for b, (re, im) in enumerate(rows_in(y, row)):
            out[b, 0, at, :] = re
            out[b, 1, at, :] = im

    strips(rows, backward)
    hand_out(place, out, sent, sems)


def return_kernel(chunks, place, kept, mhi, mlo, *refs):
    parts, refs = refs[:XA], refs[XA:]
    back, sems, xhi, xlo, y = refs[-5:]
    sent, out = (refs[:XA], refs[XA:-5]) if chunks == 1 else ((), refs[:-5])
    bring(place, parts, back, sems)

    def forward(row, places):
        values = [(back[g, 0, at, :], back[g, 1, at, :]) for _, g, at in places]
        columns_out(xhi, xlo, 0, row, values)

    by_pieces(1, forward)
    columns_mix(xhi, xlo, mhi, mlo, y)

    def turn(row, places):
        local = pl.ds(row, STRIP)
        pulled = columns_in(y, 0, row)
        following = []
        for p, (c, g, at) in enumerate(places):
            re, im = times((kept[p, 0, local, :], kept[p, 1, local, :]), pulled[p])
            out[c][g, 0, at, :] = -im
            out[c][g, 1, at, :] = -re
            following.append(times((kept[p, 2, local, :], kept[p, 3, local, :]), pulled[p]))
        columns_out(xhi, xlo, 0, row, following)

    by_pieces(chunks, turn)
    columns_mix(xhi, xlo, mhi, mlo, y)

    def backward(row, places):
        for (c, g, at), (re, im) in zip(places, columns_in(y, 0, row)):
            out[c][g, 2, at, :] = re
            out[c][g, 3, at, :] = im

    by_pieces(chunks, backward)
    if sent:
        hand_out(place, out[0], sent, sems)


def leave_kernel(pieces, first, arrived, place, index, whi, wlo, mhi, mlo, *refs):
    t0, refs = refs[:pieces], refs[pieces:]
    if arrived == 1:
        back, refs = refs[0], refs[1:]
    else:
        parts, back, sems = refs[-arrived - 9 : -9], refs[-2], refs[-1]
        bring(place, parts, back, sems, first)
        refs = refs[: -arrived - 9] + refs[-9:-2]
    before, (near, far, shi, slo, xhi, xlo, y) = refs[:-7], refs[-7:]
    chunk = t0[0].shape[2]
    half = chunk // 2
    rows = pieces * chunk

    def pieces_of(step):
        for end, side in enumerate((1 - place[1], place[1])):
            for c in range(pieces):

                def inner(row, end=end, side=side, c=c):
                    within = pl.multiple_of(side * half + row, STRIP)
                    source = pl.multiple_of(c * chunk + side * half + row, STRIP)
                    target = pl.multiple_of((end * pieces + c) * half + row, STRIP)
                    step(c, pl.ds(within, STRIP), pl.ds(source, STRIP), target)

                strips(half, inner)

    def store(b, i, target, value):
        high, low = halves(value)
        at = pl.ds(pl.multiple_of(i * rows + target, STRIP), STRIP)
        shi[b, at, :] = high
        slo[b, at, :] = low

    def forward(c, within, at, target):
        rows_out(xhi, xlo, target, [(back[b, 2, at, :], back[b, 3, at, :]) for b in range(XA)])
        for b in range(XA):
            for i in range(2):
                store(XA + b, i, target, back[b, i, at, :])

    pieces_of(forward)
    rows_mix(xhi, xlo, mhi, mlo, y)

    def turn(c, within, at, target):
        for b, value in enumerate(rows_in(y, target)):
            re, im = times((t0[c][b, 0, within, :], t0[c][b, 1, within, :]), value)
            store(b, 0, target, -im)
            store(b, 1, target, -re)

    pieces_of(turn)

    for out, old in zip((near, far), before or (None, None)):
        out[...] = jnp.zeros(out.shape, jnp.float32) if old is None else old[...]

    def across(a, b):
        return lax.dot_general(
            a, b, (((1,), (1,)), ((), ())), preferred_element_type=jnp.float32
        )

    def step(b, carry):
        high, low = shi[b], slo[b]
        values = across(high, whi[b]) + (across(low, whi[b]) + across(high, wlo[b]))
        for s in range(SLOTS):
            at = pl.ds(pl.multiple_of(index[b, s] * BLK, BLK), BLK)
            for i in range(2):
                for end, out in enumerate((near, far)):
                    start = i * rows + end * (rows // 2)
                    part = values[start : start + rows // 2, s * BLK : (s + 1) * BLK]
                    out[i, :, at] += part
        return carry

    lax.fori_loop(0, NB, step, 0)


def call(kernel, outs, scratch, mix_count, extra, *operands, parts=(), sent=()):
    specs = [
        pl.BlockSpec(memory_space=pltpu.SMEM if o.dtype == jnp.int32 else pltpu.VMEM)
        for o in operands
    ] + [pl.BlockSpec(memory_space=pl.ANY)] * len(parts)
    operands += tuple(parts)
    out_specs = [pl.BlockSpec(memory_space=pltpu.VMEM)] * len(outs)
    out_specs += [pl.BlockSpec(memory_space=pl.ANY)] * len(sent)
    outs = list(outs) + list(sent)
    moved = sum(o.size * o.dtype.itemsize for o in operands) + sum(4 * math.prod(o) for o in outs)
    return pl.pallas_call(
        kernel,
        out_shape=[jax.ShapeDtypeStruct(o, jnp.float32) for o in outs],
        in_specs=specs,
        out_specs=out_specs,
        scratch_shapes=scratch,
        compiler_params=pltpu.CompilerParams(vmem_limit_bytes=60 * 1024 * 1024),
        cost_estimate=pl.CostEstimate(
            flops=int(mix_count * 16 * 128 * 256 * 256 * 6) + extra,
            bytes_accessed=moved,
            transcendentals=0,
        ),
    )(*operands)


def mix_scratch(rows, lanes):
    return [
        pltpu.VMEM((XA, rows, lanes), jnp.bfloat16),
        pltpu.VMEM((XA, rows, lanes), jnp.bfloat16),
        pltpu.VMEM((XA, rows, lanes), jnp.float32),
    ]


def enter(place, index, own, other, weights, matrices):
    rows = 2 * own.shape[1]
    scratch = [
        pltpu.VMEM((4 * rows, NB * BLK), jnp.bfloat16),
        pltpu.VMEM((4 * rows, NB * BLK), jnp.bfloat16),
        pltpu.VMEM((XA, 2, rows, LANES), jnp.float32),
    ] + mix_scratch(2 * rows, 2 * LANES)
    outs = [(XA, 8, rows, LANES), (XA, 2, rows, LANES)]
    extra = NB * 4 * rows * 256 * 128 * 6
    return call(
        enter_kernel,
        outs,
        scratch,
        rows / XB * 2,
        extra,
        place,
        index,
        own,
        other,
        *weights,
        *matrices,
    )


def block_scratch(channels, rows=XB):
    return pltpu.VMEM((XA, channels, rows, LANES), jnp.float32)


def middle(place, arrived, matrices):
    kept, *sent = call(
        functools.partial(middle_kernel, len(arrived)),
        [(XA, 4, XB, LANES)],
        [block_scratch(4), pltpu.SemaphoreType.DMA((XA,))] + mix_scratch(2 * XB, 2 * LANES),
        4,
        0,
        place,
        *arrived,
        *matrices,
        sent=[(4, XB, LANES)] * XA,
    )
    return sent, kept


def detector(place, parts, matrices):
    return call(
        detector_kernel,
        [],
        [block_scratch(4), block_scratch(2), pltpu.SemaphoreType.DMA((XA,))]
        + mix_scratch(2 * XB, 2 * LANES),
        3,
        0,
        place,
        *matrices,
        parts=parts,
        sent=[(2, XB, LANES)] * XA,
    )


def pull(place, parts, kept, matrices, chunks):
    scratch = [block_scratch(2), pltpu.SemaphoreType.DMA((XA,))] + mix_scratch(2 * XB, LANES)
    if chunks == 1:
        scratch = [block_scratch(4)] + scratch
    return call(
        functools.partial(return_kernel, chunks),
        [] if chunks == 1 else [(XA, 4, XB // chunks, LANES)] * chunks,
        scratch,
        2,
        0,
        place,
        kept,
        *matrices,
        parts=parts,
        sent=[(4, XB, LANES)] * XA if chunks == 1 else [],
    )


def leave(place, index, back, first, t0, weights, matrices, before):
    rows = sum(t.shape[2] for t in t0)
    scratch = [
        pltpu.VMEM((NB, 2 * rows, LANES), jnp.bfloat16),
        pltpu.VMEM((NB, 2 * rows, LANES), jnp.bfloat16),
    ] + mix_scratch(rows, 2 * LANES)
    parts = back if len(back) > 1 else ()
    if parts:
        scratch += [block_scratch(4, rows), pltpu.SemaphoreType.DMA((XA,))]
    extra = NB * 2 * rows * 256 * 128 * 6
    return call(
        functools.partial(leave_kernel, len(t0), first, len(back)),
        [(2, rows // 2, NB * BLK)] * 2,
        scratch,
        rows / XB,
        extra,
        place,
        index,
        *weights,
        *matrices,
        *t0,
        *(() if parts else back),
        *before,
        parts=parts,
    )


def split_weights(block_weights):
    stacked = block_weights.reshape(ANGLES, NB, SLOTS * BLK, BLK)
    rounded = lax.reduce_precision(stacked, 8, 7)
    return rounded.astype(jnp.bfloat16), (stacked - rounded).astype(jnp.bfloat16)


def device(q, b, r):
    return q * XA + b * HALF + r


def exchange(values):
    return lax.all_to_all(
        values,
        ("parts", "fft"),
        split_axis=0,
        concat_axis=0,
        axis_index_groups=[[device(x, b, r) for x in range(2) for r in range(HALF)] for b in range(2)],
        tiled=True,
    )


def spread(parts):
    group = [(x, r) for x in range(2) for r in range(HALF)]
    return [parts[0]] + [
        lax.ppermute(
            parts[s],
            ("parts", "fft"),
            [
                (device(x, b, r), device(group[g ^ s][0], b, group[g ^ s][1]))
                for b in range(2)
                for g, (x, r) in enumerate(group)
            ],
        )
        for s in range(1, XA)
    ]


def permute(values, steps):
    pairs = [
        (device(*here, r), device(*there, r)) for here, there in steps for r in range(HALF)
    ]
    return lax.ppermute(values, ("parts", "fft"), pairs)


BESIDE = [((q, b), (1 - q, b)) for q in range(2) for b in range(2)]
ALONG = [((q, b), (q, 1 - b)) for q in range(2) for b in range(2)]
CYCLE = [((0, 0), (0, 1)), ((1, 0), (0, 0)), ((1, 1), (1, 0)), ((0, 1), (1, 1))]
ACROSS = [((0, 1), (1, 0)), ((1, 0), (0, 1))]


def after(values, others):
    return lax.optimization_barrier((values, others))[0]


def arrive(potential, direction, q, b):
    half = XB // CHUNKS // 2
    chunks = []
    beside = along = ()
    for c in range(CHUNKS):
        lower, upper = (
            jnp.concatenate(
                [v[:, (2 * c + x) * half : (2 * c + x + 1) * half] for v in (potential, direction)]
            )
            for x in range(2)
        )
        keep = jnp.where(q == 0, lower, upper)
        give = jnp.where(q == 0, upper, lower)
        beside = permute(after(give, beside), BESIDE)
        own = jnp.where(q == b, keep, beside)
        give = jnp.where(q == b, beside, keep)
        along = permute(after(give, along), ALONG)
        chunks.append((own, along, beside))
    return chunks


def depart(near, far, q, b):
    once = permute(near, CYCLE)
    twice = permute(far, ACROSS)
    same = jnp.where(q == b, far, once)
    rest = jnp.where(q == b, once, twice)
    return jnp.where(q == 0, same, rest), jnp.where(q == 0, rest, same)


def blocked_body(potential, direction, block_index, block_weights):
    q = lax.axis_index("parts")
    b = lax.axis_index("fft") // HALF
    place = jnp.stack([b, q, q * HALF + lax.axis_index("fft") % HALF]).astype(jnp.int32)
    chunks = arrive(potential, direction, q, b)
    whi, wlo = split_weights(block_weights)
    by_column = column_constants()
    column = tuple(jnp.asarray(v) for v in split_constant(by_column))
    row = tuple(jnp.asarray(v) for v in split_constant(by_column.transpose(0, 2, 1)))
    weights = [(whi[a], wlo[a]) for a in range(ANGLES)]
    arrived = [[] for _ in range(ANGLES)]
    ahead = [[] for _ in range(ANGLES)]
    for c, (own, along, _) in enumerate(chunks):
        further = chunks[c + 1] if c + 1 < CHUNKS else ((), (), ())
        own = after(own, further[2])
        for a in range(ANGLES):
            fields, t0 = enter(place, block_index[a], own, along, weights[a], row)
            arrived[a].append(exchange(after(fields, further[1]) if a else fields))
            ahead[a].append(t0)
    carried = []
    for a in range(ANGLES):
        out, kept = middle(place, arrived[a], column)
        carried.append((spread(out), kept))
    backs = [spread(detector(place, out, row)) for out, _ in carried]
    ends = 2
    span = CHUNKS // ends
    totals = [()] * ends
    for a in range(ANGLES):
        last = a == ANGLES - 1
        pulled = pull(place, backs[a], carried[a][1], column, ends if last else 1)
        if last:
            pulled = [[exchange(pulled[0])], [exchange(after(pulled[1], totals))]]
        else:
            pulled = [spread(pulled)] * ends
        for e in range(ends):
            first = 0 if last else e * (XB // ends)
            t0 = ahead[a][e * span : (e + 1) * span]
            totals[e] = leave(
                place, block_index[a], pulled[e], first, t0, weights[a], row, totals[e]
            )
    pieces = []
    half = XB // CHUNKS // 2
    for total in totals:
        lower, upper = depart(*total, q, b)
        for c in range(span):
            pieces += [v[:, c * half : (c + 1) * half] for v in (lower, upper)]
    return jnp.concatenate(pieces, axis=1)


def transform_table(count_in, count_out, length, orient):
    first = jnp.arange(count_in, dtype=jnp.int32)[:, None]
    second = jnp.arange(count_out, dtype=jnp.int32)[None, :]
    phases = orient * 2.0 * math.pi / length * (first * second % length).astype(jnp.float32)
    cosine = jnp.cos(phases)
    sine_part = jnp.sin(phases)
    return jnp.stack([jnp.stack([cosine, sine_part]), jnp.stack([-sine_part, cosine])])


def twiddle_pair(count_a, count_b, length, orient):
    first = jnp.arange(count_a, dtype=jnp.int32)[:, None]
    second = jnp.arange(count_b, dtype=jnp.int32)[None, :]
    phases = orient * 2.0 * math.pi / length * (first * second % length).astype(jnp.float32)
    return (jnp.cos(phases), jnp.sin(phases))


def spread_turn(peer_count, row_count, slot_count, orient):
    turn_re, turn_im = twiddle_pair(peer_count, row_count, NX, orient)
    shape_three = (row_count, peer_count, slot_count)
    wide_re = jnp.broadcast_to(turn_re.T[:, :, None], shape_three).reshape(
        row_count, peer_count * slot_count
    )
    wide_im = jnp.broadcast_to(turn_im.T[:, :, None], shape_three).reshape(
        row_count, peer_count * slot_count
    )
    return (wide_re, wide_im)


def complex_times(values, real_part, imag_part):
    first = values[:, 0]
    second = values[:, 1]
    return jnp.stack(
        [first * real_part - second * imag_part, first * imag_part + second * real_part], axis=1
    )


def one_hot(index_rows, block_count):
    return (index_rows[..., None] == jnp.arange(block_count, dtype=jnp.int32)).astype(jnp.float32)


def rotate(values, selector, matrices):
    height = values.shape[1]
    blocked = values.reshape(2, height, NB, BLK)
    picked = jnp.einsum("cyni,bsn->cybsi", blocked, selector, precision=PRECISE)
    rotated = jnp.einsum("cybsi,bsio->cybo", picked, matrices, precision=PRECISE)
    return rotated.reshape(2, height, SL, NX)


def rotate_back(values, selector, matrices):
    height = values.shape[1]
    blocked = values.reshape(2, height, NB, BLK)
    spread_out = jnp.einsum("cybo,bsio->cybsi", blocked, matrices, precision=PRECISE)
    summed = jnp.einsum("cybsi,bsn->cyni", spread_out, selector, precision=PRECISE)
    return summed.reshape(2, height, SL * NX)


def fresnel(peer_count, row_count, slot_count, orient):
    position_high = jnp.arange(row_count, dtype=jnp.int32)[:, None]
    position_low = jnp.arange(peer_count, dtype=jnp.int32)[None, :]
    freq_y = position_low + peer_count * position_high
    freq_y = jnp.where(freq_y < NX // 2, freq_y, freq_y - NX)
    position = lax.axis_index("fft") * slot_count + jnp.arange(slot_count, dtype=jnp.int32)
    freq_x = position // XB + XA * (position % XB)
    freq_x = jnp.where(freq_x < NX // 2, freq_x, freq_x - NX)
    squares = ((freq_y * freq_y)[:, :, None] + (freq_x * freq_x)[None, None, :]) % (2 * NX)
    phases = orient * -math.pi / NX * squares.astype(jnp.float32)
    scaling = 1.0 / (NX * NX)
    phases = phases.reshape(row_count, peer_count * slot_count)
    return (jnp.cos(phases) * scaling, jnp.sin(phases) * scaling)


def propagate(fields, kernel, peer_count, row_count, slot_count):
    field_count = fields.shape[0]
    groups = XB // slot_count
    shaped = fields.reshape(field_count, 2, row_count, XA, XB)
    partial_x = jnp.einsum(
        "fcrab,cdak->fdrkb", shaped, transform_table(XA, XA, XA, -1.0), precision=PRECISE
    )
    twist_re, twist_im = twiddle_pair(XA, XB, NX, -1.0)
    partial_x = complex_times(partial_x, twist_re, twist_im)
    partial_x = jnp.einsum(
        "fcrkb,cdbt->fdrkt", partial_x, transform_table(XB, XB, XB, -1.0), precision=PRECISE
    )
    partial_x = partial_x.reshape(field_count, 2, row_count, XA, groups, slot_count)
    outgoing = partial_x.transpose(0, 1, 3, 4, 2, 5).reshape(
        field_count, 2, peer_count, row_count * slot_count
    )
    forward_re, forward_im = spread_turn(peer_count, row_count, slot_count, -1.0)
    inverse_re, inverse_im = spread_turn(peer_count, row_count, slot_count, 1.0)
    wide = peer_count * slot_count
    incoming = lax.all_to_all(outgoing, "fft", split_axis=2, concat_axis=2, tiled=True)
    item_count = incoming.shape[0]
    lattice = incoming.reshape(item_count, 2, peer_count, row_count, slot_count)
    lattice = jnp.einsum(
        "fcprs,cdpk->fdrks",
        lattice,
        transform_table(peer_count, peer_count, peer_count, -1.0),
        precision=PRECISE,
    )
    lattice = lattice.reshape(item_count, 2, row_count, wide)
    lattice = complex_times(lattice, forward_re, forward_im)
    lattice = jnp.einsum(
        "fcrq,cdrm->fdmq",
        lattice,
        transform_table(row_count, row_count, row_count, -1.0),
        precision=PRECISE,
    )
    lattice = complex_times(lattice, kernel[0], kernel[1])
    lattice = jnp.einsum(
        "fcmq,cdmr->fdrq",
        lattice,
        transform_table(row_count, row_count, row_count, 1.0),
        precision=PRECISE,
    )
    lattice = complex_times(lattice, inverse_re, inverse_im)
    lattice = lattice.reshape(item_count, 2, row_count, peer_count, slot_count)
    lattice = jnp.einsum(
        "fcrks,cdkp->fdprs",
        lattice,
        transform_table(peer_count, peer_count, peer_count, 1.0),
        precision=PRECISE,
    )
    returning = lax.all_to_all(
        lattice.reshape(item_count, 2, peer_count, row_count * slot_count),
        "fft",
        split_axis=2,
        concat_axis=2,
        tiled=True,
    )
    restored = returning.reshape(item_count, 2, XA, groups, row_count, slot_count)
    matrix_back = transform_table(XB, XB, XB, 1.0).reshape(2, 2, groups, slot_count, XB)
    restored = jnp.einsum("fckjrs,cdjsb->fdrkb", restored, matrix_back, precision=PRECISE)
    back_re, back_im = twiddle_pair(XA, XB, NX, 1.0)
    restored = complex_times(restored, back_re, back_im)
    restored = jnp.einsum(
        "fcrkb,cdkn->fdrnb", restored, transform_table(XA, XA, XA, 1.0), precision=PRECISE
    )
    return restored.reshape(item_count, 2, row_count, NX)


def general_body(potential, direction, block_index, block_weights):
    row_count = potential.shape[1]
    peer_count = lax.axis_size("fft")
    slot_count = NX // peer_count
    ahead = fresnel(peer_count, row_count, slot_count, 1.0)
    behind = fresnel(peer_count, row_count, slot_count, -1.0)
    accumulated = jnp.zeros(potential.shape, jnp.float32)
    for angle_index in range(ANGLES):
        selector = one_hot(block_index[angle_index], NB)
        matrices = block_weights[angle_index]
        rotated = rotate(potential, selector, matrices)
        tangent = rotate(direction, selector, matrices)
        damping = jnp.exp(-rotated[1])
        trans_re = damping * jnp.cos(rotated[0])
        trans_im = damping * jnp.sin(rotated[0])
        wave_re = jnp.ones((row_count, NX), jnp.float32)
        wave_im = jnp.zeros((row_count, NX), jnp.float32)
        dwave_re = jnp.zeros((row_count, NX), jnp.float32)
        dwave_im = jnp.zeros((row_count, NX), jnp.float32)
        stored = []
        for slice_index in range(SL):
            t_re = trans_re[:, slice_index]
            t_im = trans_im[:, slice_index]
            d_re = tangent[0][:, slice_index]
            d_im = tangent[1][:, slice_index]
            phi_re = t_re * wave_re - t_im * wave_im
            phi_im = t_re * wave_im + t_im * wave_re
            dphi_re = -(d_re * phi_im + d_im * phi_re) + t_re * dwave_re - t_im * dwave_im
            dphi_im = d_re * phi_re - d_im * phi_im + t_re * dwave_im + t_im * dwave_re
            stored.append((phi_re, phi_im))
            packed = jnp.stack([jnp.stack([phi_re, phi_im]), jnp.stack([dphi_re, dphi_im])])
            propagated = propagate(packed, ahead, peer_count, row_count, slot_count)
            wave_re = propagated[0, 0]
            wave_im = propagated[0, 1]
            dwave_re = propagated[1, 0]
            dwave_im = propagated[1, 1]
        change = 2.0 * (wave_re * dwave_re + wave_im * dwave_im)
        back_re = 2.0 * change * wave_re
        back_im = 2.0 * change * wave_im
        grad_re = [None] * SL
        grad_im = [None] * SL
        for slice_index in reversed(range(SL)):
            pulled = propagate(
                jnp.stack([back_re, back_im])[None], behind, peer_count, row_count, slot_count
            )
            pb_re = pulled[0, 0]
            pb_im = pulled[0, 1]
            phi_re, phi_im = stored[slice_index]
            grad_re[slice_index] = phi_re * pb_im - phi_im * pb_re
            grad_im[slice_index] = -(phi_re * pb_re + phi_im * pb_im)
            t_re = trans_re[:, slice_index]
            t_im = trans_im[:, slice_index]
            back_re = t_re * pb_re + t_im * pb_im
            back_im = t_re * pb_im - t_im * pb_re
        gradient = jnp.stack([jnp.stack(grad_re, axis=1), jnp.stack(grad_im, axis=1)])
        accumulated = accumulated + rotate_back(gradient, selector, matrices)
    return accumulated


def body(potential, direction, block_index, block_weights):
    if lax.axis_size("parts") == 2 and lax.axis_size("fft") == XA:
        return blocked_body(potential, direction, block_index, block_weights)
    return general_body(potential, direction, block_index, block_weights)


def solution(mesh):
    return jax.shard_map(
        body,
        mesh=mesh,
        in_specs=(P("parts", "fft", None), P("parts", "fft", None), P(), P()),
        out_specs=P("parts", "fft", None),
        check_vma=False,
    )
```

```python
import functools
import math

import jax
import jax.numpy as jnp
import numpy as np
from jax import lax
from jax.experimental import pallas as pl
from jax.experimental.pallas import tpu as pltpu
from jax.sharding import PartitionSpec as P

XA = 16
XB = 128
NX = 2048
SL = 2
ANGLES = 2
BLK = 128
NB = 32
SLOTS = 2
STRIP = 16
LANES = 128
CHUNKS = 4
HALF = XA // 2


PRECISE = lax.Precision.HIGHEST


def bin_matrices():
    wavenumber = np.arange(NX)
    signed = np.where(wavenumber < NX // 2, wavenumber, wavenumber - NX)
    factor = np.exp(-1j * np.pi / NX * ((signed * signed) % (2 * NX)))
    line = np.fft.ifft(factor)
    block = np.arange(XA)
    inner = np.arange(XB)
    shifts = (XB * block[:, None, None] + inner[None, :, None] - inner[None, None, :]) % NX
    phases = np.exp(-2j * np.pi / XA * ((block[:, None] * block[None, :]) % XA))
    return np.einsum("kd,dij->kij", phases, line[shifts]) / XA


def split_constant(values):
    values = values.astype(np.float32)
    high = values.astype(jnp.bfloat16)
    low = (values - high.astype(np.float32)).astype(jnp.bfloat16)
    return high, low


def column_constants():
    bins = bin_matrices()
    top = np.concatenate([bins.real, -bins.imag], axis=2)
    bottom = np.concatenate([bins.imag, bins.real], axis=2)
    return np.concatenate([top, bottom], axis=1)


def fourth(values, orient):
    (ar, ai), (br, bi), (cr, ci), (dr, di) = values
    sr, si, er, ei = ar + cr, ai + ci, ar - cr, ai - ci
    tr, ti, fr, fi = br + dr, bi + di, br - dr, bi - di
    minus, plus = (er + fi, ei - fr), (er - fi, ei + fr)
    one, three = (minus, plus) if orient < 0 else (plus, minus)
    return [(sr + tr, si + ti), one, (sr - tr, si - ti), three]


def turned(value, step, orient):
    re, im = value
    if step == 0:
        return value
    if step == 4:
        return (im, -re) if orient < 0 else (-im, re)
    cosine = math.cos(2.0 * math.pi * step / XA)
    sine = orient * math.sin(2.0 * math.pi * step / XA)
    if step == 2:
        root = cosine
        return ((re - im) * root, (re + im) * root) if orient > 0 else ((re + im) * root, (im - re) * root)
    return (re * cosine - im * sine, re * sine + im * cosine)


def sixteenth(values, orient):
    inner = [fourth([values[4 * a + b] for a in range(4)], orient) for b in range(4)]
    out = [None] * XA
    for c in range(4):
        row = fourth([turned(inner[b][c], b * c, orient) for b in range(4)], orient)
        for d in range(4):
            out[c + 4 * d] = row[d]
    return out


def halves(value):
    high = value.astype(jnp.bfloat16)
    return high, (value - high.astype(jnp.float32)).astype(jnp.bfloat16)


def dot32(a, b):
    return jnp.dot(a, b, preferred_element_type=jnp.float32)


def times(a, b):
    return (a[0] * b[0] - a[1] * b[1], a[0] * b[1] + a[1] * b[0])


def sincos(x):
    turns = jnp.floor(x * (2.0 / math.pi) + 0.5)
    rest = ((x - turns * 1.5703125) - turns * 4.837512969970703125e-4) - turns * 7.54978995489188216e-8
    square = rest * rest
    sine = rest + rest * square * (
        -1.6666654611e-1 + square * (8.3321608736e-3 + square * -1.9515295891e-4)
    )
    cosine = (1.0 - 0.5 * square) + square * square * (
        4.166664568298827e-2 + square * (-1.388731625493765e-3 + square * 2.443315711809948e-5)
    )
    quadrant = turns.astype(jnp.int32)
    odd = (quadrant & 1) == 1
    first = jnp.where(odd, cosine, sine)
    second = jnp.where(odd, sine, cosine)
    first = jnp.where((quadrant & 2) == 2, -first, first)
    second = jnp.where(((quadrant + 1) & 2) == 2, -second, second)
    return first, second


def strips(count, step):
    def run(i, carry):
        step(pl.multiple_of(i * STRIP, STRIP))
        return carry

    lax.fori_loop(0, count // STRIP, run, 0)


def rows_out(xhi, xlo, first_row, values):
    for k, (re, im) in enumerate(sixteenth(values, -1.0)):
        for part, value in enumerate((re, im)):
            high, low = halves(value)
            at = (k, pl.ds(first_row, STRIP), pl.ds(part * LANES, LANES))
            xhi[at] = high
            xlo[at] = low


def rows_in(y, first_row):
    values = [
        tuple(y[k, pl.ds(first_row, STRIP), pl.ds(part * LANES, LANES)] for part in range(2))
        for k in range(XA)
    ]
    return sixteenth(values, 1.0)


def rows_mix(xhi, xlo, mhi, mlo, y):
    def step(k, carry):
        high, low = xhi[k], xlo[k]
        y[k] = dot32(high, mhi[k]) + (dot32(low, mhi[k]) + dot32(high, mlo[k]))
        return carry

    lax.fori_loop(0, XA, step, 0)


def columns_out(xhi, xlo, field, row, values):
    for k, (re, im) in enumerate(sixteenth(values, -1.0)):
        for part, value in enumerate((re, im)):
            high, low = halves(value)
            at = (k, pl.ds(part * XB + row, STRIP), pl.ds(field * LANES, LANES))
            xhi[at] = high
            xlo[at] = low


def columns_in(y, field, row):
    values = [
        tuple(
            y[k, pl.ds(part * XB + row, STRIP), pl.ds(field * LANES, LANES)] for part in range(2)
        )
        for k in range(XA)
    ]
    return sixteenth(values, 1.0)


def columns_mix(xhi, xlo, mhi, mlo, y):
    def step(k, carry):
        high, low = xhi[k], xlo[k]
        y[k] = dot32(mhi[k], high) + (dot32(mhi[k], low) + dot32(mlo[k], high))
        return carry

    lax.fori_loop(0, XA, step, 0)


def enter_kernel(place, index, own, other, whi, wlo, mhi, mlo, out, t0, shi, slo, field, xhi, xlo, y):
    half = own.shape[1]
    rows = 2 * half

    for number in range(4):
        for piece, side in ((own, place[0]), (other, 1 - place[0])):

            def cut(row, number=number, piece=piece, side=side):
                high, low = halves(piece[number, pl.ds(row, STRIP), :])
                first = number * rows + side * half + row
                at = pl.ds(pl.multiple_of(first, STRIP), STRIP)
                shi[at, :] = high
                slo[at, :] = low

            strips(half, cut)

    def rotated(b):
        at = [pl.ds(pl.multiple_of(index[b, s] * BLK, BLK), BLK) for s in range(SLOTS)]
        high = jnp.concatenate([shi[:, a] for a in at], axis=1)
        low = jnp.concatenate([slo[:, a] for a in at], axis=1)
        values = dot32(high, whi[b]) + (dot32(low, whi[b]) + dot32(high, wlo[b]))
        angle, loss, d_re, d_im = (values[i * rows : (i + 1) * rows] for i in range(4))
        sine, cosine = sincos(angle)
        damping = jnp.exp(-loss)
        return damping * cosine, damping * sine, d_re, d_im

    def first_slice(b, carry):
        t_re, t_im, d_re, d_im = rotated(b)
        t0[b, 0] = t_re
        t0[b, 1] = t_im
        field[b, 0] = -(d_re * t_im + d_im * t_re)
        field[b, 1] = d_re * t_re - d_im * t_im
        return carry

    lax.fori_loop(0, XA, first_slice, 0)

    def forward(row):
        at = pl.ds(row, STRIP)
        rows_out(xhi, xlo, row, [(t0[b, 0, at, :], t0[b, 1, at, :]) for b in range(XA)])
        rows_out(
            xhi,
            xlo,
            pl.multiple_of(rows + row, STRIP),
            [(field[b, 0, at, :], field[b, 1, at, :]) for b in range(XA)],
        )

    strips(rows, forward)
    rows_mix(xhi, xlo, mhi, mlo, y)

    def backward(row):
        at = pl.ds(row, STRIP)
        for number in range(2):
            values = rows_in(y, pl.multiple_of(number * rows + row, STRIP))
            for b, (re, im) in enumerate(values):
                out[b, 2 * number, at, :] = re
                out[b, 2 * number + 1, at, :] = im

    strips(rows, backward)

    def second_slice(b, carry):
        for channel, value in enumerate(rotated(XA + b)):
            out[b, 4 + channel] = value
        return carry

    lax.fori_loop(0, XA, second_slice, 0)


def by_pieces(spans, step):
    half = XB // CHUNKS // 2
    pieces = [(piece, c) for piece, span in enumerate(spans) for c in range(span)]
    for chunk, (piece, c) in enumerate(pieces):
        for x in range(2):

            def inner(row, chunk=chunk, piece=piece, c=c, x=x):
                places = []
                for p in range(XA):
                    first = (2 * c + p // HALF) * half
                    at = pl.ds(pl.multiple_of(first + row, STRIP), STRIP)
                    places.append((piece, x * HALF + p % HALF, at))
                step(pl.multiple_of((2 * chunk + x) * half + row, STRIP), places)

            strips(half, inner)


def middle_kernel(chunks, *refs):
    arrived = refs[:chunks]
    mhi, mlo, out, kept, xhi, xlo, y = refs[chunks:]

    def forward(row, places):
        for number in range(2):
            values = [
                tuple(arrived[c][g, 2 * number + i, at, :] for i in range(2)) for c, g, at in places
            ]
            columns_out(xhi, xlo, number, row, values)

    by_pieces((1,) * chunks, forward)
    columns_mix(xhi, xlo, mhi, mlo, y)

    def turn(row, places):
        local = pl.ds(row, STRIP)
        wave = columns_in(y, 0, row)
        product = []
        for p, (c, g, at) in enumerate(places):
            t = arrived[c][g, 4, at, :], arrived[c][g, 5, at, :]
            value = times(t, wave[p])
            for i, part in enumerate(value + t):
                kept[p, i, local, :] = part
            product.append(value)
        columns_out(xhi, xlo, 0, row, product)
        dwave = columns_in(y, 1, row)
        change = []
        for p, (c, g, at) in enumerate(places):
            t_re, t_im, d_re, d_im = (arrived[c][g, 4 + i, at, :] for i in range(4))
            p_re, p_im = kept[p, 0, local, :], kept[p, 1, local, :]
            re, im = times((t_re, t_im), dwave[p])
            change.append((re - (d_re * p_im + d_im * p_re), im + (d_re * p_re - d_im * p_im)))
        columns_out(xhi, xlo, 1, row, change)

    by_pieces((1,) * chunks, turn)
    columns_mix(xhi, xlo, mhi, mlo, y)

    def backward(row, places):
        for number in range(2):
            for (_, g, at), (re, im) in zip(places, columns_in(y, number, row)):
                out[g, 2 * number, at, :] = re
                out[g, 2 * number + 1, at, :] = im

    by_pieces((CHUNKS,), backward)


def detector_kernel(fields, mhi, mlo, out, xhi, xlo, y):
    rows = fields.shape[2]

    def forward(row):
        at = pl.ds(row, STRIP)
        for number in range(2):
            rows_out(
                xhi,
                xlo,
                pl.multiple_of(number * rows + row, STRIP),
                [tuple(fields[b, 2 * number + i, at, :] for i in range(2)) for b in range(XA)],
            )

    strips(rows, forward)
    rows_mix(xhi, xlo, mhi, mlo, y)

    def turn(row):
        wave = rows_in(y, row)
        dwave = rows_in(y, pl.multiple_of(rows + row, STRIP))
        back = []
        for (re, im), (d_re, d_im) in zip(wave, dwave):
            change = 4.0 * (re * d_re + im * d_im)
            back.append((change * re, -(change * im)))
        rows_out(xhi, xlo, row, back)

    strips(rows, turn)

    def step(k, carry):
        high, low = xhi[k, :rows, :], xlo[k, :rows, :]
        y[k, :rows, :] = dot32(high, mhi[k]) + (dot32(low, mhi[k]) + dot32(high, mlo[k]))
        return carry

    lax.fori_loop(0, XA, step, 0)

    def backward(row):
        at = pl.ds(row, STRIP)
        for b, (re, im) in enumerate(rows_in(y, row)):
            out[b, 0, at, :] = re
            out[b, 1, at, :] = im

    strips(rows, backward)


def return_kernel(spans, back, kept, mhi, mlo, *refs):
    out, (xhi, xlo, y) = refs[: len(spans)], refs[len(spans) :]

    def forward(row, places):
        values = [(back[g, 0, at, :], back[g, 1, at, :]) for _, g, at in places]
        columns_out(xhi, xlo, 0, row, values)

    by_pieces((CHUNKS,), forward)
    columns_mix(xhi, xlo, mhi, mlo, y)

    def turn(row, places):
        local = pl.ds(row, STRIP)
        pulled = columns_in(y, 0, row)
        following = []
        for p, (c, g, at) in enumerate(places):
            re, im = times((kept[p, 0, local, :], kept[p, 1, local, :]), pulled[p])
            out[c][g, 0, at, :] = -im
            out[c][g, 1, at, :] = -re
            following.append(times((kept[p, 2, local, :], kept[p, 3, local, :]), pulled[p]))
        columns_out(xhi, xlo, 0, row, following)

    by_pieces(spans, turn)
    columns_mix(xhi, xlo, mhi, mlo, y)

    def backward(row, places):
        for (c, g, at), (re, im) in zip(places, columns_in(y, 0, row)):
            out[c][g, 2, at, :] = re
            out[c][g, 3, at, :] = im

    by_pieces(spans, backward)


def leave_kernel(spans, place, index, back, whi, wlo, mhi, mlo, *refs):
    chunks, count = sum(spans), 2 * len(spans)
    t0, refs = refs[:chunks], refs[chunks:]
    before, outs, (shi, slo, xhi, xlo, y) = refs[: -count - 5], refs[-count - 5 : -5], refs[-5:]
    chunk = t0[0].shape[2]
    half = chunk // 2
    rows = chunks * chunk
    starts = []

    def pieces_of(step):
        starts.clear()
        done = 0
        for span in spans:
            for end, side in enumerate((1 - place[1], place[1])):
                base = (2 * done + end * span) * half
                starts.append((base, span * half))
                for c in range(span):

                    def inner(row, side=side, c=c, done=done, base=base):
                        within = pl.multiple_of(side * half + row, STRIP)
                        source = pl.multiple_of((done + c) * chunk + side * half + row, STRIP)
                        target = pl.multiple_of(base + c * half + row, STRIP)
                        step(done + c, pl.ds(within, STRIP), pl.ds(source, STRIP), target)

                    strips(half, inner)
            done += span

    def store(b, i, target, value):
        high, low = halves(value)
        at = pl.ds(pl.multiple_of(i * rows + target, STRIP), STRIP)
        shi[b, at, :] = high
        slo[b, at, :] = low

    def forward(c, within, at, target):
        rows_out(xhi, xlo, target, [(back[b, 2, at, :], back[b, 3, at, :]) for b in range(XA)])
        for b in range(XA):
            for i in range(2):
                store(XA + b, i, target, back[b, i, at, :])

    pieces_of(forward)
    rows_mix(xhi, xlo, mhi, mlo, y)

    def turn(c, within, at, target):
        for b, value in enumerate(rows_in(y, target)):
            re, im = times((t0[c][b, 0, within, :], t0[c][b, 1, within, :]), value)
            store(b, 0, target, -im)
            store(b, 1, target, -re)

    pieces_of(turn)

    for out, old in zip(outs, before or [None] * count):
        out[...] = jnp.zeros(out.shape, jnp.float32) if old is None else old[...]

    def across(a, b):
        return lax.dot_general(
            a, b, (((1,), (1,)), ((), ())), preferred_element_type=jnp.float32
        )

    def step(b, carry):
        high, low = shi[b], slo[b]
        values = across(high, whi[b]) + (across(low, whi[b]) + across(high, wlo[b]))
        for s in range(SLOTS):
            at = pl.ds(pl.multiple_of(index[b, s] * BLK, BLK), BLK)
            for i in range(2):
                for (start, size), out in zip(starts, outs):
                    start += i * rows
                    out[i, :, at] += values[start : start + size, s * BLK : (s + 1) * BLK]
        return carry

    lax.fori_loop(0, NB, step, 0)


def call(kernel, outs, scratch, mix_count, extra, *operands):
    specs = [
        pl.BlockSpec(memory_space=pltpu.SMEM if o.dtype == jnp.int32 else pltpu.VMEM)
        for o in operands
    ]
    moved = sum(o.size * o.dtype.itemsize for o in operands) + sum(4 * math.prod(o) for o in outs)
    return pl.pallas_call(
        kernel,
        out_shape=[jax.ShapeDtypeStruct(o, jnp.float32) for o in outs],
        in_specs=specs,
        out_specs=[pl.BlockSpec(memory_space=pltpu.VMEM)] * len(outs),
        scratch_shapes=scratch,
        compiler_params=pltpu.CompilerParams(vmem_limit_bytes=60 * 1024 * 1024),
        cost_estimate=pl.CostEstimate(
            flops=int(mix_count * 16 * 128 * 256 * 256 * 6) + extra,
            bytes_accessed=moved,
            transcendentals=0,
        ),
    )(*operands)


def mix_scratch(rows, lanes):
    return [
        pltpu.VMEM((XA, rows, lanes), jnp.bfloat16),
        pltpu.VMEM((XA, rows, lanes), jnp.bfloat16),
        pltpu.VMEM((XA, rows, lanes), jnp.float32),
    ]


def enter(place, index, own, other, weights, matrices):
    rows = 2 * own.shape[1]
    scratch = [
        pltpu.VMEM((4 * rows, NB * BLK), jnp.bfloat16),
        pltpu.VMEM((4 * rows, NB * BLK), jnp.bfloat16),
        pltpu.VMEM((XA, 2, rows, LANES), jnp.float32),
    ] + mix_scratch(2 * rows, 2 * LANES)
    outs = [(XA, 8, rows, LANES), (XA, 2, rows, LANES)]
    extra = NB * 4 * rows * 256 * 128 * 6
    return call(
        enter_kernel,
        outs,
        scratch,
        rows / XB * 2,
        extra,
        place,
        index,
        own,
        other,
        *weights,
        *matrices,
    )


def middle(arrived, matrices):
    return call(
        functools.partial(middle_kernel, len(arrived)),
        [(XA, 4, XB, LANES), (XA, 4, XB, LANES)],
        mix_scratch(2 * XB, 2 * LANES),
        4,
        0,
        *arrived,
        *matrices,
    )


def detector(fields, matrices):
    rows = fields.shape[2]
    return call(
        detector_kernel,
        [(XA, 2, rows, LANES)],
        mix_scratch(2 * rows, 2 * LANES),
        3,
        0,
        fields,
        *matrices,
    )[0]


def pull(back, kept, matrices, spans):
    return call(
        functools.partial(return_kernel, spans),
        [(XA, 4, span * XB // CHUNKS, LANES) for span in spans],
        mix_scratch(2 * XB, LANES),
        2,
        0,
        back,
        kept,
        *matrices,
    )


def leave(place, index, back, t0, weights, matrices, before, spans):
    rows = sum(t.shape[2] for t in t0)
    scratch = [
        pltpu.VMEM((NB, 2 * rows, LANES), jnp.bfloat16),
        pltpu.VMEM((NB, 2 * rows, LANES), jnp.bfloat16),
    ] + mix_scratch(rows, 2 * LANES)
    extra = NB * 2 * rows * 256 * 128 * 6
    outs = call(
        functools.partial(leave_kernel, spans),
        [(2, span * XB // CHUNKS // 2, NB * BLK) for span in spans for _ in range(2)],
        scratch,
        rows / XB,
        extra,
        place,
        index,
        back,
        *weights,
        *matrices,
        *t0,
        *before,
    )
    return [outs[2 * i : 2 * i + 2] for i in range(len(spans))]


def split_weights(block_weights):
    stacked = block_weights.reshape(ANGLES, NB, SLOTS * BLK, BLK)
    rounded = lax.reduce_precision(stacked, 8, 7)
    return rounded.astype(jnp.bfloat16), (stacked - rounded).astype(jnp.bfloat16)


def device(q, b, r):
    return q * XA + b * HALF + r


def exchange(values):
    return lax.all_to_all(
        values,
        ("parts", "fft"),
        split_axis=0,
        concat_axis=0,
        axis_index_groups=[[device(x, b, r) for x in range(2) for r in range(HALF)] for b in range(2)],
        tiled=True,
    )


def permute(values, steps):
    pairs = [
        (device(*here, r), device(*there, r)) for here, there in steps for r in range(HALF)
    ]
    return lax.ppermute(values, ("parts", "fft"), pairs)


BESIDE = [((q, b), (1 - q, b)) for q in range(2) for b in range(2)]
ALONG = [((q, b), (q, 1 - b)) for q in range(2) for b in range(2)]
CYCLE = [((0, 0), (0, 1)), ((1, 0), (0, 0)), ((1, 1), (1, 0)), ((0, 1), (1, 1))]
ACROSS = [((0, 1), (1, 0)), ((1, 0), (0, 1))]


def after(values, others):
    return lax.optimization_barrier((values, others))[0]


def arrive(potential, direction, q, b):
    half = XB // CHUNKS // 2

    def sides(c):
        lower, upper = (
            jnp.concatenate(
                [v[:, (2 * c + x) * half : (2 * c + x + 1) * half] for v in (potential, direction)]
            )
            for x in range(2)
        )
        return jnp.where(q == 0, lower, upper), jnp.where(q == 0, upper, lower)

    keep, give = sides(0)
    potential, direction = after((potential, direction), give)
    beside = permute(give, BESIDE)
    kept, given = zip(*[sides(c) for c in range(1, CHUNKS)])
    rest = permute(after(jnp.concatenate(given), beside), BESIDE)
    chunks = []
    along = ()
    for c in range(CHUNKS):
        if c:
            keep, beside = kept[c - 1], rest[4 * (c - 1) : 4 * c]
        own = jnp.where(q == b, keep, beside)
        give = jnp.where(q == b, beside, keep)
        along = permute(after(give, along), ALONG)
        chunks.append((own, along))
    return chunks, rest


def depart(near, far, q, b):
    once = permute(near, CYCLE)
    twice = permute(far, ACROSS)
    same = jnp.where(q == b, far, once)
    rest = jnp.where(q == b, once, twice)
    return jnp.where(q == 0, same, rest), jnp.where(q == 0, rest, same)


def blocked_body(potential, direction, block_index, block_weights):
    q = lax.axis_index("parts")
    b = lax.axis_index("fft") // HALF
    place = jnp.stack([b, q]).astype(jnp.int32)
    chunks, beside = arrive(potential, direction, q, b)
    whi, wlo = split_weights(block_weights)
    by_column = column_constants()
    column = tuple(jnp.asarray(v) for v in split_constant(by_column))
    row = tuple(jnp.asarray(v) for v in split_constant(by_column.transpose(0, 2, 1)))
    weights = [(whi[a], wlo[a]) for a in range(ANGLES)]
    arrived = [[] for _ in range(ANGLES)]
    ahead = [[] for _ in range(ANGLES)]
    for c, (own, along) in enumerate(chunks):
        further = chunks[c + 1][1] if c + 1 < CHUNKS else ()
        own = after(own, beside)
        for a in range(ANGLES):
            fields, t0 = enter(place, block_index[a], own, along, weights[a], row)
            arrived[a].append(exchange(after(fields, further) if a else fields))
            ahead[a].append(t0)
    carried = []
    for a in range(ANGLES):
        out, kept = middle(arrived[a], column)
        carried.append((exchange(out), kept))
    backs = [exchange(detector(out, row)) for out, _ in carried]
    spans = (CHUNKS // 2, CHUNKS // 4, CHUNKS // 4)
    pulled = exchange(pull(backs[0], carried[0][1], column, (CHUNKS,))[0])
    totals = leave(place, block_index[0], pulled, ahead[0], weights[0], row, (), spans)
    pulled = pull(backs[1], carried[1][1], column, spans)
    pieces = []
    half = XB // CHUNKS // 2
    done = 0
    for i, span in enumerate(spans):
        back = exchange(after(pulled[i], totals) if i else pulled[i])
        t0 = ahead[1][done : done + span]
        done += span
        total = leave(place, block_index[1], back, t0, weights[1], row, totals[i], (span,))[0]
        lower, upper = depart(*total, q, b)
        for c in range(span):
            pieces += [v[:, c * half : (c + 1) * half] for v in (lower, upper)]
    return jnp.concatenate(pieces, axis=1)


def transform_table(count_in, count_out, length, orient):
    first = jnp.arange(count_in, dtype=jnp.int32)[:, None]
    second = jnp.arange(count_out, dtype=jnp.int32)[None, :]
    phases = orient * 2.0 * math.pi / length * (first * second % length).astype(jnp.float32)
    cosine = jnp.cos(phases)
    sine_part = jnp.sin(phases)
    return jnp.stack([jnp.stack([cosine, sine_part]), jnp.stack([-sine_part, cosine])])


def twiddle_pair(count_a, count_b, length, orient):
    first = jnp.arange(count_a, dtype=jnp.int32)[:, None]
    second = jnp.arange(count_b, dtype=jnp.int32)[None, :]
    phases = orient * 2.0 * math.pi / length * (first * second % length).astype(jnp.float32)
    return (jnp.cos(phases), jnp.sin(phases))


def spread_turn(peer_count, row_count, slot_count, orient):
    turn_re, turn_im = twiddle_pair(peer_count, row_count, NX, orient)
    shape_three = (row_count, peer_count, slot_count)
    wide_re = jnp.broadcast_to(turn_re.T[:, :, None], shape_three).reshape(
        row_count, peer_count * slot_count
    )
    wide_im = jnp.broadcast_to(turn_im.T[:, :, None], shape_three).reshape(
        row_count, peer_count * slot_count
    )
    return (wide_re, wide_im)


def complex_times(values, real_part, imag_part):
    first = values[:, 0]
    second = values[:, 1]
    return jnp.stack(
        [first * real_part - second * imag_part, first * imag_part + second * real_part], axis=1
    )


def one_hot(index_rows, block_count):
    return (index_rows[..., None] == jnp.arange(block_count, dtype=jnp.int32)).astype(jnp.float32)


def rotate(values, selector, matrices):
    height = values.shape[1]
    blocked = values.reshape(2, height, NB, BLK)
    picked = jnp.einsum("cyni,bsn->cybsi", blocked, selector, precision=PRECISE)
    rotated = jnp.einsum("cybsi,bsio->cybo", picked, matrices, precision=PRECISE)
    return rotated.reshape(2, height, SL, NX)


def rotate_back(values, selector, matrices):
    height = values.shape[1]
    blocked = values.reshape(2, height, NB, BLK)
    spread_out = jnp.einsum("cybo,bsio->cybsi", blocked, matrices, precision=PRECISE)
    summed = jnp.einsum("cybsi,bsn->cyni", spread_out, selector, precision=PRECISE)
    return summed.reshape(2, height, SL * NX)


def fresnel(peer_count, row_count, slot_count, orient):
    position_high = jnp.arange(row_count, dtype=jnp.int32)[:, None]
    position_low = jnp.arange(peer_count, dtype=jnp.int32)[None, :]
    freq_y = position_low + peer_count * position_high
    freq_y = jnp.where(freq_y < NX // 2, freq_y, freq_y - NX)
    position = lax.axis_index("fft") * slot_count + jnp.arange(slot_count, dtype=jnp.int32)
    freq_x = position // XB + XA * (position % XB)
    freq_x = jnp.where(freq_x < NX // 2, freq_x, freq_x - NX)
    squares = ((freq_y * freq_y)[:, :, None] + (freq_x * freq_x)[None, None, :]) % (2 * NX)
    phases = orient * -math.pi / NX * squares.astype(jnp.float32)
    scaling = 1.0 / (NX * NX)
    phases = phases.reshape(row_count, peer_count * slot_count)
    return (jnp.cos(phases) * scaling, jnp.sin(phases) * scaling)


def propagate(fields, kernel, peer_count, row_count, slot_count):
    field_count = fields.shape[0]
    groups = XB // slot_count
    shaped = fields.reshape(field_count, 2, row_count, XA, XB)
    partial_x = jnp.einsum(
        "fcrab,cdak->fdrkb", shaped, transform_table(XA, XA, XA, -1.0), precision=PRECISE
    )
    twist_re, twist_im = twiddle_pair(XA, XB, NX, -1.0)
    partial_x = complex_times(partial_x, twist_re, twist_im)
    partial_x = jnp.einsum(
        "fcrkb,cdbt->fdrkt", partial_x, transform_table(XB, XB, XB, -1.0), precision=PRECISE
    )
    partial_x = partial_x.reshape(field_count, 2, row_count, XA, groups, slot_count)
    outgoing = partial_x.transpose(0, 1, 3, 4, 2, 5).reshape(
        field_count, 2, peer_count, row_count * slot_count
    )
    forward_re, forward_im = spread_turn(peer_count, row_count, slot_count, -1.0)
    inverse_re, inverse_im = spread_turn(peer_count, row_count, slot_count, 1.0)
    wide = peer_count * slot_count
    incoming = lax.all_to_all(outgoing, "fft", split_axis=2, concat_axis=2, tiled=True)
    item_count = incoming.shape[0]
    lattice = incoming.reshape(item_count, 2, peer_count, row_count, slot_count)
    lattice = jnp.einsum(
        "fcprs,cdpk->fdrks",
        lattice,
        transform_table(peer_count, peer_count, peer_count, -1.0),
        precision=PRECISE,
    )
    lattice = lattice.reshape(item_count, 2, row_count, wide)
    lattice = complex_times(lattice, forward_re, forward_im)
    lattice = jnp.einsum(
        "fcrq,cdrm->fdmq",
        lattice,
        transform_table(row_count, row_count, row_count, -1.0),
        precision=PRECISE,
    )
    lattice = complex_times(lattice, kernel[0], kernel[1])
    lattice = jnp.einsum(
        "fcmq,cdmr->fdrq",
        lattice,
        transform_table(row_count, row_count, row_count, 1.0),
        precision=PRECISE,
    )
    lattice = complex_times(lattice, inverse_re, inverse_im)
    lattice = lattice.reshape(item_count, 2, row_count, peer_count, slot_count)
    lattice = jnp.einsum(
        "fcrks,cdkp->fdprs",
        lattice,
        transform_table(peer_count, peer_count, peer_count, 1.0),
        precision=PRECISE,
    )
    returning = lax.all_to_all(
        lattice.reshape(item_count, 2, peer_count, row_count * slot_count),
        "fft",
        split_axis=2,
        concat_axis=2,
        tiled=True,
    )
    restored = returning.reshape(item_count, 2, XA, groups, row_count, slot_count)
    matrix_back = transform_table(XB, XB, XB, 1.0).reshape(2, 2, groups, slot_count, XB)
    restored = jnp.einsum("fckjrs,cdjsb->fdrkb", restored, matrix_back, precision=PRECISE)
    back_re, back_im = twiddle_pair(XA, XB, NX, 1.0)
    restored = complex_times(restored, back_re, back_im)
    restored = jnp.einsum(
        "fcrkb,cdkn->fdrnb", restored, transform_table(XA, XA, XA, 1.0), precision=PRECISE
    )
    return restored.reshape(item_count, 2, row_count, NX)


def general_body(potential, direction, block_index, block_weights):
    row_count = potential.shape[1]
    peer_count = lax.axis_size("fft")
    slot_count = NX // peer_count
    ahead = fresnel(peer_count, row_count, slot_count, 1.0)
    behind = fresnel(peer_count, row_count, slot_count, -1.0)
    accumulated = jnp.zeros(potential.shape, jnp.float32)
    for angle_index in range(ANGLES):
        selector = one_hot(block_index[angle_index], NB)
        matrices = block_weights[angle_index]
        rotated = rotate(potential, selector, matrices)
        tangent = rotate(direction, selector, matrices)
        damping = jnp.exp(-rotated[1])
        trans_re = damping * jnp.cos(rotated[0])
        trans_im = damping * jnp.sin(rotated[0])
        wave_re = jnp.ones((row_count, NX), jnp.float32)
        wave_im = jnp.zeros((row_count, NX), jnp.float32)
        dwave_re = jnp.zeros((row_count, NX), jnp.float32)
        dwave_im = jnp.zeros((row_count, NX), jnp.float32)
        stored = []
        for slice_index in range(SL):
            t_re = trans_re[:, slice_index]
            t_im = trans_im[:, slice_index]
            d_re = tangent[0][:, slice_index]
            d_im = tangent[1][:, slice_index]
            phi_re = t_re * wave_re - t_im * wave_im
            phi_im = t_re * wave_im + t_im * wave_re
            dphi_re = -(d_re * phi_im + d_im * phi_re) + t_re * dwave_re - t_im * dwave_im
            dphi_im = d_re * phi_re - d_im * phi_im + t_re * dwave_im + t_im * dwave_re
            stored.append((phi_re, phi_im))
            packed = jnp.stack([jnp.stack([phi_re, phi_im]), jnp.stack([dphi_re, dphi_im])])
            propagated = propagate(packed, ahead, peer_count, row_count, slot_count)
            wave_re = propagated[0, 0]
            wave_im = propagated[0, 1]
            dwave_re = propagated[1, 0]
            dwave_im = propagated[1, 1]
        change = 2.0 * (wave_re * dwave_re + wave_im * dwave_im)
        back_re = 2.0 * change * wave_re
        back_im = 2.0 * change * wave_im
        grad_re = [None] * SL
        grad_im = [None] * SL
        for slice_index in reversed(range(SL)):
            pulled = propagate(
                jnp.stack([back_re, back_im])[None], behind, peer_count, row_count, slot_count
            )
            pb_re = pulled[0, 0]
            pb_im = pulled[0, 1]
            phi_re, phi_im = stored[slice_index]
            grad_re[slice_index] = phi_re * pb_im - phi_im * pb_re
            grad_im[slice_index] = -(phi_re * pb_re + phi_im * pb_im)
            t_re = trans_re[:, slice_index]
            t_im = trans_im[:, slice_index]
            back_re = t_re * pb_re + t_im * pb_im
            back_im = t_re * pb_im - t_im * pb_re
        gradient = jnp.stack([jnp.stack(grad_re, axis=1), jnp.stack(grad_im, axis=1)])
        accumulated = accumulated + rotate_back(gradient, selector, matrices)
    return accumulated


def body(potential, direction, block_index, block_weights):
    if lax.axis_size("parts") == 2 and lax.axis_size("fft") == XA:
        return blocked_body(potential, direction, block_index, block_weights)
    return general_body(potential, direction, block_index, block_weights)


def solution(mesh):
    return jax.shard_map(
        body,
        mesh=mesh,
        in_specs=(P("parts", "fft", None), P("parts", "fft", None), P(), P()),
        out_specs=P("parts", "fft", None),
        check_vma=False,
    )
```

```python
import functools
import math

import jax
import jax.numpy as jnp
import numpy as np
from jax import lax
from jax.experimental import pallas as pl
from jax.experimental.pallas import tpu as pltpu
from jax.sharding import PartitionSpec as P

XA = 16
XB = 128
NX = 2048
SL = 2
ANGLES = 2
BLK = 128
NB = 32
SLOTS = 2
STRIP = 16
LANES = 128
CHUNKS = 4
HALF = XA // 2


PRECISE = lax.Precision.HIGHEST


def bin_matrices():
    wavenumber = np.arange(NX)
    signed = np.where(wavenumber < NX // 2, wavenumber, wavenumber - NX)
    factor = np.exp(-1j * np.pi / NX * ((signed * signed) % (2 * NX)))
    line = np.fft.ifft(factor)
    block = np.arange(XA)
    inner = np.arange(XB)
    shifts = (XB * block[:, None, None] + inner[None, :, None] - inner[None, None, :]) % NX
    phases = np.exp(-2j * np.pi / XA * ((block[:, None] * block[None, :]) % XA))
    return np.einsum("kd,dij->kij", phases, line[shifts]) / XA


def split_constant(values):
    values = values.astype(np.float32)
    high = values.astype(jnp.bfloat16)
    low = (values - high.astype(np.float32)).astype(jnp.bfloat16)
    return high, low


def column_constants():
    bins = bin_matrices()
    top = np.concatenate([bins.real, -bins.imag], axis=2)
    bottom = np.concatenate([bins.imag, bins.real], axis=2)
    return np.concatenate([top, bottom], axis=1)


def fourth(values, orient):
    (ar, ai), (br, bi), (cr, ci), (dr, di) = values
    sr, si, er, ei = ar + cr, ai + ci, ar - cr, ai - ci
    tr, ti, fr, fi = br + dr, bi + di, br - dr, bi - di
    minus, plus = (er + fi, ei - fr), (er - fi, ei + fr)
    one, three = (minus, plus) if orient < 0 else (plus, minus)
    return [(sr + tr, si + ti), one, (sr - tr, si - ti), three]


def turned(value, step, orient):
    re, im = value
    if step == 0:
        return value
    if step == 4:
        return (im, -re) if orient < 0 else (-im, re)
    cosine = math.cos(2.0 * math.pi * step / XA)
    sine = orient * math.sin(2.0 * math.pi * step / XA)
    if step == 2:
        root = cosine
        return ((re - im) * root, (re + im) * root) if orient > 0 else ((re + im) * root, (im - re) * root)
    return (re * cosine - im * sine, re * sine + im * cosine)


def sixteenth(values, orient):
    inner = [fourth([values[4 * a + b] for a in range(4)], orient) for b in range(4)]
    out = [None] * XA
    for c in range(4):
        row = fourth([turned(inner[b][c], b * c, orient) for b in range(4)], orient)
        for d in range(4):
            out[c + 4 * d] = row[d]
    return out


def halves(value):
    high = value.astype(jnp.bfloat16)
    return high, (value - high.astype(jnp.float32)).astype(jnp.bfloat16)


def dot32(a, b):
    return jnp.dot(a, b, preferred_element_type=jnp.float32)


def times(a, b):
    return (a[0] * b[0] - a[1] * b[1], a[0] * b[1] + a[1] * b[0])


def sincos(x):
    turns = jnp.floor(x * (2.0 / math.pi) + 0.5)
    rest = ((x - turns * 1.5703125) - turns * 4.837512969970703125e-4) - turns * 7.54978995489188216e-8
    square = rest * rest
    sine = rest + rest * square * (
        -1.6666654611e-1 + square * (8.3321608736e-3 + square * -1.9515295891e-4)
    )
    cosine = (1.0 - 0.5 * square) + square * square * (
        4.166664568298827e-2 + square * (-1.388731625493765e-3 + square * 2.443315711809948e-5)
    )
    quadrant = turns.astype(jnp.int32)
    odd = (quadrant & 1) == 1
    first = jnp.where(odd, cosine, sine)
    second = jnp.where(odd, sine, cosine)
    first = jnp.where((quadrant & 2) == 2, -first, first)
    second = jnp.where(((quadrant + 1) & 2) == 2, -second, second)
    return first, second


def strips(count, step):
    def run(i, carry):
        step(pl.multiple_of(i * STRIP, STRIP))
        return carry

    lax.fori_loop(0, count // STRIP, run, 0)


def rows_out(xhi, xlo, first_row, values):
    for k, (re, im) in enumerate(sixteenth(values, -1.0)):
        for part, value in enumerate((re, im)):
            high, low = halves(value)
            at = (k, pl.ds(first_row, STRIP), pl.ds(part * LANES, LANES))
            xhi[at] = high
            xlo[at] = low


def rows_in(y, first_row):
    values = [
        tuple(y[k, pl.ds(first_row, STRIP), pl.ds(part * LANES, LANES)] for part in range(2))
        for k in range(XA)
    ]
    return sixteenth(values, 1.0)


def rows_mix(xhi, xlo, mhi, mlo, y):
    def step(k, carry):
        high, low = xhi[k], xlo[k]
        y[k] = dot32(high, mhi[k]) + (dot32(low, mhi[k]) + dot32(high, mlo[k]))
        return carry

    lax.fori_loop(0, XA, step, 0)


def columns_out(xhi, xlo, field, row, values):
    for k, (re, im) in enumerate(sixteenth(values, -1.0)):
        for part, value in enumerate((re, im)):
            high, low = halves(value)
            at = (k, pl.ds(part * XB + row, STRIP), pl.ds(field * LANES, LANES))
            xhi[at] = high
            xlo[at] = low


def columns_in(y, field, row):
    values = [
        tuple(
            y[k, pl.ds(part * XB + row, STRIP), pl.ds(field * LANES, LANES)] for part in range(2)
        )
        for k in range(XA)
    ]
    return sixteenth(values, 1.0)


def columns_mix(xhi, xlo, mhi, mlo, y):
    def step(k, carry):
        high, low = xhi[k], xlo[k]
        y[k] = dot32(mhi[k], high) + (dot32(mhi[k], low) + dot32(mlo[k], high))
        return carry

    lax.fori_loop(0, XA, step, 0)


def enter_kernel(place, index, own, other, whi, wlo, mhi, mlo, out, t0, shi, slo, field, xhi, xlo, y):
    half = own.shape[1]
    rows = 2 * half

    for number in range(4):
        for piece, side in ((own, place[0]), (other, 1 - place[0])):

            def cut(row, number=number, piece=piece, side=side):
                high, low = halves(piece[number, pl.ds(row, STRIP), :])
                first = number * rows + side * half + row
                at = pl.ds(pl.multiple_of(first, STRIP), STRIP)
                shi[at, :] = high
                slo[at, :] = low

            strips(half, cut)

    def rotated(b):
        at = [pl.ds(pl.multiple_of(index[b, s] * BLK, BLK), BLK) for s in range(SLOTS)]
        high = jnp.concatenate([shi[:, a] for a in at], axis=1)
        low = jnp.concatenate([slo[:, a] for a in at], axis=1)
        values = dot32(high, whi[b]) + (dot32(low, whi[b]) + dot32(high, wlo[b]))
        angle, loss, d_re, d_im = (values[i * rows : (i + 1) * rows] for i in range(4))
        sine, cosine = sincos(angle)
        damping = jnp.exp(-loss)
        return damping * cosine, damping * sine, d_re, d_im

    def first_slice(b, carry):
        t_re, t_im, d_re, d_im = rotated(b)
        t0[b, 0] = t_re
        t0[b, 1] = t_im
        field[b, 0] = -(d_re * t_im + d_im * t_re)
        field[b, 1] = d_re * t_re - d_im * t_im
        return carry

    lax.fori_loop(0, XA, first_slice, 0)

    def forward(row):
        at = pl.ds(row, STRIP)
        rows_out(xhi, xlo, row, [(t0[b, 0, at, :], t0[b, 1, at, :]) for b in range(XA)])
        rows_out(
            xhi,
            xlo,
            pl.multiple_of(rows + row, STRIP),
            [(field[b, 0, at, :], field[b, 1, at, :]) for b in range(XA)],
        )

    strips(rows, forward)
    rows_mix(xhi, xlo, mhi, mlo, y)

    def backward(row):
        at = pl.ds(row, STRIP)
        for number in range(2):
            values = rows_in(y, pl.multiple_of(number * rows + row, STRIP))
            for b, (re, im) in enumerate(values):
                out[b, 2 * number, at, :] = re
                out[b, 2 * number + 1, at, :] = im

    strips(rows, backward)

    def second_slice(b, carry):
        for channel, value in enumerate(rotated(XA + b)):
            out[b, 4 + channel] = value
        return carry

    lax.fori_loop(0, XA, second_slice, 0)


def by_pieces(spans, step):
    half = XB // CHUNKS // 2
    pieces = [(piece, c) for piece, span in enumerate(spans) for c in range(span)]
    for chunk, (piece, c) in enumerate(pieces):
        for x in range(2):

            def inner(row, chunk=chunk, piece=piece, c=c, x=x):
                places = []
                for p in range(XA):
                    first = (2 * c + p // HALF) * half
                    at = pl.ds(pl.multiple_of(first + row, STRIP), STRIP)
                    places.append((piece, x * HALF + p % HALF, at))
                step(pl.multiple_of((2 * chunk + x) * half + row, STRIP), places)

            strips(half, inner)


def middle_kernel(chunks, *refs):
    arrived = refs[:chunks]
    mhi, mlo, out, kept, xhi, xlo, y = refs[chunks:]

    def forward(row, places):
        for number in range(2):
            values = [
                tuple(arrived[c][g, 2 * number + i, at, :] for i in range(2)) for c, g, at in places
            ]
            columns_out(xhi, xlo, number, row, values)

    by_pieces((1,) * chunks, forward)
    columns_mix(xhi, xlo, mhi, mlo, y)

    def turn(row, places):
        local = pl.ds(row, STRIP)
        wave = columns_in(y, 0, row)
        product = []
        for p, (c, g, at) in enumerate(places):
            t = arrived[c][g, 4, at, :], arrived[c][g, 5, at, :]
            value = times(t, wave[p])
            for i, part in enumerate(value + t):
                kept[p, i, local, :] = part
            product.append(value)
        columns_out(xhi, xlo, 0, row, product)
        dwave = columns_in(y, 1, row)
        change = []
        for p, (c, g, at) in enumerate(places):
            t_re, t_im, d_re, d_im = (arrived[c][g, 4 + i, at, :] for i in range(4))
            p_re, p_im = kept[p, 0, local, :], kept[p, 1, local, :]
            re, im = times((t_re, t_im), dwave[p])
            change.append((re - (d_re * p_im + d_im * p_re), im + (d_re * p_re - d_im * p_im)))
        columns_out(xhi, xlo, 1, row, change)

    by_pieces((1,) * chunks, turn)
    columns_mix(xhi, xlo, mhi, mlo, y)

    def backward(row, places):
        for number in range(2):
            for (_, g, at), (re, im) in zip(places, columns_in(y, number, row)):
                out[g, 2 * number, at, :] = re
                out[g, 2 * number + 1, at, :] = im

    by_pieces((CHUNKS,), backward)


def detector_kernel(fields, mhi, mlo, out, xhi, xlo, y):
    rows = fields.shape[2]

    def forward(row):
        at = pl.ds(row, STRIP)
        for number in range(2):
            rows_out(
                xhi,
                xlo,
                pl.multiple_of(number * rows + row, STRIP),
                [tuple(fields[b, 2 * number + i, at, :] for i in range(2)) for b in range(XA)],
            )

    strips(rows, forward)
    rows_mix(xhi, xlo, mhi, mlo, y)

    def turn(row):
        wave = rows_in(y, row)
        dwave = rows_in(y, pl.multiple_of(rows + row, STRIP))
        back = []
        for (re, im), (d_re, d_im) in zip(wave, dwave):
            change = 4.0 * (re * d_re + im * d_im)
            back.append((change * re, -(change * im)))
        rows_out(xhi, xlo, row, back)

    strips(rows, turn)

    def step(k, carry):
        high, low = xhi[k, :rows, :], xlo[k, :rows, :]
        y[k, :rows, :] = dot32(high, mhi[k]) + (dot32(low, mhi[k]) + dot32(high, mlo[k]))
        return carry

    lax.fori_loop(0, XA, step, 0)

    def backward(row):
        at = pl.ds(row, STRIP)
        for b, (re, im) in enumerate(rows_in(y, row)):
            out[b, 0, at, :] = re
            out[b, 1, at, :] = im

    strips(rows, backward)


def return_kernel(spans, back, kept, mhi, mlo, *refs):
    out, (xhi, xlo, y) = refs[: len(spans)], refs[len(spans) :]

    def forward(row, places):
        values = [(back[g, 0, at, :], back[g, 1, at, :]) for _, g, at in places]
        columns_out(xhi, xlo, 0, row, values)

    by_pieces((CHUNKS,), forward)
    columns_mix(xhi, xlo, mhi, mlo, y)

    def turn(row, places):
        local = pl.ds(row, STRIP)
        pulled = columns_in(y, 0, row)
        following = []
        for p, (c, g, at) in enumerate(places):
            re, im = times((kept[p, 0, local, :], kept[p, 1, local, :]), pulled[p])
            out[c][g, 0, at, :] = -im
            out[c][g, 1, at, :] = -re
            following.append(times((kept[p, 2, local, :], kept[p, 3, local, :]), pulled[p]))
        columns_out(xhi, xlo, 0, row, following)

    by_pieces(spans, turn)
    columns_mix(xhi, xlo, mhi, mlo, y)

    def backward(row, places):
        for (c, g, at), (re, im) in zip(places, columns_in(y, 0, row)):
            out[c][g, 2, at, :] = re
            out[c][g, 3, at, :] = im

    by_pieces(spans, backward)


def leave_kernel(spans, place, index, back, whi, wlo, mhi, mlo, *refs):
    chunks, count = sum(spans), 2 * len(spans)
    t0, refs = refs[:chunks], refs[chunks:]
    before, outs, (shi, slo, xhi, xlo, y) = refs[: -count - 5], refs[-count - 5 : -5], refs[-5:]
    chunk = t0[0].shape[2]
    half = chunk // 2
    rows = chunks * chunk
    starts = []

    def pieces_of(step):
        starts.clear()
        done = 0
        for span in spans:
            for end, side in enumerate((1 - place[1], place[1])):
                base = (2 * done + end * span) * half
                starts.append((base, span * half))
                for c in range(span):

                    def inner(row, side=side, c=c, done=done, base=base):
                        within = pl.multiple_of(side * half + row, STRIP)
                        source = pl.multiple_of((done + c) * chunk + side * half + row, STRIP)
                        target = pl.multiple_of(base + c * half + row, STRIP)
                        step(done + c, pl.ds(within, STRIP), pl.ds(source, STRIP), target)

                    strips(half, inner)
            done += span

    def store(b, i, target, value):
        high, low = halves(value)
        at = pl.ds(pl.multiple_of(i * rows + target, STRIP), STRIP)
        shi[b, at, :] = high
        slo[b, at, :] = low

    def forward(c, within, at, target):
        rows_out(xhi, xlo, target, [(back[b, 2, at, :], back[b, 3, at, :]) for b in range(XA)])
        for b in range(XA):
            for i in range(2):
                store(XA + b, i, target, back[b, i, at, :])

    pieces_of(forward)
    rows_mix(xhi, xlo, mhi, mlo, y)

    def turn(c, within, at, target):
        for b, value in enumerate(rows_in(y, target)):
            re, im = times((t0[c][b, 0, within, :], t0[c][b, 1, within, :]), value)
            store(b, 0, target, -im)
            store(b, 1, target, -re)

    pieces_of(turn)

    for out, old in zip(outs, before or [None] * count):
        out[...] = jnp.zeros(out.shape, jnp.float32) if old is None else old[...]

    def across(a, b):
        return lax.dot_general(
            a, b, (((1,), (1,)), ((), ())), preferred_element_type=jnp.float32
        )

    def step(b, carry):
        high, low = shi[b], slo[b]
        values = across(high, whi[b]) + (across(low, whi[b]) + across(high, wlo[b]))
        for s in range(SLOTS):
            at = pl.ds(pl.multiple_of(index[b, s] * BLK, BLK), BLK)
            for i in range(2):
                for (start, size), out in zip(starts, outs):
                    start += i * rows
                    out[i, :, at] += values[start : start + size, s * BLK : (s + 1) * BLK]
        return carry

    lax.fori_loop(0, NB, step, 0)


def call(kernel, outs, scratch, mix_count, extra, *operands):
    specs = [
        pl.BlockSpec(memory_space=pltpu.SMEM if o.dtype == jnp.int32 else pltpu.VMEM)
        for o in operands
    ]
    moved = sum(o.size * o.dtype.itemsize for o in operands) + sum(4 * math.prod(o) for o in outs)
    return pl.pallas_call(
        kernel,
        out_shape=[jax.ShapeDtypeStruct(o, jnp.float32) for o in outs],
        in_specs=specs,
        out_specs=[pl.BlockSpec(memory_space=pltpu.VMEM)] * len(outs),
        scratch_shapes=scratch,
        compiler_params=pltpu.CompilerParams(vmem_limit_bytes=60 * 1024 * 1024),
        cost_estimate=pl.CostEstimate(
            flops=int(mix_count * 16 * 128 * 256 * 256 * 6) + extra,
            bytes_accessed=moved,
            transcendentals=0,
        ),
    )(*operands)


def mix_scratch(rows, lanes):
    return [
        pltpu.VMEM((XA, rows, lanes), jnp.bfloat16),
        pltpu.VMEM((XA, rows, lanes), jnp.bfloat16),
        pltpu.VMEM((XA, rows, lanes), jnp.float32),
    ]


def enter(place, index, own, other, weights, matrices):
    rows = 2 * own.shape[1]
    scratch = [
        pltpu.VMEM((4 * rows, NB * BLK), jnp.bfloat16),
        pltpu.VMEM((4 * rows, NB * BLK), jnp.bfloat16),
        pltpu.VMEM((XA, 2, rows, LANES), jnp.float32),
    ] + mix_scratch(2 * rows, 2 * LANES)
    outs = [(XA, 8, rows, LANES), (XA, 2, rows, LANES)]
    extra = NB * 4 * rows * 256 * 128 * 6
    return call(
        enter_kernel,
        outs,
        scratch,
        rows / XB * 2,
        extra,
        place,
        index,
        own,
        other,
        *weights,
        *matrices,
    )


def middle(arrived, matrices):
    return call(
        functools.partial(middle_kernel, len(arrived)),
        [(XA, 4, XB, LANES), (XA, 4, XB, LANES)],
        mix_scratch(2 * XB, 2 * LANES),
        4,
        0,
        *arrived,
        *matrices,
    )


def detector(fields, matrices):
    rows = fields.shape[2]
    return call(
        detector_kernel,
        [(XA, 2, rows, LANES)],
        mix_scratch(2 * rows, 2 * LANES),
        3,
        0,
        fields,
        *matrices,
    )[0]


def pull(back, kept, matrices, spans):
    return call(
        functools.partial(return_kernel, spans),
        [(XA, 4, span * XB // CHUNKS, LANES) for span in spans],
        mix_scratch(2 * XB, LANES),
        2,
        0,
        back,
        kept,
        *matrices,
    )


def leave(place, index, back, t0, weights, matrices, before, spans):
    rows = sum(t.shape[2] for t in t0)
    scratch = [
        pltpu.VMEM((NB, 2 * rows, LANES), jnp.bfloat16),
        pltpu.VMEM((NB, 2 * rows, LANES), jnp.bfloat16),
    ] + mix_scratch(rows, 2 * LANES)
    extra = NB * 2 * rows * 256 * 128 * 6
    outs = call(
        functools.partial(leave_kernel, spans),
        [(2, span * XB // CHUNKS // 2, NB * BLK) for span in spans for _ in range(2)],
        scratch,
        rows / XB,
        extra,
        place,
        index,
        back,
        *weights,
        *matrices,
        *t0,
        *before,
    )
    return [outs[2 * i : 2 * i + 2] for i in range(len(spans))]


def split_weights(block_weights):
    stacked = block_weights.reshape(ANGLES, NB, SLOTS * BLK, BLK)
    rounded = lax.reduce_precision(stacked, 8, 7)
    return rounded.astype(jnp.bfloat16), (stacked - rounded).astype(jnp.bfloat16)


def device(q, b, r):
    return q * XA + b * HALF + r


def exchange(values):
    return lax.all_to_all(
        values,
        ("parts", "fft"),
        split_axis=0,
        concat_axis=0,
        axis_index_groups=[[device(x, b, r) for x in range(2) for r in range(HALF)] for b in range(2)],
        tiled=True,
    )


def permute(values, steps):
    pairs = [
        (device(*here, r), device(*there, r)) for here, there in steps for r in range(HALF)
    ]
    return lax.ppermute(values, ("parts", "fft"), pairs)


BESIDE = [((q, b), (1 - q, b)) for q in range(2) for b in range(2)]
ALONG = [((q, b), (q, 1 - b)) for q in range(2) for b in range(2)]
CYCLE = [((0, 0), (0, 1)), ((1, 0), (0, 0)), ((1, 1), (1, 0)), ((0, 1), (1, 1))]
ACROSS = [((0, 1), (1, 0)), ((1, 0), (0, 1))]


def after(values, others):
    return lax.optimization_barrier((values, others))[0]


def arrive(potential, direction, q, b):
    half = XB // CHUNKS // 2

    def sides(c):
        lower, upper = (
            jnp.concatenate(
                [v[:, (2 * c + x) * half : (2 * c + x + 1) * half] for v in (potential, direction)]
            )
            for x in range(2)
        )
        return jnp.where(q == 0, lower, upper), jnp.where(q == 0, upper, lower)

    keep, give = sides(0)
    potential, direction = after((potential, direction), give)
    beside = permute(give, BESIDE)
    kept, given = zip(*[sides(c) for c in range(1, CHUNKS)])
    rest = permute(after(jnp.concatenate(given), beside), BESIDE)
    chunks = []
    along = ()
    for c in range(CHUNKS):
        if c:
            keep, beside = kept[c - 1], rest[4 * (c - 1) : 4 * c]
        own = jnp.where(q == b, keep, beside)
        give = jnp.where(q == b, beside, keep)
        along = permute(after(give, along), ALONG)
        chunks.append((own, along))
    return chunks, rest


def depart(near, far):
    return permute(near, CYCLE), permute(far, ACROSS), far


def settle(once, twice, far, q, b):
    same = jnp.where(q == b, far, once)
    rest = jnp.where(q == b, once, twice)
    return jnp.where(q == 0, same, rest), jnp.where(q == 0, rest, same)


def blocked_body(potential, direction, block_index, block_weights):
    q = lax.axis_index("parts")
    b = lax.axis_index("fft") // HALF
    place = jnp.stack([b, q]).astype(jnp.int32)
    chunks, beside = arrive(potential, direction, q, b)
    whi, wlo = split_weights(block_weights)
    by_column = column_constants()
    column = tuple(jnp.asarray(v) for v in split_constant(by_column))
    row = tuple(jnp.asarray(v) for v in split_constant(by_column.transpose(0, 2, 1)))
    weights = [(whi[a], wlo[a]) for a in range(ANGLES)]
    arrived = [[] for _ in range(ANGLES)]
    ahead = [[] for _ in range(ANGLES)]
    for c, (own, along) in enumerate(chunks):
        further = chunks[c + 1][1] if c + 1 < CHUNKS else ()
        own = after(own, beside)
        for a in range(ANGLES):
            fields, t0 = enter(place, block_index[a], own, along, weights[a], row)
            beside = fields
            arrived[a].append(exchange(after(fields, further) if a else fields))
            ahead[a].append(t0)
    carried = []
    for a in range(ANGLES):
        out, kept = middle(arrived[a], column)
        carried.append((exchange(out), kept))
    backs = [exchange(detector(out, row)) for out, _ in carried]
    spans = (CHUNKS // 2, CHUNKS // 4, CHUNKS // 4)
    pulled = exchange(pull(backs[0], carried[0][1], column, (CHUNKS,))[0])
    totals = leave(place, block_index[0], pulled, ahead[0], weights[0], row, (), spans)
    pulled = pull(backs[1], carried[1][1], column, spans)
    pieces, leaving = [], []
    half = XB // CHUNKS // 2
    done = 0
    for i, span in enumerate(spans):
        back = exchange(after(pulled[i], totals) if i else pulled[i])
        t0 = ahead[1][done : done + span]
        done += span
        total = leave(place, block_index[1], back, t0, weights[1], row, totals[i], (span,))[0]
        leaving.append(depart(*total))
    for span, moved in zip(spans, after(leaving, total)):
        lower, upper = settle(*moved, q, b)
        for c in range(span):
            pieces += [v[:, c * half : (c + 1) * half] for v in (lower, upper)]
    return jnp.concatenate(pieces, axis=1)


def transform_table(count_in, count_out, length, orient):
    first = jnp.arange(count_in, dtype=jnp.int32)[:, None]
    second = jnp.arange(count_out, dtype=jnp.int32)[None, :]
    phases = orient * 2.0 * math.pi / length * (first * second % length).astype(jnp.float32)
    cosine = jnp.cos(phases)
    sine_part = jnp.sin(phases)
    return jnp.stack([jnp.stack([cosine, sine_part]), jnp.stack([-sine_part, cosine])])


def twiddle_pair(count_a, count_b, length, orient):
    first = jnp.arange(count_a, dtype=jnp.int32)[:, None]
    second = jnp.arange(count_b, dtype=jnp.int32)[None, :]
    phases = orient * 2.0 * math.pi / length * (first * second % length).astype(jnp.float32)
    return (jnp.cos(phases), jnp.sin(phases))


def spread_turn(peer_count, row_count, slot_count, orient):
    turn_re, turn_im = twiddle_pair(peer_count, row_count, NX, orient)
    shape_three = (row_count, peer_count, slot_count)
    wide_re = jnp.broadcast_to(turn_re.T[:, :, None], shape_three).reshape(
        row_count, peer_count * slot_count
    )
    wide_im = jnp.broadcast_to(turn_im.T[:, :, None], shape_three).reshape(
        row_count, peer_count * slot_count
    )
    return (wide_re, wide_im)


def complex_times(values, real_part, imag_part):
    first = values[:, 0]
    second = values[:, 1]
    return jnp.stack(
        [first * real_part - second * imag_part, first * imag_part + second * real_part], axis=1
    )


def one_hot(index_rows, block_count):
    return (index_rows[..., None] == jnp.arange(block_count, dtype=jnp.int32)).astype(jnp.float32)


def rotate(values, selector, matrices):
    height = values.shape[1]
    blocked = values.reshape(2, height, NB, BLK)
    picked = jnp.einsum("cyni,bsn->cybsi", blocked, selector, precision=PRECISE)
    rotated = jnp.einsum("cybsi,bsio->cybo", picked, matrices, precision=PRECISE)
    return rotated.reshape(2, height, SL, NX)


def rotate_back(values, selector, matrices):
    height = values.shape[1]
    blocked = values.reshape(2, height, NB, BLK)
    spread_out = jnp.einsum("cybo,bsio->cybsi", blocked, matrices, precision=PRECISE)
    summed = jnp.einsum("cybsi,bsn->cyni", spread_out, selector, precision=PRECISE)
    return summed.reshape(2, height, SL * NX)


def fresnel(peer_count, row_count, slot_count, orient):
    position_high = jnp.arange(row_count, dtype=jnp.int32)[:, None]
    position_low = jnp.arange(peer_count, dtype=jnp.int32)[None, :]
    freq_y = position_low + peer_count * position_high
    freq_y = jnp.where(freq_y < NX // 2, freq_y, freq_y - NX)
    position = lax.axis_index("fft") * slot_count + jnp.arange(slot_count, dtype=jnp.int32)
    freq_x = position // XB + XA * (position % XB)
    freq_x = jnp.where(freq_x < NX // 2, freq_x, freq_x - NX)
    squares = ((freq_y * freq_y)[:, :, None] + (freq_x * freq_x)[None, None, :]) % (2 * NX)
    phases = orient * -math.pi / NX * squares.astype(jnp.float32)
    scaling = 1.0 / (NX * NX)
    phases = phases.reshape(row_count, peer_count * slot_count)
    return (jnp.cos(phases) * scaling, jnp.sin(phases) * scaling)


def propagate(fields, kernel, peer_count, row_count, slot_count):
    field_count = fields.shape[0]
    groups = XB // slot_count
    shaped = fields.reshape(field_count, 2, row_count, XA, XB)
    partial_x = jnp.einsum(
        "fcrab,cdak->fdrkb", shaped, transform_table(XA, XA, XA, -1.0), precision=PRECISE
    )
    twist_re, twist_im = twiddle_pair(XA, XB, NX, -1.0)
    partial_x = complex_times(partial_x, twist_re, twist_im)
    partial_x = jnp.einsum(
        "fcrkb,cdbt->fdrkt", partial_x, transform_table(XB, XB, XB, -1.0), precision=PRECISE
    )
    partial_x = partial_x.reshape(field_count, 2, row_count, XA, groups, slot_count)
    outgoing = partial_x.transpose(0, 1, 3, 4, 2, 5).reshape(
        field_count, 2, peer_count, row_count * slot_count
    )
    forward_re, forward_im = spread_turn(peer_count, row_count, slot_count, -1.0)
    inverse_re, inverse_im = spread_turn(peer_count, row_count, slot_count, 1.0)
    wide = peer_count * slot_count
    incoming = lax.all_to_all(outgoing, "fft", split_axis=2, concat_axis=2, tiled=True)
    item_count = incoming.shape[0]
    lattice = incoming.reshape(item_count, 2, peer_count, row_count, slot_count)
    lattice = jnp.einsum(
        "fcprs,cdpk->fdrks",
        lattice,
        transform_table(peer_count, peer_count, peer_count, -1.0),
        precision=PRECISE,
    )
    lattice = lattice.reshape(item_count, 2, row_count, wide)
    lattice = complex_times(lattice, forward_re, forward_im)
    lattice = jnp.einsum(
        "fcrq,cdrm->fdmq",
        lattice,
        transform_table(row_count, row_count, row_count, -1.0),
        precision=PRECISE,
    )
    lattice = complex_times(lattice, kernel[0], kernel[1])
    lattice = jnp.einsum(
        "fcmq,cdmr->fdrq",
        lattice,
        transform_table(row_count, row_count, row_count, 1.0),
        precision=PRECISE,
    )
    lattice = complex_times(lattice, inverse_re, inverse_im)
    lattice = lattice.reshape(item_count, 2, row_count, peer_count, slot_count)
    lattice = jnp.einsum(
        "fcrks,cdkp->fdprs",
        lattice,
        transform_table(peer_count, peer_count, peer_count, 1.0),
        precision=PRECISE,
    )
    returning = lax.all_to_all(
        lattice.reshape(item_count, 2, peer_count, row_count * slot_count),
        "fft",
        split_axis=2,
        concat_axis=2,
        tiled=True,
    )
    restored = returning.reshape(item_count, 2, XA, groups, row_count, slot_count)
    matrix_back = transform_table(XB, XB, XB, 1.0).reshape(2, 2, groups, slot_count, XB)
    restored = jnp.einsum("fckjrs,cdjsb->fdrkb", restored, matrix_back, precision=PRECISE)
    back_re, back_im = twiddle_pair(XA, XB, NX, 1.0)
    restored = complex_times(restored, back_re, back_im)
    restored = jnp.einsum(
        "fcrkb,cdkn->fdrnb", restored, transform_table(XA, XA, XA, 1.0), precision=PRECISE
    )
    return restored.reshape(item_count, 2, row_count, NX)


def general_body(potential, direction, block_index, block_weights):
    row_count = potential.shape[1]
    peer_count = lax.axis_size("fft")
    slot_count = NX // peer_count
    ahead = fresnel(peer_count, row_count, slot_count, 1.0)
    behind = fresnel(peer_count, row_count, slot_count, -1.0)
    accumulated = jnp.zeros(potential.shape, jnp.float32)
    for angle_index in range(ANGLES):
        selector = one_hot(block_index[angle_index], NB)
        matrices = block_weights[angle_index]
        rotated = rotate(potential, selector, matrices)
        tangent = rotate(direction, selector, matrices)
        damping = jnp.exp(-rotated[1])
        trans_re = damping * jnp.cos(rotated[0])
        trans_im = damping * jnp.sin(rotated[0])
        wave_re = jnp.ones((row_count, NX), jnp.float32)
        wave_im = jnp.zeros((row_count, NX), jnp.float32)
        dwave_re = jnp.zeros((row_count, NX), jnp.float32)
        dwave_im = jnp.zeros((row_count, NX), jnp.float32)
        stored = []
        for slice_index in range(SL):
            t_re = trans_re[:, slice_index]
            t_im = trans_im[:, slice_index]
            d_re = tangent[0][:, slice_index]
            d_im = tangent[1][:, slice_index]
            phi_re = t_re * wave_re - t_im * wave_im
            phi_im = t_re * wave_im + t_im * wave_re
            dphi_re = -(d_re * phi_im + d_im * phi_re) + t_re * dwave_re - t_im * dwave_im
            dphi_im = d_re * phi_re - d_im * phi_im + t_re * dwave_im + t_im * dwave_re
            stored.append((phi_re, phi_im))
            packed = jnp.stack([jnp.stack([phi_re, phi_im]), jnp.stack([dphi_re, dphi_im])])
            propagated = propagate(packed, ahead, peer_count, row_count, slot_count)
            wave_re = propagated[0, 0]
            wave_im = propagated[0, 1]
            dwave_re = propagated[1, 0]
            dwave_im = propagated[1, 1]
        change = 2.0 * (wave_re * dwave_re + wave_im * dwave_im)
        back_re = 2.0 * change * wave_re
        back_im = 2.0 * change * wave_im
        grad_re = [None] * SL
        grad_im = [None] * SL
        for slice_index in reversed(range(SL)):
            pulled = propagate(
                jnp.stack([back_re, back_im])[None], behind, peer_count, row_count, slot_count
            )
            pb_re = pulled[0, 0]
            pb_im = pulled[0, 1]
            phi_re, phi_im = stored[slice_index]
            grad_re[slice_index] = phi_re * pb_im - phi_im * pb_re
            grad_im[slice_index] = -(phi_re * pb_re + phi_im * pb_im)
            t_re = trans_re[:, slice_index]
            t_im = trans_im[:, slice_index]
            back_re = t_re * pb_re + t_im * pb_im
            back_im = t_re * pb_im - t_im * pb_re
        gradient = jnp.stack([jnp.stack(grad_re, axis=1), jnp.stack(grad_im, axis=1)])
        accumulated = accumulated + rotate_back(gradient, selector, matrices)
    return accumulated


def body(potential, direction, block_index, block_weights):
    if lax.axis_size("parts") == 2 and lax.axis_size("fft") == XA:
        return blocked_body(potential, direction, block_index, block_weights)
    return general_body(potential, direction, block_index, block_weights)


def solution(mesh):
    return jax.shard_map(
        body,
        mesh=mesh,
        in_specs=(P("parts", "fft", None), P("parts", "fft", None), P(), P()),
        out_specs=P("parts", "fft", None),
        check_vma=False,
    )
```

```python
import functools
import math

import jax
import jax.numpy as jnp
import numpy as np
from jax import lax
from jax.experimental import pallas as pl
from jax.experimental.pallas import tpu as pltpu
from jax.sharding import PartitionSpec as P

XA = 16
XB = 128
NX = 2048
SL = 2
ANGLES = 2
BLK = 128
NB = 32
SLOTS = 2
STRIP = 16
LANES = 128
CHUNKS = 4
HALF = XA // 2


PRECISE = lax.Precision.HIGHEST


def bin_matrices():
    wavenumber = np.arange(NX)
    signed = np.where(wavenumber < NX // 2, wavenumber, wavenumber - NX)
    factor = np.exp(-1j * np.pi / NX * ((signed * signed) % (2 * NX)))
    line = np.fft.ifft(factor)
    block = np.arange(XA)
    inner = np.arange(XB)
    shifts = (XB * block[:, None, None] + inner[None, :, None] - inner[None, None, :]) % NX
    phases = np.exp(-2j * np.pi / XA * ((block[:, None] * block[None, :]) % XA))
    return np.einsum("kd,dij->kij", phases, line[shifts]) / XA


def split_constant(values):
    values = values.astype(np.float32)
    high = values.astype(jnp.bfloat16)
    low = (values - high.astype(np.float32)).astype(jnp.bfloat16)
    return high, low


def column_constants():
    bins = bin_matrices()
    top = np.concatenate([bins.real, -bins.imag], axis=2)
    bottom = np.concatenate([bins.imag, bins.real], axis=2)
    return np.concatenate([top, bottom], axis=1)


def fourth(values, orient):
    (ar, ai), (br, bi), (cr, ci), (dr, di) = values
    sr, si, er, ei = ar + cr, ai + ci, ar - cr, ai - ci
    tr, ti, fr, fi = br + dr, bi + di, br - dr, bi - di
    minus, plus = (er + fi, ei - fr), (er - fi, ei + fr)
    one, three = (minus, plus) if orient < 0 else (plus, minus)
    return [(sr + tr, si + ti), one, (sr - tr, si - ti), three]


def turned(value, step, orient):
    re, im = value
    if step == 0:
        return value
    if step == 4:
        return (im, -re) if orient < 0 else (-im, re)
    cosine = math.cos(2.0 * math.pi * step / XA)
    sine = orient * math.sin(2.0 * math.pi * step / XA)
    if step == 2:
        root = cosine
        return ((re - im) * root, (re + im) * root) if orient > 0 else ((re + im) * root, (im - re) * root)
    return (re * cosine - im * sine, re * sine + im * cosine)


def sixteenth(values, orient):
    inner = [fourth([values[4 * a + b] for a in range(4)], orient) for b in range(4)]
    out = [None] * XA
    for c in range(4):
        row = fourth([turned(inner[b][c], b * c, orient) for b in range(4)], orient)
        for d in range(4):
            out[c + 4 * d] = row[d]
    return out


def halves(value):
    high = value.astype(jnp.bfloat16)
    return high, (value - high.astype(jnp.float32)).astype(jnp.bfloat16)


def dot32(a, b):
    return jnp.dot(a, b, preferred_element_type=jnp.float32)


def times(a, b):
    return (a[0] * b[0] - a[1] * b[1], a[0] * b[1] + a[1] * b[0])


def sincos(x):
    turns = jnp.floor(x * (2.0 / math.pi) + 0.5)
    rest = ((x - turns * 1.5703125) - turns * 4.837512969970703125e-4) - turns * 7.54978995489188216e-8
    square = rest * rest
    sine = rest + rest * square * (
        -1.6666654611e-1 + square * (8.3321608736e-3 + square * -1.9515295891e-4)
    )
    cosine = (1.0 - 0.5 * square) + square * square * (
        4.166664568298827e-2 + square * (-1.388731625493765e-3 + square * 2.443315711809948e-5)
    )
    quadrant = turns.astype(jnp.int32)
    odd = (quadrant & 1) == 1
    first = jnp.where(odd, cosine, sine)
    second = jnp.where(odd, sine, cosine)
    first = jnp.where((quadrant & 2) == 2, -first, first)
    second = jnp.where(((quadrant + 1) & 2) == 2, -second, second)
    return first, second


def strips(count, step):
    def run(i, carry):
        step(pl.multiple_of(i * STRIP, STRIP))
        return carry

    lax.fori_loop(0, count // STRIP, run, 0)


def rows_out(xhi, xlo, first_row, values):
    for k, (re, im) in enumerate(sixteenth(values, -1.0)):
        for part, value in enumerate((re, im)):
            high, low = halves(value)
            at = (k, pl.ds(first_row, STRIP), pl.ds(part * LANES, LANES))
            xhi[at] = high
            xlo[at] = low


def rows_in(y, first_row):
    values = [
        tuple(y[k, pl.ds(first_row, STRIP), pl.ds(part * LANES, LANES)] for part in range(2))
        for k in range(XA)
    ]
    return sixteenth(values, 1.0)


def rows_mix(xhi, xlo, mhi, mlo, y):
    def step(k, carry):
        high, low = xhi[k], xlo[k]
        y[k] = dot32(high, mhi[k]) + (dot32(low, mhi[k]) + dot32(high, mlo[k]))
        return carry

    lax.fori_loop(0, XA, step, 0)


def columns_out(xhi, xlo, field, row, values):
    for k, (re, im) in enumerate(sixteenth(values, -1.0)):
        for part, value in enumerate((re, im)):
            high, low = halves(value)
            at = (k, pl.ds(part * XB + row, STRIP), pl.ds(field * LANES, LANES))
            xhi[at] = high
            xlo[at] = low


def columns_in(y, field, row):
    values = [
        tuple(
            y[k, pl.ds(part * XB + row, STRIP), pl.ds(field * LANES, LANES)] for part in range(2)
        )
        for k in range(XA)
    ]
    return sixteenth(values, 1.0)


def columns_mix(xhi, xlo, mhi, mlo, y):
    def step(k, carry):
        high, low = xhi[k], xlo[k]
        y[k] = dot32(mhi[k], high) + (dot32(mhi[k], low) + dot32(mlo[k], high))
        return carry

    lax.fori_loop(0, XA, step, 0)


def enter_kernel(angles, place, *refs):
    indices, (own, other), refs = refs[:angles], refs[angles : angles + 2], refs[angles + 2 :]
    weights, (mhi, mlo, out), refs = refs[: 2 * angles], refs[2 * angles : 2 * angles + 3], refs[2 * angles + 3 :]
    fronts, (shi, slo, field, xhi, xlo, y) = refs[:angles], refs[angles:]
    half = own.shape[1]
    rows = 2 * half

    for number in range(4):
        for piece, side in ((own, place[0]), (other, 1 - place[0])):

            def cut(row, number=number, piece=piece, side=side):
                high, low = halves(piece[number, pl.ds(row, STRIP), :])
                first = number * rows + side * half + row
                at = pl.ds(pl.multiple_of(first, STRIP), STRIP)
                shi[at, :] = high
                slo[at, :] = low

            strips(half, cut)

    for a in range(angles):
        enter_angle(
            indices[a], weights[2 * a], weights[2 * a + 1], mhi, mlo,
            out, 8 * a, fronts[a], shi, slo, field, xhi, xlo, y,
        )


def enter_angle(index, whi, wlo, mhi, mlo, out, base, t0, shi, slo, field, xhi, xlo, y):
    rows = t0.shape[2]

    def rotated(b):
        at = [pl.ds(pl.multiple_of(index[b, s] * BLK, BLK), BLK) for s in range(SLOTS)]
        high = jnp.concatenate([shi[:, a] for a in at], axis=1)
        low = jnp.concatenate([slo[:, a] for a in at], axis=1)
        values = dot32(high, whi[b]) + (dot32(low, whi[b]) + dot32(high, wlo[b]))
        angle, loss, d_re, d_im = (values[i * rows : (i + 1) * rows] for i in range(4))
        sine, cosine = sincos(angle)
        damping = jnp.exp(-loss)
        return damping * cosine, damping * sine, d_re, d_im

    def first_slice(b, carry):
        t_re, t_im, d_re, d_im = rotated(b)
        t0[b, 0] = t_re
        t0[b, 1] = t_im
        field[b, 0] = -(d_re * t_im + d_im * t_re)
        field[b, 1] = d_re * t_re - d_im * t_im
        return carry

    lax.fori_loop(0, XA, first_slice, 0)

    def forward(row):
        at = pl.ds(row, STRIP)
        rows_out(xhi, xlo, row, [(t0[b, 0, at, :], t0[b, 1, at, :]) for b in range(XA)])
        rows_out(
            xhi,
            xlo,
            pl.multiple_of(rows + row, STRIP),
            [(field[b, 0, at, :], field[b, 1, at, :]) for b in range(XA)],
        )

    strips(rows, forward)
    rows_mix(xhi, xlo, mhi, mlo, y)

    def backward(row):
        at = pl.ds(row, STRIP)
        for number in range(2):
            values = rows_in(y, pl.multiple_of(number * rows + row, STRIP))
            for b, (re, im) in enumerate(values):
                out[b, base + 2 * number, at, :] = re
                out[b, base + 2 * number + 1, at, :] = im

    strips(rows, backward)

    def second_slice(b, carry):
        for channel, value in enumerate(rotated(XA + b)):
            out[b, base + 4 + channel] = value
        return carry

    lax.fori_loop(0, XA, second_slice, 0)


def by_pieces(spans, step):
    half = XB // CHUNKS // 2
    pieces = [(piece, c) for piece, span in enumerate(spans) for c in range(span)]
    for chunk, (piece, c) in enumerate(pieces):
        for x in range(2):

            def inner(row, chunk=chunk, piece=piece, c=c, x=x):
                places = []
                for p in range(XA):
                    first = (2 * c + p // HALF) * half
                    at = pl.ds(pl.multiple_of(first + row, STRIP), STRIP)
                    places.append((piece, x * HALF + p % HALF, at))
                step(pl.multiple_of((2 * chunk + x) * half + row, STRIP), places)

            strips(half, inner)


def middle_kernel(bases, *refs):
    chunks = len(bases)
    arrived = refs[:chunks]
    mhi, mlo, out, kept, xhi, xlo, y = refs[chunks:]

    def forward(row, places):
        for number in range(2):
            values = [
                tuple(arrived[c][g, bases[c] + 2 * number + i, at, :] for i in range(2)) for c, g, at in places
            ]
            columns_out(xhi, xlo, number, row, values)

    by_pieces((1,) * chunks, forward)
    columns_mix(xhi, xlo, mhi, mlo, y)

    def turn(row, places):
        local = pl.ds(row, STRIP)
        wave = columns_in(y, 0, row)
        product = []
        for p, (c, g, at) in enumerate(places):
            t = tuple(arrived[c][g, bases[c] + i, at, :] for i in (4, 5))
            value = times(t, wave[p])
            for i, part in enumerate(value + t):
                kept[p, i, local, :] = part
            product.append(value)
        columns_out(xhi, xlo, 0, row, product)
        dwave = columns_in(y, 1, row)
        change = []
        for p, (c, g, at) in enumerate(places):
            t_re, t_im, d_re, d_im = (arrived[c][g, bases[c] + 4 + i, at, :] for i in range(4))
            p_re, p_im = kept[p, 0, local, :], kept[p, 1, local, :]
            re, im = times((t_re, t_im), dwave[p])
            change.append((re - (d_re * p_im + d_im * p_re), im + (d_re * p_re - d_im * p_im)))
        columns_out(xhi, xlo, 1, row, change)

    by_pieces((1,) * chunks, turn)
    columns_mix(xhi, xlo, mhi, mlo, y)

    def backward(row, places):
        for number in range(2):
            for (_, g, at), (re, im) in zip(places, columns_in(y, number, row)):
                out[g, 2 * number, at, :] = re
                out[g, 2 * number + 1, at, :] = im

    by_pieces((CHUNKS,), backward)


def detector_kernel(fields, mhi, mlo, out, xhi, xlo, y):
    rows = fields.shape[2]

    def forward(row):
        at = pl.ds(row, STRIP)
        for number in range(2):
            rows_out(
                xhi,
                xlo,
                pl.multiple_of(number * rows + row, STRIP),
                [tuple(fields[b, 2 * number + i, at, :] for i in range(2)) for b in range(XA)],
            )

    strips(rows, forward)
    rows_mix(xhi, xlo, mhi, mlo, y)

    def turn(row):
        wave = rows_in(y, row)
        dwave = rows_in(y, pl.multiple_of(rows + row, STRIP))
        back = []
        for (re, im), (d_re, d_im) in zip(wave, dwave):
            change = 4.0 * (re * d_re + im * d_im)
            back.append((change * re, -(change * im)))
        rows_out(xhi, xlo, row, back)

    strips(rows, turn)

    def step(k, carry):
        high, low = xhi[k, :rows, :], xlo[k, :rows, :]
        y[k, :rows, :] = dot32(high, mhi[k]) + (dot32(low, mhi[k]) + dot32(high, mlo[k]))
        return carry

    lax.fori_loop(0, XA, step, 0)

    def backward(row):
        at = pl.ds(row, STRIP)
        for b, (re, im) in enumerate(rows_in(y, row)):
            out[b, 0, at, :] = re
            out[b, 1, at, :] = im

    strips(rows, backward)


def return_kernel(spans, back, kept, mhi, mlo, *refs):
    out, (xhi, xlo, y) = refs[: len(spans)], refs[len(spans) :]

    def forward(row, places):
        values = [(back[g, 0, at, :], back[g, 1, at, :]) for _, g, at in places]
        columns_out(xhi, xlo, 0, row, values)

    by_pieces((CHUNKS,), forward)
    columns_mix(xhi, xlo, mhi, mlo, y)

    def turn(row, places):
        local = pl.ds(row, STRIP)
        pulled = columns_in(y, 0, row)
        following = []
        for p, (c, g, at) in enumerate(places):
            re, im = times((kept[p, 0, local, :], kept[p, 1, local, :]), pulled[p])
            out[c][g, 0, at, :] = -im
            out[c][g, 1, at, :] = -re
            following.append(times((kept[p, 2, local, :], kept[p, 3, local, :]), pulled[p]))
        columns_out(xhi, xlo, 0, row, following)

    by_pieces(spans, turn)
    columns_mix(xhi, xlo, mhi, mlo, y)

    def backward(row, places):
        for (c, g, at), (re, im) in zip(places, columns_in(y, 0, row)):
            out[c][g, 2, at, :] = re
            out[c][g, 3, at, :] = im

    by_pieces(spans, backward)


def leave_kernel(spans, place, index, back, whi, wlo, mhi, mlo, *refs):
    chunks, count = sum(spans), 2 * len(spans)
    t0, refs = refs[:chunks], refs[chunks:]
    before, outs, (shi, slo, xhi, xlo, y) = refs[: -count - 5], refs[-count - 5 : -5], refs[-5:]
    chunk = t0[0].shape[2]
    half = chunk // 2
    rows = chunks * chunk
    starts = []

    def pieces_of(step):
        starts.clear()
        done = 0
        for span in spans:
            for end, side in enumerate((1 - place[1], place[1])):
                base = (2 * done + end * span) * half
                starts.append((base, span * half))
                for c in range(span):

                    def inner(row, side=side, c=c, done=done, base=base):
                        within = pl.multiple_of(side * half + row, STRIP)
                        source = pl.multiple_of((done + c) * chunk + side * half + row, STRIP)
                        target = pl.multiple_of(base + c * half + row, STRIP)
                        step(done + c, pl.ds(within, STRIP), pl.ds(source, STRIP), target)

                    strips(half, inner)
            done += span

    def store(b, i, target, value):
        high, low = halves(value)
        at = pl.ds(pl.multiple_of(i * rows + target, STRIP), STRIP)
        shi[b, at, :] = high
        slo[b, at, :] = low

    def forward(c, within, at, target):
        rows_out(xhi, xlo, target, [(back[b, 2, at, :], back[b, 3, at, :]) for b in range(XA)])
        for b in range(XA):
            for i in range(2):
                store(XA + b, i, target, back[b, i, at, :])

    pieces_of(forward)
    rows_mix(xhi, xlo, mhi, mlo, y)

    def turn(c, within, at, target):
        for b, value in enumerate(rows_in(y, target)):
            re, im = times((t0[c][b, 0, within, :], t0[c][b, 1, within, :]), value)
            store(b, 0, target, -im)
            store(b, 1, target, -re)

    pieces_of(turn)

    for out, old in zip(outs, before or [None] * count):
        out[...] = jnp.zeros(out.shape, jnp.float32) if old is None else old[...]

    def across(a, b):
        return lax.dot_general(
            a, b, (((1,), (1,)), ((), ())), preferred_element_type=jnp.float32
        )

    def step(b, carry):
        high, low = shi[b], slo[b]
        values = across(high, whi[b]) + (across(low, whi[b]) + across(high, wlo[b]))
        for s in range(SLOTS):
            at = pl.ds(pl.multiple_of(index[b, s] * BLK, BLK), BLK)
            for i in range(2):
                for (start, size), out in zip(starts, outs):
                    start += i * rows
                    out[i, :, at] += values[start : start + size, s * BLK : (s + 1) * BLK]
        return carry

    lax.fori_loop(0, NB, step, 0)


def call(kernel, outs, scratch, mix_count, extra, *operands):
    specs = [
        pl.BlockSpec(memory_space=pltpu.SMEM if o.dtype == jnp.int32 else pltpu.VMEM)
        for o in operands
    ]
    moved = sum(o.size * o.dtype.itemsize for o in operands) + sum(4 * math.prod(o) for o in outs)
    return pl.pallas_call(
        kernel,
        out_shape=[jax.ShapeDtypeStruct(o, jnp.float32) for o in outs],
        in_specs=specs,
        out_specs=[pl.BlockSpec(memory_space=pltpu.VMEM)] * len(outs),
        scratch_shapes=scratch,
        compiler_params=pltpu.CompilerParams(vmem_limit_bytes=60 * 1024 * 1024),
        cost_estimate=pl.CostEstimate(
            flops=int(mix_count * 16 * 128 * 256 * 256 * 6) + extra,
            bytes_accessed=moved,
            transcendentals=0,
        ),
    )(*operands)


def mix_scratch(rows, lanes):
    return [
        pltpu.VMEM((XA, rows, lanes), jnp.bfloat16),
        pltpu.VMEM((XA, rows, lanes), jnp.bfloat16),
        pltpu.VMEM((XA, rows, lanes), jnp.float32),
    ]


def enter(place, indices, own, other, weights, matrices):
    angles = len(indices)
    rows = 2 * own.shape[1]
    scratch = [
        pltpu.VMEM((4 * rows, NB * BLK), jnp.bfloat16),
        pltpu.VMEM((4 * rows, NB * BLK), jnp.bfloat16),
        pltpu.VMEM((XA, 2, rows, LANES), jnp.float32),
    ] + mix_scratch(2 * rows, 2 * LANES)
    fields, *fronts = call(
        functools.partial(enter_kernel, angles),
        [(XA, 8 * angles, rows, LANES)] + [(XA, 2, rows, LANES)] * angles,
        scratch,
        rows / XB * 2 * angles,
        NB * 4 * rows * 256 * 128 * 6 * angles,
        place,
        *indices,
        own,
        other,
        *[w for pair in weights for w in pair],
        *matrices,
    )
    return fields, fronts


def middle(arrived, bases, matrices):
    return call(
        functools.partial(middle_kernel, bases),
        [(XA, 4, XB, LANES), (XA, 4, XB, LANES)],
        mix_scratch(2 * XB, 2 * LANES),
        4,
        0,
        *arrived,
        *matrices,
    )


def detector(fields, matrices):
    rows = fields.shape[2]
    return call(
        detector_kernel,
        [(XA, 2, rows, LANES)],
        mix_scratch(2 * rows, 2 * LANES),
        3,
        0,
        fields,
        *matrices,
    )[0]


def pull(back, kept, matrices, spans):
    return call(
        functools.partial(return_kernel, spans),
        [(XA, 4, span * XB // CHUNKS, LANES) for span in spans],
        mix_scratch(2 * XB, LANES),
        2,
        0,
        back,
        kept,
        *matrices,
    )


def leave(place, index, back, t0, weights, matrices, before, spans):
    rows = sum(t.shape[2] for t in t0)
    scratch = [
        pltpu.VMEM((NB, 2 * rows, LANES), jnp.bfloat16),
        pltpu.VMEM((NB, 2 * rows, LANES), jnp.bfloat16),
    ] + mix_scratch(rows, 2 * LANES)
    extra = NB * 2 * rows * 256 * 128 * 6
    outs = call(
        functools.partial(leave_kernel, spans),
        [(2, span * XB // CHUNKS // 2, NB * BLK) for span in spans for _ in range(2)],
        scratch,
        rows / XB,
        extra,
        place,
        index,
        back,
        *weights,
        *matrices,
        *t0,
        *before,
    )
    return [outs[2 * i : 2 * i + 2] for i in range(len(spans))]


def split_weights(block_weights):
    stacked = block_weights.reshape(ANGLES, NB, SLOTS * BLK, BLK)
    rounded = lax.reduce_precision(stacked, 8, 7)
    return rounded.astype(jnp.bfloat16), (stacked - rounded).astype(jnp.bfloat16)


def device(q, b, r):
    return q * XA + b * HALF + r


def exchange(values):
    return lax.all_to_all(
        values,
        ("parts", "fft"),
        split_axis=0,
        concat_axis=0,
        axis_index_groups=[[device(x, b, r) for x in range(2) for r in range(HALF)] for b in range(2)],
        tiled=True,
    )


def permute(values, steps):
    pairs = [
        (device(*here, r), device(*there, r)) for here, there in steps for r in range(HALF)
    ]
    return lax.ppermute(values, ("parts", "fft"), pairs)


BESIDE = [((q, b), (1 - q, b)) for q in range(2) for b in range(2)]
ALONG = [((q, b), (q, 1 - b)) for q in range(2) for b in range(2)]
CYCLE = [((0, 0), (0, 1)), ((1, 0), (0, 0)), ((1, 1), (1, 0)), ((0, 1), (1, 1))]
ACROSS = [((0, 1), (1, 0)), ((1, 0), (0, 1))]


def after(values, others):
    return lax.optimization_barrier((values, others))[0]


def arrive(potential, direction, q, b):
    half = XB // CHUNKS // 2

    def sides(c):
        lower, upper = (
            jnp.concatenate(
                [v[:, (2 * c + x) * half : (2 * c + x + 1) * half] for v in (potential, direction)]
            )
            for x in range(2)
        )
        return jnp.where(q == 0, lower, upper), jnp.where(q == 0, upper, lower)

    keep, give = sides(0)
    potential, direction = after((potential, direction), give)
    beside = permute(give, BESIDE)
    kept, given = zip(*[sides(c) for c in range(1, CHUNKS)])
    rest = permute(after(jnp.concatenate(given), beside), BESIDE)
    chunks = []
    along = ()
    for c in range(CHUNKS):
        if c:
            keep, beside = kept[c - 1], rest[4 * (c - 1) : 4 * c]
        own = jnp.where(q == b, keep, beside)
        give = jnp.where(q == b, beside, keep)
        along = permute(after(give, along), ALONG)
        chunks.append((own, along))
    return chunks, rest


def depart(near, far):
    return permute(near, CYCLE), permute(far, ACROSS), far


def settle(once, twice, far, q, b):
    same = jnp.where(q == b, far, once)
    rest = jnp.where(q == b, once, twice)
    return jnp.where(q == 0, same, rest), jnp.where(q == 0, rest, same)


def blocked_body(potential, direction, block_index, block_weights):
    q = lax.axis_index("parts")
    b = lax.axis_index("fft") // HALF
    place = jnp.stack([b, q]).astype(jnp.int32)
    chunks, beside = arrive(potential, direction, q, b)
    whi, wlo = split_weights(block_weights)
    by_column = column_constants()
    column = tuple(jnp.asarray(v) for v in split_constant(by_column))
    row = tuple(jnp.asarray(v) for v in split_constant(by_column.transpose(0, 2, 1)))
    weights = [(whi[a], wlo[a]) for a in range(ANGLES)]
    angles = range(ANGLES)
    arrived = [[] for _ in angles]
    bases = [[] for _ in angles]
    ahead = [[] for _ in angles]
    for c, (own, along) in enumerate(chunks):
        own = after(own, beside)
        for part in (angles,) if c + 1 < CHUNKS else [[a] for a in angles]:
            fields, fronts = enter(
                place, [block_index[a] for a in part], own, along, [weights[a] for a in part], row
            )
            fields = exchange(fields)
            for i, a in enumerate(part):
                arrived[a].append(fields)
                bases[a].append(8 * i)
                ahead[a].append(fronts[i])
    carried = []
    for a in angles:
        out, kept = middle(arrived[a], tuple(bases[a]), column)
        carried.append((exchange(out), kept))
    backs = [exchange(detector(out, row)) for out, _ in carried]
    most, half = CHUNKS // 2, XB // CHUNKS // 2
    rest = (CHUNKS // 4, CHUNKS // 4)
    spans = (most,) + rest

    def home(a, back, first, before, spans):
        t0 = ahead[a][first : first + sum(spans)]
        return leave(place, block_index[a], back, t0, weights[a], row, before, spans)

    early = pull(backs[0], carried[0][1], column, (most, sum(rest)))
    late = pull(backs[1], carried[1][1], column, spans)
    back = exchange(early[0])
    next_back = exchange(late[0])
    (start,) = home(0, back, 0, (), (most,))
    back = exchange(after(early[1], start))
    totals = home(1, next_back, 0, start, (most,))
    next_back = exchange(after(late[1], totals))
    starts = home(0, back, most, (), rest)
    back = exchange(after(late[2], starts))
    totals += home(1, next_back, most, starts[0], rest[:1])
    totals += home(1, back, most + rest[0], starts[1], rest[1:])
    pieces = []
    leaving = [depart(*total) for total in totals]
    total = totals[-1]
    for span, moved in zip(spans, after(leaving, total)):
        lower, upper = settle(*moved, q, b)
        for c in range(span):
            pieces += [v[:, c * half : (c + 1) * half] for v in (lower, upper)]
    return jnp.concatenate(pieces, axis=1)


def transform_table(count_in, count_out, length, orient):
    first = jnp.arange(count_in, dtype=jnp.int32)[:, None]
    second = jnp.arange(count_out, dtype=jnp.int32)[None, :]
    phases = orient * 2.0 * math.pi / length * (first * second % length).astype(jnp.float32)
    cosine = jnp.cos(phases)
    sine_part = jnp.sin(phases)
    return jnp.stack([jnp.stack([cosine, sine_part]), jnp.stack([-sine_part, cosine])])


def twiddle_pair(count_a, count_b, length, orient):
    first = jnp.arange(count_a, dtype=jnp.int32)[:, None]
    second = jnp.arange(count_b, dtype=jnp.int32)[None, :]
    phases = orient * 2.0 * math.pi / length * (first * second % length).astype(jnp.float32)
    return (jnp.cos(phases), jnp.sin(phases))


def spread_turn(peer_count, row_count, slot_count, orient):
    turn_re, turn_im = twiddle_pair(peer_count, row_count, NX, orient)
    shape_three = (row_count, peer_count, slot_count)
    wide_re = jnp.broadcast_to(turn_re.T[:, :, None], shape_three).reshape(
        row_count, peer_count * slot_count
    )
    wide_im = jnp.broadcast_to(turn_im.T[:, :, None], shape_three).reshape(
        row_count, peer_count * slot_count
    )
    return (wide_re, wide_im)


def complex_times(values, real_part, imag_part):
    first = values[:, 0]
    second = values[:, 1]
    return jnp.stack(
        [first * real_part - second * imag_part, first * imag_part + second * real_part], axis=1
    )


def one_hot(index_rows, block_count):
    return (index_rows[..., None] == jnp.arange(block_count, dtype=jnp.int32)).astype(jnp.float32)


def rotate(values, selector, matrices):
    height = values.shape[1]
    blocked = values.reshape(2, height, NB, BLK)
    picked = jnp.einsum("cyni,bsn->cybsi", blocked, selector, precision=PRECISE)
    rotated = jnp.einsum("cybsi,bsio->cybo", picked, matrices, precision=PRECISE)
    return rotated.reshape(2, height, SL, NX)


def rotate_back(values, selector, matrices):
    height = values.shape[1]
    blocked = values.reshape(2, height, NB, BLK)
    spread_out = jnp.einsum("cybo,bsio->cybsi", blocked, matrices, precision=PRECISE)
    summed = jnp.einsum("cybsi,bsn->cyni", spread_out, selector, precision=PRECISE)
    return summed.reshape(2, height, SL * NX)


def fresnel(peer_count, row_count, slot_count, orient):
    position_high = jnp.arange(row_count, dtype=jnp.int32)[:, None]
    position_low = jnp.arange(peer_count, dtype=jnp.int32)[None, :]
    freq_y = position_low + peer_count * position_high
    freq_y = jnp.where(freq_y < NX // 2, freq_y, freq_y - NX)
    position = lax.axis_index("fft") * slot_count + jnp.arange(slot_count, dtype=jnp.int32)
    freq_x = position // XB + XA * (position % XB)
    freq_x = jnp.where(freq_x < NX // 2, freq_x, freq_x - NX)
    squares = ((freq_y * freq_y)[:, :, None] + (freq_x * freq_x)[None, None, :]) % (2 * NX)
    phases = orient * -math.pi / NX * squares.astype(jnp.float32)
    scaling = 1.0 / (NX * NX)
    phases = phases.reshape(row_count, peer_count * slot_count)
    return (jnp.cos(phases) * scaling, jnp.sin(phases) * scaling)


def propagate(fields, kernel, peer_count, row_count, slot_count):
    field_count = fields.shape[0]
    groups = XB // slot_count
    shaped = fields.reshape(field_count, 2, row_count, XA, XB)
    partial_x = jnp.einsum(
        "fcrab,cdak->fdrkb", shaped, transform_table(XA, XA, XA, -1.0), precision=PRECISE
    )
    twist_re, twist_im = twiddle_pair(XA, XB, NX, -1.0)
    partial_x = complex_times(partial_x, twist_re, twist_im)
    partial_x = jnp.einsum(
        "fcrkb,cdbt->fdrkt", partial_x, transform_table(XB, XB, XB, -1.0), precision=PRECISE
    )
    partial_x = partial_x.reshape(field_count, 2, row_count, XA, groups, slot_count)
    outgoing = partial_x.transpose(0, 1, 3, 4, 2, 5).reshape(
        field_count, 2, peer_count, row_count * slot_count
    )
    forward_re, forward_im = spread_turn(peer_count, row_count, slot_count, -1.0)
    inverse_re, inverse_im = spread_turn(peer_count, row_count, slot_count, 1.0)
    wide = peer_count * slot_count
    incoming = lax.all_to_all(outgoing, "fft", split_axis=2, concat_axis=2, tiled=True)
    item_count = incoming.shape[0]
    lattice = incoming.reshape(item_count, 2, peer_count, row_count, slot_count)
    lattice = jnp.einsum(
        "fcprs,cdpk->fdrks",
        lattice,
        transform_table(peer_count, peer_count, peer_count, -1.0),
        precision=PRECISE,
    )
    lattice = lattice.reshape(item_count, 2, row_count, wide)
    lattice = complex_times(lattice, forward_re, forward_im)
    lattice = jnp.einsum(
        "fcrq,cdrm->fdmq",
        lattice,
        transform_table(row_count, row_count, row_count, -1.0),
        precision=PRECISE,
    )
    lattice = complex_times(lattice, kernel[0], kernel[1])
    lattice = jnp.einsum(
        "fcmq,cdmr->fdrq",
        lattice,
        transform_table(row_count, row_count, row_count, 1.0),
        precision=PRECISE,
    )
    lattice = complex_times(lattice, inverse_re, inverse_im)
    lattice = lattice.reshape(item_count, 2, row_count, peer_count, slot_count)
    lattice = jnp.einsum(
        "fcrks,cdkp->fdprs",
        lattice,
        transform_table(peer_count, peer_count, peer_count, 1.0),
        precision=PRECISE,
    )
    returning = lax.all_to_all(
        lattice.reshape(item_count, 2, peer_count, row_count * slot_count),
        "fft",
        split_axis=2,
        concat_axis=2,
        tiled=True,
    )
    restored = returning.reshape(item_count, 2, XA, groups, row_count, slot_count)
    matrix_back = transform_table(XB, XB, XB, 1.0).reshape(2, 2, groups, slot_count, XB)
    restored = jnp.einsum("fckjrs,cdjsb->fdrkb", restored, matrix_back, precision=PRECISE)
    back_re, back_im = twiddle_pair(XA, XB, NX, 1.0)
    restored = complex_times(restored, back_re, back_im)
    restored = jnp.einsum(
        "fcrkb,cdkn->fdrnb", restored, transform_table(XA, XA, XA, 1.0), precision=PRECISE
    )
    return restored.reshape(item_count, 2, row_count, NX)


def general_body(potential, direction, block_index, block_weights):
    row_count = potential.shape[1]
    peer_count = lax.axis_size("fft")
    slot_count = NX // peer_count
    ahead = fresnel(peer_count, row_count, slot_count, 1.0)
    behind = fresnel(peer_count, row_count, slot_count, -1.0)
    accumulated = jnp.zeros(potential.shape, jnp.float32)
    for angle_index in range(ANGLES):
        selector = one_hot(block_index[angle_index], NB)
        matrices = block_weights[angle_index]
        rotated = rotate(potential, selector, matrices)
        tangent = rotate(direction, selector, matrices)
        damping = jnp.exp(-rotated[1])
        trans_re = damping * jnp.cos(rotated[0])
        trans_im = damping * jnp.sin(rotated[0])
        wave_re = jnp.ones((row_count, NX), jnp.float32)
        wave_im = jnp.zeros((row_count, NX), jnp.float32)
        dwave_re = jnp.zeros((row_count, NX), jnp.float32)
        dwave_im = jnp.zeros((row_count, NX), jnp.float32)
        stored = []
        for slice_index in range(SL):
            t_re = trans_re[:, slice_index]
            t_im = trans_im[:, slice_index]
            d_re = tangent[0][:, slice_index]
            d_im = tangent[1][:, slice_index]
            phi_re = t_re * wave_re - t_im * wave_im
            phi_im = t_re * wave_im + t_im * wave_re
            dphi_re = -(d_re * phi_im + d_im * phi_re) + t_re * dwave_re - t_im * dwave_im
            dphi_im = d_re * phi_re - d_im * phi_im + t_re * dwave_im + t_im * dwave_re
            stored.append((phi_re, phi_im))
            packed = jnp.stack([jnp.stack([phi_re, phi_im]), jnp.stack([dphi_re, dphi_im])])
            propagated = propagate(packed, ahead, peer_count, row_count, slot_count)
            wave_re = propagated[0, 0]
            wave_im = propagated[0, 1]
            dwave_re = propagated[1, 0]
            dwave_im = propagated[1, 1]
        change = 2.0 * (wave_re * dwave_re + wave_im * dwave_im)
        back_re = 2.0 * change * wave_re
        back_im = 2.0 * change * wave_im
        grad_re = [None] * SL
        grad_im = [None] * SL
        for slice_index in reversed(range(SL)):
            pulled = propagate(
                jnp.stack([back_re, back_im])[None], behind, peer_count, row_count, slot_count
            )
            pb_re = pulled[0, 0]
            pb_im = pulled[0, 1]
            phi_re, phi_im = stored[slice_index]
            grad_re[slice_index] = phi_re * pb_im - phi_im * pb_re
            grad_im[slice_index] = -(phi_re * pb_re + phi_im * pb_im)
            t_re = trans_re[:, slice_index]
            t_im = trans_im[:, slice_index]
            back_re = t_re * pb_re + t_im * pb_im
            back_im = t_re * pb_im - t_im * pb_re
        gradient = jnp.stack([jnp.stack(grad_re, axis=1), jnp.stack(grad_im, axis=1)])
        accumulated = accumulated + rotate_back(gradient, selector, matrices)
    return accumulated


def body(potential, direction, block_index, block_weights):
    if lax.axis_size("parts") == 2 and lax.axis_size("fft") == XA:
        return blocked_body(potential, direction, block_index, block_weights)
    return general_body(potential, direction, block_index, block_weights)


def solution(mesh):
    return jax.shard_map(
        body,
        mesh=mesh,
        in_specs=(P("parts", "fft", None), P("parts", "fft", None), P(), P()),
        out_specs=P("parts", "fft", None),
        check_vma=False,
    )
```

```python
import functools
import math

import jax
import jax.numpy as jnp
import numpy as np
from jax import lax
from jax.experimental import pallas as pl
from jax.experimental.pallas import tpu as pltpu
from jax.sharding import PartitionSpec as P

XA = 16
XB = 128
NX = 2048
SL = 2
ANGLES = 2
BLK = 128
NB = 32
SLOTS = 2
STRIP = 16
LANES = 128
CHUNKS = 4
HALF = XA // 2


PRECISE = lax.Precision.HIGHEST


def bin_matrices():
    wavenumber = np.arange(NX)
    signed = np.where(wavenumber < NX // 2, wavenumber, wavenumber - NX)
    factor = np.exp(-1j * np.pi / NX * ((signed * signed) % (2 * NX)))
    line = np.fft.ifft(factor)
    block = np.arange(XA)
    inner = np.arange(XB)
    shifts = (XB * block[:, None, None] + inner[None, :, None] - inner[None, None, :]) % NX
    phases = np.exp(-2j * np.pi / XA * ((block[:, None] * block[None, :]) % XA))
    return np.einsum("kd,dij->kij", phases, line[shifts]) / XA


def split_constant(values):
    values = values.astype(np.float32)
    high = values.astype(jnp.bfloat16)
    low = (values - high.astype(np.float32)).astype(jnp.bfloat16)
    return high, low


def column_constants():
    bins = bin_matrices()
    top = np.concatenate([bins.real, -bins.imag], axis=2)
    bottom = np.concatenate([bins.imag, bins.real], axis=2)
    return np.concatenate([top, bottom], axis=1)


def fourth(values, orient):
    (ar, ai), (br, bi), (cr, ci), (dr, di) = values
    sr, si, er, ei = ar + cr, ai + ci, ar - cr, ai - ci
    tr, ti, fr, fi = br + dr, bi + di, br - dr, bi - di
    minus, plus = (er + fi, ei - fr), (er - fi, ei + fr)
    one, three = (minus, plus) if orient < 0 else (plus, minus)
    return [(sr + tr, si + ti), one, (sr - tr, si - ti), three]


def turned(value, step, orient):
    re, im = value
    if step == 0:
        return value
    if step == 4:
        return (im, -re) if orient < 0 else (-im, re)
    cosine = math.cos(2.0 * math.pi * step / XA)
    sine = orient * math.sin(2.0 * math.pi * step / XA)
    if step == 2:
        root = cosine
        return ((re - im) * root, (re + im) * root) if orient > 0 else ((re + im) * root, (im - re) * root)
    return (re * cosine - im * sine, re * sine + im * cosine)


def sixteenth(values, orient):
    inner = [fourth([values[4 * a + b] for a in range(4)], orient) for b in range(4)]
    out = [None] * XA
    for c in range(4):
        row = fourth([turned(inner[b][c], b * c, orient) for b in range(4)], orient)
        for d in range(4):
            out[c + 4 * d] = row[d]
    return out


def halves(value):
    high = value.astype(jnp.bfloat16)
    return high, (value - high.astype(jnp.float32)).astype(jnp.bfloat16)


def dot32(a, b):
    return jnp.dot(a, b, preferred_element_type=jnp.float32)


def times(a, b):
    return (a[0] * b[0] - a[1] * b[1], a[0] * b[1] + a[1] * b[0])


def sincos(x):
    turns = jnp.floor(x * (2.0 / math.pi) + 0.5)
    rest = ((x - turns * 1.5703125) - turns * 4.837512969970703125e-4) - turns * 7.54978995489188216e-8
    square = rest * rest
    sine = rest + rest * square * (
        -1.6666654611e-1 + square * (8.3321608736e-3 + square * -1.9515295891e-4)
    )
    cosine = (1.0 - 0.5 * square) + square * square * (
        4.166664568298827e-2 + square * (-1.388731625493765e-3 + square * 2.443315711809948e-5)
    )
    quadrant = turns.astype(jnp.int32)
    odd = (quadrant & 1) == 1
    first = jnp.where(odd, cosine, sine)
    second = jnp.where(odd, sine, cosine)
    first = jnp.where((quadrant & 2) == 2, -first, first)
    second = jnp.where(((quadrant + 1) & 2) == 2, -second, second)
    return first, second


def strips(count, step):
    def run(i, carry):
        step(pl.multiple_of(i * STRIP, STRIP))
        return carry

    lax.fori_loop(0, count // STRIP, run, 0)


def rows_out(xhi, xlo, first_row, values):
    for k, (re, im) in enumerate(sixteenth(values, -1.0)):
        for part, value in enumerate((re, im)):
            high, low = halves(value)
            at = (k, pl.ds(first_row, STRIP), pl.ds(part * LANES, LANES))
            xhi[at] = high
            xlo[at] = low


def rows_in(y, first_row):
    values = [
        tuple(y[k, pl.ds(first_row, STRIP), pl.ds(part * LANES, LANES)] for part in range(2))
        for k in range(XA)
    ]
    return sixteenth(values, 1.0)


def rows_mix(xhi, xlo, mhi, mlo, y):
    def step(k, carry):
        high, low = xhi[k], xlo[k]
        y[k] = dot32(high, mhi[k]) + (dot32(low, mhi[k]) + dot32(high, mlo[k]))
        return carry

    lax.fori_loop(0, XA, step, 0)


def columns_out(xhi, xlo, field, row, values):
    for k, (re, im) in enumerate(sixteenth(values, -1.0)):
        for part, value in enumerate((re, im)):
            high, low = halves(value)
            at = (k, pl.ds(part * XB + row, STRIP), pl.ds(field * LANES, LANES))
            xhi[at] = high
            xlo[at] = low


def columns_in(y, field, row):
    values = [
        tuple(
            y[k, pl.ds(part * XB + row, STRIP), pl.ds(field * LANES, LANES)] for part in range(2)
        )
        for k in range(XA)
    ]
    return sixteenth(values, 1.0)


def columns_mix(xhi, xlo, mhi, mlo, y):
    def step(k, carry):
        high, low = xhi[k], xlo[k]
        y[k] = dot32(mhi[k], high) + (dot32(mhi[k], low) + dot32(mlo[k], high))
        return carry

    lax.fori_loop(0, XA, step, 0)


def enter_kernel(angles, place, *refs):
    indices, (own, other), refs = refs[:angles], refs[angles : angles + 2], refs[angles + 2 :]
    weights, (mhi, mlo, out), refs = refs[: 2 * angles], refs[2 * angles : 2 * angles + 3], refs[2 * angles + 3 :]
    fronts, (shi, slo, field, xhi, xlo, y) = refs[:angles], refs[angles:]
    half = own.shape[1]
    rows = 2 * half

    for number in range(4):
        for piece, side in ((own, place[0]), (other, 1 - place[0])):

            def cut(row, number=number, piece=piece, side=side):
                high, low = halves(piece[number, pl.ds(row, STRIP), :])
                first = number * rows + side * half + row
                at = pl.ds(pl.multiple_of(first, STRIP), STRIP)
                shi[at, :] = high
                slo[at, :] = low

            strips(half, cut)

    for a in range(angles):
        enter_angle(
            indices[a], weights[2 * a], weights[2 * a + 1], mhi, mlo,
            out, 8 * a, fronts[a], shi, slo, field, xhi, xlo, y,
        )


def enter_angle(index, whi, wlo, mhi, mlo, out, base, t0, shi, slo, field, xhi, xlo, y):
    rows = t0.shape[2]

    def rotated(b):
        at = [pl.ds(pl.multiple_of(index[b, s] * BLK, BLK), BLK) for s in range(SLOTS)]
        high = jnp.concatenate([shi[:, a] for a in at], axis=1)
        low = jnp.concatenate([slo[:, a] for a in at], axis=1)
        values = dot32(high, whi[b]) + (dot32(low, whi[b]) + dot32(high, wlo[b]))
        angle, loss, d_re, d_im = (values[i * rows : (i + 1) * rows] for i in range(4))
        sine, cosine = sincos(angle)
        damping = jnp.exp(-loss)
        return damping * cosine, damping * sine, d_re, d_im

    def first_slice(b, carry):
        t_re, t_im, d_re, d_im = rotated(b)
        t0[b, 0] = t_re
        t0[b, 1] = t_im
        field[b, 0] = -(d_re * t_im + d_im * t_re)
        field[b, 1] = d_re * t_re - d_im * t_im
        return carry

    lax.fori_loop(0, XA, first_slice, 0)

    def forward(row):
        at = pl.ds(row, STRIP)
        rows_out(xhi, xlo, row, [(t0[b, 0, at, :], t0[b, 1, at, :]) for b in range(XA)])
        rows_out(
            xhi,
            xlo,
            pl.multiple_of(rows + row, STRIP),
            [(field[b, 0, at, :], field[b, 1, at, :]) for b in range(XA)],
        )

    strips(rows, forward)
    rows_mix(xhi, xlo, mhi, mlo, y)

    def backward(row):
        at = pl.ds(row, STRIP)
        for number in range(2):
            values = rows_in(y, pl.multiple_of(number * rows + row, STRIP))
            for b, (re, im) in enumerate(values):
                out[b, base + 2 * number, at, :] = re
                out[b, base + 2 * number + 1, at, :] = im

    strips(rows, backward)

    def second_slice(b, carry):
        for channel, value in enumerate(rotated(XA + b)):
            out[b, base + 4 + channel] = value
        return carry

    lax.fori_loop(0, XA, second_slice, 0)


def by_pieces(spans, step):
    half = XB // CHUNKS // 2
    pieces = [(piece, c) for piece, span in enumerate(spans) for c in range(span)]
    for chunk, (piece, c) in enumerate(pieces):
        for x in range(2):

            def inner(row, chunk=chunk, piece=piece, c=c, x=x):
                places = []
                for p in range(XA):
                    first = (2 * c + p // HALF) * half
                    at = pl.ds(pl.multiple_of(first + row, STRIP), STRIP)
                    places.append((piece, x * HALF + p % HALF, at))
                step(pl.multiple_of((2 * chunk + x) * half + row, STRIP), places)

            strips(half, inner)


def middle_kernel(bases, *refs):
    chunks = len(bases)
    arrived = refs[:chunks]
    mhi, mlo, out, kept, xhi, xlo, y = refs[chunks:]

    def forward(row, places):
        for number in range(2):
            values = [
                tuple(arrived[c][g, bases[c] + 2 * number + i, at, :] for i in range(2)) for c, g, at in places
            ]
            columns_out(xhi, xlo, number, row, values)

    by_pieces((1,) * chunks, forward)
    columns_mix(xhi, xlo, mhi, mlo, y)

    def turn(row, places):
        local = pl.ds(row, STRIP)
        wave = columns_in(y, 0, row)
        product = []
        for p, (c, g, at) in enumerate(places):
            t = tuple(arrived[c][g, bases[c] + i, at, :] for i in (4, 5))
            value = times(t, wave[p])
            for i, part in enumerate(value + t):
                kept[p, i, local, :] = part
            product.append(value)
        columns_out(xhi, xlo, 0, row, product)
        dwave = columns_in(y, 1, row)
        change = []
        for p, (c, g, at) in enumerate(places):
            t_re, t_im, d_re, d_im = (arrived[c][g, bases[c] + 4 + i, at, :] for i in range(4))
            p_re, p_im = kept[p, 0, local, :], kept[p, 1, local, :]
            re, im = times((t_re, t_im), dwave[p])
            change.append((re - (d_re * p_im + d_im * p_re), im + (d_re * p_re - d_im * p_im)))
        columns_out(xhi, xlo, 1, row, change)

    by_pieces((1,) * chunks, turn)
    columns_mix(xhi, xlo, mhi, mlo, y)

    def backward(row, places):
        for number in range(2):
            for (_, g, at), (re, im) in zip(places, columns_in(y, number, row)):
                out[g, 2 * number, at, :] = re
                out[g, 2 * number + 1, at, :] = im

    by_pieces((CHUNKS,), backward)


def detector_kernel(fields, mhi, mlo, out, xhi, xlo, y):
    rows = fields.shape[2]

    def forward(row):
        at = pl.ds(row, STRIP)
        for number in range(2):
            rows_out(
                xhi,
                xlo,
                pl.multiple_of(number * rows + row, STRIP),
                [tuple(fields[b, 2 * number + i, at, :] for i in range(2)) for b in range(XA)],
            )

    strips(rows, forward)
    rows_mix(xhi, xlo, mhi, mlo, y)

    def turn(row):
        wave = rows_in(y, row)
        dwave = rows_in(y, pl.multiple_of(rows + row, STRIP))
        back = []
        for (re, im), (d_re, d_im) in zip(wave, dwave):
            change = 4.0 * (re * d_re + im * d_im)
            back.append((change * re, -(change * im)))
        rows_out(xhi, xlo, row, back)

    strips(rows, turn)

    def step(k, carry):
        high, low = xhi[k, :rows, :], xlo[k, :rows, :]
        y[k, :rows, :] = dot32(high, mhi[k]) + (dot32(low, mhi[k]) + dot32(high, mlo[k]))
        return carry

    lax.fori_loop(0, XA, step, 0)

    def backward(row):
        at = pl.ds(row, STRIP)
        for b, (re, im) in enumerate(rows_in(y, row)):
            out[b, 0, at, :] = re
            out[b, 1, at, :] = im

    strips(rows, backward)


def return_kernel(spans, back, kept, mhi, mlo, *refs):
    out, (xhi, xlo, y) = refs[: len(spans)], refs[len(spans) :]

    def forward(row, places):
        values = [(back[g, 0, at, :], back[g, 1, at, :]) for _, g, at in places]
        columns_out(xhi, xlo, 0, row, values)

    by_pieces((CHUNKS,), forward)
    columns_mix(xhi, xlo, mhi, mlo, y)

    def turn(row, places):
        local = pl.ds(row, STRIP)
        pulled = columns_in(y, 0, row)
        following = []
        for p, (c, g, at) in enumerate(places):
            re, im = times((kept[p, 0, local, :], kept[p, 1, local, :]), pulled[p])
            out[c][g, 0, at, :] = -im
            out[c][g, 1, at, :] = -re
            following.append(times((kept[p, 2, local, :], kept[p, 3, local, :]), pulled[p]))
        columns_out(xhi, xlo, 0, row, following)

    by_pieces(spans, turn)
    columns_mix(xhi, xlo, mhi, mlo, y)

    def backward(row, places):
        for (c, g, at), (re, im) in zip(places, columns_in(y, 0, row)):
            out[c][g, 2, at, :] = re
            out[c][g, 3, at, :] = im

    by_pieces(spans, backward)


def leave_kernel(spans, place, index, back, whi, wlo, mhi, mlo, *refs):
    chunks, count = sum(spans), 2 * len(spans)
    t0, refs = refs[:chunks], refs[chunks:]
    before, outs, (shi, slo, xhi, xlo, y) = refs[: -count - 5], refs[-count - 5 : -5], refs[-5:]
    chunk = t0[0].shape[2]
    half = chunk // 2
    rows = chunks * chunk
    starts = []

    def pieces_of(step):
        starts.clear()
        done = 0
        for span in spans:
            for end, side in enumerate((1 - place[1], place[1])):
                base = (2 * done + end * span) * half
                starts.append((base, span * half))
                for c in range(span):

                    def inner(row, side=side, c=c, done=done, base=base):
                        within = pl.multiple_of(side * half + row, STRIP)
                        source = pl.multiple_of((done + c) * chunk + side * half + row, STRIP)
                        target = pl.multiple_of(base + c * half + row, STRIP)
                        step(done + c, pl.ds(within, STRIP), pl.ds(source, STRIP), target)

                    strips(half, inner)
            done += span

    def store(b, i, target, value):
        high, low = halves(value)
        at = pl.ds(pl.multiple_of(i * rows + target, STRIP), STRIP)
        shi[b, at, :] = high
        slo[b, at, :] = low

    def forward(c, within, at, target):
        rows_out(xhi, xlo, target, [(back[b, 2, at, :], back[b, 3, at, :]) for b in range(XA)])
        for b in range(XA):
            for i in range(2):
                store(XA + b, i, target, back[b, i, at, :])

    pieces_of(forward)
    rows_mix(xhi, xlo, mhi, mlo, y)

    def turn(c, within, at, target):
        for b, value in enumerate(rows_in(y, target)):
            re, im = times((t0[c][b, 0, within, :], t0[c][b, 1, within, :]), value)
            store(b, 0, target, -im)
            store(b, 1, target, -re)

    pieces_of(turn)

    for out, old in zip(outs, before or [None] * count):
        out[...] = jnp.zeros(out.shape, jnp.float32) if old is None else old[...]

    def across(a, b):
        return lax.dot_general(
            a, b, (((1,), (1,)), ((), ())), preferred_element_type=jnp.float32
        )

    def step(b, carry):
        high, low = shi[b], slo[b]
        values = across(high, whi[b]) + (across(low, whi[b]) + across(high, wlo[b]))
        for s in range(SLOTS):
            at = pl.ds(pl.multiple_of(index[b, s] * BLK, BLK), BLK)
            for i in range(2):
                for (start, size), out in zip(starts, outs):
                    start += i * rows
                    out[i, :, at] += values[start : start + size, s * BLK : (s + 1) * BLK]
        return carry

    lax.fori_loop(0, NB, step, 0)


def call(kernel, outs, scratch, mix_count, extra, *operands):
    specs = [
        pl.BlockSpec(memory_space=pltpu.SMEM if o.dtype == jnp.int32 else pltpu.VMEM)
        for o in operands
    ]
    moved = sum(o.size * o.dtype.itemsize for o in operands) + sum(4 * math.prod(o) for o in outs)
    return pl.pallas_call(
        kernel,
        out_shape=[jax.ShapeDtypeStruct(o, jnp.float32) for o in outs],
        in_specs=specs,
        out_specs=[pl.BlockSpec(memory_space=pltpu.VMEM)] * len(outs),
        scratch_shapes=scratch,
        compiler_params=pltpu.CompilerParams(vmem_limit_bytes=60 * 1024 * 1024),
        cost_estimate=pl.CostEstimate(
            flops=int(mix_count * 16 * 128 * 256 * 256 * 6) + extra,
            bytes_accessed=moved,
            transcendentals=0,
        ),
    )(*operands)


def mix_scratch(rows, lanes):
    return [
        pltpu.VMEM((XA, rows, lanes), jnp.bfloat16),
        pltpu.VMEM((XA, rows, lanes), jnp.bfloat16),
        pltpu.VMEM((XA, rows, lanes), jnp.float32),
    ]


def enter(place, indices, own, other, weights, matrices):
    angles = len(indices)
    rows = 2 * own.shape[1]
    scratch = [
        pltpu.VMEM((4 * rows, NB * BLK), jnp.bfloat16),
        pltpu.VMEM((4 * rows, NB * BLK), jnp.bfloat16),
        pltpu.VMEM((XA, 2, rows, LANES), jnp.float32),
    ] + mix_scratch(2 * rows, 2 * LANES)
    fields, *fronts = call(
        functools.partial(enter_kernel, angles),
        [(XA, 8 * angles, rows, LANES)] + [(XA, 2, rows, LANES)] * angles,
        scratch,
        rows / XB * 2 * angles,
        NB * 4 * rows * 256 * 128 * 6 * angles,
        place,
        *indices,
        own,
        other,
        *[w for pair in weights for w in pair],
        *matrices,
    )
    return fields, fronts


def middle(arrived, bases, matrices):
    return call(
        functools.partial(middle_kernel, bases),
        [(XA, 4, XB, LANES), (XA, 4, XB, LANES)],
        mix_scratch(2 * XB, 2 * LANES),
        4,
        0,
        *arrived,
        *matrices,
    )


def detector(fields, matrices):
    rows = fields.shape[2]
    return call(
        detector_kernel,
        [(XA, 2, rows, LANES)],
        mix_scratch(2 * rows, 2 * LANES),
        3,
        0,
        fields,
        *matrices,
    )[0]


def pull(back, kept, matrices, spans):
    return call(
        functools.partial(return_kernel, spans),
        [(XA, 4, span * XB // CHUNKS, LANES) for span in spans],
        mix_scratch(2 * XB, LANES),
        2,
        0,
        back,
        kept,
        *matrices,
    )


def leave(place, index, back, t0, weights, matrices, before, spans):
    rows = sum(t.shape[2] for t in t0)
    scratch = [
        pltpu.VMEM((NB, 2 * rows, LANES), jnp.bfloat16),
        pltpu.VMEM((NB, 2 * rows, LANES), jnp.bfloat16),
    ] + mix_scratch(rows, 2 * LANES)
    extra = NB * 2 * rows * 256 * 128 * 6
    outs = call(
        functools.partial(leave_kernel, spans),
        [(2, span * XB // CHUNKS // 2, NB * BLK) for span in spans for _ in range(2)],
        scratch,
        rows / XB,
        extra,
        place,
        index,
        back,
        *weights,
        *matrices,
        *t0,
        *before,
    )
    return [outs[2 * i : 2 * i + 2] for i in range(len(spans))]


def split_weights(block_weights):
    stacked = block_weights.reshape(ANGLES, NB, SLOTS * BLK, BLK)
    rounded = lax.reduce_precision(stacked, 8, 7)
    return rounded.astype(jnp.bfloat16), (stacked - rounded).astype(jnp.bfloat16)


def device(q, b, r):
    return q * XA + b * HALF + r


def exchange(values):
    return lax.all_to_all(
        values,
        ("parts", "fft"),
        split_axis=0,
        concat_axis=0,
        axis_index_groups=[[device(x, b, r) for x in range(2) for r in range(HALF)] for b in range(2)],
        tiled=True,
    )


def permute(values, steps):
    pairs = [
        (device(*here, r), device(*there, r)) for here, there in steps for r in range(HALF)
    ]
    return lax.ppermute(values, ("parts", "fft"), pairs)


BESIDE = [((q, b), (1 - q, b)) for q in range(2) for b in range(2)]
ALONG = [((q, b), (q, 1 - b)) for q in range(2) for b in range(2)]
CYCLE = [((0, 0), (0, 1)), ((1, 0), (0, 0)), ((1, 1), (1, 0)), ((0, 1), (1, 1))]
ACROSS = [((0, 1), (1, 0)), ((1, 0), (0, 1))]


def after(values, others):
    return lax.optimization_barrier((values, others))[0]


def arrive(potential, direction, q, b):
    half = XB // CHUNKS // 2

    def sides(c):
        lower, upper = (
            jnp.concatenate(
                [v[:, (2 * c + x) * half : (2 * c + x + 1) * half] for v in (potential, direction)]
            )
            for x in range(2)
        )
        return jnp.where(q == 0, lower, upper), jnp.where(q == 0, upper, lower)

    keep, give = sides(0)
    potential, direction = after((potential, direction), give)
    beside = permute(give, BESIDE)
    kept, given = zip(*[sides(c) for c in range(1, CHUNKS)])
    rest = permute(after(jnp.concatenate(given), beside), BESIDE)
    chunks = []
    for c in range(CHUNKS):
        if c:
            keep, beside = kept[c - 1], rest[4 * (c - 1) : 4 * c]
        chunks.append((jnp.where(q == b, keep, beside), jnp.where(q == b, beside, keep)))
    return chunks, rest


def depart(near, far):
    return permute(near, CYCLE), permute(far, ACROSS), far


def settle(once, twice, far, q, b):
    same = jnp.where(q == b, far, once)
    rest = jnp.where(q == b, once, twice)
    return jnp.where(q == 0, same, rest), jnp.where(q == 0, rest, same)


def blocked_body(potential, direction, block_index, block_weights):
    q = lax.axis_index("parts")
    b = lax.axis_index("fft") // HALF
    place = jnp.stack([b, q]).astype(jnp.int32)
    chunks, beside = arrive(potential, direction, q, b)
    whi, wlo = split_weights(block_weights)
    by_column = column_constants()
    column = tuple(jnp.asarray(v) for v in split_constant(by_column))
    row = tuple(jnp.asarray(v) for v in split_constant(by_column.transpose(0, 2, 1)))
    weights = [(whi[a], wlo[a]) for a in range(ANGLES)]
    angles = range(ANGLES)
    arrived = [[] for _ in angles]
    bases = [[] for _ in angles]
    ahead = [[] for _ in angles]
    fields = ()
    for c, (own, give) in enumerate(chunks):
        along = permute(after(give, fields), ALONG)
        own = after(own, beside)
        for part in (angles,) if c + 1 < CHUNKS else [[a] for a in angles]:
            fields, fronts = enter(
                place, [block_index[a] for a in part], own, along, [weights[a] for a in part], row
            )
            moved = exchange(fields)
            for i, a in enumerate(part):
                arrived[a].append(moved)
                bases[a].append(8 * i)
                ahead[a].append(fronts[i])
    carried = []
    for a in angles:
        out, kept = middle(arrived[a], tuple(bases[a]), column)
        carried.append((exchange(out), kept))
    backs = [exchange(detector(out, row)) for out, _ in carried]
    most, half = CHUNKS // 2, XB // CHUNKS // 2
    rest = (CHUNKS // 4, CHUNKS // 4)
    spans = (most,) + rest

    def home(a, back, first, before, spans):
        t0 = ahead[a][first : first + sum(spans)]
        return leave(place, block_index[a], back, t0, weights[a], row, before, spans)

    early = pull(backs[0], carried[0][1], column, (most, sum(rest)))
    late = pull(backs[1], carried[1][1], column, spans)
    back = exchange(early[0])
    next_back = exchange(late[0])
    (start,) = home(0, back, 0, (), (most,))
    back = exchange(after(early[1], start))
    totals = home(1, next_back, 0, start, (most,))
    next_back = exchange(after(late[1], totals))
    starts = home(0, back, most, (), rest)
    back = exchange(after(late[2], starts))
    totals += home(1, next_back, most, starts[0], rest[:1])
    leaving = [depart(*total) for total in totals]
    back = after(back, leaving[0])
    totals += home(1, back, most + rest[0], starts[1], rest[1:])
    leaving.append(depart(*totals[-1]))
    pieces = []
    total = totals[-1]
    for span, moved in zip(spans, after(leaving, total)):
        lower, upper = settle(*moved, q, b)
        for c in range(span):
            pieces += [v[:, c * half : (c + 1) * half] for v in (lower, upper)]
    return jnp.concatenate(pieces, axis=1)


def transform_table(count_in, count_out, length, orient):
    first = jnp.arange(count_in, dtype=jnp.int32)[:, None]
    second = jnp.arange(count_out, dtype=jnp.int32)[None, :]
    phases = orient * 2.0 * math.pi / length * (first * second % length).astype(jnp.float32)
    cosine = jnp.cos(phases)
    sine_part = jnp.sin(phases)
    return jnp.stack([jnp.stack([cosine, sine_part]), jnp.stack([-sine_part, cosine])])


def twiddle_pair(count_a, count_b, length, orient):
    first = jnp.arange(count_a, dtype=jnp.int32)[:, None]
    second = jnp.arange(count_b, dtype=jnp.int32)[None, :]
    phases = orient * 2.0 * math.pi / length * (first * second % length).astype(jnp.float32)
    return (jnp.cos(phases), jnp.sin(phases))


def spread_turn(peer_count, row_count, slot_count, orient):
    turn_re, turn_im = twiddle_pair(peer_count, row_count, NX, orient)
    shape_three = (row_count, peer_count, slot_count)
    wide_re = jnp.broadcast_to(turn_re.T[:, :, None], shape_three).reshape(
        row_count, peer_count * slot_count
    )
    wide_im = jnp.broadcast_to(turn_im.T[:, :, None], shape_three).reshape(
        row_count, peer_count * slot_count
    )
    return (wide_re, wide_im)


def complex_times(values, real_part, imag_part):
    first = values[:, 0]
    second = values[:, 1]
    return jnp.stack(
        [first * real_part - second * imag_part, first * imag_part + second * real_part], axis=1
    )


def one_hot(index_rows, block_count):
    return (index_rows[..., None] == jnp.arange(block_count, dtype=jnp.int32)).astype(jnp.float32)


def rotate(values, selector, matrices):
    height = values.shape[1]
    blocked = values.reshape(2, height, NB, BLK)
    picked = jnp.einsum("cyni,bsn->cybsi", blocked, selector, precision=PRECISE)
    rotated = jnp.einsum("cybsi,bsio->cybo", picked, matrices, precision=PRECISE)
    return rotated.reshape(2, height, SL, NX)


def rotate_back(values, selector, matrices):
    height = values.shape[1]
    blocked = values.reshape(2, height, NB, BLK)
    spread_out = jnp.einsum("cybo,bsio->cybsi", blocked, matrices, precision=PRECISE)
    summed = jnp.einsum("cybsi,bsn->cyni", spread_out, selector, precision=PRECISE)
    return summed.reshape(2, height, SL * NX)


def fresnel(peer_count, row_count, slot_count, orient):
    position_high = jnp.arange(row_count, dtype=jnp.int32)[:, None]
    position_low = jnp.arange(peer_count, dtype=jnp.int32)[None, :]
    freq_y = position_low + peer_count * position_high
    freq_y = jnp.where(freq_y < NX // 2, freq_y, freq_y - NX)
    position = lax.axis_index("fft") * slot_count + jnp.arange(slot_count, dtype=jnp.int32)
    freq_x = position // XB + XA * (position % XB)
    freq_x = jnp.where(freq_x < NX // 2, freq_x, freq_x - NX)
    squares = ((freq_y * freq_y)[:, :, None] + (freq_x * freq_x)[None, None, :]) % (2 * NX)
    phases = orient * -math.pi / NX * squares.astype(jnp.float32)
    scaling = 1.0 / (NX * NX)
    phases = phases.reshape(row_count, peer_count * slot_count)
    return (jnp.cos(phases) * scaling, jnp.sin(phases) * scaling)


def propagate(fields, kernel, peer_count, row_count, slot_count):
    field_count = fields.shape[0]
    groups = XB // slot_count
    shaped = fields.reshape(field_count, 2, row_count, XA, XB)
    partial_x = jnp.einsum(
        "fcrab,cdak->fdrkb", shaped, transform_table(XA, XA, XA, -1.0), precision=PRECISE
    )
    twist_re, twist_im = twiddle_pair(XA, XB, NX, -1.0)
    partial_x = complex_times(partial_x, twist_re, twist_im)
    partial_x = jnp.einsum(
        "fcrkb,cdbt->fdrkt", partial_x, transform_table(XB, XB, XB, -1.0), precision=PRECISE
    )
    partial_x = partial_x.reshape(field_count, 2, row_count, XA, groups, slot_count)
    outgoing = partial_x.transpose(0, 1, 3, 4, 2, 5).reshape(
        field_count, 2, peer_count, row_count * slot_count
    )
    forward_re, forward_im = spread_turn(peer_count, row_count, slot_count, -1.0)
    inverse_re, inverse_im = spread_turn(peer_count, row_count, slot_count, 1.0)
    wide = peer_count * slot_count
    incoming = lax.all_to_all(outgoing, "fft", split_axis=2, concat_axis=2, tiled=True)
    item_count = incoming.shape[0]
    lattice = incoming.reshape(item_count, 2, peer_count, row_count, slot_count)
    lattice = jnp.einsum(
        "fcprs,cdpk->fdrks",
        lattice,
        transform_table(peer_count, peer_count, peer_count, -1.0),
        precision=PRECISE,
    )
    lattice = lattice.reshape(item_count, 2, row_count, wide)
    lattice = complex_times(lattice, forward_re, forward_im)
    lattice = jnp.einsum(
        "fcrq,cdrm->fdmq",
        lattice,
        transform_table(row_count, row_count, row_count, -1.0),
        precision=PRECISE,
    )
    lattice = complex_times(lattice, kernel[0], kernel[1])
    lattice = jnp.einsum(
        "fcmq,cdmr->fdrq",
        lattice,
        transform_table(row_count, row_count, row_count, 1.0),
        precision=PRECISE,
    )
    lattice = complex_times(lattice, inverse_re, inverse_im)
    lattice = lattice.reshape(item_count, 2, row_count, peer_count, slot_count)
    lattice = jnp.einsum(
        "fcrks,cdkp->fdprs",
        lattice,
        transform_table(peer_count, peer_count, peer_count, 1.0),
        precision=PRECISE,
    )
    returning = lax.all_to_all(
        lattice.reshape(item_count, 2, peer_count, row_count * slot_count),
        "fft",
        split_axis=2,
        concat_axis=2,
        tiled=True,
    )
    restored = returning.reshape(item_count, 2, XA, groups, row_count, slot_count)
    matrix_back = transform_table(XB, XB, XB, 1.0).reshape(2, 2, groups, slot_count, XB)
    restored = jnp.einsum("fckjrs,cdjsb->fdrkb", restored, matrix_back, precision=PRECISE)
    back_re, back_im = twiddle_pair(XA, XB, NX, 1.0)
    restored = complex_times(restored, back_re, back_im)
    restored = jnp.einsum(
        "fcrkb,cdkn->fdrnb", restored, transform_table(XA, XA, XA, 1.0), precision=PRECISE
    )
    return restored.reshape(item_count, 2, row_count, NX)


def general_body(potential, direction, block_index, block_weights):
    row_count = potential.shape[1]
    peer_count = lax.axis_size("fft")
    slot_count = NX // peer_count
    ahead = fresnel(peer_count, row_count, slot_count, 1.0)
    behind = fresnel(peer_count, row_count, slot_count, -1.0)
    accumulated = jnp.zeros(potential.shape, jnp.float32)
    for angle_index in range(ANGLES):
        selector = one_hot(block_index[angle_index], NB)
        matrices = block_weights[angle_index]
        rotated = rotate(potential, selector, matrices)
        tangent = rotate(direction, selector, matrices)
        damping = jnp.exp(-rotated[1])
        trans_re = damping * jnp.cos(rotated[0])
        trans_im = damping * jnp.sin(rotated[0])
        wave_re = jnp.ones((row_count, NX), jnp.float32)
        wave_im = jnp.zeros((row_count, NX), jnp.float32)
        dwave_re = jnp.zeros((row_count, NX), jnp.float32)
        dwave_im = jnp.zeros((row_count, NX), jnp.float32)
        stored = []
        for slice_index in range(SL):
            t_re = trans_re[:, slice_index]
            t_im = trans_im[:, slice_index]
            d_re = tangent[0][:, slice_index]
            d_im = tangent[1][:, slice_index]
            phi_re = t_re * wave_re - t_im * wave_im
            phi_im = t_re * wave_im + t_im * wave_re
            dphi_re = -(d_re * phi_im + d_im * phi_re) + t_re * dwave_re - t_im * dwave_im
            dphi_im = d_re * phi_re - d_im * phi_im + t_re * dwave_im + t_im * dwave_re
            stored.append((phi_re, phi_im))
            packed = jnp.stack([jnp.stack([phi_re, phi_im]), jnp.stack([dphi_re, dphi_im])])
            propagated = propagate(packed, ahead, peer_count, row_count, slot_count)
            wave_re = propagated[0, 0]
            wave_im = propagated[0, 1]
            dwave_re = propagated[1, 0]
            dwave_im = propagated[1, 1]
        change = 2.0 * (wave_re * dwave_re + wave_im * dwave_im)
        back_re = 2.0 * change * wave_re
        back_im = 2.0 * change * wave_im
        grad_re = [None] * SL
        grad_im = [None] * SL
        for slice_index in reversed(range(SL)):
            pulled = propagate(
                jnp.stack([back_re, back_im])[None], behind, peer_count, row_count, slot_count
            )
            pb_re = pulled[0, 0]
            pb_im = pulled[0, 1]
            phi_re, phi_im = stored[slice_index]
            grad_re[slice_index] = phi_re * pb_im - phi_im * pb_re
            grad_im[slice_index] = -(phi_re * pb_re + phi_im * pb_im)
            t_re = trans_re[:, slice_index]
            t_im = trans_im[:, slice_index]
            back_re = t_re * pb_re + t_im * pb_im
            back_im = t_re * pb_im - t_im * pb_re
        gradient = jnp.stack([jnp.stack(grad_re, axis=1), jnp.stack(grad_im, axis=1)])
        accumulated = accumulated + rotate_back(gradient, selector, matrices)
    return accumulated


def body(potential, direction, block_index, block_weights):
    if lax.axis_size("parts") == 2 and lax.axis_size("fft") == XA:
        return blocked_body(potential, direction, block_index, block_weights)
    return general_body(potential, direction, block_index, block_weights)


def solution(mesh):
    return jax.shard_map(
        body,
        mesh=mesh,
        in_specs=(P("parts", "fft", None), P("parts", "fft", None), P(), P()),
        out_specs=P("parts", "fft", None),
        check_vma=False,
    )
```

```python
import functools
import math

import jax
import jax.numpy as jnp
import numpy as np
from jax import lax
from jax.experimental import pallas as pl
from jax.experimental.pallas import tpu as pltpu
from jax.sharding import PartitionSpec as P

XA = 16
XB = 128
NX = 2048
SL = 2
ANGLES = 2
BLK = 128
NB = 32
SLOTS = 2
STRIP = 16
LANES = 128
CHUNKS = 4
HALF = XA // 2


PRECISE = lax.Precision.HIGHEST


def bin_matrices():
    wavenumber = np.arange(NX)
    signed = np.where(wavenumber < NX // 2, wavenumber, wavenumber - NX)
    factor = np.exp(-1j * np.pi / NX * ((signed * signed) % (2 * NX)))
    line = np.fft.ifft(factor)
    block = np.arange(XA)
    inner = np.arange(XB)
    shifts = (XB * block[:, None, None] + inner[None, :, None] - inner[None, None, :]) % NX
    phases = np.exp(-2j * np.pi / XA * ((block[:, None] * block[None, :]) % XA))
    return np.einsum("kd,dij->kij", phases, line[shifts]) / XA


def split_constant(values):
    values = values.astype(np.float32)
    high = values.astype(jnp.bfloat16)
    low = (values - high.astype(np.float32)).astype(jnp.bfloat16)
    return high, low


def column_constants():
    bins = bin_matrices()
    top = np.concatenate([bins.real, -bins.imag], axis=2)
    bottom = np.concatenate([bins.imag, bins.real], axis=2)
    return np.concatenate([top, bottom], axis=1)


def fourth(values, orient):
    (ar, ai), (br, bi), (cr, ci), (dr, di) = values
    sr, si, er, ei = ar + cr, ai + ci, ar - cr, ai - ci
    tr, ti, fr, fi = br + dr, bi + di, br - dr, bi - di
    minus, plus = (er + fi, ei - fr), (er - fi, ei + fr)
    one, three = (minus, plus) if orient < 0 else (plus, minus)
    return [(sr + tr, si + ti), one, (sr - tr, si - ti), three]


def turned(value, step, orient):
    re, im = value
    if step == 0:
        return value
    if step == 4:
        return (im, -re) if orient < 0 else (-im, re)
    cosine = math.cos(2.0 * math.pi * step / XA)
    sine = orient * math.sin(2.0 * math.pi * step / XA)
    if step == 2:
        root = cosine
        return ((re - im) * root, (re + im) * root) if orient > 0 else ((re + im) * root, (im - re) * root)
    return (re * cosine - im * sine, re * sine + im * cosine)


def sixteenth(values, orient):
    inner = [fourth([values[4 * a + b] for a in range(4)], orient) for b in range(4)]
    out = [None] * XA
    for c in range(4):
        row = fourth([turned(inner[b][c], b * c, orient) for b in range(4)], orient)
        for d in range(4):
            out[c + 4 * d] = row[d]
    return out


def halves(value):
    high = value.astype(jnp.bfloat16)
    return high, (value - high.astype(jnp.float32)).astype(jnp.bfloat16)


def dot32(a, b):
    return jnp.dot(a, b, preferred_element_type=jnp.float32)


def times(a, b):
    return (a[0] * b[0] - a[1] * b[1], a[0] * b[1] + a[1] * b[0])


def sincos(x):
    turns = jnp.floor(x * (2.0 / math.pi) + 0.5)
    rest = ((x - turns * 1.5703125) - turns * 4.837512969970703125e-4) - turns * 7.54978995489188216e-8
    square = rest * rest
    sine = rest + rest * square * (
        -1.6666654611e-1 + square * (8.3321608736e-3 + square * -1.9515295891e-4)
    )
    cosine = (1.0 - 0.5 * square) + square * square * (
        4.166664568298827e-2 + square * (-1.388731625493765e-3 + square * 2.443315711809948e-5)
    )
    quadrant = turns.astype(jnp.int32)
    odd = (quadrant & 1) == 1
    first = jnp.where(odd, cosine, sine)
    second = jnp.where(odd, sine, cosine)
    first = jnp.where((quadrant & 2) == 2, -first, first)
    second = jnp.where(((quadrant + 1) & 2) == 2, -second, second)
    return first, second


def strips(count, step):
    def run(i, carry):
        step(pl.multiple_of(i * STRIP, STRIP))
        return carry

    lax.fori_loop(0, count // STRIP, run, 0)


def rows_out(xhi, xlo, first_row, values):
    for k, (re, im) in enumerate(sixteenth(values, -1.0)):
        for part, value in enumerate((re, im)):
            high, low = halves(value)
            at = (k, pl.ds(first_row, STRIP), pl.ds(part * LANES, LANES))
            xhi[at] = high
            xlo[at] = low


def rows_in(y, first_row):
    values = [
        tuple(y[k, pl.ds(first_row, STRIP), pl.ds(part * LANES, LANES)] for part in range(2))
        for k in range(XA)
    ]
    return sixteenth(values, 1.0)


def rows_mix(xhi, xlo, mhi, mlo, y):
    def step(k, carry):
        high, low = xhi[k], xlo[k]
        y[k] = dot32(high, mhi[k]) + (dot32(low, mhi[k]) + dot32(high, mlo[k]))
        return carry

    lax.fori_loop(0, XA, step, 0)


def columns_out(xhi, xlo, field, row, values):
    for k, (re, im) in enumerate(sixteenth(values, -1.0)):
        for part, value in enumerate((re, im)):
            high, low = halves(value)
            at = (k, pl.ds(part * XB + row, STRIP), pl.ds(field * LANES, LANES))
            xhi[at] = high
            xlo[at] = low


def columns_in(y, field, row):
    values = [
        tuple(
            y[k, pl.ds(part * XB + row, STRIP), pl.ds(field * LANES, LANES)] for part in range(2)
        )
        for k in range(XA)
    ]
    return sixteenth(values, 1.0)


def columns_mix(xhi, xlo, mhi, mlo, y):
    def step(k, carry):
        high, low = xhi[k], xlo[k]
        y[k] = dot32(mhi[k], high) + (dot32(mhi[k], low) + dot32(mlo[k], high))
        return carry

    lax.fori_loop(0, XA, step, 0)


def enter_kernel(angles, place, *refs):
    indices, (own, other), refs = refs[:angles], refs[angles : angles + 2], refs[angles + 2 :]
    weights, (mhi, mlo, out), refs = refs[: 2 * angles], refs[2 * angles : 2 * angles + 3], refs[2 * angles + 3 :]
    fronts, (shi, slo, field, xhi, xlo, y) = refs[:angles], refs[angles:]
    half = own.shape[1]
    rows = 2 * half

    for number in range(4):
        for piece, side in ((own, place[0]), (other, 1 - place[0])):

            def cut(row, number=number, piece=piece, side=side):
                high, low = halves(piece[number, pl.ds(row, STRIP), :])
                first = number * rows + side * half + row
                at = pl.ds(pl.multiple_of(first, STRIP), STRIP)
                shi[at, :] = high
                slo[at, :] = low

            strips(half, cut)

    for a in range(angles):
        enter_angle(
            indices[a], weights[2 * a], weights[2 * a + 1], mhi, mlo,
            out, 8 * a, fronts[a], shi, slo, field, xhi, xlo, y,
        )


def enter_angle(index, whi, wlo, mhi, mlo, out, base, t0, shi, slo, field, xhi, xlo, y):
    rows = t0.shape[2]

    def rotated(b):
        at = [pl.ds(pl.multiple_of(index[b, s] * BLK, BLK), BLK) for s in range(SLOTS)]
        high = jnp.concatenate([shi[:, a] for a in at], axis=1)
        low = jnp.concatenate([slo[:, a] for a in at], axis=1)
        values = dot32(high, whi[b]) + (dot32(low, whi[b]) + dot32(high, wlo[b]))
        angle, loss, d_re, d_im = (values[i * rows : (i + 1) * rows] for i in range(4))
        sine, cosine = sincos(angle)
        damping = jnp.exp(-loss)
        return damping * cosine, damping * sine, d_re, d_im

    def first_slice(b, carry):
        t_re, t_im, d_re, d_im = rotated(b)
        t0[b, 0] = t_re
        t0[b, 1] = t_im
        field[b, 0] = -(d_re * t_im + d_im * t_re)
        field[b, 1] = d_re * t_re - d_im * t_im
        return carry

    lax.fori_loop(0, XA, first_slice, 0)

    def forward(row):
        at = pl.ds(row, STRIP)
        rows_out(xhi, xlo, row, [(t0[b, 0, at, :], t0[b, 1, at, :]) for b in range(XA)])
        rows_out(
            xhi,
            xlo,
            pl.multiple_of(rows + row, STRIP),
            [(field[b, 0, at, :], field[b, 1, at, :]) for b in range(XA)],
        )

    strips(rows, forward)
    rows_mix(xhi, xlo, mhi, mlo, y)

    def backward(row):
        at = pl.ds(row, STRIP)
        for number in range(2):
            values = rows_in(y, pl.multiple_of(number * rows + row, STRIP))
            for b, (re, im) in enumerate(values):
                out[b, base + 2 * number, at, :] = re
                out[b, base + 2 * number + 1, at, :] = im

    strips(rows, backward)

    def second_slice(b, carry):
        for channel, value in enumerate(rotated(XA + b)):
            out[b, base + 4 + channel] = value
        return carry

    lax.fori_loop(0, XA, second_slice, 0)


def by_pieces(spans, step):
    half = XB // CHUNKS // 2
    pieces = [(piece, c) for piece, span in enumerate(spans) for c in range(span)]
    for chunk, (piece, c) in enumerate(pieces):
        for x in range(2):

            def inner(row, chunk=chunk, piece=piece, c=c, x=x):
                places = []
                for p in range(XA):
                    first = (2 * c + p // HALF) * half
                    at = pl.ds(pl.multiple_of(first + row, STRIP), STRIP)
                    places.append((piece, x * HALF + p % HALF, at))
                step(pl.multiple_of((2 * chunk + x) * half + row, STRIP), places)

            strips(half, inner)


def middle_kernel(bases, *refs):
    chunks = len(bases)
    arrived = refs[:chunks]
    mhi, mlo, out, kept, xhi, xlo, y = refs[chunks:]

    def forward(row, places):
        for number in range(2):
            values = [
                tuple(arrived[c][g, bases[c] + 2 * number + i, at, :] for i in range(2)) for c, g, at in places
            ]
            columns_out(xhi, xlo, number, row, values)

    by_pieces((1,) * chunks, forward)
    columns_mix(xhi, xlo, mhi, mlo, y)

    def turn(row, places):
        local = pl.ds(row, STRIP)
        wave = columns_in(y, 0, row)
        product = []
        for p, (c, g, at) in enumerate(places):
            t = tuple(arrived[c][g, bases[c] + i, at, :] for i in (4, 5))
            value = times(t, wave[p])
            for i, part in enumerate(value + t):
                kept[p, i, local, :] = part
            product.append(value)
        columns_out(xhi, xlo, 0, row, product)
        dwave = columns_in(y, 1, row)
        change = []
        for p, (c, g, at) in enumerate(places):
            t_re, t_im, d_re, d_im = (arrived[c][g, bases[c] + 4 + i, at, :] for i in range(4))
            p_re, p_im = kept[p, 0, local, :], kept[p, 1, local, :]
            re, im = times((t_re, t_im), dwave[p])
            change.append((re - (d_re * p_im + d_im * p_re), im + (d_re * p_re - d_im * p_im)))
        columns_out(xhi, xlo, 1, row, change)

    by_pieces((1,) * chunks, turn)
    columns_mix(xhi, xlo, mhi, mlo, y)

    def backward(row, places):
        for number in range(2):
            for (_, g, at), (re, im) in zip(places, columns_in(y, number, row)):
                out[g, 2 * number, at, :] = re
                out[g, 2 * number + 1, at, :] = im

    by_pieces((CHUNKS,), backward)


def detector_kernel(fields, mhi, mlo, out, xhi, xlo, y):
    rows = fields.shape[2]

    def forward(row):
        at = pl.ds(row, STRIP)
        for number in range(2):
            rows_out(
                xhi,
                xlo,
                pl.multiple_of(number * rows + row, STRIP),
                [tuple(fields[b, 2 * number + i, at, :] for i in range(2)) for b in range(XA)],
            )

    strips(rows, forward)
    rows_mix(xhi, xlo, mhi, mlo, y)

    def turn(row):
        wave = rows_in(y, row)
        dwave = rows_in(y, pl.multiple_of(rows + row, STRIP))
        back = []
        for (re, im), (d_re, d_im) in zip(wave, dwave):
            change = 4.0 * (re * d_re + im * d_im)
            back.append((change * re, -(change * im)))
        rows_out(xhi, xlo, row, back)

    strips(rows, turn)

    def step(k, carry):
        high, low = xhi[k, :rows, :], xlo[k, :rows, :]
        y[k, :rows, :] = dot32(high, mhi[k]) + (dot32(low, mhi[k]) + dot32(high, mlo[k]))
        return carry

    lax.fori_loop(0, XA, step, 0)

    def backward(row):
        at = pl.ds(row, STRIP)
        for b, (re, im) in enumerate(rows_in(y, row)):
            out[b, 0, at, :] = re
            out[b, 1, at, :] = im

    strips(rows, backward)


def return_kernel(spans, back, kept, mhi, mlo, *refs):
    out, (xhi, xlo, y) = refs[: len(spans)], refs[len(spans) :]

    def forward(row, places):
        values = [(back[g, 0, at, :], back[g, 1, at, :]) for _, g, at in places]
        columns_out(xhi, xlo, 0, row, values)

    by_pieces((CHUNKS,), forward)
    columns_mix(xhi, xlo, mhi, mlo, y)

    def turn(row, places):
        local = pl.ds(row, STRIP)
        pulled = columns_in(y, 0, row)
        following = []
        for p, (c, g, at) in enumerate(places):
            re, im = times((kept[p, 0, local, :], kept[p, 1, local, :]), pulled[p])
            out[c][g, 0, at, :] = -im
            out[c][g, 1, at, :] = -re
            following.append(times((kept[p, 2, local, :], kept[p, 3, local, :]), pulled[p]))
        columns_out(xhi, xlo, 0, row, following)

    by_pieces(spans, turn)
    columns_mix(xhi, xlo, mhi, mlo, y)

    def backward(row, places):
        for (c, g, at), (re, im) in zip(places, columns_in(y, 0, row)):
            out[c][g, 2, at, :] = re
            out[c][g, 3, at, :] = im

    by_pieces(spans, backward)


def leave_kernel(spans, place, index, back, whi, wlo, mhi, mlo, *refs):
    chunks, count = sum(spans), 2 * len(spans)
    t0, refs = refs[:chunks], refs[chunks:]
    before, outs, (shi, slo, xhi, xlo, y) = refs[: -count - 5], refs[-count - 5 : -5], refs[-5:]
    chunk = t0[0].shape[2]
    half = chunk // 2
    rows = chunks * chunk
    starts = []

    def pieces_of(step):
        starts.clear()
        done = 0
        for span in spans:
            for end, side in enumerate((1 - place[1], place[1])):
                base = (2 * done + end * span) * half
                starts.append((base, span * half))
                for c in range(span):

                    def inner(row, side=side, c=c, done=done, base=base):
                        within = pl.multiple_of(side * half + row, STRIP)
                        source = pl.multiple_of((done + c) * chunk + side * half + row, STRIP)
                        target = pl.multiple_of(base + c * half + row, STRIP)
                        step(done + c, pl.ds(within, STRIP), pl.ds(source, STRIP), target)

                    strips(half, inner)
            done += span

    def store(b, i, target, value):
        high, low = halves(value)
        at = pl.ds(pl.multiple_of(i * rows + target, STRIP), STRIP)
        shi[b, at, :] = high
        slo[b, at, :] = low

    def forward(c, within, at, target):
        rows_out(xhi, xlo, target, [(back[b, 2, at, :], back[b, 3, at, :]) for b in range(XA)])
        for b in range(XA):
            for i in range(2):
                store(XA + b, i, target, back[b, i, at, :])

    pieces_of(forward)
    rows_mix(xhi, xlo, mhi, mlo, y)

    def turn(c, within, at, target):
        for b, value in enumerate(rows_in(y, target)):
            re, im = times((t0[c][b, 0, within, :], t0[c][b, 1, within, :]), value)
            store(b, 0, target, -im)
            store(b, 1, target, -re)

    pieces_of(turn)

    for out, old in zip(outs, before or [None] * count):
        out[...] = jnp.zeros(out.shape, jnp.float32) if old is None else old[...]

    def across(a, b):
        return lax.dot_general(
            a, b, (((1,), (1,)), ((), ())), preferred_element_type=jnp.float32
        )

    def step(b, carry):
        high, low = shi[b], slo[b]
        values = across(high, whi[b]) + (across(low, whi[b]) + across(high, wlo[b]))
        for s in range(SLOTS):
            at = pl.ds(pl.multiple_of(index[b, s] * BLK, BLK), BLK)
            for i in range(2):
                for (start, size), out in zip(starts, outs):
                    start += i * rows
                    out[i, :, at] += values[start : start + size, s * BLK : (s + 1) * BLK]
        return carry

    lax.fori_loop(0, NB, step, 0)


def call(kernel, outs, scratch, mix_count, extra, *operands):
    specs = [
        pl.BlockSpec(memory_space=pltpu.SMEM if o.dtype == jnp.int32 else pltpu.VMEM)
        for o in operands
    ]
    moved = sum(o.size * o.dtype.itemsize for o in operands) + sum(4 * math.prod(o) for o in outs)
    return pl.pallas_call(
        kernel,
        out_shape=[jax.ShapeDtypeStruct(o, jnp.float32) for o in outs],
        in_specs=specs,
        out_specs=[pl.BlockSpec(memory_space=pltpu.VMEM)] * len(outs),
        scratch_shapes=scratch,
        compiler_params=pltpu.CompilerParams(vmem_limit_bytes=60 * 1024 * 1024),
        cost_estimate=pl.CostEstimate(
            flops=int(mix_count * 16 * 128 * 256 * 256 * 6) + extra,
            bytes_accessed=moved,
            transcendentals=0,
        ),
    )(*operands)


def mix_scratch(rows, lanes):
    return [
        pltpu.VMEM((XA, rows, lanes), jnp.bfloat16),
        pltpu.VMEM((XA, rows, lanes), jnp.bfloat16),
        pltpu.VMEM((XA, rows, lanes), jnp.float32),
    ]


def enter(place, indices, own, other, weights, matrices):
    angles = len(indices)
    rows = 2 * own.shape[1]
    scratch = [
        pltpu.VMEM((4 * rows, NB * BLK), jnp.bfloat16),
        pltpu.VMEM((4 * rows, NB * BLK), jnp.bfloat16),
        pltpu.VMEM((XA, 2, rows, LANES), jnp.float32),
    ] + mix_scratch(2 * rows, 2 * LANES)
    fields, *fronts = call(
        functools.partial(enter_kernel, angles),
        [(XA, 8 * angles, rows, LANES)] + [(XA, 2, rows, LANES)] * angles,
        scratch,
        rows / XB * 2 * angles,
        NB * 4 * rows * 256 * 128 * 6 * angles,
        place,
        *indices,
        own,
        other,
        *[w for pair in weights for w in pair],
        *matrices,
    )
    return fields, fronts


def middle(arrived, bases, matrices):
    return call(
        functools.partial(middle_kernel, bases),
        [(XA, 4, XB, LANES), (XA, 4, XB, LANES)],
        mix_scratch(2 * XB, 2 * LANES),
        4,
        0,
        *arrived,
        *matrices,
    )


def detector(fields, matrices):
    rows = fields.shape[2]
    return call(
        detector_kernel,
        [(XA, 2, rows, LANES)],
        mix_scratch(2 * rows, 2 * LANES),
        3,
        0,
        fields,
        *matrices,
    )[0]


def pull(back, kept, matrices, spans):
    return call(
        functools.partial(return_kernel, spans),
        [(XA, 4, span * XB // CHUNKS, LANES) for span in spans],
        mix_scratch(2 * XB, LANES),
        2,
        0,
        back,
        kept,
        *matrices,
    )


def leave(place, index, back, t0, weights, matrices, before, spans):
    rows = sum(t.shape[2] for t in t0)
    scratch = [
        pltpu.VMEM((NB, 2 * rows, LANES), jnp.bfloat16),
        pltpu.VMEM((NB, 2 * rows, LANES), jnp.bfloat16),
    ] + mix_scratch(rows, 2 * LANES)
    extra = NB * 2 * rows * 256 * 128 * 6
    outs = call(
        functools.partial(leave_kernel, spans),
        [(2, span * XB // CHUNKS // 2, NB * BLK) for span in spans for _ in range(2)],
        scratch,
        rows / XB,
        extra,
        place,
        index,
        back,
        *weights,
        *matrices,
        *t0,
        *before,
    )
    return [outs[2 * i : 2 * i + 2] for i in range(len(spans))]


def split_weights(block_weights):
    stacked = block_weights.reshape(ANGLES, NB, SLOTS * BLK, BLK)
    rounded = lax.reduce_precision(stacked, 8, 7)
    return rounded.astype(jnp.bfloat16), (stacked - rounded).astype(jnp.bfloat16)


def device(q, b, r):
    return q * XA + b * HALF + r


def exchange(values):
    return lax.all_to_all(
        values,
        ("parts", "fft"),
        split_axis=0,
        concat_axis=0,
        axis_index_groups=[[device(x, b, r) for x in range(2) for r in range(HALF)] for b in range(2)],
        tiled=True,
    )


def permute(values, steps):
    pairs = [
        (device(*here, r), device(*there, r)) for here, there in steps for r in range(HALF)
    ]
    return lax.ppermute(values, ("parts", "fft"), pairs)


BESIDE = [((q, b), (1 - q, b)) for q in range(2) for b in range(2)]
ALONG = [((q, b), (q, 1 - b)) for q in range(2) for b in range(2)]
CYCLE = [((0, 0), (0, 1)), ((1, 0), (0, 0)), ((1, 1), (1, 0)), ((0, 1), (1, 1))]
ACROSS = [((0, 1), (1, 0)), ((1, 0), (0, 1))]


def after(values, others):
    return lax.optimization_barrier((values, others))[0]


def arrive(potential, direction, q, b):
    half = XB // CHUNKS // 2

    def sides(c):
        lower, upper = (
            jnp.concatenate(
                [v[:, (2 * c + x) * half : (2 * c + x + 1) * half] for v in (potential, direction)]
            )
            for x in range(2)
        )
        return jnp.where(q == 0, lower, upper), jnp.where(q == 0, upper, lower)

    keep, give = sides(0)
    potential, direction = after((potential, direction), give)
    beside = permute(give, BESIDE)
    kept, given = zip(*[sides(c) for c in range(1, CHUNKS)])
    rest = permute(after(jnp.concatenate(given), beside), BESIDE)
    chunks = []
    for c in range(CHUNKS):
        if c:
            keep, beside = kept[c - 1], rest[4 * (c - 1) : 4 * c]
        chunks.append((jnp.where(q == b, keep, beside), jnp.where(q == b, beside, keep)))
    return chunks, rest


def depart(near, far):
    return permute(near, CYCLE), permute(far, ACROSS), far


def settle(once, twice, far, q, b):
    same = jnp.where(q == b, far, once)
    rest = jnp.where(q == b, once, twice)
    return jnp.where(q == 0, same, rest), jnp.where(q == 0, rest, same)


def blocked_body(potential, direction, block_index, block_weights):
    q = lax.axis_index("parts")
    b = lax.axis_index("fft") // HALF
    place = jnp.stack([b, q]).astype(jnp.int32)
    chunks, beside = arrive(potential, direction, q, b)
    whi, wlo = split_weights(block_weights)
    by_column = column_constants()
    column = tuple(jnp.asarray(v) for v in split_constant(by_column))
    row = tuple(jnp.asarray(v) for v in split_constant(by_column.transpose(0, 2, 1)))
    weights = [(whi[a], wlo[a]) for a in range(ANGLES)]
    angles = range(ANGLES)
    arrived = [[] for _ in angles]
    bases = [[] for _ in angles]
    ahead = [[] for _ in angles]
    fields = moved = earlier = ()
    for c, (own, give) in enumerate(chunks):
        along = permute(after(give, (fields, earlier)), ALONG)
        earlier = moved
        own = after(own, beside)
        for part in (angles,) if c + 1 < CHUNKS else [[a] for a in angles]:
            fields, fronts = enter(
                place, [block_index[a] for a in part], own, along, [weights[a] for a in part], row
            )
            moved = exchange(fields)
            for i, a in enumerate(part):
                arrived[a].append(moved)
                bases[a].append(8 * i)
                ahead[a].append(fronts[i])
    carried = []
    for a in angles:
        out, kept = middle(arrived[a], tuple(bases[a]), column)
        carried.append((exchange(out), kept))
    backs = [exchange(detector(out, row)) for out, _ in carried]
    most, half = CHUNKS // 2, XB // CHUNKS // 2
    rest = (CHUNKS // 4, CHUNKS // 4)
    spans = (most,) + rest

    def home(a, back, first, before, spans):
        t0 = ahead[a][first : first + sum(spans)]
        return leave(place, block_index[a], back, t0, weights[a], row, before, spans)

    early = pull(backs[0], carried[0][1], column, (most, sum(rest)))
    late = pull(backs[1], carried[1][1], column, spans)
    back = exchange(early[0])
    next_back = exchange(late[0])
    (start,) = home(0, back, 0, (), (most,))
    back = exchange(after(early[1], start))
    totals = home(1, next_back, 0, start, (most,))
    next_back = exchange(after(late[1], totals))
    starts = home(0, back, most, (), rest)
    leaving = [depart(*totals[0])]
    back = exchange(after(late[2], (starts, leaving)))
    totals += home(1, next_back, most, starts[0], rest[:1])
    totals += home(1, back, most + rest[0], starts[1], rest[1:])
    leaving += [depart(*total) for total in totals[1:]]
    pieces = []
    total = totals[-1]
    for span, moved in zip(spans, after(leaving, total)):
        lower, upper = settle(*moved, q, b)
        for c in range(span):
            pieces += [v[:, c * half : (c + 1) * half] for v in (lower, upper)]
    return jnp.concatenate(pieces, axis=1)


def transform_table(count_in, count_out, length, orient):
    first = jnp.arange(count_in, dtype=jnp.int32)[:, None]
    second = jnp.arange(count_out, dtype=jnp.int32)[None, :]
    phases = orient * 2.0 * math.pi / length * (first * second % length).astype(jnp.float32)
    cosine = jnp.cos(phases)
    sine_part = jnp.sin(phases)
    return jnp.stack([jnp.stack([cosine, sine_part]), jnp.stack([-sine_part, cosine])])


def twiddle_pair(count_a, count_b, length, orient):
    first = jnp.arange(count_a, dtype=jnp.int32)[:, None]
    second = jnp.arange(count_b, dtype=jnp.int32)[None, :]
    phases = orient * 2.0 * math.pi / length * (first * second % length).astype(jnp.float32)
    return (jnp.cos(phases), jnp.sin(phases))


def spread_turn(peer_count, row_count, slot_count, orient):
    turn_re, turn_im = twiddle_pair(peer_count, row_count, NX, orient)
    shape_three = (row_count, peer_count, slot_count)
    wide_re = jnp.broadcast_to(turn_re.T[:, :, None], shape_three).reshape(
        row_count, peer_count * slot_count
    )
    wide_im = jnp.broadcast_to(turn_im.T[:, :, None], shape_three).reshape(
        row_count, peer_count * slot_count
    )
    return (wide_re, wide_im)


def complex_times(values, real_part, imag_part):
    first = values[:, 0]
    second = values[:, 1]
    return jnp.stack(
        [first * real_part - second * imag_part, first * imag_part + second * real_part], axis=1
    )


def one_hot(index_rows, block_count):
    return (index_rows[..., None] == jnp.arange(block_count, dtype=jnp.int32)).astype(jnp.float32)


def rotate(values, selector, matrices):
    height = values.shape[1]
    blocked = values.reshape(2, height, NB, BLK)
    picked = jnp.einsum("cyni,bsn->cybsi", blocked, selector, precision=PRECISE)
    rotated = jnp.einsum("cybsi,bsio->cybo", picked, matrices, precision=PRECISE)
    return rotated.reshape(2, height, SL, NX)


def rotate_back(values, selector, matrices):
    height = values.shape[1]
    blocked = values.reshape(2, height, NB, BLK)
    spread_out = jnp.einsum("cybo,bsio->cybsi", blocked, matrices, precision=PRECISE)
    summed = jnp.einsum("cybsi,bsn->cyni", spread_out, selector, precision=PRECISE)
    return summed.reshape(2, height, SL * NX)


def fresnel(peer_count, row_count, slot_count, orient):
    position_high = jnp.arange(row_count, dtype=jnp.int32)[:, None]
    position_low = jnp.arange(peer_count, dtype=jnp.int32)[None, :]
    freq_y = position_low + peer_count * position_high
    freq_y = jnp.where(freq_y < NX // 2, freq_y, freq_y - NX)
    position = lax.axis_index("fft") * slot_count + jnp.arange(slot_count, dtype=jnp.int32)
    freq_x = position // XB + XA * (position % XB)
    freq_x = jnp.where(freq_x < NX // 2, freq_x, freq_x - NX)
    squares = ((freq_y * freq_y)[:, :, None] + (freq_x * freq_x)[None, None, :]) % (2 * NX)
    phases = orient * -math.pi / NX * squares.astype(jnp.float32)
    scaling = 1.0 / (NX * NX)
    phases = phases.reshape(row_count, peer_count * slot_count)
    return (jnp.cos(phases) * scaling, jnp.sin(phases) * scaling)


def propagate(fields, kernel, peer_count, row_count, slot_count):
    field_count = fields.shape[0]
    groups = XB // slot_count
    shaped = fields.reshape(field_count, 2, row_count, XA, XB)
    partial_x = jnp.einsum(
        "fcrab,cdak->fdrkb", shaped, transform_table(XA, XA, XA, -1.0), precision=PRECISE
    )
    twist_re, twist_im = twiddle_pair(XA, XB, NX, -1.0)
    partial_x = complex_times(partial_x, twist_re, twist_im)
    partial_x = jnp.einsum(
        "fcrkb,cdbt->fdrkt", partial_x, transform_table(XB, XB, XB, -1.0), precision=PRECISE
    )
    partial_x = partial_x.reshape(field_count, 2, row_count, XA, groups, slot_count)
    outgoing = partial_x.transpose(0, 1, 3, 4, 2, 5).reshape(
        field_count, 2, peer_count, row_count * slot_count
    )
    forward_re, forward_im = spread_turn(peer_count, row_count, slot_count, -1.0)
    inverse_re, inverse_im = spread_turn(peer_count, row_count, slot_count, 1.0)
    wide = peer_count * slot_count
    incoming = lax.all_to_all(outgoing, "fft", split_axis=2, concat_axis=2, tiled=True)
    item_count = incoming.shape[0]
    lattice = incoming.reshape(item_count, 2, peer_count, row_count, slot_count)
    lattice = jnp.einsum(
        "fcprs,cdpk->fdrks",
        lattice,
        transform_table(peer_count, peer_count, peer_count, -1.0),
        precision=PRECISE,
    )
    lattice = lattice.reshape(item_count, 2, row_count, wide)
    lattice = complex_times(lattice, forward_re, forward_im)
    lattice = jnp.einsum(
        "fcrq,cdrm->fdmq",
        lattice,
        transform_table(row_count, row_count, row_count, -1.0),
        precision=PRECISE,
    )
    lattice = complex_times(lattice, kernel[0], kernel[1])
    lattice = jnp.einsum(
        "fcmq,cdmr->fdrq",
        lattice,
        transform_table(row_count, row_count, row_count, 1.0),
        precision=PRECISE,
    )
    lattice = complex_times(lattice, inverse_re, inverse_im)
    lattice = lattice.reshape(item_count, 2, row_count, peer_count, slot_count)
    lattice = jnp.einsum(
        "fcrks,cdkp->fdprs",
        lattice,
        transform_table(peer_count, peer_count, peer_count, 1.0),
        precision=PRECISE,
    )
    returning = lax.all_to_all(
        lattice.reshape(item_count, 2, peer_count, row_count * slot_count),
        "fft",
        split_axis=2,
        concat_axis=2,
        tiled=True,
    )
    restored = returning.reshape(item_count, 2, XA, groups, row_count, slot_count)
    matrix_back = transform_table(XB, XB, XB, 1.0).reshape(2, 2, groups, slot_count, XB)
    restored = jnp.einsum("fckjrs,cdjsb->fdrkb", restored, matrix_back, precision=PRECISE)
    back_re, back_im = twiddle_pair(XA, XB, NX, 1.0)
    restored = complex_times(restored, back_re, back_im)
    restored = jnp.einsum(
        "fcrkb,cdkn->fdrnb", restored, transform_table(XA, XA, XA, 1.0), precision=PRECISE
    )
    return restored.reshape(item_count, 2, row_count, NX)


def general_body(potential, direction, block_index, block_weights):
    row_count = potential.shape[1]
    peer_count = lax.axis_size("fft")
    slot_count = NX // peer_count
    ahead = fresnel(peer_count, row_count, slot_count, 1.0)
    behind = fresnel(peer_count, row_count, slot_count, -1.0)
    accumulated = jnp.zeros(potential.shape, jnp.float32)
    for angle_index in range(ANGLES):
        selector = one_hot(block_index[angle_index], NB)
        matrices = block_weights[angle_index]
        rotated = rotate(potential, selector, matrices)
        tangent = rotate(direction, selector, matrices)
        damping = jnp.exp(-rotated[1])
        trans_re = damping * jnp.cos(rotated[0])
        trans_im = damping * jnp.sin(rotated[0])
        wave_re = jnp.ones((row_count, NX), jnp.float32)
        wave_im = jnp.zeros((row_count, NX), jnp.float32)
        dwave_re = jnp.zeros((row_count, NX), jnp.float32)
        dwave_im = jnp.zeros((row_count, NX), jnp.float32)
        stored = []
        for slice_index in range(SL):
            t_re = trans_re[:, slice_index]
            t_im = trans_im[:, slice_index]
            d_re = tangent[0][:, slice_index]
            d_im = tangent[1][:, slice_index]
            phi_re = t_re * wave_re - t_im * wave_im
            phi_im = t_re * wave_im + t_im * wave_re
            dphi_re = -(d_re * phi_im + d_im * phi_re) + t_re * dwave_re - t_im * dwave_im
            dphi_im = d_re * phi_re - d_im * phi_im + t_re * dwave_im + t_im * dwave_re
            stored.append((phi_re, phi_im))
            packed = jnp.stack([jnp.stack([phi_re, phi_im]), jnp.stack([dphi_re, dphi_im])])
            propagated = propagate(packed, ahead, peer_count, row_count, slot_count)
            wave_re = propagated[0, 0]
            wave_im = propagated[0, 1]
            dwave_re = propagated[1, 0]
            dwave_im = propagated[1, 1]
        change = 2.0 * (wave_re * dwave_re + wave_im * dwave_im)
        back_re = 2.0 * change * wave_re
        back_im = 2.0 * change * wave_im
        grad_re = [None] * SL
        grad_im = [None] * SL
        for slice_index in reversed(range(SL)):
            pulled = propagate(
                jnp.stack([back_re, back_im])[None], behind, peer_count, row_count, slot_count
            )
            pb_re = pulled[0, 0]
            pb_im = pulled[0, 1]
            phi_re, phi_im = stored[slice_index]
            grad_re[slice_index] = phi_re * pb_im - phi_im * pb_re
            grad_im[slice_index] = -(phi_re * pb_re + phi_im * pb_im)
            t_re = trans_re[:, slice_index]
            t_im = trans_im[:, slice_index]
            back_re = t_re * pb_re + t_im * pb_im
            back_im = t_re * pb_im - t_im * pb_re
        gradient = jnp.stack([jnp.stack(grad_re, axis=1), jnp.stack(grad_im, axis=1)])
        accumulated = accumulated + rotate_back(gradient, selector, matrices)
    return accumulated


def body(potential, direction, block_index, block_weights):
    if lax.axis_size("parts") == 2 and lax.axis_size("fft") == XA:
        return blocked_body(potential, direction, block_index, block_weights)
    return general_body(potential, direction, block_index, block_weights)


def solution(mesh):
    return jax.shard_map(
        body,
        mesh=mesh,
        in_specs=(P("parts", "fft", None), P("parts", "fft", None), P(), P()),
        out_specs=P("parts", "fft", None),
        check_vma=False,
    )
```

```python
import functools
import math

import jax
import jax.numpy as jnp
import numpy as np
from jax import lax
from jax.experimental import pallas as pl
from jax.experimental.pallas import tpu as pltpu
from jax.sharding import PartitionSpec as P

XA = 16
XB = 128
NX = 2048
SL = 2
ANGLES = 2
BLK = 128
NB = 32
SLOTS = 2
STRIP = 16
LANES = 128
CHUNKS = 4
HALF = XA // 2


PRECISE = lax.Precision.HIGHEST


def bin_matrices():
    wavenumber = np.arange(NX)
    signed = np.where(wavenumber < NX // 2, wavenumber, wavenumber - NX)
    factor = np.exp(-1j * np.pi / NX * ((signed * signed) % (2 * NX)))
    line = np.fft.ifft(factor)
    block = np.arange(XA)
    inner = np.arange(XB)
    shifts = (XB * block[:, None, None] + inner[None, :, None] - inner[None, None, :]) % NX
    phases = np.exp(-2j * np.pi / XA * ((block[:, None] * block[None, :]) % XA))
    return np.einsum("kd,dij->kij", phases, line[shifts]) / XA


def split_constant(values):
    values = values.astype(np.float32)
    high = values.astype(jnp.bfloat16)
    low = (values - high.astype(np.float32)).astype(jnp.bfloat16)
    return high, low


def column_constants():
    bins = bin_matrices()
    top = np.concatenate([bins.real, -bins.imag], axis=2)
    bottom = np.concatenate([bins.imag, bins.real], axis=2)
    return np.concatenate([top, bottom], axis=1)


def fourth(values, orient):
    (ar, ai), (br, bi), (cr, ci), (dr, di) = values
    sr, si, er, ei = ar + cr, ai + ci, ar - cr, ai - ci
    tr, ti, fr, fi = br + dr, bi + di, br - dr, bi - di
    minus, plus = (er + fi, ei - fr), (er - fi, ei + fr)
    one, three = (minus, plus) if orient < 0 else (plus, minus)
    return [(sr + tr, si + ti), one, (sr - tr, si - ti), three]


def turned(value, step, orient):
    re, im = value
    if step == 0:
        return value
    if step == 4:
        return (im, -re) if orient < 0 else (-im, re)
    cosine = math.cos(2.0 * math.pi * step / XA)
    sine = orient * math.sin(2.0 * math.pi * step / XA)
    if step == 2:
        root = cosine
        return ((re - im) * root, (re + im) * root) if orient > 0 else ((re + im) * root, (im - re) * root)
    return (re * cosine - im * sine, re * sine + im * cosine)


def sixteenth(values, orient):
    inner = [fourth([values[4 * a + b] for a in range(4)], orient) for b in range(4)]
    out = [None] * XA
    for c in range(4):
        row = fourth([turned(inner[b][c], b * c, orient) for b in range(4)], orient)
        for d in range(4):
            out[c + 4 * d] = row[d]
    return out


def halves(value):
    high = value.astype(jnp.bfloat16)
    return high, (value - high.astype(jnp.float32)).astype(jnp.bfloat16)


def dot32(a, b):
    return jnp.dot(a, b, preferred_element_type=jnp.float32)


def times(a, b):
    return (a[0] * b[0] - a[1] * b[1], a[0] * b[1] + a[1] * b[0])


def sincos(x):
    turns = jnp.floor(x * (2.0 / math.pi) + 0.5)
    rest = ((x - turns * 1.5703125) - turns * 4.837512969970703125e-4) - turns * 7.54978995489188216e-8
    square = rest * rest
    sine = rest + rest * square * (
        -1.6666654611e-1 + square * (8.3321608736e-3 + square * -1.9515295891e-4)
    )
    cosine = (1.0 - 0.5 * square) + square * square * (
        4.166664568298827e-2 + square * (-1.388731625493765e-3 + square * 2.443315711809948e-5)
    )
    quadrant = turns.astype(jnp.int32)
    odd = (quadrant & 1) == 1
    first = jnp.where(odd, cosine, sine)
    second = jnp.where(odd, sine, cosine)
    first = jnp.where((quadrant & 2) == 2, -first, first)
    second = jnp.where(((quadrant + 1) & 2) == 2, -second, second)
    return first, second


def strips(count, step):
    def run(i, carry):
        step(pl.multiple_of(i * STRIP, STRIP))
        return carry

    lax.fori_loop(0, count // STRIP, run, 0)


def rows_out(xhi, xlo, first_row, values):
    for k, (re, im) in enumerate(sixteenth(values, -1.0)):
        for part, value in enumerate((re, im)):
            high, low = halves(value)
            at = (k, pl.ds(first_row, STRIP), pl.ds(part * LANES, LANES))
            xhi[at] = high
            xlo[at] = low


def rows_in(y, first_row):
    values = [
        tuple(y[k, pl.ds(first_row, STRIP), pl.ds(part * LANES, LANES)] for part in range(2))
        for k in range(XA)
    ]
    return sixteenth(values, 1.0)


def rows_mix(xhi, xlo, mhi, mlo, y):
    def step(k, carry):
        high, low = xhi[k], xlo[k]
        y[k] = dot32(high, mhi[k]) + (dot32(low, mhi[k]) + dot32(high, mlo[k]))
        return carry

    lax.fori_loop(0, XA, step, 0)


def columns_out(xhi, xlo, field, row, values):
    for k, (re, im) in enumerate(sixteenth(values, -1.0)):
        for part, value in enumerate((re, im)):
            high, low = halves(value)
            at = (k, pl.ds(part * XB + row, STRIP), pl.ds(field * LANES, LANES))
            xhi[at] = high
            xlo[at] = low


def columns_in(y, field, row):
    values = [
        tuple(
            y[k, pl.ds(part * XB + row, STRIP), pl.ds(field * LANES, LANES)] for part in range(2)
        )
        for k in range(XA)
    ]
    return sixteenth(values, 1.0)


def columns_mix(xhi, xlo, mhi, mlo, y):
    def step(k, carry):
        high, low = xhi[k], xlo[k]
        y[k] = dot32(mhi[k], high) + (dot32(mhi[k], low) + dot32(mlo[k], high))
        return carry

    lax.fori_loop(0, XA, step, 0)


def enter_kernel(angles, place, *refs):
    indices, (own, other), refs = refs[:angles], refs[angles : angles + 2], refs[angles + 2 :]
    weights, (mhi, mlo, out), refs = refs[: 2 * angles], refs[2 * angles : 2 * angles + 3], refs[2 * angles + 3 :]
    fronts, (shi, slo, field, xhi, xlo, y) = refs[:angles], refs[angles:]
    half = own.shape[1]
    rows = 2 * half

    for number in range(4):
        for piece, side in ((own, place[0]), (other, 1 - place[0])):

            def cut(row, number=number, piece=piece, side=side):
                high, low = halves(piece[number, pl.ds(row, STRIP), :])
                first = number * rows + side * half + row
                at = pl.ds(pl.multiple_of(first, STRIP), STRIP)
                shi[at, :] = high
                slo[at, :] = low

            strips(half, cut)

    for a in range(angles):
        enter_angle(
            indices[a], weights[2 * a], weights[2 * a + 1], mhi, mlo,
            out, 8 * a, fronts[a], shi, slo, field, xhi, xlo, y,
        )


def enter_angle(index, whi, wlo, mhi, mlo, out, base, t0, shi, slo, field, xhi, xlo, y):
    rows = t0.shape[2]

    def rotated(b):
        at = [pl.ds(pl.multiple_of(index[b, s] * BLK, BLK), BLK) for s in range(SLOTS)]
        high = jnp.concatenate([shi[:, a] for a in at], axis=1)
        low = jnp.concatenate([slo[:, a] for a in at], axis=1)
        values = dot32(high, whi[b]) + (dot32(low, whi[b]) + dot32(high, wlo[b]))
        angle, loss, d_re, d_im = (values[i * rows : (i + 1) * rows] for i in range(4))
        sine, cosine = sincos(angle)
        damping = jnp.exp(-loss)
        return damping * cosine, damping * sine, d_re, d_im

    def first_slice(b, carry):
        t_re, t_im, d_re, d_im = rotated(b)
        t0[b, 0] = t_re
        t0[b, 1] = t_im
        field[b, 0] = -(d_re * t_im + d_im * t_re)
        field[b, 1] = d_re * t_re - d_im * t_im
        return carry

    lax.fori_loop(0, XA, first_slice, 0)

    def forward(row):
        at = pl.ds(row, STRIP)
        rows_out(xhi, xlo, row, [(t0[b, 0, at, :], t0[b, 1, at, :]) for b in range(XA)])
        rows_out(
            xhi,
            xlo,
            pl.multiple_of(rows + row, STRIP),
            [(field[b, 0, at, :], field[b, 1, at, :]) for b in range(XA)],
        )

    strips(rows, forward)
    rows_mix(xhi, xlo, mhi, mlo, y)

    def backward(row):
        at = pl.ds(row, STRIP)
        for number in range(2):
            values = rows_in(y, pl.multiple_of(number * rows + row, STRIP))
            for b, (re, im) in enumerate(values):
                out[b, base + 2 * number, at, :] = re
                out[b, base + 2 * number + 1, at, :] = im

    strips(rows, backward)

    def second_slice(b, carry):
        for channel, value in enumerate(rotated(XA + b)):
            out[b, base + 4 + channel] = value
        return carry

    lax.fori_loop(0, XA, second_slice, 0)


def by_pieces(spans, step):
    half = XB // CHUNKS // 2
    pieces = [(piece, c) for piece, span in enumerate(spans) for c in range(span)]
    for chunk, (piece, c) in enumerate(pieces):
        for x in range(2):

            def inner(row, chunk=chunk, piece=piece, c=c, x=x):
                places = []
                for p in range(XA):
                    first = (2 * c + p // HALF) * half
                    at = pl.ds(pl.multiple_of(first + row, STRIP), STRIP)
                    places.append((piece, x * HALF + p % HALF, at))
                step(pl.multiple_of((2 * chunk + x) * half + row, STRIP), places)

            strips(half, inner)


def middle_kernel(bases, *refs):
    chunks = len(bases)
    arrived = refs[:chunks]
    mhi, mlo, out, kept, xhi, xlo, y = refs[chunks:]

    def forward(row, places):
        for number in range(2):
            values = [
                tuple(arrived[c][g, bases[c] + 2 * number + i, at, :] for i in range(2)) for c, g, at in places
            ]
            columns_out(xhi, xlo, number, row, values)

    by_pieces((1,) * chunks, forward)
    columns_mix(xhi, xlo, mhi, mlo, y)

    def turn(row, places):
        local = pl.ds(row, STRIP)
        wave = columns_in(y, 0, row)
        product = []
        for p, (c, g, at) in enumerate(places):
            t = tuple(arrived[c][g, bases[c] + i, at, :] for i in (4, 5))
            value = times(t, wave[p])
            for i, part in enumerate(value + t):
                kept[p, i, local, :] = part
            product.append(value)
        columns_out(xhi, xlo, 0, row, product)
        dwave = columns_in(y, 1, row)
        change = []
        for p, (c, g, at) in enumerate(places):
            t_re, t_im, d_re, d_im = (arrived[c][g, bases[c] + 4 + i, at, :] for i in range(4))
            p_re, p_im = kept[p, 0, local, :], kept[p, 1, local, :]
            re, im = times((t_re, t_im), dwave[p])
            change.append((re - (d_re * p_im + d_im * p_re), im + (d_re * p_re - d_im * p_im)))
        columns_out(xhi, xlo, 1, row, change)

    by_pieces((1,) * chunks, turn)
    columns_mix(xhi, xlo, mhi, mlo, y)

    def backward(row, places):
        for number in range(2):
            for (_, g, at), (re, im) in zip(places, columns_in(y, number, row)):
                out[g, 2 * number, at, :] = re
                out[g, 2 * number + 1, at, :] = im

    by_pieces((CHUNKS,), backward)


def detector_kernel(fields, mhi, mlo, out, xhi, xlo, y):
    rows = fields.shape[2]

    def forward(row):
        at = pl.ds(row, STRIP)
        for number in range(2):
            rows_out(
                xhi,
                xlo,
                pl.multiple_of(number * rows + row, STRIP),
                [tuple(fields[b, 2 * number + i, at, :] for i in range(2)) for b in range(XA)],
            )

    strips(rows, forward)
    rows_mix(xhi, xlo, mhi, mlo, y)

    def turn(row):
        wave = rows_in(y, row)
        dwave = rows_in(y, pl.multiple_of(rows + row, STRIP))
        back = []
        for (re, im), (d_re, d_im) in zip(wave, dwave):
            change = 4.0 * (re * d_re + im * d_im)
            back.append((change * re, -(change * im)))
        rows_out(xhi, xlo, row, back)

    strips(rows, turn)

    def step(k, carry):
        high, low = xhi[k, :rows, :], xlo[k, :rows, :]
        y[k, :rows, :] = dot32(high, mhi[k]) + (dot32(low, mhi[k]) + dot32(high, mlo[k]))
        return carry

    lax.fori_loop(0, XA, step, 0)

    def backward(row):
        at = pl.ds(row, STRIP)
        for b, (re, im) in enumerate(rows_in(y, row)):
            out[b, 0, at, :] = re
            out[b, 1, at, :] = im

    strips(rows, backward)


def return_kernel(spans, back, kept, mhi, mlo, *refs):
    out, (xhi, xlo, y) = refs[: len(spans)], refs[len(spans) :]

    def forward(row, places):
        values = [(back[g, 0, at, :], back[g, 1, at, :]) for _, g, at in places]
        columns_out(xhi, xlo, 0, row, values)

    by_pieces((CHUNKS,), forward)
    columns_mix(xhi, xlo, mhi, mlo, y)

    def turn(row, places):
        local = pl.ds(row, STRIP)
        pulled = columns_in(y, 0, row)
        following = []
        for p, (c, g, at) in enumerate(places):
            re, im = times((kept[p, 0, local, :], kept[p, 1, local, :]), pulled[p])
            out[c][g, 0, at, :] = -im
            out[c][g, 1, at, :] = -re
            following.append(times((kept[p, 2, local, :], kept[p, 3, local, :]), pulled[p]))
        columns_out(xhi, xlo, 0, row, following)

    by_pieces(spans, turn)
    columns_mix(xhi, xlo, mhi, mlo, y)

    def backward(row, places):
        for (c, g, at), (re, im) in zip(places, columns_in(y, 0, row)):
            out[c][g, 2, at, :] = re
            out[c][g, 3, at, :] = im

    by_pieces(spans, backward)


def leave_kernel(spans, place, index, back, whi, wlo, mhi, mlo, *refs):
    chunks, count = sum(spans), 2 * len(spans)
    t0, refs = refs[:chunks], refs[chunks:]
    before, outs, (shi, slo, xhi, xlo, y) = refs[: -count - 5], refs[-count - 5 : -5], refs[-5:]
    chunk = t0[0].shape[2]
    half = chunk // 2
    rows = chunks * chunk
    starts = []

    def pieces_of(step):
        starts.clear()
        done = 0
        for span in spans:
            for end, side in enumerate((1 - place[1], place[1])):
                base = (2 * done + end * span) * half
                starts.append((base, span * half))
                for c in range(span):

                    def inner(row, side=side, c=c, done=done, base=base):
                        within = pl.multiple_of(side * half + row, STRIP)
                        source = pl.multiple_of((done + c) * chunk + side * half + row, STRIP)
                        target = pl.multiple_of(base + c * half + row, STRIP)
                        step(done + c, pl.ds(within, STRIP), pl.ds(source, STRIP), target)

                    strips(half, inner)
            done += span

    def store(b, i, target, value):
        high, low = halves(value)
        at = pl.ds(pl.multiple_of(i * rows + target, STRIP), STRIP)
        shi[b, at, :] = high
        slo[b, at, :] = low

    def forward(c, within, at, target):
        rows_out(xhi, xlo, target, [(back[b, 2, at, :], back[b, 3, at, :]) for b in range(XA)])
        for b in range(XA):
            for i in range(2):
                store(XA + b, i, target, back[b, i, at, :])

    pieces_of(forward)
    rows_mix(xhi, xlo, mhi, mlo, y)

    def turn(c, within, at, target):
        for b, value in enumerate(rows_in(y, target)):
            re, im = times((t0[c][b, 0, within, :], t0[c][b, 1, within, :]), value)
            store(b, 0, target, -im)
            store(b, 1, target, -re)

    pieces_of(turn)

    for out, old in zip(outs, before or [None] * count):
        out[...] = jnp.zeros(out.shape, jnp.float32) if old is None else old[...]

    def across(a, b):
        return lax.dot_general(
            a, b, (((1,), (1,)), ((), ())), preferred_element_type=jnp.float32
        )

    def step(b, carry):
        high, low = shi[b], slo[b]
        values = across(high, whi[b]) + (across(low, whi[b]) + across(high, wlo[b]))
        for s in range(SLOTS):
            at = pl.ds(pl.multiple_of(index[b, s] * BLK, BLK), BLK)
            for i in range(2):
                for (start, size), out in zip(starts, outs):
                    start += i * rows
                    out[i, :, at] += values[start : start + size, s * BLK : (s + 1) * BLK]
        return carry

    lax.fori_loop(0, NB, step, 0)


def call(kernel, outs, scratch, mix_count, extra, *operands):
    specs = [
        pl.BlockSpec(memory_space=pltpu.SMEM if o.dtype == jnp.int32 else pltpu.VMEM)
        for o in operands
    ]
    moved = sum(o.size * o.dtype.itemsize for o in operands) + sum(4 * math.prod(o) for o in outs)
    return pl.pallas_call(
        kernel,
        out_shape=[jax.ShapeDtypeStruct(o, jnp.float32) for o in outs],
        in_specs=specs,
        out_specs=[pl.BlockSpec(memory_space=pltpu.VMEM)] * len(outs),
        scratch_shapes=scratch,
        compiler_params=pltpu.CompilerParams(vmem_limit_bytes=60 * 1024 * 1024),
        cost_estimate=pl.CostEstimate(
            flops=int(mix_count * 16 * 128 * 256 * 256 * 6) + extra,
            bytes_accessed=moved,
            transcendentals=0,
        ),
    )(*operands)


def mix_scratch(rows, lanes):
    return [
        pltpu.VMEM((XA, rows, lanes), jnp.bfloat16),
        pltpu.VMEM((XA, rows, lanes), jnp.bfloat16),
        pltpu.VMEM((XA, rows, lanes), jnp.float32),
    ]


def enter(place, indices, own, other, weights, matrices):
    angles = len(indices)
    rows = 2 * own.shape[1]
    scratch = [
        pltpu.VMEM((4 * rows, NB * BLK), jnp.bfloat16),
        pltpu.VMEM((4 * rows, NB * BLK), jnp.bfloat16),
        pltpu.VMEM((XA, 2, rows, LANES), jnp.float32),
    ] + mix_scratch(2 * rows, 2 * LANES)
    fields, *fronts = call(
        functools.partial(enter_kernel, angles),
        [(XA, 8 * angles, rows, LANES)] + [(XA, 2, rows, LANES)] * angles,
        scratch,
        rows / XB * 2 * angles,
        NB * 4 * rows * 256 * 128 * 6 * angles,
        place,
        *indices,
        own,
        other,
        *[w for pair in weights for w in pair],
        *matrices,
    )
    return fields, fronts


def middle(arrived, bases, matrices):
    return call(
        functools.partial(middle_kernel, bases),
        [(XA, 4, XB, LANES), (XA, 4, XB, LANES)],
        mix_scratch(2 * XB, 2 * LANES),
        4,
        0,
        *arrived,
        *matrices,
    )


def detector(fields, matrices):
    rows = fields.shape[2]
    return call(
        detector_kernel,
        [(XA, 2, rows, LANES)],
        mix_scratch(2 * rows, 2 * LANES),
        3,
        0,
        fields,
        *matrices,
    )[0]


def pull(back, kept, matrices, spans):
    return call(
        functools.partial(return_kernel, spans),
        [(XA, 4, span * XB // CHUNKS, LANES) for span in spans],
        mix_scratch(2 * XB, LANES),
        2,
        0,
        back,
        kept,
        *matrices,
    )


def leave(place, index, back, t0, weights, matrices, before, spans):
    rows = sum(t.shape[2] for t in t0)
    scratch = [
        pltpu.VMEM((NB, 2 * rows, LANES), jnp.bfloat16),
        pltpu.VMEM((NB, 2 * rows, LANES), jnp.bfloat16),
    ] + mix_scratch(rows, 2 * LANES)
    extra = NB * 2 * rows * 256 * 128 * 6
    outs = call(
        functools.partial(leave_kernel, spans),
        [(2, span * XB // CHUNKS // 2, NB * BLK) for span in spans for _ in range(2)],
        scratch,
        rows / XB,
        extra,
        place,
        index,
        back,
        *weights,
        *matrices,
        *t0,
        *before,
    )
    return [outs[2 * i : 2 * i + 2] for i in range(len(spans))]


def split_weights(block_weights):
    stacked = block_weights.reshape(ANGLES, NB, SLOTS * BLK, BLK)
    rounded = lax.reduce_precision(stacked, 8, 7)
    return rounded.astype(jnp.bfloat16), (stacked - rounded).astype(jnp.bfloat16)


def device(q, b, r):
    return q * XA + b * HALF + r


def exchange(values):
    return lax.all_to_all(
        values,
        ("parts", "fft"),
        split_axis=0,
        concat_axis=0,
        axis_index_groups=[[device(x, b, r) for x in range(2) for r in range(HALF)] for b in range(2)],
        tiled=True,
    )


def permute(values, steps):
    pairs = [
        (device(*here, r), device(*there, r)) for here, there in steps for r in range(HALF)
    ]
    return lax.ppermute(values, ("parts", "fft"), pairs)


BESIDE = [((q, b), (1 - q, b)) for q in range(2) for b in range(2)]
ALONG = [((q, b), (q, 1 - b)) for q in range(2) for b in range(2)]
CYCLE = [((0, 0), (0, 1)), ((1, 0), (0, 0)), ((1, 1), (1, 0)), ((0, 1), (1, 1))]
ACROSS = [((0, 1), (1, 0)), ((1, 0), (0, 1))]


def after(values, others):
    return lax.optimization_barrier((values, others))[0]


def arrive(potential, direction, q, b):
    half = XB // CHUNKS // 2

    def sides(c):
        lower, upper = (
            jnp.concatenate(
                [v[:, (2 * c + x) * half : (2 * c + x + 1) * half] for v in (potential, direction)]
            )
            for x in range(2)
        )
        return jnp.where(q == 0, lower, upper), jnp.where(q == 0, upper, lower)

    keep, give = sides(0)
    potential, direction = after((potential, direction), give)
    beside = permute(give, BESIDE)
    kept, given = zip(*[sides(c) for c in range(1, CHUNKS)])
    rest = permute(after(jnp.concatenate(given), beside), BESIDE)
    chunks = []
    along = ()
    for c in range(CHUNKS):
        if c:
            keep, beside = kept[c - 1], rest[4 * (c - 1) : 4 * c]
        own = jnp.where(q == b, keep, beside)
        give = jnp.where(q == b, beside, keep)
        along = permute(after(give, along), ALONG)
        chunks.append((own, along))
    return chunks


def depart(near, far):
    return permute(near, CYCLE), permute(far, ACROSS), far


def settle(once, twice, far, q, b):
    same = jnp.where(q == b, far, once)
    rest = jnp.where(q == b, once, twice)
    return jnp.where(q == 0, same, rest), jnp.where(q == 0, rest, same)


def blocked_body(potential, direction, block_index, block_weights):
    q = lax.axis_index("parts")
    b = lax.axis_index("fft") // HALF
    place = jnp.stack([b, q]).astype(jnp.int32)
    chunks = arrive(potential, direction, q, b)
    whi, wlo = split_weights(block_weights)
    by_column = column_constants()
    column = tuple(jnp.asarray(v) for v in split_constant(by_column))
    row = tuple(jnp.asarray(v) for v in split_constant(by_column.transpose(0, 2, 1)))
    weights = [(whi[a], wlo[a]) for a in range(ANGLES)]
    angles = range(ANGLES)
    arrived = [[] for _ in angles]
    bases = [[] for _ in angles]
    ahead = [[] for _ in angles]
    fields = ()
    for c, (own, along) in enumerate(chunks):
        further = chunks[c + 1][1] if c + 1 < CHUNKS else ()
        own = after(own, fields)
        for a in angles:
            fields, (front,) = enter(place, [block_index[a]], own, along, [weights[a]], row)
            arrived[a].append(exchange(after(fields, further) if a else fields))
            bases[a].append(0)
            ahead[a].append(front)
    carried = []
    for a in angles:
        out, kept = middle(arrived[a], tuple(bases[a]), column)
        carried.append((exchange(out), kept))
    backs = [exchange(detector(out, row)) for out, _ in carried]
    most, half = CHUNKS // 2, XB // CHUNKS // 2
    rest = (CHUNKS // 4, CHUNKS // 4)
    spans = (most,) + rest

    def home(a, back, first, before, spans):
        t0 = ahead[a][first : first + sum(spans)]
        return leave(place, block_index[a], back, t0, weights[a], row, before, spans)

    early = pull(backs[0], carried[0][1], column, (most, sum(rest)))
    late = pull(backs[1], carried[1][1], column, spans)
    back = exchange(early[0])
    next_back = exchange(late[0])
    (start,) = home(0, back, 0, (), (most,))
    back = exchange(after(early[1], start))
    totals = home(1, next_back, 0, start, (most,))
    next_back = exchange(after(late[1], totals))
    starts = home(0, back, most, (), rest)
    back = exchange(after(late[2], starts))
    totals += home(1, next_back, most, starts[0], rest[:1])
    totals += home(1, back, most + rest[0], starts[1], rest[1:])
    pieces = []
    leaving = [depart(*total) for total in totals]
    total = totals[-1]
    for span, moved in zip(spans, after(leaving, total)):
        lower, upper = settle(*moved, q, b)
        for c in range(span):
            pieces += [v[:, c * half : (c + 1) * half] for v in (lower, upper)]
    return jnp.concatenate(pieces, axis=1)


def transform_table(count_in, count_out, length, orient):
    first = jnp.arange(count_in, dtype=jnp.int32)[:, None]
    second = jnp.arange(count_out, dtype=jnp.int32)[None, :]
    phases = orient * 2.0 * math.pi / length * (first * second % length).astype(jnp.float32)
    cosine = jnp.cos(phases)
    sine_part = jnp.sin(phases)
    return jnp.stack([jnp.stack([cosine, sine_part]), jnp.stack([-sine_part, cosine])])


def twiddle_pair(count_a, count_b, length, orient):
    first = jnp.arange(count_a, dtype=jnp.int32)[:, None]
    second = jnp.arange(count_b, dtype=jnp.int32)[None, :]
    phases = orient * 2.0 * math.pi / length * (first * second % length).astype(jnp.float32)
    return (jnp.cos(phases), jnp.sin(phases))


def spread_turn(peer_count, row_count, slot_count, orient):
    turn_re, turn_im = twiddle_pair(peer_count, row_count, NX, orient)
    shape_three = (row_count, peer_count, slot_count)
    wide_re = jnp.broadcast_to(turn_re.T[:, :, None], shape_three).reshape(
        row_count, peer_count * slot_count
    )
    wide_im = jnp.broadcast_to(turn_im.T[:, :, None], shape_three).reshape(
        row_count, peer_count * slot_count
    )
    return (wide_re, wide_im)


def complex_times(values, real_part, imag_part):
    first = values[:, 0]
    second = values[:, 1]
    return jnp.stack(
        [first * real_part - second * imag_part, first * imag_part + second * real_part], axis=1
    )


def one_hot(index_rows, block_count):
    return (index_rows[..., None] == jnp.arange(block_count, dtype=jnp.int32)).astype(jnp.float32)


def rotate(values, selector, matrices):
    height = values.shape[1]
    blocked = values.reshape(2, height, NB, BLK)
    picked = jnp.einsum("cyni,bsn->cybsi", blocked, selector, precision=PRECISE)
    rotated = jnp.einsum("cybsi,bsio->cybo", picked, matrices, precision=PRECISE)
    return rotated.reshape(2, height, SL, NX)


def rotate_back(values, selector, matrices):
    height = values.shape[1]
    blocked = values.reshape(2, height, NB, BLK)
    spread_out = jnp.einsum("cybo,bsio->cybsi", blocked, matrices, precision=PRECISE)
    summed = jnp.einsum("cybsi,bsn->cyni", spread_out, selector, precision=PRECISE)
    return summed.reshape(2, height, SL * NX)


def fresnel(peer_count, row_count, slot_count, orient):
    position_high = jnp.arange(row_count, dtype=jnp.int32)[:, None]
    position_low = jnp.arange(peer_count, dtype=jnp.int32)[None, :]
    freq_y = position_low + peer_count * position_high
    freq_y = jnp.where(freq_y < NX // 2, freq_y, freq_y - NX)
    position = lax.axis_index("fft") * slot_count + jnp.arange(slot_count, dtype=jnp.int32)
    freq_x = position // XB + XA * (position % XB)
    freq_x = jnp.where(freq_x < NX // 2, freq_x, freq_x - NX)
    squares = ((freq_y * freq_y)[:, :, None] + (freq_x * freq_x)[None, None, :]) % (2 * NX)
    phases = orient * -math.pi / NX * squares.astype(jnp.float32)
    scaling = 1.0 / (NX * NX)
    phases = phases.reshape(row_count, peer_count * slot_count)
    return (jnp.cos(phases) * scaling, jnp.sin(phases) * scaling)


def propagate(fields, kernel, peer_count, row_count, slot_count):
    field_count = fields.shape[0]
    groups = XB // slot_count
    shaped = fields.reshape(field_count, 2, row_count, XA, XB)
    partial_x = jnp.einsum(
        "fcrab,cdak->fdrkb", shaped, transform_table(XA, XA, XA, -1.0), precision=PRECISE
    )
    twist_re, twist_im = twiddle_pair(XA, XB, NX, -1.0)
    partial_x = complex_times(partial_x, twist_re, twist_im)
    partial_x = jnp.einsum(
        "fcrkb,cdbt->fdrkt", partial_x, transform_table(XB, XB, XB, -1.0), precision=PRECISE
    )
    partial_x = partial_x.reshape(field_count, 2, row_count, XA, groups, slot_count)
    outgoing = partial_x.transpose(0, 1, 3, 4, 2, 5).reshape(
        field_count, 2, peer_count, row_count * slot_count
    )
    forward_re, forward_im = spread_turn(peer_count, row_count, slot_count, -1.0)
    inverse_re, inverse_im = spread_turn(peer_count, row_count, slot_count, 1.0)
    wide = peer_count * slot_count
    incoming = lax.all_to_all(outgoing, "fft", split_axis=2, concat_axis=2, tiled=True)
    item_count = incoming.shape[0]
    lattice = incoming.reshape(item_count, 2, peer_count, row_count, slot_count)
    lattice = jnp.einsum(
        "fcprs,cdpk->fdrks",
        lattice,
        transform_table(peer_count, peer_count, peer_count, -1.0),
        precision=PRECISE,
    )
    lattice = lattice.reshape(item_count, 2, row_count, wide)
    lattice = complex_times(lattice, forward_re, forward_im)
    lattice = jnp.einsum(
        "fcrq,cdrm->fdmq",
        lattice,
        transform_table(row_count, row_count, row_count, -1.0),
        precision=PRECISE,
    )
    lattice = complex_times(lattice, kernel[0], kernel[1])
    lattice = jnp.einsum(
        "fcmq,cdmr->fdrq",
        lattice,
        transform_table(row_count, row_count, row_count, 1.0),
        precision=PRECISE,
    )
    lattice = complex_times(lattice, inverse_re, inverse_im)
    lattice = lattice.reshape(item_count, 2, row_count, peer_count, slot_count)
    lattice = jnp.einsum(
        "fcrks,cdkp->fdprs",
        lattice,
        transform_table(peer_count, peer_count, peer_count, 1.0),
        precision=PRECISE,
    )
    returning = lax.all_to_all(
        lattice.reshape(item_count, 2, peer_count, row_count * slot_count),
        "fft",
        split_axis=2,
        concat_axis=2,
        tiled=True,
    )
    restored = returning.reshape(item_count, 2, XA, groups, row_count, slot_count)
    matrix_back = transform_table(XB, XB, XB, 1.0).reshape(2, 2, groups, slot_count, XB)
    restored = jnp.einsum("fckjrs,cdjsb->fdrkb", restored, matrix_back, precision=PRECISE)
    back_re, back_im = twiddle_pair(XA, XB, NX, 1.0)
    restored = complex_times(restored, back_re, back_im)
    restored = jnp.einsum(
        "fcrkb,cdkn->fdrnb", restored, transform_table(XA, XA, XA, 1.0), precision=PRECISE
    )
    return restored.reshape(item_count, 2, row_count, NX)


def general_body(potential, direction, block_index, block_weights):
    row_count = potential.shape[1]
    peer_count = lax.axis_size("fft")
    slot_count = NX // peer_count
    ahead = fresnel(peer_count, row_count, slot_count, 1.0)
    behind = fresnel(peer_count, row_count, slot_count, -1.0)
    accumulated = jnp.zeros(potential.shape, jnp.float32)
    for angle_index in range(ANGLES):
        selector = one_hot(block_index[angle_index], NB)
        matrices = block_weights[angle_index]
        rotated = rotate(potential, selector, matrices)
        tangent = rotate(direction, selector, matrices)
        damping = jnp.exp(-rotated[1])
        trans_re = damping * jnp.cos(rotated[0])
        trans_im = damping * jnp.sin(rotated[0])
        wave_re = jnp.ones((row_count, NX), jnp.float32)
        wave_im = jnp.zeros((row_count, NX), jnp.float32)
        dwave_re = jnp.zeros((row_count, NX), jnp.float32)
        dwave_im = jnp.zeros((row_count, NX), jnp.float32)
        stored = []
        for slice_index in range(SL):
            t_re = trans_re[:, slice_index]
            t_im = trans_im[:, slice_index]
            d_re = tangent[0][:, slice_index]
            d_im = tangent[1][:, slice_index]
            phi_re = t_re * wave_re - t_im * wave_im
            phi_im = t_re * wave_im + t_im * wave_re
            dphi_re = -(d_re * phi_im + d_im * phi_re) + t_re * dwave_re - t_im * dwave_im
            dphi_im = d_re * phi_re - d_im * phi_im + t_re * dwave_im + t_im * dwave_re
            stored.append((phi_re, phi_im))
            packed = jnp.stack([jnp.stack([phi_re, phi_im]), jnp.stack([dphi_re, dphi_im])])
            propagated = propagate(packed, ahead, peer_count, row_count, slot_count)
            wave_re = propagated[0, 0]
            wave_im = propagated[0, 1]
            dwave_re = propagated[1, 0]
            dwave_im = propagated[1, 1]
        change = 2.0 * (wave_re * dwave_re + wave_im * dwave_im)
        back_re = 2.0 * change * wave_re
        back_im = 2.0 * change * wave_im
        grad_re = [None] * SL
        grad_im = [None] * SL
        for slice_index in reversed(range(SL)):
            pulled = propagate(
                jnp.stack([back_re, back_im])[None], behind, peer_count, row_count, slot_count
            )
            pb_re = pulled[0, 0]
            pb_im = pulled[0, 1]
            phi_re, phi_im = stored[slice_index]
            grad_re[slice_index] = phi_re * pb_im - phi_im * pb_re
            grad_im[slice_index] = -(phi_re * pb_re + phi_im * pb_im)
            t_re = trans_re[:, slice_index]
            t_im = trans_im[:, slice_index]
            back_re = t_re * pb_re + t_im * pb_im
            back_im = t_re * pb_im - t_im * pb_re
        gradient = jnp.stack([jnp.stack(grad_re, axis=1), jnp.stack(grad_im, axis=1)])
        accumulated = accumulated + rotate_back(gradient, selector, matrices)
    return accumulated


def body(potential, direction, block_index, block_weights):
    if lax.axis_size("parts") == 2 and lax.axis_size("fft") == XA:
        return blocked_body(potential, direction, block_index, block_weights)
    return general_body(potential, direction, block_index, block_weights)


def solution(mesh):
    return jax.shard_map(
        body,
        mesh=mesh,
        in_specs=(P("parts", "fft", None), P("parts", "fft", None), P(), P()),
        out_specs=P("parts", "fft", None),
        check_vma=False,
    )
```

```python
import functools
import math

import jax
import jax.numpy as jnp
import numpy as np
from jax import lax
from jax.experimental import pallas as pl
from jax.experimental.pallas import tpu as pltpu
from jax.sharding import PartitionSpec as P

XA = 16
XB = 128
NX = 2048
SL = 2
ANGLES = 2
BLK = 128
NB = 32
SLOTS = 2
STRIP = 16
LANES = 128
CHUNKS = 4
HALF = XA // 2


PRECISE = lax.Precision.HIGHEST


def bin_matrices():
    wavenumber = np.arange(NX)
    signed = np.where(wavenumber < NX // 2, wavenumber, wavenumber - NX)
    factor = np.exp(-1j * np.pi / NX * ((signed * signed) % (2 * NX)))
    line = np.fft.ifft(factor)
    block = np.arange(XA)
    inner = np.arange(XB)
    shifts = (XB * block[:, None, None] + inner[None, :, None] - inner[None, None, :]) % NX
    phases = np.exp(-2j * np.pi / XA * ((block[:, None] * block[None, :]) % XA))
    return np.einsum("kd,dij->kij", phases, line[shifts]) / XA


def split_constant(values):
    values = values.astype(np.float32)
    high = values.astype(jnp.bfloat16)
    low = (values - high.astype(np.float32)).astype(jnp.bfloat16)
    return high, low


def column_constants():
    bins = bin_matrices()
    top = np.concatenate([bins.real, -bins.imag], axis=2)
    bottom = np.concatenate([bins.imag, bins.real], axis=2)
    return np.concatenate([top, bottom], axis=1)


def fourth(values, orient):
    (ar, ai), (br, bi), (cr, ci), (dr, di) = values
    sr, si, er, ei = ar + cr, ai + ci, ar - cr, ai - ci
    tr, ti, fr, fi = br + dr, bi + di, br - dr, bi - di
    minus, plus = (er + fi, ei - fr), (er - fi, ei + fr)
    one, three = (minus, plus) if orient < 0 else (plus, minus)
    return [(sr + tr, si + ti), one, (sr - tr, si - ti), three]


def turned(value, step, orient):
    re, im = value
    if step == 0:
        return value
    if step == 4:
        return (im, -re) if orient < 0 else (-im, re)
    cosine = math.cos(2.0 * math.pi * step / XA)
    sine = orient * math.sin(2.0 * math.pi * step / XA)
    if step == 2:
        root = cosine
        return ((re - im) * root, (re + im) * root) if orient > 0 else ((re + im) * root, (im - re) * root)
    return (re * cosine - im * sine, re * sine + im * cosine)


def sixteenth(values, orient):
    inner = [fourth([values[4 * a + b] for a in range(4)], orient) for b in range(4)]
    out = [None] * XA
    for c in range(4):
        row = fourth([turned(inner[b][c], b * c, orient) for b in range(4)], orient)
        for d in range(4):
            out[c + 4 * d] = row[d]
    return out


def halves(value):
    high = value.astype(jnp.bfloat16)
    return high, (value - high.astype(jnp.float32)).astype(jnp.bfloat16)


def dot32(a, b):
    return jnp.dot(a, b, preferred_element_type=jnp.float32)


def split_dot(high, low, whi, wlo):
    count = high.shape[0]
    both = dot32(jnp.concatenate([high, low], axis=0), whi)
    return both[:count] + (both[count:] + dot32(high, wlo))


def times(a, b):
    return (a[0] * b[0] - a[1] * b[1], a[0] * b[1] + a[1] * b[0])


def sincos(x):
    turns = jnp.floor(x * (2.0 / math.pi) + 0.5)
    rest = ((x - turns * 1.5703125) - turns * 4.837512969970703125e-4) - turns * 7.54978995489188216e-8
    square = rest * rest
    sine = rest + rest * square * (
        -1.6666654611e-1 + square * (8.3321608736e-3 + square * -1.9515295891e-4)
    )
    cosine = (1.0 - 0.5 * square) + square * square * (
        4.166664568298827e-2 + square * (-1.388731625493765e-3 + square * 2.443315711809948e-5)
    )
    quadrant = turns.astype(jnp.int32)
    odd = (quadrant & 1) == 1
    first = jnp.where(odd, cosine, sine)
    second = jnp.where(odd, sine, cosine)
    first = jnp.where((quadrant & 2) == 2, -first, first)
    second = jnp.where(((quadrant + 1) & 2) == 2, -second, second)
    return first, second


def strips(count, step):
    def run(i, carry):
        step(pl.multiple_of(i * STRIP, STRIP))
        return carry

    lax.fori_loop(0, count // STRIP, run, 0)


def rows_out(xhi, xlo, first_row, values):
    for k, (re, im) in enumerate(sixteenth(values, -1.0)):
        for part, value in enumerate((re, im)):
            high, low = halves(value)
            at = (k, pl.ds(first_row, STRIP), pl.ds(part * LANES, LANES))
            xhi[at] = high
            xlo[at] = low


def rows_in(y, first_row):
    values = [
        tuple(y[k, pl.ds(first_row, STRIP), pl.ds(part * LANES, LANES)] for part in range(2))
        for k in range(XA)
    ]
    return sixteenth(values, 1.0)


def rows_mix(xhi, xlo, mhi, mlo, y):
    def step(k, carry):
        y[k] = split_dot(xhi[k], xlo[k], mhi[k], mlo[k])
        return carry

    lax.fori_loop(0, XA, step, 0)


def columns_out(xhi, xlo, field, row, values):
    for k, (re, im) in enumerate(sixteenth(values, -1.0)):
        for part, value in enumerate((re, im)):
            high, low = halves(value)
            at = (k, pl.ds(part * XB + row, STRIP), pl.ds(field * LANES, LANES))
            xhi[at] = high
            xlo[at] = low


def columns_in(y, field, row):
    values = [
        tuple(
            y[k, pl.ds(part * XB + row, STRIP), pl.ds(field * LANES, LANES)] for part in range(2)
        )
        for k in range(XA)
    ]
    return sixteenth(values, 1.0)


def columns_mix(xhi, xlo, mhi, mlo, y):
    def step(k, carry):
        both = dot32(jnp.concatenate([mhi[k], mlo[k]], axis=0), xhi[k])
        y[k] = both[: 2 * XB] + (both[2 * XB :] + dot32(mhi[k], xlo[k]))
        return carry

    lax.fori_loop(0, XA, step, 0)


def enter_kernel(angles, place, *refs):
    indices, (own, other), refs = refs[:angles], refs[angles : angles + 2], refs[angles + 2 :]
    weights, (mhi, mlo, out), refs = refs[: 2 * angles], refs[2 * angles : 2 * angles + 3], refs[2 * angles + 3 :]
    fronts, (shi, slo, field, xhi, xlo, y) = refs[:angles], refs[angles:]
    half = own.shape[1]
    rows = 2 * half

    for number in range(4):
        for piece, side in ((own, place[0]), (other, 1 - place[0])):

            def cut(row, number=number, piece=piece, side=side):
                high, low = halves(piece[number, pl.ds(row, STRIP), :])
                first = number * rows + side * half + row
                at = pl.ds(pl.multiple_of(first, STRIP), STRIP)
                shi[at, :] = high
                slo[at, :] = low

            strips(half, cut)

    for a in range(angles):
        enter_angle(
            indices[a], weights[2 * a], weights[2 * a + 1], mhi, mlo,
            out, 8 * a, fronts[a], shi, slo, field, xhi, xlo, y,
        )


def enter_angle(index, whi, wlo, mhi, mlo, out, base, t0, shi, slo, field, xhi, xlo, y):
    rows = t0.shape[2]

    def rotated(b):
        at = [pl.ds(pl.multiple_of(index[b, s] * BLK, BLK), BLK) for s in range(SLOTS)]
        high = jnp.concatenate([shi[:, a] for a in at], axis=1)
        low = jnp.concatenate([slo[:, a] for a in at], axis=1)
        values = split_dot(high, low, whi[b], wlo[b])
        angle, loss, d_re, d_im = (values[i * rows : (i + 1) * rows] for i in range(4))
        sine, cosine = sincos(angle)
        damping = jnp.exp(-loss)
        return damping * cosine, damping * sine, d_re, d_im

    def first_slice(b, carry):
        t_re, t_im, d_re, d_im = rotated(b)
        t0[b, 0] = t_re
        t0[b, 1] = t_im
        field[b, 0] = -(d_re * t_im + d_im * t_re)
        field[b, 1] = d_re * t_re - d_im * t_im
        return carry

    lax.fori_loop(0, XA, first_slice, 0)

    def forward(row):
        at = pl.ds(row, STRIP)
        rows_out(xhi, xlo, row, [(t0[b, 0, at, :], t0[b, 1, at, :]) for b in range(XA)])
        rows_out(
            xhi,
            xlo,
            pl.multiple_of(rows + row, STRIP),
            [(field[b, 0, at, :], field[b, 1, at, :]) for b in range(XA)],
        )

    strips(rows, forward)
    rows_mix(xhi, xlo, mhi, mlo, y)

    def backward(row):
        at = pl.ds(row, STRIP)
        for number in range(2):
            values = rows_in(y, pl.multiple_of(number * rows + row, STRIP))
            for b, (re, im) in enumerate(values):
                out[b, base + 2 * number, at, :] = re
                out[b, base + 2 * number + 1, at, :] = im

    strips(rows, backward)

    def second_slice(b, carry):
        for channel, value in enumerate(rotated(XA + b)):
            out[b, base + 4 + channel] = value
        return carry

    lax.fori_loop(0, XA, second_slice, 0)


def by_pieces(spans, step):
    half = XB // CHUNKS // 2
    pieces = [(piece, c) for piece, span in enumerate(spans) for c in range(span)]
    for chunk, (piece, c) in enumerate(pieces):
        for x in range(2):

            def inner(row, chunk=chunk, piece=piece, c=c, x=x):
                places = []
                for p in range(XA):
                    first = (2 * c + p // HALF) * half
                    at = pl.ds(pl.multiple_of(first + row, STRIP), STRIP)
                    places.append((piece, x * HALF + p % HALF, at))
                step(pl.multiple_of((2 * chunk + x) * half + row, STRIP), places)

            strips(half, inner)


def middle_kernel(bases, *refs):
    chunks = len(bases)
    arrived = refs[:chunks]
    mhi, mlo, out, kept, xhi, xlo, y = refs[chunks:]

    def forward(row, places):
        for number in range(2):
            values = [
                tuple(arrived[c][g, bases[c] + 2 * number + i, at, :] for i in range(2)) for c, g, at in places
            ]
            columns_out(xhi, xlo, number, row, values)

    by_pieces((1,) * chunks, forward)
    columns_mix(xhi, xlo, mhi, mlo, y)

    def turn(row, places):
        local = pl.ds(row, STRIP)
        wave = columns_in(y, 0, row)
        product = []
        for p, (c, g, at) in enumerate(places):
            t = tuple(arrived[c][g, bases[c] + i, at, :] for i in (4, 5))
            value = times(t, wave[p])
            for i, part in enumerate(value + t):
                kept[p, i, local, :] = part
            product.append(value)
        columns_out(xhi, xlo, 0, row, product)
        dwave = columns_in(y, 1, row)
        change = []
        for p, (c, g, at) in enumerate(places):
            t_re, t_im, d_re, d_im = (arrived[c][g, bases[c] + 4 + i, at, :] for i in range(4))
            p_re, p_im = kept[p, 0, local, :], kept[p, 1, local, :]
            re, im = times((t_re, t_im), dwave[p])
            change.append((re - (d_re * p_im + d_im * p_re), im + (d_re * p_re - d_im * p_im)))
        columns_out(xhi, xlo, 1, row, change)

    by_pieces((1,) * chunks, turn)
    columns_mix(xhi, xlo, mhi, mlo, y)

    def backward(row, places):
        for number in range(2):
            for (_, g, at), (re, im) in zip(places, columns_in(y, number, row)):
                out[g, 2 * number, at, :] = re
                out[g, 2 * number + 1, at, :] = im

    by_pieces((CHUNKS,), backward)


def detector_kernel(fields, mhi, mlo, out, xhi, xlo, y):
    rows = fields.shape[2]

    def forward(row):
        at = pl.ds(row, STRIP)
        for number in range(2):
            rows_out(
                xhi,
                xlo,
                pl.multiple_of(number * rows + row, STRIP),
                [tuple(fields[b, 2 * number + i, at, :] for i in range(2)) for b in range(XA)],
            )

    strips(rows, forward)
    rows_mix(xhi, xlo, mhi, mlo, y)

    def turn(row):
        wave = rows_in(y, row)
        dwave = rows_in(y, pl.multiple_of(rows + row, STRIP))
        back = []
        for (re, im), (d_re, d_im) in zip(wave, dwave):
            change = 4.0 * (re * d_re + im * d_im)
            back.append((change * re, -(change * im)))
        rows_out(xhi, xlo, row, back)

    strips(rows, turn)

    def step(k, carry):
        y[k, :rows, :] = split_dot(xhi[k, :rows, :], xlo[k, :rows, :], mhi[k], mlo[k])
        return carry

    lax.fori_loop(0, XA, step, 0)

    def backward(row):
        at = pl.ds(row, STRIP)
        for b, (re, im) in enumerate(rows_in(y, row)):
            out[b, 0, at, :] = re
            out[b, 1, at, :] = im

    strips(rows, backward)


def return_kernel(spans, back, kept, mhi, mlo, *refs):
    out, (xhi, xlo, y) = refs[: len(spans)], refs[len(spans) :]

    def forward(row, places):
        values = [(back[g, 0, at, :], back[g, 1, at, :]) for _, g, at in places]
        columns_out(xhi, xlo, 0, row, values)

    by_pieces((CHUNKS,), forward)
    columns_mix(xhi, xlo, mhi, mlo, y)

    def turn(row, places):
        local = pl.ds(row, STRIP)
        pulled = columns_in(y, 0, row)
        following = []
        for p, (c, g, at) in enumerate(places):
            re, im = times((kept[p, 0, local, :], kept[p, 1, local, :]), pulled[p])
            out[c][g, 0, at, :] = -im
            out[c][g, 1, at, :] = -re
            following.append(times((kept[p, 2, local, :], kept[p, 3, local, :]), pulled[p]))
        columns_out(xhi, xlo, 0, row, following)

    by_pieces(spans, turn)
    columns_mix(xhi, xlo, mhi, mlo, y)

    def backward(row, places):
        for (c, g, at), (re, im) in zip(places, columns_in(y, 0, row)):
            out[c][g, 2, at, :] = re
            out[c][g, 3, at, :] = im

    by_pieces(spans, backward)


def leave_kernel(spans, place, index, back, whi, wlo, mhi, mlo, *refs):
    chunks, count = sum(spans), 2 * len(spans)
    t0, refs = refs[:chunks], refs[chunks:]
    before, outs, (shi, slo, xhi, xlo, y) = refs[: -count - 5], refs[-count - 5 : -5], refs[-5:]
    chunk = t0[0].shape[2]
    half = chunk // 2
    rows = chunks * chunk
    starts = []

    def pieces_of(step):
        starts.clear()
        done = 0
        for span in spans:
            for end, side in enumerate((1 - place[1], place[1])):
                base = (2 * done + end * span) * half
                starts.append((base, span * half))
                for c in range(span):

                    def inner(row, side=side, c=c, done=done, base=base):
                        within = pl.multiple_of(side * half + row, STRIP)
                        source = pl.multiple_of((done + c) * chunk + side * half + row, STRIP)
                        target = pl.multiple_of(base + c * half + row, STRIP)
                        step(done + c, pl.ds(within, STRIP), pl.ds(source, STRIP), target)

                    strips(half, inner)
            done += span

    def store(b, i, target, value):
        high, low = halves(value)
        at = pl.ds(pl.multiple_of(i * rows + target, STRIP), STRIP)
        shi[b, at, :] = high
        slo[b, at, :] = low

    def forward(c, within, at, target):
        rows_out(xhi, xlo, target, [(back[b, 2, at, :], back[b, 3, at, :]) for b in range(XA)])
        for b in range(XA):
            for i in range(2):
                store(XA + b, i, target, back[b, i, at, :])

    pieces_of(forward)
    rows_mix(xhi, xlo, mhi, mlo, y)

    def turn(c, within, at, target):
        for b, value in enumerate(rows_in(y, target)):
            re, im = times((t0[c][b, 0, within, :], t0[c][b, 1, within, :]), value)
            store(b, 0, target, -im)
            store(b, 1, target, -re)

    pieces_of(turn)

    for out, old in zip(outs, before or [None] * count):
        out[...] = jnp.zeros(out.shape, jnp.float32) if old is None else old[...]

    def across(a, b):
        return lax.dot_general(
            a, b, (((1,), (1,)), ((), ())), preferred_element_type=jnp.float32
        )

    def step(b, carry):
        high, low = shi[b], slo[b]
        both = across(jnp.concatenate([high, low], axis=0), whi[b])
        values = both[: 2 * rows] + (both[2 * rows :] + across(high, wlo[b]))
        for s in range(SLOTS):
            at = pl.ds(pl.multiple_of(index[b, s] * BLK, BLK), BLK)
            for i in range(2):
                for (start, size), out in zip(starts, outs):
                    start += i * rows
                    out[i, :, at] += values[start : start + size, s * BLK : (s + 1) * BLK]
        return carry

    lax.fori_loop(0, NB, step, 0)


def call(kernel, outs, scratch, mix_count, extra, *operands):
    specs = [
        pl.BlockSpec(memory_space=pltpu.SMEM if o.dtype == jnp.int32 else pltpu.VMEM)
        for o in operands
    ]
    moved = sum(o.size * o.dtype.itemsize for o in operands) + sum(4 * math.prod(o) for o in outs)
    return pl.pallas_call(
        kernel,
        out_shape=[jax.ShapeDtypeStruct(o, jnp.float32) for o in outs],
        in_specs=specs,
        out_specs=[pl.BlockSpec(memory_space=pltpu.VMEM)] * len(outs),
        scratch_shapes=scratch,
        compiler_params=pltpu.CompilerParams(vmem_limit_bytes=60 * 1024 * 1024),
        cost_estimate=pl.CostEstimate(
            flops=int(mix_count * 16 * 128 * 256 * 256 * 6) + extra,
            bytes_accessed=moved,
            transcendentals=0,
        ),
    )(*operands)


def mix_scratch(rows, lanes):
    return [
        pltpu.VMEM((XA, rows, lanes), jnp.bfloat16),
        pltpu.VMEM((XA, rows, lanes), jnp.bfloat16),
        pltpu.VMEM((XA, rows, lanes), jnp.float32),
    ]


def enter(place, indices, own, other, weights, matrices):
    angles = len(indices)
    rows = 2 * own.shape[1]
    scratch = [
        pltpu.VMEM((4 * rows, NB * BLK), jnp.bfloat16),
        pltpu.VMEM((4 * rows, NB * BLK), jnp.bfloat16),
        pltpu.VMEM((XA, 2, rows, LANES), jnp.float32),
    ] + mix_scratch(2 * rows, 2 * LANES)
    fields, *fronts = call(
        functools.partial(enter_kernel, angles),
        [(XA, 8 * angles, rows, LANES)] + [(XA, 2, rows, LANES)] * angles,
        scratch,
        rows / XB * 2 * angles,
        NB * 4 * rows * 256 * 128 * 6 * angles,
        place,
        *indices,
        own,
        other,
        *[w for pair in weights for w in pair],
        *matrices,
    )
    return fields, fronts


def middle(arrived, bases, matrices):
    return call(
        functools.partial(middle_kernel, bases),
        [(XA, 4, XB, LANES), (XA, 4, XB, LANES)],
        mix_scratch(2 * XB, 2 * LANES),
        4,
        0,
        *arrived,
        *matrices,
    )


def detector(fields, matrices):
    rows = fields.shape[2]
    return call(
        detector_kernel,
        [(XA, 2, rows, LANES)],
        mix_scratch(2 * rows, 2 * LANES),
        3,
        0,
        fields,
        *matrices,
    )[0]


def pull(back, kept, matrices, spans):
    return call(
        functools.partial(return_kernel, spans),
        [(XA, 4, span * XB // CHUNKS, LANES) for span in spans],
        mix_scratch(2 * XB, LANES),
        2,
        0,
        back,
        kept,
        *matrices,
    )


def leave(place, index, back, t0, weights, matrices, before, spans):
    rows = sum(t.shape[2] for t in t0)
    scratch = [
        pltpu.VMEM((NB, 2 * rows, LANES), jnp.bfloat16),
        pltpu.VMEM((NB, 2 * rows, LANES), jnp.bfloat16),
    ] + mix_scratch(rows, 2 * LANES)
    extra = NB * 2 * rows * 256 * 128 * 6
    outs = call(
        functools.partial(leave_kernel, spans),
        [(2, span * XB // CHUNKS // 2, NB * BLK) for span in spans for _ in range(2)],
        scratch,
        rows / XB,
        extra,
        place,
        index,
        back,
        *weights,
        *matrices,
        *t0,
        *before,
    )
    return [outs[2 * i : 2 * i + 2] for i in range(len(spans))]


def split_weights(block_weights):
    stacked = block_weights.reshape(ANGLES, NB, SLOTS * BLK, BLK)
    rounded = lax.reduce_precision(stacked, 8, 7)
    return rounded.astype(jnp.bfloat16), (stacked - rounded).astype(jnp.bfloat16)


def device(q, b, r):
    return q * XA + b * HALF + r


def exchange(values):
    return lax.all_to_all(
        values,
        ("parts", "fft"),
        split_axis=0,
        concat_axis=0,
        axis_index_groups=[[device(x, b, r) for x in range(2) for r in range(HALF)] for b in range(2)],
        tiled=True,
    )


def permute(values, steps):
    pairs = [
        (device(*here, r), device(*there, r)) for here, there in steps for r in range(HALF)
    ]
    return lax.ppermute(values, ("parts", "fft"), pairs)


BESIDE = [((q, b), (1 - q, b)) for q in range(2) for b in range(2)]
ALONG = [((q, b), (q, 1 - b)) for q in range(2) for b in range(2)]
CYCLE = [((0, 0), (0, 1)), ((1, 0), (0, 0)), ((1, 1), (1, 0)), ((0, 1), (1, 1))]
ACROSS = [((0, 1), (1, 0)), ((1, 0), (0, 1))]


def after(values, others):
    return lax.optimization_barrier((values, others))[0]


def arrive(potential, direction, q, b):
    half = XB // CHUNKS // 2

    def sides(c):
        lower, upper = (
            jnp.concatenate(
                [v[:, (2 * c + x) * half : (2 * c + x + 1) * half] for v in (potential, direction)]
            )
            for x in range(2)
        )
        return jnp.where(q == 0, lower, upper), jnp.where(q == 0, upper, lower)

    keep, give = sides(0)
    potential, direction = after((potential, direction), give)
    beside = permute(give, BESIDE)
    kept, given = zip(*[sides(c) for c in range(1, CHUNKS)])
    rest = permute(after(jnp.concatenate(given), beside), BESIDE)
    chunks = []
    along = ()
    for c in range(CHUNKS):
        if c:
            keep, beside = kept[c - 1], rest[4 * (c - 1) : 4 * c]
        own = jnp.where(q == b, keep, beside)
        give = jnp.where(q == b, beside, keep)
        along = permute(after(give, along), ALONG)
        chunks.append((own, along))
    return chunks


def depart(near, far):
    return permute(near, CYCLE), permute(far, ACROSS), far


def settle(once, twice, far, q, b):
    same = jnp.where(q == b, far, once)
    rest = jnp.where(q == b, once, twice)
    return jnp.where(q == 0, same, rest), jnp.where(q == 0, rest, same)


def blocked_body(potential, direction, block_index, block_weights):
    q = lax.axis_index("parts")
    b = lax.axis_index("fft") // HALF
    place = jnp.stack([b, q]).astype(jnp.int32)
    chunks = arrive(potential, direction, q, b)
    whi, wlo = split_weights(block_weights)
    by_column = column_constants()
    column = tuple(jnp.asarray(v) for v in split_constant(by_column))
    row = tuple(jnp.asarray(v) for v in split_constant(by_column.transpose(0, 2, 1)))
    weights = [(whi[a], wlo[a]) for a in range(ANGLES)]
    angles = range(ANGLES)
    arrived = [[] for _ in angles]
    bases = [[] for _ in angles]
    ahead = [[] for _ in angles]
    fields = ()
    for c, (own, along) in enumerate(chunks):
        further = chunks[c + 1][1] if c + 1 < CHUNKS else ()
        own = after(own, fields)
        for a in angles:
            fields, (front,) = enter(place, [block_index[a]], own, along, [weights[a]], row)
            arrived[a].append(exchange(after(fields, further) if a else fields))
            bases[a].append(0)
            ahead[a].append(front)
    carried = []
    for a in angles:
        out, kept = middle(arrived[a], tuple(bases[a]), column)
        carried.append((exchange(out), kept))
    backs = [exchange(detector(out, row)) for out, _ in carried]
    most, half = CHUNKS // 2, XB // CHUNKS // 2
    spans = (most, CHUNKS - most)

    def home(a, back, first, before, spans):
        t0 = ahead[a][first : first + sum(spans)]
        return leave(place, block_index[a], back, t0, weights[a], row, before, spans)

    early = pull(backs[0], carried[0][1], column, (CHUNKS,))
    late = pull(backs[1], carried[1][1], column, spans)
    back = exchange(early[0])
    next_back = exchange(late[0])
    starts = home(0, back, 0, (), spans)
    back = exchange(after(late[1], starts))
    totals = home(1, next_back, 0, starts[0], spans[:1])
    totals += home(1, back, most, starts[1], spans[1:])
    pieces = []
    leaving = [depart(*total) for total in totals]
    total = totals[-1]
    for span, moved in zip(spans, after(leaving, total)):
        lower, upper = settle(*moved, q, b)
        for c in range(span):
            pieces += [v[:, c * half : (c + 1) * half] for v in (lower, upper)]
    return jnp.concatenate(pieces, axis=1)


def transform_table(count_in, count_out, length, orient):
    first = jnp.arange(count_in, dtype=jnp.int32)[:, None]
    second = jnp.arange(count_out, dtype=jnp.int32)[None, :]
    phases = orient * 2.0 * math.pi / length * (first * second % length).astype(jnp.float32)
    cosine = jnp.cos(phases)
    sine_part = jnp.sin(phases)
    return jnp.stack([jnp.stack([cosine, sine_part]), jnp.stack([-sine_part, cosine])])


def twiddle_pair(count_a, count_b, length, orient):
    first = jnp.arange(count_a, dtype=jnp.int32)[:, None]
    second = jnp.arange(count_b, dtype=jnp.int32)[None, :]
    phases = orient * 2.0 * math.pi / length * (first * second % length).astype(jnp.float32)
    return (jnp.cos(phases), jnp.sin(phases))


def spread_turn(peer_count, row_count, slot_count, orient):
    turn_re, turn_im = twiddle_pair(peer_count, row_count, NX, orient)
    shape_three = (row_count, peer_count, slot_count)
    wide_re = jnp.broadcast_to(turn_re.T[:, :, None], shape_three).reshape(
        row_count, peer_count * slot_count
    )
    wide_im = jnp.broadcast_to(turn_im.T[:, :, None], shape_three).reshape(
        row_count, peer_count * slot_count
    )
    return (wide_re, wide_im)


def complex_times(values, real_part, imag_part):
    first = values[:, 0]
    second = values[:, 1]
    return jnp.stack(
        [first * real_part - second * imag_part, first * imag_part + second * real_part], axis=1
    )


def one_hot(index_rows, block_count):
    return (index_rows[..., None] == jnp.arange(block_count, dtype=jnp.int32)).astype(jnp.float32)


def rotate(values, selector, matrices):
    height = values.shape[1]
    blocked = values.reshape(2, height, NB, BLK)
    picked = jnp.einsum("cyni,bsn->cybsi", blocked, selector, precision=PRECISE)
    rotated = jnp.einsum("cybsi,bsio->cybo", picked, matrices, precision=PRECISE)
    return rotated.reshape(2, height, SL, NX)


def rotate_back(values, selector, matrices):
    height = values.shape[1]
    blocked = values.reshape(2, height, NB, BLK)
    spread_out = jnp.einsum("cybo,bsio->cybsi", blocked, matrices, precision=PRECISE)
    summed = jnp.einsum("cybsi,bsn->cyni", spread_out, selector, precision=PRECISE)
    return summed.reshape(2, height, SL * NX)


def fresnel(peer_count, row_count, slot_count, orient):
    position_high = jnp.arange(row_count, dtype=jnp.int32)[:, None]
    position_low = jnp.arange(peer_count, dtype=jnp.int32)[None, :]
    freq_y = position_low + peer_count * position_high
    freq_y = jnp.where(freq_y < NX // 2, freq_y, freq_y - NX)
    position = lax.axis_index("fft") * slot_count + jnp.arange(slot_count, dtype=jnp.int32)
    freq_x = position // XB + XA * (position % XB)
    freq_x = jnp.where(freq_x < NX // 2, freq_x, freq_x - NX)
    squares = ((freq_y * freq_y)[:, :, None] + (freq_x * freq_x)[None, None, :]) % (2 * NX)
    phases = orient * -math.pi / NX * squares.astype(jnp.float32)
    scaling = 1.0 / (NX * NX)
    phases = phases.reshape(row_count, peer_count * slot_count)
    return (jnp.cos(phases) * scaling, jnp.sin(phases) * scaling)


def propagate(fields, kernel, peer_count, row_count, slot_count):
    field_count = fields.shape[0]
    groups = XB // slot_count
    shaped = fields.reshape(field_count, 2, row_count, XA, XB)
    partial_x = jnp.einsum(
        "fcrab,cdak->fdrkb", shaped, transform_table(XA, XA, XA, -1.0), precision=PRECISE
    )
    twist_re, twist_im = twiddle_pair(XA, XB, NX, -1.0)
    partial_x = complex_times(partial_x, twist_re, twist_im)
    partial_x = jnp.einsum(
        "fcrkb,cdbt->fdrkt", partial_x, transform_table(XB, XB, XB, -1.0), precision=PRECISE
    )
    partial_x = partial_x.reshape(field_count, 2, row_count, XA, groups, slot_count)
    outgoing = partial_x.transpose(0, 1, 3, 4, 2, 5).reshape(
        field_count, 2, peer_count, row_count * slot_count
    )
    forward_re, forward_im = spread_turn(peer_count, row_count, slot_count, -1.0)
    inverse_re, inverse_im = spread_turn(peer_count, row_count, slot_count, 1.0)
    wide = peer_count * slot_count
    incoming = lax.all_to_all(outgoing, "fft", split_axis=2, concat_axis=2, tiled=True)
    item_count = incoming.shape[0]
    lattice = incoming.reshape(item_count, 2, peer_count, row_count, slot_count)
    lattice = jnp.einsum(
        "fcprs,cdpk->fdrks",
        lattice,
        transform_table(peer_count, peer_count, peer_count, -1.0),
        precision=PRECISE,
    )
    lattice = lattice.reshape(item_count, 2, row_count, wide)
    lattice = complex_times(lattice, forward_re, forward_im)
    lattice = jnp.einsum(
        "fcrq,cdrm->fdmq",
        lattice,
        transform_table(row_count, row_count, row_count, -1.0),
        precision=PRECISE,
    )
    lattice = complex_times(lattice, kernel[0], kernel[1])
    lattice = jnp.einsum(
        "fcmq,cdmr->fdrq",
        lattice,
        transform_table(row_count, row_count, row_count, 1.0),
        precision=PRECISE,
    )
    lattice = complex_times(lattice, inverse_re, inverse_im)
    lattice = lattice.reshape(item_count, 2, row_count, peer_count, slot_count)
    lattice = jnp.einsum(
        "fcrks,cdkp->fdprs",
        lattice,
        transform_table(peer_count, peer_count, peer_count, 1.0),
        precision=PRECISE,
    )
    returning = lax.all_to_all(
        lattice.reshape(item_count, 2, peer_count, row_count * slot_count),
        "fft",
        split_axis=2,
        concat_axis=2,
        tiled=True,
    )
    restored = returning.reshape(item_count, 2, XA, groups, row_count, slot_count)
    matrix_back = transform_table(XB, XB, XB, 1.0).reshape(2, 2, groups, slot_count, XB)
    restored = jnp.einsum("fckjrs,cdjsb->fdrkb", restored, matrix_back, precision=PRECISE)
    back_re, back_im = twiddle_pair(XA, XB, NX, 1.0)
    restored = complex_times(restored, back_re, back_im)
    restored = jnp.einsum(
        "fcrkb,cdkn->fdrnb", restored, transform_table(XA, XA, XA, 1.0), precision=PRECISE
    )
    return restored.reshape(item_count, 2, row_count, NX)


def general_body(potential, direction, block_index, block_weights):
    row_count = potential.shape[1]
    peer_count = lax.axis_size("fft")
    slot_count = NX // peer_count
    ahead = fresnel(peer_count, row_count, slot_count, 1.0)
    behind = fresnel(peer_count, row_count, slot_count, -1.0)
    accumulated = jnp.zeros(potential.shape, jnp.float32)
    for angle_index in range(ANGLES):
        selector = one_hot(block_index[angle_index], NB)
        matrices = block_weights[angle_index]
        rotated = rotate(potential, selector, matrices)
        tangent = rotate(direction, selector, matrices)
        damping = jnp.exp(-rotated[1])
        trans_re = damping * jnp.cos(rotated[0])
        trans_im = damping * jnp.sin(rotated[0])
        wave_re = jnp.ones((row_count, NX), jnp.float32)
        wave_im = jnp.zeros((row_count, NX), jnp.float32)
        dwave_re = jnp.zeros((row_count, NX), jnp.float32)
        dwave_im = jnp.zeros((row_count, NX), jnp.float32)
        stored = []
        for slice_index in range(SL):
            t_re = trans_re[:, slice_index]
            t_im = trans_im[:, slice_index]
            d_re = tangent[0][:, slice_index]
            d_im = tangent[1][:, slice_index]
            phi_re = t_re * wave_re - t_im * wave_im
            phi_im = t_re * wave_im + t_im * wave_re
            dphi_re = -(d_re * phi_im + d_im * phi_re) + t_re * dwave_re - t_im * dwave_im
            dphi_im = d_re * phi_re - d_im * phi_im + t_re * dwave_im + t_im * dwave_re
            stored.append((phi_re, phi_im))
            packed = jnp.stack([jnp.stack([phi_re, phi_im]), jnp.stack([dphi_re, dphi_im])])
            propagated = propagate(packed, ahead, peer_count, row_count, slot_count)
            wave_re = propagated[0, 0]
            wave_im = propagated[0, 1]
            dwave_re = propagated[1, 0]
            dwave_im = propagated[1, 1]
        change = 2.0 * (wave_re * dwave_re + wave_im * dwave_im)
        back_re = 2.0 * change * wave_re
        back_im = 2.0 * change * wave_im
        grad_re = [None] * SL
        grad_im = [None] * SL
        for slice_index in reversed(range(SL)):
            pulled = propagate(
                jnp.stack([back_re, back_im])[None], behind, peer_count, row_count, slot_count
            )
            pb_re = pulled[0, 0]
            pb_im = pulled[0, 1]
            phi_re, phi_im = stored[slice_index]
            grad_re[slice_index] = phi_re * pb_im - phi_im * pb_re
            grad_im[slice_index] = -(phi_re * pb_re + phi_im * pb_im)
            t_re = trans_re[:, slice_index]
            t_im = trans_im[:, slice_index]
            back_re = t_re * pb_re + t_im * pb_im
            back_im = t_re * pb_im - t_im * pb_re
        gradient = jnp.stack([jnp.stack(grad_re, axis=1), jnp.stack(grad_im, axis=1)])
        accumulated = accumulated + rotate_back(gradient, selector, matrices)
    return accumulated


def body(potential, direction, block_index, block_weights):
    if lax.axis_size("parts") == 2 and lax.axis_size("fft") == XA:
        return blocked_body(potential, direction, block_index, block_weights)
    return general_body(potential, direction, block_index, block_weights)


def solution(mesh):
    return jax.shard_map(
        body,
        mesh=mesh,
        in_specs=(P("parts", "fft", None), P("parts", "fft", None), P(), P()),
        out_specs=P("parts", "fft", None),
        check_vma=False,
    )
```

```python
import functools
import math

import jax
import jax.numpy as jnp
import numpy as np
from jax import lax
from jax.experimental import pallas as pl
from jax.experimental.pallas import tpu as pltpu
from jax.sharding import PartitionSpec as P

XA = 16
XB = 128
NX = 2048
SL = 2
ANGLES = 2
BLK = 128
NB = 32
SLOTS = 2
STRIP = 16
LANES = 128
CHUNKS = 4
HALF = XA // 2


PRECISE = lax.Precision.HIGHEST


def bin_matrices():
    wavenumber = np.arange(NX)
    signed = np.where(wavenumber < NX // 2, wavenumber, wavenumber - NX)
    factor = np.exp(-1j * np.pi / NX * ((signed * signed) % (2 * NX)))
    line = np.fft.ifft(factor)
    block = np.arange(XA)
    inner = np.arange(XB)
    shifts = (XB * block[:, None, None] + inner[None, :, None] - inner[None, None, :]) % NX
    phases = np.exp(-2j * np.pi / XA * ((block[:, None] * block[None, :]) % XA))
    return np.einsum("kd,dij->kij", phases, line[shifts]) / XA


def split_constant(values):
    values = values.astype(np.float32)
    high = values.astype(jnp.bfloat16)
    low = (values - high.astype(np.float32)).astype(jnp.bfloat16)
    return high, low


def column_constants():
    bins = bin_matrices()
    top = np.concatenate([bins.real, -bins.imag], axis=2)
    bottom = np.concatenate([bins.imag, bins.real], axis=2)
    return np.concatenate([top, bottom], axis=1)


def fourth(values, orient):
    (ar, ai), (br, bi), (cr, ci), (dr, di) = values
    sr, si, er, ei = ar + cr, ai + ci, ar - cr, ai - ci
    tr, ti, fr, fi = br + dr, bi + di, br - dr, bi - di
    minus, plus = (er + fi, ei - fr), (er - fi, ei + fr)
    one, three = (minus, plus) if orient < 0 else (plus, minus)
    return [(sr + tr, si + ti), one, (sr - tr, si - ti), three]


def turned(value, step, orient):
    re, im = value
    if step == 0:
        return value
    if step == 4:
        return (im, -re) if orient < 0 else (-im, re)
    cosine = math.cos(2.0 * math.pi * step / XA)
    sine = orient * math.sin(2.0 * math.pi * step / XA)
    if step == 2:
        root = cosine
        return ((re - im) * root, (re + im) * root) if orient > 0 else ((re + im) * root, (im - re) * root)
    return (re * cosine - im * sine, re * sine + im * cosine)


def sixteenth(values, orient):
    inner = [fourth([values[4 * a + b] for a in range(4)], orient) for b in range(4)]
    out = [None] * XA
    for c in range(4):
        row = fourth([turned(inner[b][c], b * c, orient) for b in range(4)], orient)
        for d in range(4):
            out[c + 4 * d] = row[d]
    return out


def halves(value):
    high = value.astype(jnp.bfloat16)
    return high, (value - high.astype(jnp.float32)).astype(jnp.bfloat16)


def dot32(a, b):
    return jnp.dot(a, b, preferred_element_type=jnp.float32)


def split_dot(high, low, whi, wlo):
    count = high.shape[0]
    both = dot32(jnp.concatenate([high, low], axis=0), whi)
    return both[:count] + (both[count:] + dot32(high, wlo))


def times(a, b):
    return (a[0] * b[0] - a[1] * b[1], a[0] * b[1] + a[1] * b[0])


def sincos(x):
    turns = jnp.floor(x * (2.0 / math.pi) + 0.5)
    rest = ((x - turns * 1.5703125) - turns * 4.837512969970703125e-4) - turns * 7.54978995489188216e-8
    square = rest * rest
    sine = rest + rest * square * (
        -1.6666654611e-1 + square * (8.3321608736e-3 + square * -1.9515295891e-4)
    )
    cosine = (1.0 - 0.5 * square) + square * square * (
        4.166664568298827e-2 + square * (-1.388731625493765e-3 + square * 2.443315711809948e-5)
    )
    quadrant = turns.astype(jnp.int32)
    odd = (quadrant & 1) == 1
    first = jnp.where(odd, cosine, sine)
    second = jnp.where(odd, sine, cosine)
    first = jnp.where((quadrant & 2) == 2, -first, first)
    second = jnp.where(((quadrant + 1) & 2) == 2, -second, second)
    return first, second


def strips(count, step):
    def run(i, carry):
        step(pl.multiple_of(i * STRIP, STRIP))
        return carry

    lax.fori_loop(0, count // STRIP, run, 0)


def rows_out(xhi, xlo, first_row, values):
    for k, (re, im) in enumerate(sixteenth(values, -1.0)):
        for part, value in enumerate((re, im)):
            high, low = halves(value)
            at = (k, pl.ds(first_row, STRIP), pl.ds(part * LANES, LANES))
            xhi[at] = high
            xlo[at] = low


def rows_in(y, first_row):
    values = [
        tuple(y[k, pl.ds(first_row, STRIP), pl.ds(part * LANES, LANES)] for part in range(2))
        for k in range(XA)
    ]
    return sixteenth(values, 1.0)


def rows_mix(xhi, xlo, mhi, mlo, y):
    def step(k, carry):
        y[k] = split_dot(xhi[k], xlo[k], mhi[k], mlo[k])
        return carry

    lax.fori_loop(0, XA, step, 0)


def columns_out(xhi, xlo, field, row, values):
    for k, (re, im) in enumerate(sixteenth(values, -1.0)):
        for part, value in enumerate((re, im)):
            high, low = halves(value)
            at = (k, pl.ds(part * XB + row, STRIP), pl.ds(field * LANES, LANES))
            xhi[at] = high
            xlo[at] = low


def columns_in(y, field, row):
    values = [
        tuple(
            y[k, pl.ds(part * XB + row, STRIP), pl.ds(field * LANES, LANES)] for part in range(2)
        )
        for k in range(XA)
    ]
    return sixteenth(values, 1.0)


def columns_mix(xhi, xlo, mhi, mlo, y):
    def step(k, carry):
        both = dot32(jnp.concatenate([mhi[k], mlo[k]], axis=0), xhi[k])
        y[k] = both[: 2 * XB] + (both[2 * XB :] + dot32(mhi[k], xlo[k]))
        return carry

    lax.fori_loop(0, XA, step, 0)


def enter_kernel(angles, place, *refs):
    indices, (own, other), refs = refs[:angles], refs[angles : angles + 2], refs[angles + 2 :]
    weights, (mhi, mlo, out), refs = refs[: 2 * angles], refs[2 * angles : 2 * angles + 3], refs[2 * angles + 3 :]
    fronts, (shi, slo, field, xhi, xlo, y) = refs[:angles], refs[angles:]
    half = own.shape[1]
    rows = 2 * half

    for number in range(4):
        for piece, side in ((own, place[0]), (other, 1 - place[0])):

            def cut(row, number=number, piece=piece, side=side):
                high, low = halves(piece[number, pl.ds(row, STRIP), :])
                first = number * rows + side * half + row
                at = pl.ds(pl.multiple_of(first, STRIP), STRIP)
                shi[at, :] = high
                slo[at, :] = low

            strips(half, cut)

    for a in range(angles):
        enter_angle(
            indices[a], weights[2 * a], weights[2 * a + 1], mhi, mlo,
            out, 8 * a, fronts[a], shi, slo, field, xhi, xlo, y,
        )


def enter_angle(index, whi, wlo, mhi, mlo, out, base, t0, shi, slo, field, xhi, xlo, y):
    rows = t0.shape[2]

    def rotated(b):
        at = [pl.ds(pl.multiple_of(index[b, s] * BLK, BLK), BLK) for s in range(SLOTS)]
        high = jnp.concatenate([shi[:, a] for a in at], axis=1)
        low = jnp.concatenate([slo[:, a] for a in at], axis=1)
        values = split_dot(high, low, whi[b], wlo[b])
        angle, loss, d_re, d_im = (values[i * rows : (i + 1) * rows] for i in range(4))
        sine, cosine = sincos(angle)
        damping = jnp.exp(-loss)
        return damping * cosine, damping * sine, d_re, d_im

    def first_slice(b, carry):
        t_re, t_im, d_re, d_im = rotated(b)
        t0[b, 0] = t_re
        t0[b, 1] = t_im
        field[b, 0] = -(d_re * t_im + d_im * t_re)
        field[b, 1] = d_re * t_re - d_im * t_im
        return carry

    lax.fori_loop(0, XA, first_slice, 0)

    def forward(row):
        at = pl.ds(row, STRIP)
        rows_out(xhi, xlo, row, [(t0[b, 0, at, :], t0[b, 1, at, :]) for b in range(XA)])
        rows_out(
            xhi,
            xlo,
            pl.multiple_of(rows + row, STRIP),
            [(field[b, 0, at, :], field[b, 1, at, :]) for b in range(XA)],
        )

    strips(rows, forward)
    rows_mix(xhi, xlo, mhi, mlo, y)

    def backward(row):
        at = pl.ds(row, STRIP)
        for number in range(2):
            values = rows_in(y, pl.multiple_of(number * rows + row, STRIP))
            for b, (re, im) in enumerate(values):
                out[b, base + 2 * number, at, :] = re
                out[b, base + 2 * number + 1, at, :] = im

    strips(rows, backward)

    def second_slice(b, carry):
        for channel, value in enumerate(rotated(XA + b)):
            out[b, base + 4 + channel] = value
        return carry

    lax.fori_loop(0, XA, second_slice, 0)


def by_pieces(spans, step):
    half = XB // CHUNKS // 2
    pieces = [(piece, c) for piece, span in enumerate(spans) for c in range(span)]
    for chunk, (piece, c) in enumerate(pieces):
        for x in range(2):

            def inner(row, chunk=chunk, piece=piece, c=c, x=x):
                places = []
                for p in range(XA):
                    first = (2 * c + p // HALF) * half
                    at = pl.ds(pl.multiple_of(first + row, STRIP), STRIP)
                    places.append((piece, x * HALF + p % HALF, at))
                step(pl.multiple_of((2 * chunk + x) * half + row, STRIP), places)

            strips(half, inner)


def middle_kernel(bases, *refs):
    chunks = len(bases)
    arrived = refs[:chunks]
    mhi, mlo, out, kept, xhi, xlo, y = refs[chunks:]

    def forward(row, places):
        for number in range(2):
            values = [
                tuple(arrived[c][g, bases[c] + 2 * number + i, at, :] for i in range(2)) for c, g, at in places
            ]
            columns_out(xhi, xlo, number, row, values)

    by_pieces((1,) * chunks, forward)
    columns_mix(xhi, xlo, mhi, mlo, y)

    def turn(row, places):
        local = pl.ds(row, STRIP)
        wave = columns_in(y, 0, row)
        product = []
        for p, (c, g, at) in enumerate(places):
            t = tuple(arrived[c][g, bases[c] + i, at, :] for i in (4, 5))
            value = times(t, wave[p])
            for i, part in enumerate(value + t):
                kept[p, i, local, :] = part
            product.append(value)
        columns_out(xhi, xlo, 0, row, product)
        dwave = columns_in(y, 1, row)
        change = []
        for p, (c, g, at) in enumerate(places):
            t_re, t_im, d_re, d_im = (arrived[c][g, bases[c] + 4 + i, at, :] for i in range(4))
            p_re, p_im = kept[p, 0, local, :], kept[p, 1, local, :]
            re, im = times((t_re, t_im), dwave[p])
            change.append((re - (d_re * p_im + d_im * p_re), im + (d_re * p_re - d_im * p_im)))
        columns_out(xhi, xlo, 1, row, change)

    by_pieces((1,) * chunks, turn)
    columns_mix(xhi, xlo, mhi, mlo, y)

    def backward(row, places):
        for number in range(2):
            for (_, g, at), (re, im) in zip(places, columns_in(y, number, row)):
                out[g, 2 * number, at, :] = re
                out[g, 2 * number + 1, at, :] = im

    by_pieces((CHUNKS,), backward)


def detector_kernel(fields, mhi, mlo, out, xhi, xlo, y):
    rows = fields.shape[2]

    def forward(row):
        at = pl.ds(row, STRIP)
        for number in range(2):
            rows_out(
                xhi,
                xlo,
                pl.multiple_of(number * rows + row, STRIP),
                [tuple(fields[b, 2 * number + i, at, :] for i in range(2)) for b in range(XA)],
            )

    strips(rows, forward)
    rows_mix(xhi, xlo, mhi, mlo, y)

    def turn(row):
        wave = rows_in(y, row)
        dwave = rows_in(y, pl.multiple_of(rows + row, STRIP))
        back = []
        for (re, im), (d_re, d_im) in zip(wave, dwave):
            change = 4.0 * (re * d_re + im * d_im)
            back.append((change * re, -(change * im)))
        rows_out(xhi, xlo, row, back)

    strips(rows, turn)

    def step(k, carry):
        y[k, :rows, :] = split_dot(xhi[k, :rows, :], xlo[k, :rows, :], mhi[k], mlo[k])
        return carry

    lax.fori_loop(0, XA, step, 0)

    def backward(row):
        at = pl.ds(row, STRIP)
        for b, (re, im) in enumerate(rows_in(y, row)):
            out[b, 0, at, :] = re
            out[b, 1, at, :] = im

    strips(rows, backward)


def return_kernel(spans, back, kept, mhi, mlo, *refs):
    out, (xhi, xlo, y) = refs[: len(spans)], refs[len(spans) :]

    def forward(row, places):
        values = [(back[g, 0, at, :], back[g, 1, at, :]) for _, g, at in places]
        columns_out(xhi, xlo, 0, row, values)

    by_pieces((CHUNKS,), forward)
    columns_mix(xhi, xlo, mhi, mlo, y)

    def turn(row, places):
        local = pl.ds(row, STRIP)
        pulled = columns_in(y, 0, row)
        following = []
        for p, (c, g, at) in enumerate(places):
            re, im = times((kept[p, 0, local, :], kept[p, 1, local, :]), pulled[p])
            out[c][g, 0, at, :] = -im
            out[c][g, 1, at, :] = -re
            following.append(times((kept[p, 2, local, :], kept[p, 3, local, :]), pulled[p]))
        columns_out(xhi, xlo, 0, row, following)

    by_pieces(spans, turn)
    columns_mix(xhi, xlo, mhi, mlo, y)

    def backward(row, places):
        for (c, g, at), (re, im) in zip(places, columns_in(y, 0, row)):
            out[c][g, 2, at, :] = re
            out[c][g, 3, at, :] = im

    by_pieces(spans, backward)


def leave_kernel(spans, place, index, back, whi, wlo, mhi, mlo, *refs):
    chunks, count = sum(spans), 2 * len(spans)
    t0, refs = refs[:chunks], refs[chunks:]
    before, outs, (shi, slo, xhi, xlo, y) = refs[: -count - 5], refs[-count - 5 : -5], refs[-5:]
    chunk = t0[0].shape[2]
    half = chunk // 2
    rows = chunks * chunk
    starts = []

    def pieces_of(step):
        starts.clear()
        done = 0
        for span in spans:
            for end, side in enumerate((1 - place[1], place[1])):
                base = (2 * done + end * span) * half
                starts.append((base, span * half))
                for c in range(span):

                    def inner(row, side=side, c=c, done=done, base=base):
                        within = pl.multiple_of(side * half + row, STRIP)
                        source = pl.multiple_of((done + c) * chunk + side * half + row, STRIP)
                        target = pl.multiple_of(base + c * half + row, STRIP)
                        step(done + c, pl.ds(within, STRIP), pl.ds(source, STRIP), target)

                    strips(half, inner)
            done += span

    def store(b, i, target, value):
        high, low = halves(value)
        at = pl.ds(pl.multiple_of(i * rows + target, STRIP), STRIP)
        shi[b, at, :] = high
        slo[b, at, :] = low

    def forward(c, within, at, target):
        rows_out(xhi, xlo, target, [(back[b, 2, at, :], back[b, 3, at, :]) for b in range(XA)])
        for b in range(XA):
            for i in range(2):
                store(XA + b, i, target, back[b, i, at, :])

    pieces_of(forward)
    rows_mix(xhi, xlo, mhi, mlo, y)

    def turn(c, within, at, target):
        for b, value in enumerate(rows_in(y, target)):
            re, im = times((t0[c][b, 0, within, :], t0[c][b, 1, within, :]), value)
            store(b, 0, target, -im)
            store(b, 1, target, -re)

    pieces_of(turn)

    for out, old in zip(outs, before or [None] * count):
        out[...] = jnp.zeros(out.shape, jnp.float32) if old is None else old[...]

    def across(a, b):
        return lax.dot_general(
            a, b, (((1,), (1,)), ((), ())), preferred_element_type=jnp.float32
        )

    def step(b, carry):
        high, low = shi[b], slo[b]
        both = across(jnp.concatenate([high, low], axis=0), whi[b])
        values = both[: 2 * rows] + (both[2 * rows :] + across(high, wlo[b]))
        for s in range(SLOTS):
            at = pl.ds(pl.multiple_of(index[b, s] * BLK, BLK), BLK)
            for i in range(2):
                for (start, size), out in zip(starts, outs):
                    start += i * rows
                    out[i, :, at] += values[start : start + size, s * BLK : (s + 1) * BLK]
        return carry

    lax.fori_loop(0, NB, step, 0)


def call(kernel, outs, scratch, mix_count, extra, *operands):
    specs = [
        pl.BlockSpec(memory_space=pltpu.SMEM if o.dtype == jnp.int32 else pltpu.VMEM)
        for o in operands
    ]
    moved = sum(o.size * o.dtype.itemsize for o in operands) + sum(4 * math.prod(o) for o in outs)
    return pl.pallas_call(
        kernel,
        out_shape=[jax.ShapeDtypeStruct(o, jnp.float32) for o in outs],
        in_specs=specs,
        out_specs=[pl.BlockSpec(memory_space=pltpu.VMEM)] * len(outs),
        scratch_shapes=scratch,
        compiler_params=pltpu.CompilerParams(vmem_limit_bytes=60 * 1024 * 1024),
        cost_estimate=pl.CostEstimate(
            flops=int(mix_count * 16 * 128 * 256 * 256 * 6) + extra,
            bytes_accessed=moved,
            transcendentals=0,
        ),
    )(*operands)


def mix_scratch(rows, lanes):
    return [
        pltpu.VMEM((XA, rows, lanes), jnp.bfloat16),
        pltpu.VMEM((XA, rows, lanes), jnp.bfloat16),
        pltpu.VMEM((XA, rows, lanes), jnp.float32),
    ]


def enter(place, indices, own, other, weights, matrices):
    angles = len(indices)
    rows = 2 * own.shape[1]
    scratch = [
        pltpu.VMEM((4 * rows, NB * BLK), jnp.bfloat16),
        pltpu.VMEM((4 * rows, NB * BLK), jnp.bfloat16),
        pltpu.VMEM((XA, 2, rows, LANES), jnp.float32),
    ] + mix_scratch(2 * rows, 2 * LANES)
    fields, *fronts = call(
        functools.partial(enter_kernel, angles),
        [(XA, 8 * angles, rows, LANES)] + [(XA, 2, rows, LANES)] * angles,
        scratch,
        rows / XB * 2 * angles,
        NB * 4 * rows * 256 * 128 * 6 * angles,
        place,
        *indices,
        own,
        other,
        *[w for pair in weights for w in pair],
        *matrices,
    )
    return fields, fronts


def middle(arrived, bases, matrices):
    return call(
        functools.partial(middle_kernel, bases),
        [(XA, 4, XB, LANES), (XA, 4, XB, LANES)],
        mix_scratch(2 * XB, 2 * LANES),
        4,
        0,
        *arrived,
        *matrices,
    )


def detector(fields, matrices):
    rows = fields.shape[2]
    return call(
        detector_kernel,
        [(XA, 2, rows, LANES)],
        mix_scratch(2 * rows, 2 * LANES),
        3,
        0,
        fields,
        *matrices,
    )[0]


def pull(back, kept, matrices, spans):
    return call(
        functools.partial(return_kernel, spans),
        [(XA, 4, span * XB // CHUNKS, LANES) for span in spans],
        mix_scratch(2 * XB, LANES),
        2,
        0,
        back,
        kept,
        *matrices,
    )


def leave(place, index, back, t0, weights, matrices, before, spans):
    rows = sum(t.shape[2] for t in t0)
    scratch = [
        pltpu.VMEM((NB, 2 * rows, LANES), jnp.bfloat16),
        pltpu.VMEM((NB, 2 * rows, LANES), jnp.bfloat16),
    ] + mix_scratch(rows, 2 * LANES)
    extra = NB * 2 * rows * 256 * 128 * 6
    outs = call(
        functools.partial(leave_kernel, spans),
        [(2, span * XB // CHUNKS // 2, NB * BLK) for span in spans for _ in range(2)],
        scratch,
        rows / XB,
        extra,
        place,
        index,
        back,
        *weights,
        *matrices,
        *t0,
        *before,
    )
    return [outs[2 * i : 2 * i + 2] for i in range(len(spans))]


def split_weights(block_weights):
    stacked = block_weights.reshape(ANGLES, NB, SLOTS * BLK, BLK)
    rounded = lax.reduce_precision(stacked, 8, 7)
    return rounded.astype(jnp.bfloat16), (stacked - rounded).astype(jnp.bfloat16)


def device(q, b, r):
    return q * XA + b * HALF + r


def exchange(values):
    return lax.all_to_all(
        values,
        ("parts", "fft"),
        split_axis=0,
        concat_axis=0,
        axis_index_groups=[[device(x, b, r) for x in range(2) for r in range(HALF)] for b in range(2)],
        tiled=True,
    )


def permute(values, steps):
    pairs = [
        (device(*here, r), device(*there, r)) for here, there in steps for r in range(HALF)
    ]
    return lax.ppermute(values, ("parts", "fft"), pairs)


BESIDE = [((q, b), (1 - q, b)) for q in range(2) for b in range(2)]
ALONG = [((q, b), (q, 1 - b)) for q in range(2) for b in range(2)]
CYCLE = [((0, 0), (0, 1)), ((1, 0), (0, 0)), ((1, 1), (1, 0)), ((0, 1), (1, 1))]
ACROSS = [((0, 1), (1, 0)), ((1, 0), (0, 1))]


def after(values, others):
    return lax.optimization_barrier((values, others))[0]


def arrive(potential, direction, q, b):
    half = XB // CHUNKS // 2

    def sides(c):
        lower, upper = (
            jnp.concatenate(
                [v[:, (2 * c + x) * half : (2 * c + x + 1) * half] for v in (potential, direction)]
            )
            for x in range(2)
        )
        return jnp.where(q == 0, lower, upper), jnp.where(q == 0, upper, lower)

    keep, give = sides(0)
    potential, direction = after((potential, direction), give)
    beside = permute(give, BESIDE)
    kept, given = zip(*[sides(c) for c in range(1, CHUNKS)])
    rest = permute(after(jnp.concatenate(given), beside), BESIDE)
    chunks = []
    along = ()
    for c in range(CHUNKS):
        if c:
            keep, beside = kept[c - 1], rest[4 * (c - 1) : 4 * c]
        own = jnp.where(q == b, keep, beside)
        give = jnp.where(q == b, beside, keep)
        along = permute(after(give, along), ALONG)
        chunks.append((own, along))
    return chunks


def depart(near, far):
    return permute(near, CYCLE), permute(far, ACROSS), far


def settle(once, twice, far, q, b):
    same = jnp.where(q == b, far, once)
    rest = jnp.where(q == b, once, twice)
    return jnp.where(q == 0, same, rest), jnp.where(q == 0, rest, same)


def blocked_body(potential, direction, block_index, block_weights):
    q = lax.axis_index("parts")
    b = lax.axis_index("fft") // HALF
    place = jnp.stack([b, q]).astype(jnp.int32)
    chunks = arrive(potential, direction, q, b)
    whi, wlo = split_weights(block_weights)
    by_column = column_constants()
    column = tuple(jnp.asarray(v) for v in split_constant(by_column))
    row = tuple(jnp.asarray(v) for v in split_constant(by_column.transpose(0, 2, 1)))
    weights = [(whi[a], wlo[a]) for a in range(ANGLES)]
    angles = range(ANGLES)
    arrived = [[] for _ in angles]
    bases = [[] for _ in angles]
    ahead = [[] for _ in angles]
    fields = ()
    for c, (own, along) in enumerate(chunks):
        further = chunks[c + 1][1] if c + 1 < CHUNKS else ()
        own = after(own, fields)
        for a in angles:
            fields, (front,) = enter(place, [block_index[a]], own, along, [weights[a]], row)
            arrived[a].append(exchange(after(fields, further) if a else fields))
            bases[a].append(0)
            ahead[a].append(front)
    carried = []
    for a in angles:
        out, kept = middle(arrived[a], tuple(bases[a]), column)
        carried.append((exchange(out), kept))
    backs = [exchange(detector(out, row)) for out, _ in carried]
    most, half = CHUNKS // 2, XB // CHUNKS // 2
    spans = (most, CHUNKS - most)

    def home(a, back, first, before, spans):
        t0 = ahead[a][first : first + sum(spans)]
        return leave(place, block_index[a], back, t0, weights[a], row, before, spans)

    early = pull(backs[0], carried[0][1], column, spans)
    late = pull(backs[1], carried[1][1], column, spans)
    back = exchange(early[0])
    next_back = exchange(late[0])
    (start,) = home(0, back, 0, (), spans[:1])
    back = exchange(after(early[1], start))
    totals = home(1, next_back, 0, start, spans[:1])
    next_back = exchange(after(late[1], totals))
    (start,) = home(0, back, most, (), spans[1:])
    totals += home(1, next_back, most, start, spans[1:])
    pieces = []
    leaving = [depart(*total) for total in totals]
    total = totals[-1]
    for span, moved in zip(spans, after(leaving, total)):
        lower, upper = settle(*moved, q, b)
        for c in range(span):
            pieces += [v[:, c * half : (c + 1) * half] for v in (lower, upper)]
    return jnp.concatenate(pieces, axis=1)


def transform_table(count_in, count_out, length, orient):
    first = jnp.arange(count_in, dtype=jnp.int32)[:, None]
    second = jnp.arange(count_out, dtype=jnp.int32)[None, :]
    phases = orient * 2.0 * math.pi / length * (first * second % length).astype(jnp.float32)
    cosine = jnp.cos(phases)
    sine_part = jnp.sin(phases)
    return jnp.stack([jnp.stack([cosine, sine_part]), jnp.stack([-sine_part, cosine])])


def twiddle_pair(count_a, count_b, length, orient):
    first = jnp.arange(count_a, dtype=jnp.int32)[:, None]
    second = jnp.arange(count_b, dtype=jnp.int32)[None, :]
    phases = orient * 2.0 * math.pi / length * (first * second % length).astype(jnp.float32)
    return (jnp.cos(phases), jnp.sin(phases))


def spread_turn(peer_count, row_count, slot_count, orient):
    turn_re, turn_im = twiddle_pair(peer_count, row_count, NX, orient)
    shape_three = (row_count, peer_count, slot_count)
    wide_re = jnp.broadcast_to(turn_re.T[:, :, None], shape_three).reshape(
        row_count, peer_count * slot_count
    )
    wide_im = jnp.broadcast_to(turn_im.T[:, :, None], shape_three).reshape(
        row_count, peer_count * slot_count
    )
    return (wide_re, wide_im)


def complex_times(values, real_part, imag_part):
    first = values[:, 0]
    second = values[:, 1]
    return jnp.stack(
        [first * real_part - second * imag_part, first * imag_part + second * real_part], axis=1
    )


def one_hot(index_rows, block_count):
    return (index_rows[..., None] == jnp.arange(block_count, dtype=jnp.int32)).astype(jnp.float32)


def rotate(values, selector, matrices):
    height = values.shape[1]
    blocked = values.reshape(2, height, NB, BLK)
    picked = jnp.einsum("cyni,bsn->cybsi", blocked, selector, precision=PRECISE)
    rotated = jnp.einsum("cybsi,bsio->cybo", picked, matrices, precision=PRECISE)
    return rotated.reshape(2, height, SL, NX)


def rotate_back(values, selector, matrices):
    height = values.shape[1]
    blocked = values.reshape(2, height, NB, BLK)
    spread_out = jnp.einsum("cybo,bsio->cybsi", blocked, matrices, precision=PRECISE)
    summed = jnp.einsum("cybsi,bsn->cyni", spread_out, selector, precision=PRECISE)
    return summed.reshape(2, height, SL * NX)


def fresnel(peer_count, row_count, slot_count, orient):
    position_high = jnp.arange(row_count, dtype=jnp.int32)[:, None]
    position_low = jnp.arange(peer_count, dtype=jnp.int32)[None, :]
    freq_y = position_low + peer_count * position_high
    freq_y = jnp.where(freq_y < NX // 2, freq_y, freq_y - NX)
    position = lax.axis_index("fft") * slot_count + jnp.arange(slot_count, dtype=jnp.int32)
    freq_x = position // XB + XA * (position % XB)
    freq_x = jnp.where(freq_x < NX // 2, freq_x, freq_x - NX)
    squares = ((freq_y * freq_y)[:, :, None] + (freq_x * freq_x)[None, None, :]) % (2 * NX)
    phases = orient * -math.pi / NX * squares.astype(jnp.float32)
    scaling = 1.0 / (NX * NX)
    phases = phases.reshape(row_count, peer_count * slot_count)
    return (jnp.cos(phases) * scaling, jnp.sin(phases) * scaling)


def propagate(fields, kernel, peer_count, row_count, slot_count):
    field_count = fields.shape[0]
    groups = XB // slot_count
    shaped = fields.reshape(field_count, 2, row_count, XA, XB)
    partial_x = jnp.einsum(
        "fcrab,cdak->fdrkb", shaped, transform_table(XA, XA, XA, -1.0), precision=PRECISE
    )
    twist_re, twist_im = twiddle_pair(XA, XB, NX, -1.0)
    partial_x = complex_times(partial_x, twist_re, twist_im)
    partial_x = jnp.einsum(
        "fcrkb,cdbt->fdrkt", partial_x, transform_table(XB, XB, XB, -1.0), precision=PRECISE
    )
    partial_x = partial_x.reshape(field_count, 2, row_count, XA, groups, slot_count)
    outgoing = partial_x.transpose(0, 1, 3, 4, 2, 5).reshape(
        field_count, 2, peer_count, row_count * slot_count
    )
    forward_re, forward_im = spread_turn(peer_count, row_count, slot_count, -1.0)
    inverse_re, inverse_im = spread_turn(peer_count, row_count, slot_count, 1.0)
    wide = peer_count * slot_count
    incoming = lax.all_to_all(outgoing, "fft", split_axis=2, concat_axis=2, tiled=True)
    item_count = incoming.shape[0]
    lattice = incoming.reshape(item_count, 2, peer_count, row_count, slot_count)
    lattice = jnp.einsum(
        "fcprs,cdpk->fdrks",
        lattice,
        transform_table(peer_count, peer_count, peer_count, -1.0),
        precision=PRECISE,
    )
    lattice = lattice.reshape(item_count, 2, row_count, wide)
    lattice = complex_times(lattice, forward_re, forward_im)
    lattice = jnp.einsum(
        "fcrq,cdrm->fdmq",
        lattice,
        transform_table(row_count, row_count, row_count, -1.0),
        precision=PRECISE,
    )
    lattice = complex_times(lattice, kernel[0], kernel[1])
    lattice = jnp.einsum(
        "fcmq,cdmr->fdrq",
        lattice,
        transform_table(row_count, row_count, row_count, 1.0),
        precision=PRECISE,
    )
    lattice = complex_times(lattice, inverse_re, inverse_im)
    lattice = lattice.reshape(item_count, 2, row_count, peer_count, slot_count)
    lattice = jnp.einsum(
        "fcrks,cdkp->fdprs",
        lattice,
        transform_table(peer_count, peer_count, peer_count, 1.0),
        precision=PRECISE,
    )
    returning = lax.all_to_all(
        lattice.reshape(item_count, 2, peer_count, row_count * slot_count),
        "fft",
        split_axis=2,
        concat_axis=2,
        tiled=True,
    )
    restored = returning.reshape(item_count, 2, XA, groups, row_count, slot_count)
    matrix_back = transform_table(XB, XB, XB, 1.0).reshape(2, 2, groups, slot_count, XB)
    restored = jnp.einsum("fckjrs,cdjsb->fdrkb", restored, matrix_back, precision=PRECISE)
    back_re, back_im = twiddle_pair(XA, XB, NX, 1.0)
    restored = complex_times(restored, back_re, back_im)
    restored = jnp.einsum(
        "fcrkb,cdkn->fdrnb", restored, transform_table(XA, XA, XA, 1.0), precision=PRECISE
    )
    return restored.reshape(item_count, 2, row_count, NX)


def general_body(potential, direction, block_index, block_weights):
    row_count = potential.shape[1]
    peer_count = lax.axis_size("fft")
    slot_count = NX // peer_count
    ahead = fresnel(peer_count, row_count, slot_count, 1.0)
    behind = fresnel(peer_count, row_count, slot_count, -1.0)
    accumulated = jnp.zeros(potential.shape, jnp.float32)
    for angle_index in range(ANGLES):
        selector = one_hot(block_index[angle_index], NB)
        matrices = block_weights[angle_index]
        rotated = rotate(potential, selector, matrices)
        tangent = rotate(direction, selector, matrices)
        damping = jnp.exp(-rotated[1])
        trans_re = damping * jnp.cos(rotated[0])
        trans_im = damping * jnp.sin(rotated[0])
        wave_re = jnp.ones((row_count, NX), jnp.float32)
        wave_im = jnp.zeros((row_count, NX), jnp.float32)
        dwave_re = jnp.zeros((row_count, NX), jnp.float32)
        dwave_im = jnp.zeros((row_count, NX), jnp.float32)
        stored = []
        for slice_index in range(SL):
            t_re = trans_re[:, slice_index]
            t_im = trans_im[:, slice_index]
            d_re = tangent[0][:, slice_index]
            d_im = tangent[1][:, slice_index]
            phi_re = t_re * wave_re - t_im * wave_im
            phi_im = t_re * wave_im + t_im * wave_re
            dphi_re = -(d_re * phi_im + d_im * phi_re) + t_re * dwave_re - t_im * dwave_im
            dphi_im = d_re * phi_re - d_im * phi_im + t_re * dwave_im + t_im * dwave_re
            stored.append((phi_re, phi_im))
            packed = jnp.stack([jnp.stack([phi_re, phi_im]), jnp.stack([dphi_re, dphi_im])])
            propagated = propagate(packed, ahead, peer_count, row_count, slot_count)
            wave_re = propagated[0, 0]
            wave_im = propagated[0, 1]
            dwave_re = propagated[1, 0]
            dwave_im = propagated[1, 1]
        change = 2.0 * (wave_re * dwave_re + wave_im * dwave_im)
        back_re = 2.0 * change * wave_re
        back_im = 2.0 * change * wave_im
        grad_re = [None] * SL
        grad_im = [None] * SL
        for slice_index in reversed(range(SL)):
            pulled = propagate(
                jnp.stack([back_re, back_im])[None], behind, peer_count, row_count, slot_count
            )
            pb_re = pulled[0, 0]
            pb_im = pulled[0, 1]
            phi_re, phi_im = stored[slice_index]
            grad_re[slice_index] = phi_re * pb_im - phi_im * pb_re
            grad_im[slice_index] = -(phi_re * pb_re + phi_im * pb_im)
            t_re = trans_re[:, slice_index]
            t_im = trans_im[:, slice_index]
            back_re = t_re * pb_re + t_im * pb_im
            back_im = t_re * pb_im - t_im * pb_re
        gradient = jnp.stack([jnp.stack(grad_re, axis=1), jnp.stack(grad_im, axis=1)])
        accumulated = accumulated + rotate_back(gradient, selector, matrices)
    return accumulated


def body(potential, direction, block_index, block_weights):
    if lax.axis_size("parts") == 2 and lax.axis_size("fft") == XA:
        return blocked_body(potential, direction, block_index, block_weights)
    return general_body(potential, direction, block_index, block_weights)


def solution(mesh):
    return jax.shard_map(
        body,
        mesh=mesh,
        in_specs=(P("parts", "fft", None), P("parts", "fft", None), P(), P()),
        out_specs=P("parts", "fft", None),
        check_vma=False,
    )
```
